32 devices in a mesh: aisle: 8 (over y, x, core), span: 4 (over z).
Axes of the slice: x: 2, y: 2, z: 4, core: 2. Of those that a mesh axis runs over, the one named last changes fastest.
Arguments:
- room_pops: float32 [19, 32, 16, 512], P(None, 'aisle', 'span'), may hold values from 0.5 to 1.5
- plenum_pops: float32 [19, 32, 16, 128], P(None, 'aisle', 'span'), may hold values from 0.5 to 1.5
- tile_cell: int32 [256], P('aisle'), may hold values from 0 to 15
- tile_owner: int32 [256, 1], P('aisle'), may hold values from 0 to 3; in each aligned block of 8 rows (0 to 7, 8 to 15, ...) at most 4 rows name the same one
- tile_class: int32 [256], P('aisle'), may hold values from 0 to 3
Outputs:
- room_next: float32 [19, 32, 16, 512], P(None, 'aisle', 'span')
- plenum_next: float32 [19, 32, 16, 128], P(None, 'aisle', 'span')
The draws below stay inside these ranges and needn't reach their ends.
Inputs may be any that keep to these rules, and one draw needn't show every extreme that they name: `tile_owner`: among the 8 rows of each aligned block of rows, at most 4 name the same owner, and exactly 4 do in some blocks.
All inputs are finite; a program needn't handle non-finite values.
Results may differ from the reference program's by a relative error of at most 0.00005.
Values sent between devices are 32-bit elements; how exact they have to be, the bound alone decides.
No kernel may reach another device: no remote copies, remote signals or barrier semaphores. Data moves between devices by JAX's collectives and lax.ppermute only.
A program may use at most 64 MiB of HBM per device.

```python
import math
import jax
import jax.numpy as jnp
import numpy as np
from jax import lax

CA = 4
CS = 4
HR = 512
HP = 128
CAP = 4
NT = 8
TILES = 256
NXA = 32
NYS = 16
N_SPAN = 4


def touch_ends(drawn, stream_key, low, high):
    extent = drawn.shape
    place = [jax.random.randint(jax.random.fold_in(stream_key, axis), (), 0, extent[axis]) for axis in range(len(extent))]
    drawn = drawn.at[tuple(place)].set(low)
    longest = extent.index(max(extent))
    place[longest] = (place[longest] + 1) % extent[longest]
    return drawn.at[tuple(place)].set(high)


def levels(key, dims, split, smallest, high):
    loudness, own = 1.0, jax.random.fold_in(key, 6)
    for position, blocks in split:
        heights = jnp.exp(jax.random.uniform(jax.random.fold_in(own, position), (blocks,), jnp.float32, smallest / len(split), high / len(split)))
        loudness = loudness * jnp.repeat(heights, dims[position] // blocks).reshape([-1 if axis == position else 1 for axis in range(len(dims))])
    return loudness


def deal_out(own_key, own, number, rows, amount, top, most, slope):
    ranking = jax.random.permutation(own_key, amount)
    packed, common = load_shares(amount, rows * top, most, slope, True), load_shares(amount, rows * top, most, slope, False)
    places = jnp.arange(amount)

    def named(tallies, offset_by):
        used = int((tallies > 0).sum())
        fixed = max(1, used // 4)
        shifted = fixed + (places - fixed + offset_by * (used - fixed)) % max(1, amount - fixed)
        return jnp.zeros((amount,), jnp.int32).at[ranking[jnp.where(places < fixed, places, shifted)]].set(jnp.asarray(tallies, jnp.int32))

    tallies = jnp.where(number % 4 == 0, named(packed, number // 4), named(common, number - number // 4 - 1))
    mixed = jax.random.permutation(jax.random.fold_in(own, 3), amount)
    giver, sink = mixed[0:amount // 2 * 2:2], mixed[1:amount // 2 * 2:2]
    room = jnp.minimum(tallies[giver] - 1, most - tallies[sink]) // 2
    room = jnp.where((giver == ranking[0]) | (sink == ranking[0]) | (tallies[sink] == 0), 0, jnp.maximum(room, 0))
    shifted = jax.random.randint(jax.random.fold_in(own, 4), (amount // 2,), 0, 1 << 20) % (room + 1)
    tallies = tallies.at[giver].add(-shifted).at[sink].add(shifted)
    members = jnp.searchsorted(jnp.cumsum(tallies), jnp.arange(rows * top), side="right").astype(jnp.int32)
    table = members.reshape(top, rows).T
    table = table[jax.random.permutation(jax.random.fold_in(own, 1), rows)]
    offset_by = jax.random.randint(jax.random.fold_in(own, 2), (rows, 1), 0, top)
    return jnp.take_along_axis(table, (jnp.arange(top)[None, :] + offset_by) % top, axis=1)


def load_shares(amount, total, bound, slope, full):
    weights = [(1 << 20) // math.isqrt(rank ** slope) + 1 for rank in range(1, amount + 1)]
    largest = bound if full else min(bound, max(-(-total // amount), total * weights[0] // sum(weights)))
    least = 1 if total - largest >= amount - 1 else 0
    holding, spare = [largest] + [least] * (amount - 1), total - largest - least * (amount - 1)
    while spare > 0:
        movable = [i for i in range(1, amount) if holding[i] < largest] or [i for i in range(1, amount) if holding[i] < bound]
        mass, remaining = sum([weights[i] for i in movable]), spare
        for i in movable:
            extra = min(bound - holding[i], max(1, remaining * weights[i] // mass), spare)
            holding[i] = holding[i] + extra
            spare = spare - extra
    return np.array(holding)


def setup_inputs(seed: int = 0) -> dict:
    key_list = jax.random.split(jax.random.key(seed), 6)
    room_pops = jnp.clip(0.5 + 1.0 * jax.random.uniform(key_list[0], (19, NXA, NYS, HR), jnp.float32) ** levels(key_list[0], (19, NXA, NYS, HR), ((1, 8), (2, 4)), -0.2, 0.2), 0.5, 1.5)
    plenum_pops = jnp.clip(0.5 + 1.0 * jax.random.uniform(key_list[1], (19, NXA, NYS, HP), jnp.float32) ** levels(key_list[1], (19, NXA, NYS, HP), ((1, 8), (2, 4)), -0.2, 0.2), 0.5, 1.5)
    tile_cell = touch_ends(jax.random.randint(key_list[2], (TILES,), 0, CA * CS), jax.random.fold_in(key_list[2], 1), 0, (CA * CS) - 1).astype(jnp.int32)
    tile_owner_keys = jax.random.split(jax.random.fold_in(key_list[3], 1), TILES // NT)
    tile_owner_turns = jax.random.permutation(jax.random.fold_in(key_list[3], 3), TILES // NT)
    tile_owner = jax.vmap(lambda own, number: deal_out(jax.random.fold_in(key_list[3], 2), own, number, NT, N_SPAN, 1, CAP, 2))(tile_owner_keys, tile_owner_turns).reshape((TILES, 1))
    tile_class = touch_ends(jax.random.randint(key_list[4], (TILES,), 0, 4), jax.random.fold_in(key_list[4], 1), 0, 3).astype(jnp.int32)
    return {"room_pops": room_pops, "plenum_pops": plenum_pops, "tile_cell": tile_cell, "tile_owner": tile_owner, "tile_class": tile_class}


VELOCITIES = [(0, 0, 0), (1, 0, 0), (-1, 0, 0), (0, 1, 0), (0, -1, 0), (0, 0, 1), (0, 0, -1),
              (1, 1, 0), (-1, -1, 0), (1, -1, 0), (-1, 1, 0), (1, 0, 1), (-1, 0, -1), (1, 0, -1),
              (-1, 0, 1), (0, 1, 1), (0, -1, -1), (0, 1, -1), (0, -1, 1)]
WEIGHTS = [1.0 / 3.0] + [1.0 / 18.0] * 6 + [1.0 / 36.0] * 12
UPWARD = [5, 11, 14, 15, 18]
OMEGA = 1.25


def collide(pops):
    weights = jnp.array(WEIGHTS, jnp.float32).reshape(19, 1, 1, 1)
    vel = jnp.array(VELOCITIES, jnp.float32)
    weighted = pops * weights
    rho = jnp.sum(weighted, axis=0)
    moment = jnp.tensordot(vel.T, weighted, axes=1, precision=lax.Precision.HIGHEST)
    speed = moment / rho
    usq = jnp.sum(speed * speed, axis=0)
    along = jnp.tensordot(vel, speed, axes=1, precision=lax.Precision.HIGHEST)
    equil = rho * (1.0 + 3.0 * along + 4.5 * along * along - 1.5 * usq)
    return pops - OMEGA * (pops - equil)


def clamp_move(field, sign, axis):
    size = field.shape[axis]
    if sign == 1:
        return jnp.concatenate([lax.slice_in_dim(field, 0, 1, axis=axis), lax.slice_in_dim(field, 0, size - 1, axis=axis)], axis=axis)
    if sign == -1:
        return jnp.concatenate([lax.slice_in_dim(field, 1, size, axis=axis), lax.slice_in_dim(field, size - 1, size, axis=axis)], axis=axis)
    return field


def stream(post):
    moved = []
    for index in range(19):
        cx, cy, cz = VELOCITIES[index]
        field = jnp.roll(post[index], cx, axis=0)
        field = clamp_move(field, cy, 1)
        field = clamp_move(field, cz, 2)
        moved.append(field)
    return jnp.stack(moved, 0)


def reference(room_pops, plenum_pops, tile_cell, tile_owner, tile_class):
    plenum_post = collide(plenum_pops)
    room_post = collide(room_pops)
    plenum_next = stream(plenum_post)
    room_moved = stream(room_post)
    rows = jnp.arange(TILES, dtype=jnp.int32)
    block_a = rows // (N_SPAN * NT)
    block_s = (rows // NT) % N_SPAN
    cell_a = tile_cell // CS
    cell_s = tile_cell % CS
    open_area = 0.15 * (tile_class.astype(jnp.float32) + 1.0)
    pos_x = block_a * CA + cell_a
    src_y = block_s * CS + cell_s
    dst_y = tile_owner[:, 0] * CS + cell_s
    upward = jnp.array(UPWARD, jnp.int32)
    jets = plenum_post[upward[:, None], pos_x[None, :], src_y[None, :], :] * open_area[None, :, None]
    room_next = room_moved.at[upward[:, None], pos_x[None, :], dst_y[None, :], :HP].add(jets)
    return room_next, plenum_next
```

```python
import functools

import jax
import jax.numpy as jnp
from jax import lax
from jax.experimental import pallas as pl
from jax.experimental.pallas import tpu as pltpu
from jax.sharding import PartitionSpec as P

VELOCITIES = [
    (0, 0, 0),
    (1, 0, 0),
    (-1, 0, 0),
    (0, 1, 0),
    (0, -1, 0),
    (0, 0, 1),
    (0, 0, -1),
    (1, 1, 0),
    (-1, -1, 0),
    (1, -1, 0),
    (-1, 1, 0),
    (1, 0, 1),
    (-1, 0, -1),
    (1, 0, -1),
    (-1, 0, 1),
    (0, 1, 1),
    (0, -1, -1),
    (0, 1, -1),
    (0, -1, 1),
]
UPWARD = [5, 11, 14, 15, 18]
OMEGA = 1.25
CAP = 4
X_UP = [q for q in range(19) if VELOCITIES[q][0] == 1]
X_DOWN = [q for q in range(19) if VELOCITIES[q][0] == -1]
Y_UP = [q for q in range(19) if VELOCITIES[q][1] == 1]
Y_DOWN = [q for q in range(19) if VELOCITIES[q][1] == -1]
F32 = jnp.float32
VMEM = pl.BlockSpec(memory_space=pltpu.VMEM)
HBM = pl.BlockSpec(memory_space=pltpu.HBM)


def collide(g):
    total = lambda i: g[i] + g[i + 1]
    apart = lambda i: g[i] - g[i + 1]
    dx, dy, dz = apart(1), apart(3), apart(5)
    d7, d9, d11, d13, d15, d17 = (apart(i) for i in (7, 9, 11, 13, 15, 17))
    edges = (total(7) + total(9)) + (total(11) + total(13)) + (total(15) + total(17))
    faces = total(1) + total(3) + total(5)
    rho = g[0] * (1.0 / 3.0) + faces * (1.0 / 18.0) + edges * (1.0 / 36.0)
    mx = dx * (1.0 / 18.0) + ((d7 + d9) + (d11 + d13)) * (1.0 / 36.0)
    my = dy * (1.0 / 18.0) + ((d7 - d9) + (d15 + d17)) * (1.0 / 36.0)
    mz = dz * (1.0 / 18.0) + ((d11 - d13) + (d15 - d17)) * (1.0 / 36.0)
    inv = 1.0 / rho
    base = OMEGA * rho - (1.5 * OMEGA) * inv * (mx * mx + my * my + mz * mz)
    square = (4.5 * OMEGA) * inv
    out = [None] * 19
    out[0] = base + (1.0 - OMEGA) * g[0]
    along = {1: mx, 3: my, 5: mz, 7: mx + my, 9: mx - my, 11: mx + mz, 13: mx - mz, 15: my + mz, 17: my - mz}
    for i, c in along.items():
        even = base + square * c * c
        odd = (3.0 * OMEGA) * c
        out[i] = (even + odd) + (1.0 - OMEGA) * g[i]
        out[i + 1] = (even - odd) + (1.0 - OMEGA) * g[i + 1]
    return out


def raised(value, cz):
    if cz == 0:
        return value
    size = value.shape[-1]
    lane = lax.broadcasted_iota(jnp.int32, value.shape, value.ndim - 1)
    if cz == 1:
        return jnp.where(lane == 0, value, pltpu.roll(value, 1, value.ndim - 1))
    return jnp.where(lane == size - 1, value, pltpu.roll(value, size - 1, value.ndim - 1))


def collide_kernel(sizes, relayed, room_in, plen_in, cell_in, owner_in, class_in, room_post, plen_post, swap_a, swap_b, *rest):
    ca, cs, hr, hp, n_span, per_brick = sizes
    jets = rest[:-7]
    columns, room_buf, plen_buf, cells, owners, classes, sems = rest[-7:]
    copies = [pltpu.make_async_copy(src, dst, sems.at[i]) for i, (src, dst) in enumerate(
        ((plen_in, plen_buf), (cell_in, cells), (owner_in, owners), (class_in, classes), (room_in, room_buf)))]
    for copy in copies:
        copy.start()
    for part in jets:
        part[...] = jnp.zeros_like(part)
    copies[0].wait()
    for x in range(ca):
        for h in range(0, hp, 128):
            post = collide([plen_buf[q, x, :, h : h + 128] for q in range(19)])
            for q in range(19):
                plen_post[q, x, :, h : h + 128] = post[q]
            for k, q in enumerate(UPWARD):
                for y in range(cs):
                    columns[x * cs + y, :, k * hp + h : k * hp + h + 128] = post[q][y : y + 1]
    for copy in copies[1:4]:
        copy.wait()
    here = lax.axis_index("span")
    first = here * per_brick

    def send_jet(i, carry):
        t = first + i
        owner, cell = owners[t, 0], cells[t]
        share = 0.15 * (classes[t].astype(F32) + 1.0)
        slot = lax.fori_loop(0, i, lambda j, n: n + (owners[first + j, 0] == owner).astype(jnp.int32), 0)
        column = share * columns[cell]
        if not relayed:
            jets[0][owner, slot] = column
            return carry
        apart = owner ^ here

        @pl.when(apart < 2)
        def _():
            jets[0][apart, slot] = column

        @pl.when(apart >= 2)
        def _():
            jets[1][apart - 2, slot] = column

        return carry

    lax.fori_loop(0, per_brick, send_jet, 0)
    copies[4].wait()

    def room_plane(x, carry):
        for h in range(0, hr, 128):
            post = collide([room_buf[q, x, :, h : h + 128] for q in range(19)])
            for q in range(19):
                room_post[q, x, :, h : h + 128] = post[q]
        return carry

    lax.fori_loop(0, ca, room_plane, 0)
    even = lax.axis_index("aisle") % 2 == 0
    for k in range(5):
        up, down = X_UP[k], X_DOWN[k]
        for source, low, high in ((room_post, 0, hr), (plen_post, hr, hr + hp)):
            rising = raised(source[up, ca - 1], VELOCITIES[up][2])
            falling = raised(source[down, 0], VELOCITIES[down][2])
            swap_a[k, :, low:high] = jnp.where(even, rising, falling)
            swap_b[k, :, low:high] = jnp.where(even, falling, rising)


def local_kernel(sizes, room_post, plen_post, cell_in, owner_in, room_part, plen_part, span_up, span_down, places):
    ca, cs, hr, hp, n_span, per_brick = sizes
    for source, dest, low, high in ((plen_post, plen_part, hr, hr + hp), (room_post, room_part, 0, hr)):
        for q in range(19):
            cx, cy, cz = VELOCITIES[q]
            for x in range(ca):
                if not 0 <= x - cx < ca:
                    continue
                value = raised(source[q, x - cx], cz)
                if cy == 1:
                    span_up[Y_UP.index(q), x : x + 1, low:high] = value[cs - 1 : cs]
                    dest[q, x, 0:1] = value[0:1]
                    dest[q, x, 1:cs] = value[: cs - 1]
                elif cy == -1:
                    span_down[Y_DOWN.index(q), x : x + 1, low:high] = value[0:1]
                    dest[q, x, cs - 1 : cs] = value[cs - 1 : cs]
                    dest[q, x, : cs - 1] = value[1:cs]
                else:
                    dest[q, x] = value
    places[...] = jnp.zeros_like(places)
    here = lax.axis_index("span")
    row = lax.broadcasted_iota(jnp.int32, (cs, 128), 0)

    def brick(b, carry):
        def place(i, slot):
            t = b * per_brick + i
            mine = owner_in[t, 0] == here

            @pl.when(mine)
            def _():
                cell = cell_in[t]
                places[b * CAP + slot, cell // cs] = (row == cell % cs).astype(F32)

            return slot + mine.astype(jnp.int32)

        lax.fori_loop(0, per_brick, place, 0)
        return carry

    lax.fori_loop(0, n_span, brick, 0)


def corner_rows(ca, cs, even, got_a, got_b, rows):
    for q, plane, y in ((7, Y_UP, cs - 1), (10, Y_UP, cs - 1), (8, Y_DOWN, 0), (9, Y_DOWN, 0)):
        if VELOCITIES[q][0] == 1:
            k, x = X_UP.index(q), 0
            row = jnp.where(even, got_b[k, y : y + 1], got_a[k, y : y + 1])
        else:
            k, x = X_DOWN.index(q), ca - 1
            row = jnp.where(even, got_a[k, y : y + 1], got_b[k, y : y + 1])
        rows(plane, q, x, row)


def pack_kernel(sizes, relayed, got_a, got_b, span_up, span_down, *rest):
    ca, cs, hr, hp, n_span, per_brick = sizes
    if relayed:
        jets, got_jets, cross_a, cross_b = rest
    else:
        cross_a, cross_b = rest
    here = lax.axis_index("span")
    even = lax.axis_index("aisle") % 2 == 0
    low = here % 2 == 0
    for k in range(5):
        rising, falling = span_up[k], span_down[k]
        cross_a[k] = jnp.where(low, rising, falling)
        cross_b[k] = jnp.where(low, falling, rising)

    def rows(plane, q, x, row):
        k = plane.index(q)

        @pl.when(low == (plane is Y_UP))
        def _():
            cross_a[k, x : x + 1] = row

        @pl.when(low != (plane is Y_UP))
        def _():
            cross_b[k, x : x + 1] = row

    corner_rows(ca, cs, even, got_a, got_b, rows)
    if relayed:
        for s in range(CAP):
            cross_a[5, s : s + 1] = jets[1, s]
            cross_a[6, s : s + 1] = got_jets[1, s]


def jet_sums(sizes, start, places, bricks, put):
    ca, cs, hr, hp, n_span, per_brick = sizes
    for x in range(ca):
        marks = [[places[b * CAP + s, x] for s in range(CAP)] for b, _ in bricks]
        for k in range(5):
            for h in range(0, hp, 128):
                total = start(k, x, h)
                for (_, jet), brick_marks in zip(bricks, marks):
                    for s in range(CAP):
                        total = total + brick_marks[s] * jet(s, k * hp + h)
                put(k, x, h, total)


def aisle_kernel(sizes, relayed, room_in, plen_in, got_a, got_b, jets, got_jets, places, room, plen, inflow):
    ca, cs, hr, hp, n_span, per_brick = sizes
    even = lax.axis_index("aisle") % 2 == 0
    here = lax.axis_index("span")
    for k in range(5):
        for q, x, first, second in ((X_UP[k], 0, got_b, got_a), (X_DOWN[k], ca - 1, got_a, got_b)):
            cy = VELOCITIES[q][1]
            for dest, low, high in ((plen, hr, hr + hp), (room, 0, hr)):
                value = jnp.where(even, first[k, :, low:high], second[k, :, low:high])
                if cy == 1:
                    dest[q, x, 0:1] = value[0:1]
                    dest[q, x, 1:cs] = value[: cs - 1]
                elif cy == -1:
                    dest[q, x, cs - 1 : cs] = value[cs - 1 : cs]
                    dest[q, x, : cs - 1] = value[1:cs]
                else:
                    dest[q, x] = value

    def put(k, x, h, total):
        inflow[k, x, :, h : h + 128] = total

    if relayed:
        own = (here, lambda s, h: jets[0, s, :, h : h + 128])
        second = (here ^ 2, lambda s, h: got_jets[0, s, :, h : h + 128])
        jet_sums(sizes, lambda k, x, h: jnp.zeros((cs, 128), F32), places, [own, second], put)
    else:
        inflow[...] = jnp.zeros_like(inflow)

        def brick(b, carry):
            one = (b, lambda s, h: got_jets[b, s, :, h : h + 128])
            jet_sums(sizes, lambda k, x, h: inflow[k, x, :, h : h + 128], places, [one], put)
            return carry

        lax.fori_loop(0, n_span, brick, 0)


def finish_kernel(sizes, relayed, room_in, plen_in, got_a, got_b, places, inflow, room, plen, room_out, plen_out, sems):
    ca, cs, hr, hp, n_span, per_brick = sizes
    here = lax.axis_index("span")
    low = here % 2 == 0

    def enter(got, up):
        planes, y = (Y_UP, 0) if up else (Y_DOWN, cs - 1)
        for k, q in enumerate(planes):
            for x in range(ca):
                plen[q, x, y : y + 1] = got[k, x : x + 1, hr : hr + hp]
                room[q, x, y : y + 1] = got[k, x : x + 1, 0:hr]

    @pl.when(low)
    def _():
        enter(got_a, False)

    @pl.when(jnp.logical_not(low))
    def _():
        enter(got_a, True)

    @pl.when(jnp.logical_and(low, here > 0))
    def _():
        enter(got_b, True)

    @pl.when(jnp.logical_and(jnp.logical_not(low), here < n_span - 1))
    def _():
        enter(got_b, False)

    plen_copy = pltpu.make_async_copy(plen, plen_out, sems.at[0])
    plen_copy.start()
    bricks = []
    if relayed:
        bricks = [(here ^ 1, lambda s, h: got_a[5, s : s + 1, h : h + 128]),
                  (here ^ 3, lambda s, h: got_a[6, s : s + 1, h : h + 128])]

    def put(k, x, h, total):
        room[UPWARD[k], x, :, h : h + 128] = total

    jet_sums(sizes, lambda k, x, h: room[UPWARD[k], x, :, h : h + 128] + inflow[k, x, :, h : h + 128], places, bricks, put)
    room_copy = pltpu.make_async_copy(room, room_out, sems.at[1])
    room_copy.start()
    plen_copy.wait()
    room_copy.wait()


def call(kernel, outs, in_specs, out_specs=None, scratch=(), aliases={}, flops=100_000, moved=1_000_000):
    return pl.pallas_call(
        kernel,
        out_shape=outs,
        in_specs=in_specs,
        out_specs=[VMEM] * len(outs) if out_specs is None else out_specs,
        scratch_shapes=list(scratch),
        input_output_aliases=aliases,
        cost_estimate=pl.CostEstimate(flops=flops, bytes_accessed=moved, transcendentals=0),
        compiler_params=pltpu.CompilerParams(vmem_limit_bytes=40 * 2**20),
    )


def swap(value, axis, odd, wraps):
    count = lax.axis_size(axis)
    pairs = []
    for i in range(count):
        j = (i ^ 1) if not odd else (i + 1 if i % 2 else i - 1)
        if wraps or 0 <= j < count:
            pairs.append((i, j % count))
    return lax.ppermute(value, axis, pairs)


def shards(room_pops, plenum_pops, tile_cell, tile_owner, tile_class):
    n_span = lax.axis_size("span")
    _, ca, cs, hr = room_pops.shape
    hp = plenum_pops.shape[3]
    rows = tile_cell.shape[0]
    per_brick = rows // n_span
    sizes = (ca, cs, hr, hp, n_span, per_brick)
    relayed = n_span == 4
    near = pltpu.VMEM
    room_shape, plen_shape = room_pops.shape, plenum_pops.shape
    halo_x, halo_y = (5, cs, hr + hp), (5, ca, hr + hp)
    smem = pl.BlockSpec(memory_space=pltpu.SMEM)

    jets_shape = (2 if relayed else n_span, CAP, 1, 5 * hp)
    room_post, plen_post, swap_a, swap_b, *jets = call(
        functools.partial(collide_kernel, sizes, relayed),
        [near(room_shape, F32), near(plen_shape, F32), near(halo_x, F32), near(halo_x, F32)]
        + [near(jets_shape, F32)] * (2 if relayed else 1),
        [HBM] * 5,
        scratch=[pltpu.VMEM((ca * cs, 1, 5 * hp), F32), pltpu.VMEM(room_shape, F32), pltpu.VMEM(plen_shape, F32),
                 pltpu.SMEM((rows,), jnp.int32), pltpu.SMEM((rows, 1), jnp.int32), pltpu.SMEM((rows,), jnp.int32),
                 pltpu.SemaphoreType.DMA((5,))],
    )(room_pops, plenum_pops, tile_cell, tile_owner, tile_class)

    got_a = swap(swap_a, "aisle", False, True)
    got_b = swap(swap_b, "aisle", True, True)
    if relayed:
        got_jets = lax.ppermute(jets[1], "span", [(i, i ^ 2) for i in range(4)])
    else:
        got_jets = lax.all_to_all(jets[0], "span", 0, 0, tiled=True)

    room_part, plen_part, span_up, span_down, places = call(
        functools.partial(local_kernel, sizes),
        [near(room_shape, F32), near(plen_shape, F32), near(halo_y, F32), near(halo_y, F32),
         near((n_span * CAP, ca, cs, 128), F32)],
        [VMEM, VMEM, smem, smem],
    )(room_post, plen_post, tile_cell, tile_owner)

    cross_a_shape = (7, ca, hr + hp) if relayed else halo_y
    cross_a, cross_b = call(
        functools.partial(pack_kernel, sizes, relayed),
        [near(cross_a_shape, F32), near(halo_y, F32)],
        [VMEM] * (6 if relayed else 4),
    )(got_a, got_b, span_up, span_down, *((jets[0], got_jets) if relayed else ()))

    in_a = swap(cross_a, "span", False, False)
    in_b = swap(cross_b, "span", True, False)
    room_part, plen_part, inflow = call(
        functools.partial(aisle_kernel, sizes, relayed),
        [near(room_shape, F32), near(plen_shape, F32), near((5, ca, cs, hp), F32)],
        [VMEM] * 7,
        aliases={0: 0, 1: 1},
    )(room_part, plen_part, got_a, got_b, jets[0], got_jets, places)

    _, _, room_next, plenum_next = call(
        functools.partial(finish_kernel, sizes, relayed),
        [near(room_shape, F32), near(plen_shape, F32), jax.ShapeDtypeStruct(room_shape, F32),
         jax.ShapeDtypeStruct(plen_shape, F32)],
        [VMEM] * 6,
        out_specs=[VMEM, VMEM, HBM, HBM],
        scratch=[pltpu.SemaphoreType.DMA((2,))],
        aliases={0: 0, 1: 1},
    )(room_part, plen_part, in_a, in_b, places, inflow)
    return room_next, plenum_next


def solution(mesh):
    return jax.shard_map(
        shards,
        mesh=mesh,
        in_specs=(
            P(None, "aisle", "span", None),
            P(None, "aisle", "span", None),
            P("aisle"),
            P("aisle", None),
            P("aisle"),
        ),
        out_specs=(P(None, "aisle", "span", None), P(None, "aisle", "span", None)),
        check_vma=False,
    )
```

```python
import functools

import jax
import jax.numpy as jnp
from jax import lax
from jax.experimental import pallas as pl
from jax.experimental.pallas import tpu as pltpu
from jax.sharding import PartitionSpec as P

VELOCITIES = [
    (0, 0, 0),
    (1, 0, 0),
    (-1, 0, 0),
    (0, 1, 0),
    (0, -1, 0),
    (0, 0, 1),
    (0, 0, -1),
    (1, 1, 0),
    (-1, -1, 0),
    (1, -1, 0),
    (-1, 1, 0),
    (1, 0, 1),
    (-1, 0, -1),
    (1, 0, -1),
    (-1, 0, 1),
    (0, 1, 1),
    (0, -1, -1),
    (0, 1, -1),
    (0, -1, 1),
]
UPWARD = [5, 11, 14, 15, 18]
OMEGA = 1.25
CAP = 4
X_UP = [q for q in range(19) if VELOCITIES[q][0] == 1]
X_DOWN = [q for q in range(19) if VELOCITIES[q][0] == -1]
Y_UP = [q for q in range(19) if VELOCITIES[q][1] == 1]
Y_DOWN = [q for q in range(19) if VELOCITIES[q][1] == -1]
F32 = jnp.float32
VMEM = pl.BlockSpec(memory_space=pltpu.VMEM)
HBM = pl.BlockSpec(memory_space=pltpu.HBM)


def collide(g):
    total = lambda i: g[i] + g[i + 1]
    apart = lambda i: g[i] - g[i + 1]
    dx, dy, dz = apart(1), apart(3), apart(5)
    d7, d9, d11, d13, d15, d17 = (apart(i) for i in (7, 9, 11, 13, 15, 17))
    edges = (total(7) + total(9)) + (total(11) + total(13)) + (total(15) + total(17))
    faces = total(1) + total(3) + total(5)
    rho = g[0] * (1.0 / 3.0) + faces * (1.0 / 18.0) + edges * (1.0 / 36.0)
    mx = dx * (1.0 / 18.0) + ((d7 + d9) + (d11 + d13)) * (1.0 / 36.0)
    my = dy * (1.0 / 18.0) + ((d7 - d9) + (d15 + d17)) * (1.0 / 36.0)
    mz = dz * (1.0 / 18.0) + ((d11 - d13) + (d15 - d17)) * (1.0 / 36.0)
    inv = 1.0 / rho
    base = OMEGA * rho - (1.5 * OMEGA) * inv * (mx * mx + my * my + mz * mz)
    square = (4.5 * OMEGA) * inv
    out = [None] * 19
    out[0] = base + (1.0 - OMEGA) * g[0]
    along = {1: mx, 3: my, 5: mz, 7: mx + my, 9: mx - my, 11: mx + mz, 13: mx - mz, 15: my + mz, 17: my - mz}
    for i, c in along.items():
        even = base + square * c * c
        odd = (3.0 * OMEGA) * c
        out[i] = (even + odd) + (1.0 - OMEGA) * g[i]
        out[i + 1] = (even - odd) + (1.0 - OMEGA) * g[i + 1]
    return out


def raised(value, cz):
    if cz == 0:
        return value
    size = value.shape[-1]
    lane = lax.broadcasted_iota(jnp.int32, value.shape, value.ndim - 1)
    if cz == 1:
        return jnp.where(lane == 0, value, pltpu.roll(value, 1, value.ndim - 1))
    return jnp.where(lane == size - 1, value, pltpu.roll(value, size - 1, value.ndim - 1))


def collide_kernel(sizes, relayed, room_in, plen_in, cell_in, owner_in, class_in, room_post, plen_post, swap_a, swap_b, *rest):
    ca, cs, hr, hp, n_span, per_brick = sizes
    jets = rest[:-7]
    columns, room_buf, plen_buf, cells, owners, classes, sems = rest[-7:]
    copies = [pltpu.make_async_copy(src, dst, sems.at[i]) for i, (src, dst) in enumerate(
        ((plen_in, plen_buf), (cell_in, cells), (owner_in, owners), (class_in, classes), (room_in, room_buf)))]
    for copy in copies:
        copy.start()
    for part in jets:
        part[...] = jnp.zeros_like(part)
    copies[0].wait()
    for x in range(ca):
        for h in range(0, hp, 128):
            post = collide([plen_buf[q, x, :, h : h + 128] for q in range(19)])
            for q in range(19):
                plen_post[q, x, :, h : h + 128] = post[q]
            for k, q in enumerate(UPWARD):
                for y in range(cs):
                    columns[x * cs + y, :, k * hp + h : k * hp + h + 128] = post[q][y : y + 1]
    for copy in copies[1:4]:
        copy.wait()
    here = lax.axis_index("span")
    first = here * per_brick

    def send_jet(i, carry):
        t = first + i
        owner, cell = owners[t], cells[t]
        share = 0.15 * (classes[t].astype(F32) + 1.0)
        slot = lax.fori_loop(0, i, lambda j, n: n + (owners[first + j] == owner).astype(jnp.int32), 0)
        column = share * columns[cell]
        if not relayed:
            jets[0][owner, slot] = column
            return carry
        apart = owner ^ here

        @pl.when(apart < 2)
        def _():
            jets[0][apart, slot] = column

        @pl.when(apart >= 2)
        def _():
            jets[1][apart - 2, slot] = column

        return carry

    lax.fori_loop(0, per_brick, send_jet, 0)
    copies[4].wait()

    def room_plane(x, carry):
        for h in range(0, hr, 128):
            post = collide([room_buf[q, x, :, h : h + 128] for q in range(19)])
            for q in range(19):
                room_post[q, x, :, h : h + 128] = post[q]
        return carry

    lax.fori_loop(0, ca, room_plane, 0)
    even = lax.axis_index("aisle") % 2 == 0
    for k in range(5):
        up, down = X_UP[k], X_DOWN[k]
        for source, low, high in ((room_post, 0, hr), (plen_post, hr, hr + hp)):
            rising = raised(source[up, ca - 1], VELOCITIES[up][2])
            falling = raised(source[down, 0], VELOCITIES[down][2])
            swap_a[k, :, low:high] = jnp.where(even, rising, falling)
            swap_b[k, :, low:high] = jnp.where(even, falling, rising)


def local_kernel(sizes, room_post, plen_post, cell_in, owner_in, room_part, plen_part, span_up, span_down, places):
    ca, cs, hr, hp, n_span, per_brick = sizes
    for source, dest, low, high in ((plen_post, plen_part, hr, hr + hp), (room_post, room_part, 0, hr)):
        for q in range(19):
            cx, cy, cz = VELOCITIES[q]
            for x in range(ca):
                if not 0 <= x - cx < ca:
                    continue
                value = raised(source[q, x - cx], cz)
                if cy == 1:
                    span_up[Y_UP.index(q), x : x + 1, low:high] = value[cs - 1 : cs]
                    dest[q, x, 0:1] = value[0:1]
                    dest[q, x, 1:cs] = value[: cs - 1]
                elif cy == -1:
                    span_down[Y_DOWN.index(q), x : x + 1, low:high] = value[0:1]
                    dest[q, x, cs - 1 : cs] = value[cs - 1 : cs]
                    dest[q, x, : cs - 1] = value[1:cs]
                else:
                    dest[q, x] = value
    places[...] = jnp.zeros_like(places)
    here = lax.axis_index("span")
    row = lax.broadcasted_iota(jnp.int32, (cs, 128), 0)

    def brick(b, carry):
        def place(i, slot):
            t = b * per_brick + i
            mine = owner_in[t] == here

            @pl.when(mine)
            def _():
                cell = cell_in[t]
                places[b * CAP + slot, cell // cs] = (row == cell % cs).astype(F32)

            return slot + mine.astype(jnp.int32)

        lax.fori_loop(0, per_brick, place, 0)
        return carry

    lax.fori_loop(0, n_span, brick, 0)


def corner_rows(ca, cs, even, got_a, got_b, rows):
    for q, plane, y in ((7, Y_UP, cs - 1), (10, Y_UP, cs - 1), (8, Y_DOWN, 0), (9, Y_DOWN, 0)):
        if VELOCITIES[q][0] == 1:
            k, x = X_UP.index(q), 0
            row = jnp.where(even, got_b[k, y : y + 1], got_a[k, y : y + 1])
        else:
            k, x = X_DOWN.index(q), ca - 1
            row = jnp.where(even, got_a[k, y : y + 1], got_b[k, y : y + 1])
        rows(plane, q, x, row)


def pack_kernel(sizes, relayed, got_a, got_b, span_up, span_down, *rest):
    ca, cs, hr, hp, n_span, per_brick = sizes
    if relayed:
        jets, got_jets, cross_a, cross_b = rest
    else:
        cross_a, cross_b = rest
    here = lax.axis_index("span")
    even = lax.axis_index("aisle") % 2 == 0
    low = here % 2 == 0
    for k in range(5):
        rising, falling = span_up[k], span_down[k]
        cross_a[k] = jnp.where(low, rising, falling)
        cross_b[k] = jnp.where(low, falling, rising)

    def rows(plane, q, x, row):
        k = plane.index(q)

        @pl.when(low == (plane is Y_UP))
        def _():
            cross_a[k, x : x + 1] = row

        @pl.when(low != (plane is Y_UP))
        def _():
            cross_b[k, x : x + 1] = row

    corner_rows(ca, cs, even, got_a, got_b, rows)
    if relayed:
        for s in range(CAP):
            cross_a[5, s : s + 1] = jets[1, s]
            cross_a[6, s : s + 1] = got_jets[1, s]


def jet_sums(sizes, start, places, bricks, put):
    ca, cs, hr, hp, n_span, per_brick = sizes
    for x in range(ca):
        marks = [[places[b * CAP + s, x] for s in range(CAP)] for b, _ in bricks]
        for k in range(5):
            for h in range(0, hp, 128):
                total = start(k, x, h)
                for (_, jet), brick_marks in zip(bricks, marks):
                    for s in range(CAP):
                        total = total + brick_marks[s] * jet(s, k * hp + h)
                put(k, x, h, total)


def aisle_kernel(sizes, relayed, room_in, plen_in, got_a, got_b, jets, got_jets, places, room, plen, inflow):
    ca, cs, hr, hp, n_span, per_brick = sizes
    even = lax.axis_index("aisle") % 2 == 0
    here = lax.axis_index("span")
    for k in range(5):
        for q, x, first, second in ((X_UP[k], 0, got_b, got_a), (X_DOWN[k], ca - 1, got_a, got_b)):
            cy = VELOCITIES[q][1]
            for dest, low, high in ((plen, hr, hr + hp), (room, 0, hr)):
                value = jnp.where(even, first[k, :, low:high], second[k, :, low:high])
                if cy == 1:
                    dest[q, x, 0:1] = value[0:1]
                    dest[q, x, 1:cs] = value[: cs - 1]
                elif cy == -1:
                    dest[q, x, cs - 1 : cs] = value[cs - 1 : cs]
                    dest[q, x, : cs - 1] = value[1:cs]
                else:
                    dest[q, x] = value

    def put(k, x, h, total):
        inflow[k, x, :, h : h + 128] = total

    if relayed:
        own = (here, lambda s, h: jets[0, s, :, h : h + 128])
        second = (here ^ 2, lambda s, h: got_jets[0, s, :, h : h + 128])
        jet_sums(sizes, lambda k, x, h: jnp.zeros((cs, 128), F32), places, [own, second], put)
    else:
        inflow[...] = jnp.zeros_like(inflow)

        def brick(b, carry):
            one = (b, lambda s, h: got_jets[b, s, :, h : h + 128])
            jet_sums(sizes, lambda k, x, h: inflow[k, x, :, h : h + 128], places, [one], put)
            return carry

        lax.fori_loop(0, n_span, brick, 0)


def finish_kernel(sizes, relayed, room_in, plen_in, got_a, got_b, places, inflow, room, plen, room_out, plen_out, sems):
    ca, cs, hr, hp, n_span, per_brick = sizes
    here = lax.axis_index("span")
    low = here % 2 == 0

    def enter(got, up):
        planes, y = (Y_UP, 0) if up else (Y_DOWN, cs - 1)
        for k, q in enumerate(planes):
            for x in range(ca):
                plen[q, x, y : y + 1] = got[k, x : x + 1, hr : hr + hp]
                room[q, x, y : y + 1] = got[k, x : x + 1, 0:hr]

    @pl.when(low)
    def _():
        enter(got_a, False)

    @pl.when(jnp.logical_not(low))
    def _():
        enter(got_a, True)

    @pl.when(jnp.logical_and(low, here > 0))
    def _():
        enter(got_b, True)

    @pl.when(jnp.logical_and(jnp.logical_not(low), here < n_span - 1))
    def _():
        enter(got_b, False)

    plen_copy = pltpu.make_async_copy(plen, plen_out, sems.at[0])
    plen_copy.start()
    bricks = []
    if relayed:
        bricks = [(here ^ 1, lambda s, h: got_a[5, s : s + 1, h : h + 128]),
                  (here ^ 3, lambda s, h: got_a[6, s : s + 1, h : h + 128])]

    def put(k, x, h, total):
        room[UPWARD[k], x, :, h : h + 128] = total

    jet_sums(sizes, lambda k, x, h: room[UPWARD[k], x, :, h : h + 128] + inflow[k, x, :, h : h + 128], places, bricks, put)
    room_copy = pltpu.make_async_copy(room, room_out, sems.at[1])
    room_copy.start()
    plen_copy.wait()
    room_copy.wait()


def call(kernel, outs, in_specs, out_specs=None, scratch=(), aliases={}, flops=100_000, moved=1_000_000):
    return pl.pallas_call(
        kernel,
        out_shape=outs,
        in_specs=in_specs,
        out_specs=[VMEM] * len(outs) if out_specs is None else out_specs,
        scratch_shapes=list(scratch),
        input_output_aliases=aliases,
        cost_estimate=pl.CostEstimate(flops=flops, bytes_accessed=moved, transcendentals=0),
        compiler_params=pltpu.CompilerParams(vmem_limit_bytes=40 * 2**20),
    )


def swap(value, axis, odd, wraps):
    count = lax.axis_size(axis)
    pairs = []
    for i in range(count):
        j = (i ^ 1) if not odd else (i + 1 if i % 2 else i - 1)
        if wraps or 0 <= j < count:
            pairs.append((i, j % count))
    return lax.ppermute(value, axis, pairs)


def shards(room_pops, plenum_pops, tile_cell, tile_owner, tile_class):
    n_span = lax.axis_size("span")
    _, ca, cs, hr = room_pops.shape
    hp = plenum_pops.shape[3]
    rows = tile_cell.shape[0]
    per_brick = rows // n_span
    sizes = (ca, cs, hr, hp, n_span, per_brick)
    relayed = n_span == 4
    tile_owner = tile_owner.reshape(rows)
    far = lambda value: pltpu.with_memory_space_constraint(value, pltpu.HBM)
    near = pltpu.VMEM
    room_shape, plen_shape = room_pops.shape, plenum_pops.shape
    halo_x, halo_y = (5, cs, hr + hp), (5, ca, hr + hp)
    smem = pl.BlockSpec(memory_space=pltpu.SMEM)

    jets_shape = (2 if relayed else n_span, CAP, 1, 5 * hp)
    room_post, plen_post, swap_a, swap_b, *jets = call(
        functools.partial(collide_kernel, sizes, relayed),
        [near(room_shape, F32), near(plen_shape, F32), near(halo_x, F32), near(halo_x, F32)]
        + [near(jets_shape, F32)] * (2 if relayed else 1),
        [HBM] * 5,
        scratch=[pltpu.VMEM((ca * cs, 1, 5 * hp), F32), pltpu.VMEM(room_shape, F32), pltpu.VMEM(plen_shape, F32),
                 pltpu.SMEM((rows,), jnp.int32), pltpu.SMEM((rows,), jnp.int32), pltpu.SMEM((rows,), jnp.int32),
                 pltpu.SemaphoreType.DMA((5,))],
    )(far(room_pops), far(plenum_pops), far(tile_cell), far(tile_owner), far(tile_class))

    got_a = swap(swap_a, "aisle", False, True)
    got_b = swap(swap_b, "aisle", True, True)
    if relayed:
        got_jets = lax.ppermute(jets[1], "span", [(i, i ^ 2) for i in range(4)])
    else:
        got_jets = lax.all_to_all(jets[0], "span", 0, 0, tiled=True)

    room_part, plen_part, span_up, span_down, places = call(
        functools.partial(local_kernel, sizes),
        [near(room_shape, F32), near(plen_shape, F32), near(halo_y, F32), near(halo_y, F32),
         near((n_span * CAP, ca, cs, 128), F32)],
        [VMEM, VMEM, smem, smem],
    )(room_post, plen_post, tile_cell, tile_owner)

    cross_a_shape = (7, ca, hr + hp) if relayed else halo_y
    cross_a, cross_b = call(
        functools.partial(pack_kernel, sizes, relayed),
        [near(cross_a_shape, F32), near(halo_y, F32)],
        [VMEM] * (6 if relayed else 4),
    )(got_a, got_b, span_up, span_down, *((jets[0], got_jets) if relayed else ()))

    in_a = swap(cross_a, "span", False, False)
    in_b = swap(cross_b, "span", True, False)
    room_part, plen_part, inflow = call(
        functools.partial(aisle_kernel, sizes, relayed),
        [near(room_shape, F32), near(plen_shape, F32), near((5, ca, cs, hp), F32)],
        [VMEM] * 7,
        aliases={0: 0, 1: 1},
    )(room_part, plen_part, got_a, got_b, jets[0], got_jets, places)

    _, _, room_next, plenum_next = call(
        functools.partial(finish_kernel, sizes, relayed),
        [near(room_shape, F32), near(plen_shape, F32), jax.ShapeDtypeStruct(room_shape, F32),
         jax.ShapeDtypeStruct(plen_shape, F32)],
        [VMEM] * 6,
        out_specs=[VMEM, VMEM, HBM, HBM],
        scratch=[pltpu.SemaphoreType.DMA((2,))],
        aliases={0: 0, 1: 1},
    )(room_part, plen_part, in_a, in_b, places, inflow)
    return room_next, plenum_next


def solution(mesh):
    return jax.shard_map(
        shards,
        mesh=mesh,
        in_specs=(
            P(None, "aisle", "span", None),
            P(None, "aisle", "span", None),
            P("aisle"),
            P("aisle", None),
            P("aisle"),
        ),
        out_specs=(P(None, "aisle", "span", None), P(None, "aisle", "span", None)),
        check_vma=False,
    )
```

```python
import functools

import jax
import jax.numpy as jnp
from jax import lax
from jax.experimental import pallas as pl
from jax.experimental.pallas import tpu as pltpu
from jax.sharding import PartitionSpec as P

VELOCITIES = [
    (0, 0, 0),
    (1, 0, 0),
    (-1, 0, 0),
    (0, 1, 0),
    (0, -1, 0),
    (0, 0, 1),
    (0, 0, -1),
    (1, 1, 0),
    (-1, -1, 0),
    (1, -1, 0),
    (-1, 1, 0),
    (1, 0, 1),
    (-1, 0, -1),
    (1, 0, -1),
    (-1, 0, 1),
    (0, 1, 1),
    (0, -1, -1),
    (0, 1, -1),
    (0, -1, 1),
]
UPWARD = [5, 11, 14, 15, 18]
OMEGA = 1.25
CAP = 4
X_UP = [q for q in range(19) if VELOCITIES[q][0] == 1]
X_DOWN = [q for q in range(19) if VELOCITIES[q][0] == -1]
Y_UP = [q for q in range(19) if VELOCITIES[q][1] == 1]
Y_DOWN = [q for q in range(19) if VELOCITIES[q][1] == -1]
F32 = jnp.float32
LANES = 128
VMEM = pl.BlockSpec(memory_space=pltpu.VMEM)
HBM = pl.BlockSpec(memory_space=pltpu.HBM)


def collide(g):
    total = lambda i: g[i] + g[i + 1]
    apart = lambda i: g[i] - g[i + 1]
    dx, dy, dz = apart(1), apart(3), apart(5)
    d7, d9, d11, d13, d15, d17 = (apart(i) for i in (7, 9, 11, 13, 15, 17))
    edges = (total(7) + total(9)) + (total(11) + total(13)) + (total(15) + total(17))
    faces = total(1) + total(3) + total(5)
    rho = g[0] * (1.0 / 3.0) + faces * (1.0 / 18.0) + edges * (1.0 / 36.0)
    mx = dx * (1.0 / 18.0) + ((d7 + d9) + (d11 + d13)) * (1.0 / 36.0)
    my = dy * (1.0 / 18.0) + ((d7 - d9) + (d15 + d17)) * (1.0 / 36.0)
    mz = dz * (1.0 / 18.0) + ((d11 - d13) + (d15 - d17)) * (1.0 / 36.0)
    inv = 1.0 / rho
    base = OMEGA * rho - (1.5 * OMEGA) * inv * (mx * mx + my * my + mz * mz)
    square = (4.5 * OMEGA) * inv
    out = [None] * 19
    out[0] = base + (1.0 - OMEGA) * g[0]
    along = {1: mx, 3: my, 5: mz, 7: mx + my, 9: mx - my, 11: mx + mz, 13: mx - mz, 15: my + mz, 17: my - mz}
    for i, c in along.items():
        even = base + square * c * c
        odd = (3.0 * OMEGA) * c
        out[i] = (even + odd) + (1.0 - OMEGA) * g[i]
        out[i + 1] = (even - odd) + (1.0 - OMEGA) * g[i + 1]
    return out


def raised(value, cz, rows):
    if cz == 0:
        return value
    lane = lax.broadcasted_iota(jnp.int32, value.shape, 1)
    row = lax.broadcasted_iota(jnp.int32, value.shape, 0)
    total = value.shape[0]
    shift, edge = (1, 0) if cz == 1 else (LANES - 1, LANES - 1)
    turned = pltpu.roll(value, shift, 1)
    if rows == total:
        return jnp.where(lane == edge, value, turned)
    carried = pltpu.roll(turned, rows if cz == 1 else total - rows, 0)
    clamped = row < rows if cz == 1 else row >= total - rows
    return jnp.where(lane == edge, jnp.where(clamped, value, carried), turned)


def crossed(value, cy, cs):
    if cy == 0:
        return value
    row = lax.broadcasted_iota(jnp.int32, value.shape, 0) % cs
    turned = pltpu.roll(value, 1 if cy == 1 else value.shape[0] - 1, 0)
    return jnp.where(row == (0 if cy == 1 else cs - 1), value, turned)


def turned_to(value, source, dest):
    shift = (dest - source) % value.shape[0]
    return value if shift == 0 else pltpu.roll(value, shift, 0)


def plenum_kernel(sizes, relayed, room_in, plen_in, cell_in, owner_in, class_in, room_near, plen_post, *rest):
    ca, cs, blocks, n_span, per_brick = sizes
    jets = rest[:-6]
    columns, plen_buf, cells, owners, classes, sems = rest[-6:]
    copies = [pltpu.make_async_copy(src, dst, sems.at[i]) for i, (src, dst) in enumerate(
        ((plen_in, plen_buf), (cell_in, cells), (owner_in, owners), (class_in, classes), (room_in, room_near)))]
    for copy in copies:
        copy.start()
    for part in jets:
        part[...] = jnp.zeros_like(part)
    copies[0].wait()
    for r in range(0, ca * cs, 8):
        post = collide([plen_buf[q, r : r + 8] for q in range(19)])
        for q in range(19):
            plen_post[q, r : r + 8] = post[q]
        for k, q in enumerate(UPWARD):
            for y in range(8):
                columns[r + y, :, k * LANES : (k + 1) * LANES] = post[q][y : y + 1]
    for copy in copies[1:4]:
        copy.wait()
    here = lax.axis_index("span")
    first = here * per_brick

    def send_jet(i, carry):
        t = first + i
        owner = owners[t]
        share = 0.15 * (classes[t].astype(F32) + 1.0)
        slot = lax.fori_loop(0, i, lambda j, n: n + (owners[first + j] == owner).astype(jnp.int32), 0)
        column = share * columns[cells[t]]
        if not relayed:
            jets[0][owner, slot] = column
            return carry
        apart = owner ^ here

        @pl.when(apart < 2)
        def _():
            jets[0][apart, slot] = column

        @pl.when(apart >= 2)
        def _():
            jets[1][apart - 2, slot] = column

        return carry

    lax.fori_loop(0, per_brick, send_jet, 0)
    copies[4].wait()


def room_kernel(sizes, room_near, plen_post, room_post, swap_a, swap_b):
    ca, cs, blocks, n_span, per_brick = sizes
    rows = blocks * cs

    def plane(x, carry):
        for r in range(0, rows, 8):
            post = collide([room_near[q, x, r : r + 8] for q in range(19)])
            for q in range(19):
                room_post[q, x, r : r + 8] = post[q]
        return carry

    lax.fori_loop(0, ca, plane, 0)
    even = lax.axis_index("aisle") % 2 == 0
    for k in range(5):
        up, down = X_UP[k], X_DOWN[k]
        rising = raised(room_post[up, ca - 1], VELOCITIES[up][2], cs)
        falling = raised(room_post[down, 0], VELOCITIES[down][2], cs)
        swap_a[k * rows : (k + 1) * rows] = jnp.where(even, rising, falling)
        swap_b[k * rows : (k + 1) * rows] = jnp.where(even, falling, rising)
        rising = raised(plen_post[up, (ca - 1) * cs : ca * cs], VELOCITIES[up][2], cs)
        falling = raised(plen_post[down, 0:cs], VELOCITIES[down][2], cs)
        low = 5 * rows + k * cs
        swap_a[low : low + cs] = jnp.where(even, rising, falling)
        swap_b[low : low + cs] = jnp.where(even, falling, rising)


def local_kernel(sizes, room_post, plen_post, cell_in, owner_in, room_part, plen_part, span_up, span_down, places,
                 cells, owners, sems):
    ca, cs, blocks, n_span, per_brick = sizes
    rows = blocks * cs
    copies = [pltpu.make_async_copy(src, dst, sems.at[i]) for i, (src, dst) in enumerate(
        ((cell_in, cells), (owner_in, owners)))]
    for copy in copies:
        copy.start()
    group = lax.broadcasted_iota(jnp.int32, (rows, LANES), 0) % cs
    for q in range(19):
        cx, cy, cz = VELOCITIES[q]
        edge = cs - 1 if cy == 1 else 0
        span, planes = (span_up, Y_UP) if cy == 1 else (span_down, Y_DOWN)
        packed = None
        for x in range(ca):
            if not 0 <= x - cx < ca:
                continue
            value = raised(room_post[q, x - cx], cz, cs)
            room_part[q, x] = crossed(value, cy, cs)
            if cy:
                ready = turned_to(value, edge, x)
                packed = ready if packed is None else jnp.where(group == x, ready, packed)
        value = raised(plen_post[q], cz, ca * cs)
        if cx == 1:
            value = pltpu.roll(value, cs, 0)
        elif cx == -1:
            value = pltpu.roll(value, ca * cs - cs, 0)
        plen_part[q] = crossed(value, cy, cs)
        if cy:
            k = planes.index(q)
            span[k * rows : (k + 1) * rows] = packed
            for x in range(ca):
                to = 5 * rows + k * ca + x
                span[to : to + 1] = value[x * cs + edge : x * cs + edge + 1]
    places[...] = jnp.zeros_like(places)
    here = lax.axis_index("span")
    row = lax.broadcasted_iota(jnp.int32, (ca * cs, LANES), 0)
    for copy in copies:
        copy.wait()

    def brick(b, carry):
        def place(i, slot):
            t = b * per_brick + i
            mine = owners[t] == here

            @pl.when(mine)
            def _():
                places[b * CAP + slot] = (row == cells[t]).astype(F32)

            return slot + mine.astype(jnp.int32)

        lax.fori_loop(0, per_brick, place, 0)
        return carry

    lax.fori_loop(0, n_span, brick, 0)


def pack_kernel(sizes, relayed, got_a, got_b, span_up, span_down, *rest):
    ca, cs, blocks, n_span, per_brick = sizes
    rows = blocks * cs
    if relayed:
        jets, got_jets, cross_a, cross_b = rest
    else:
        cross_a, cross_b = rest
    even = lax.axis_index("aisle") % 2 == 0
    low = lax.axis_index("span") % 2 == 0
    halo = span_up.shape[0]
    group = lax.broadcasted_iota(jnp.int32, (rows, LANES), 0) % cs

    def corner(q, low, high):
        if VELOCITIES[q][0] == 1:
            k = X_UP.index(q)
            return jnp.where(even, got_b[low(k) : high(k)], got_a[low(k) : high(k)])
        k = X_DOWN.index(q)
        return jnp.where(even, got_a[low(k) : high(k)], got_b[low(k) : high(k)])

    for k in range(5):
        sides = []
        for span, planes, edge in ((span_up, Y_UP, cs - 1), (span_down, Y_DOWN, 0)):
            q = planes[k]
            value = span[k * rows : (k + 1) * rows]
            if VELOCITIES[q][0]:
                x = 0 if VELOCITIES[q][0] == 1 else ca - 1
                came = corner(q, lambda k: k * rows, lambda k: (k + 1) * rows)
                value = jnp.where(group == x, turned_to(came, edge, x), value)
            sides.append(value)
        cross_a[k * rows : (k + 1) * rows] = jnp.where(low, sides[0], sides[1])
        cross_b[k * rows : (k + 1) * rows] = jnp.where(low, sides[1], sides[0])
    for r in range(5 * rows, halo, 8):
        rising, falling = span_up[r : r + 8], span_down[r : r + 8]
        cross_a[r : r + 8] = jnp.where(low, rising, falling)
        cross_b[r : r + 8] = jnp.where(low, falling, rising)
    for planes, edge in ((Y_UP, cs - 1), (Y_DOWN, 0)):
        for k, q in enumerate(planes):
            if VELOCITIES[q][0]:
                x = 0 if VELOCITIES[q][0] == 1 else ca - 1
                at = lambda k: 5 * rows + k * cs + edge
                came = corner(q, at, lambda k: at(k) + 1)
                to = 5 * rows + k * ca + x

                @pl.when(low == (planes is Y_UP))
                def _():
                    cross_a[to : to + 1] = came

                @pl.when(low != (planes is Y_UP))
                def _():
                    cross_b[to : to + 1] = came

    if relayed:
        for b, source in enumerate((jets, got_jets)):
            for s in range(CAP):
                for k in range(5):
                    to = halo + (b * CAP + s) * 5 + k
                    cross_a[to : to + 1] = source[1, s, :, k * LANES : (k + 1) * LANES]


def jet_sums(start, places, bricks):
    sums = [start(k) for k in range(5)]
    for b, jet in bricks:
        for s in range(CAP):
            marks = places[b * CAP + s]
            sums = [total + marks * jet(s, k) for k, total in enumerate(sums)]
    return sums


def aisle_kernel(sizes, relayed, room_in, plen_in, got_a, got_b, jets, got_jets, places, room, plen, inflow):
    ca, cs, blocks, n_span, per_brick = sizes
    rows = blocks * cs
    even = lax.axis_index("aisle") % 2 == 0
    here = lax.axis_index("span")
    for k in range(5):
        for q, x, first, second in ((X_UP[k], 0, got_b, got_a), (X_DOWN[k], ca - 1, got_a, got_b)):
            cy = VELOCITIES[q][1]
            low, high = k * rows, (k + 1) * rows
            room[q, x] = crossed(jnp.where(even, first[low:high], second[low:high]), cy, cs)
            low = 5 * rows + k * cs
            value = jnp.where(even, first[low : low + cs], second[low : low + cs])
            at = x * cs
            if cy == 1:
                plen[q, at : at + 1] = value[0:1]
                plen[q, at + 1 : at + cs] = value[: cs - 1]
            elif cy == -1:
                plen[q, at + cs - 1 : at + cs] = value[cs - 1 : cs]
                plen[q, at : at + cs - 1] = value[1:cs]
            else:
                plen[q, at : at + cs] = value

    def put(sums):
        for k in range(5):
            inflow[k] = sums[k]

    def reader(source, b):
        return lambda s, k: source[b, s, :, k * LANES : (k + 1) * LANES]

    if relayed:
        put(jet_sums(lambda k: jnp.zeros((ca * cs, LANES), F32), places,
                     [(here, reader(jets, 0)), (here ^ 2, reader(got_jets, 0))]))
    else:
        inflow[...] = jnp.zeros_like(inflow)

        def brick(b, carry):
            put(jet_sums(lambda k: inflow[k], places, [(b, reader(got_jets, b))]))
            return carry

        lax.fori_loop(0, n_span, brick, 0)


def finish_kernel(sizes, relayed, room_in, plen_in, got_a, got_b, places, inflow, room, plen, room_out, plen_out, sems):
    ca, cs, blocks, n_span, per_brick = sizes
    rows = blocks * cs
    here = lax.axis_index("span")
    low = here % 2 == 0
    halo = 5 * (rows + cs)
    halo = halo + -halo % 8
    group = lax.broadcasted_iota(jnp.int32, (rows, LANES), 0) % cs

    def enter(got, up):
        planes, y = (Y_UP, 0) if up else (Y_DOWN, cs - 1)
        for k, q in enumerate(planes):
            came = got[k * rows : (k + 1) * rows]
            for x in range(ca):
                room[q, x] = jnp.where(group == y, turned_to(came, x, y), room[q, x])
                at = 5 * rows + k * ca + x
                plen[q, x * cs + y : x * cs + y + 1] = got[at : at + 1]

    @pl.when(low)
    def _():
        enter(got_a, False)

    @pl.when(jnp.logical_not(low))
    def _():
        enter(got_a, True)

    @pl.when(jnp.logical_and(low, here > 0))
    def _():
        enter(got_b, True)

    @pl.when(jnp.logical_and(jnp.logical_not(low), here < n_span - 1))
    def _():
        enter(got_b, False)

    plen_copy = pltpu.make_async_copy(plen, plen_out, sems.at[0])
    plen_copy.start()
    bricks = []
    if relayed:
        def reader(b):
            return lambda s, k: got_a[halo + (b * CAP + s) * 5 + k : halo + (b * CAP + s) * 5 + k + 1]

        bricks = [(here ^ 1, reader(0)), (here ^ 3, reader(1))]
    sums = jet_sums(lambda k: inflow[k], places, bricks)
    for k, q in enumerate(UPWARD):
        for x in range(ca):
            room[q, x, 0:cs] = room[q, x, 0:cs] + sums[k][x * cs : (x + 1) * cs]
    room_copy = pltpu.make_async_copy(room, room_out, sems.at[1])
    room_copy.start()
    plen_copy.wait()
    room_copy.wait()


def call(kernel, outs, in_specs, out_specs=None, scratch=(), aliases={}, flops=100_000, moved=1_000_000):
    return pl.pallas_call(
        kernel,
        out_shape=outs,
        in_specs=in_specs,
        out_specs=[VMEM] * len(outs) if out_specs is None else out_specs,
        scratch_shapes=list(scratch),
        input_output_aliases=aliases,
        cost_estimate=pl.CostEstimate(flops=flops, bytes_accessed=moved, transcendentals=0),
        compiler_params=pltpu.CompilerParams(vmem_limit_bytes=40 * 2**20),
    )


def swap(value, axis, odd, wraps):
    count = lax.axis_size(axis)
    pairs = []
    for i in range(count):
        j = (i ^ 1) if not odd else (i + 1 if i % 2 else i - 1)
        if wraps or 0 <= j < count:
            pairs.append((i, j % count))
    return lax.ppermute(value, axis, pairs)


def shards(room_pops, plenum_pops, tile_cell, tile_owner, tile_class):
    n_span = lax.axis_size("span")
    _, ca, cs, hr = room_pops.shape
    hp = plenum_pops.shape[3]
    blocks = hr // LANES
    rows = blocks * cs
    tiles = tile_cell.shape[0]
    sizes = (ca, cs, blocks, n_span, tiles // n_span)
    relayed = n_span == 4
    near = lambda shape: pltpu.VMEM(shape, F32)
    far = lambda value: pltpu.with_memory_space_constraint(value, pltpu.HBM)
    room_shape, plen_shape = (19, ca, rows, LANES), (19, ca * cs, LANES)
    halo = 5 * (rows + cs)
    halo = halo + -halo % 8
    room = far(room_pops.reshape(19, ca, cs, blocks, LANES).transpose(0, 1, 3, 2, 4).reshape(room_shape))
    plen = far(plenum_pops.reshape(plen_shape))
    tile_cell, tile_owner, tile_class = far(tile_cell), far(tile_owner.reshape(tiles)), far(tile_class)
    numbers = pltpu.SMEM((tiles,), jnp.int32)

    jets_shape = (2 if relayed else n_span, CAP, 1, 5 * hp)
    room_near, plen_post, *jets = call(
        functools.partial(plenum_kernel, sizes, relayed),
        [near(room_shape), near(plen_shape)] + [near(jets_shape)] * (2 if relayed else 1),
        [HBM] * 5,
        scratch=[pltpu.VMEM((ca * cs, 1, 5 * hp), F32), pltpu.VMEM(plen_shape, F32), numbers, numbers, numbers,
                 pltpu.SemaphoreType.DMA((5,))],
    )(room, plen, tile_cell, tile_owner, tile_class)
    if relayed:
        got_jets = lax.ppermute(jets[1], "span", [(i, i ^ 2) for i in range(4)])
    else:
        got_jets = lax.all_to_all(jets[0], "span", 0, 0, tiled=True)

    room_post, swap_a, swap_b = call(
        functools.partial(room_kernel, sizes),
        [near(room_shape), near((halo, LANES)), near((halo, LANES))],
        [VMEM] * 2,
    )(room_near, plen_post)
    got_a = swap(swap_a, "aisle", False, True)
    got_b = swap(swap_b, "aisle", True, True)

    room_part, plen_part, span_up, span_down, places = call(
        functools.partial(local_kernel, sizes),
        [near(room_shape), near(plen_shape), near((halo, LANES)), near((halo, LANES)),
         near((n_span * CAP, ca * cs, LANES))],
        [VMEM, VMEM, HBM, HBM],
        scratch=[numbers, numbers, pltpu.SemaphoreType.DMA((2,))],
    )(room_post, plen_post, tile_cell, tile_owner)

    cross_shape = (halo + 2 * CAP * 5, LANES) if relayed else (halo, LANES)
    cross_a, cross_b = call(
        functools.partial(pack_kernel, sizes, relayed),
        [near(cross_shape), near((halo, LANES))],
        [VMEM] * (6 if relayed else 4),
    )(got_a, got_b, span_up, span_down, *((jets[0], got_jets) if relayed else ()))

    in_b = swap(cross_b, "span", True, False)
    in_a = swap(cross_a, "span", False, False)
    room_part, plen_part, inflow = call(
        functools.partial(aisle_kernel, sizes, relayed),
        [near(room_shape), near(plen_shape), near((5, ca * cs, LANES))],
        [VMEM] * 7,
        aliases={0: 0, 1: 1},
    )(room_part, plen_part, got_a, got_b, jets[0], got_jets, places)

    _, _, room_next, plenum_next = call(
        functools.partial(finish_kernel, sizes, relayed),
        [near(room_shape), near(plen_shape), jax.ShapeDtypeStruct(room_shape, F32),
         jax.ShapeDtypeStruct(plen_shape, F32)],
        [VMEM] * 6,
        out_specs=[VMEM, VMEM, HBM, HBM],
        scratch=[pltpu.SemaphoreType.DMA((2,))],
        aliases={0: 0, 1: 1},
    )(room_part, plen_part, in_a, in_b, places, inflow)
    room_next = room_next.reshape(19, ca, blocks, cs, LANES).transpose(0, 1, 3, 2, 4).reshape(room_pops.shape)
    return room_next, plenum_next.reshape(plenum_pops.shape)


def solution(mesh):
    return jax.shard_map(
        shards,
        mesh=mesh,
        in_specs=(
            P(None, "aisle", "span", None),
            P(None, "aisle", "span", None),
            P("aisle"),
            P("aisle", None),
            P("aisle"),
        ),
        out_specs=(P(None, "aisle", "span", None), P(None, "aisle", "span", None)),
        check_vma=False,
    )
```

```python
import functools

import jax
import jax.numpy as jnp
from jax import lax
from jax.experimental import pallas as pl
from jax.experimental.pallas import tpu as pltpu
from jax.sharding import PartitionSpec as P

VELOCITIES = [
    (0, 0, 0),
    (1, 0, 0),
    (-1, 0, 0),
    (0, 1, 0),
    (0, -1, 0),
    (0, 0, 1),
    (0, 0, -1),
    (1, 1, 0),
    (-1, -1, 0),
    (1, -1, 0),
    (-1, 1, 0),
    (1, 0, 1),
    (-1, 0, -1),
    (1, 0, -1),
    (-1, 0, 1),
    (0, 1, 1),
    (0, -1, -1),
    (0, 1, -1),
    (0, -1, 1),
]
UPWARD = [5, 11, 14, 15, 18]
OMEGA = 1.25
CAP = 4
X_UP = [q for q in range(19) if VELOCITIES[q][0] == 1]
X_DOWN = [q for q in range(19) if VELOCITIES[q][0] == -1]
Y_UP = [q for q in range(19) if VELOCITIES[q][1] == 1]
Y_DOWN = [q for q in range(19) if VELOCITIES[q][1] == -1]
F32 = jnp.float32
LANES = 128
VMEM = pl.BlockSpec(memory_space=pltpu.VMEM)
HBM = pl.BlockSpec(memory_space=pltpu.HBM)


def collide(g):
    total = lambda i: g[i] + g[i + 1]
    apart = lambda i: g[i] - g[i + 1]
    dx, dy, dz = apart(1), apart(3), apart(5)
    d7, d9, d11, d13, d15, d17 = (apart(i) for i in (7, 9, 11, 13, 15, 17))
    edges = (total(7) + total(9)) + (total(11) + total(13)) + (total(15) + total(17))
    faces = total(1) + total(3) + total(5)
    rho = g[0] * (1.0 / 3.0) + faces * (1.0 / 18.0) + edges * (1.0 / 36.0)
    mx = dx * (1.0 / 18.0) + ((d7 + d9) + (d11 + d13)) * (1.0 / 36.0)
    my = dy * (1.0 / 18.0) + ((d7 - d9) + (d15 + d17)) * (1.0 / 36.0)
    mz = dz * (1.0 / 18.0) + ((d11 - d13) + (d15 - d17)) * (1.0 / 36.0)
    inv = 1.0 / rho
    base = OMEGA * rho - (1.5 * OMEGA) * inv * (mx * mx + my * my + mz * mz)
    square = (4.5 * OMEGA) * inv
    out = [None] * 19
    out[0] = base + (1.0 - OMEGA) * g[0]
    along = {1: mx, 3: my, 5: mz, 7: mx + my, 9: mx - my, 11: mx + mz, 13: mx - mz, 15: my + mz, 17: my - mz}
    for i, c in along.items():
        even = base + square * c * c
        odd = (3.0 * OMEGA) * c
        out[i] = (even + odd) + (1.0 - OMEGA) * g[i]
        out[i + 1] = (even - odd) + (1.0 - OMEGA) * g[i + 1]
    return out


def raised(value, cz, rows):
    if cz == 0:
        return value
    lane = lax.broadcasted_iota(jnp.int32, value.shape, 1)
    row = lax.broadcasted_iota(jnp.int32, value.shape, 0)
    total = value.shape[0]
    shift, edge = (1, 0) if cz == 1 else (LANES - 1, LANES - 1)
    turned = pltpu.roll(value, shift, 1)
    if rows == total:
        return jnp.where(lane == edge, value, turned)
    carried = pltpu.roll(turned, rows if cz == 1 else total - rows, 0)
    clamped = row < rows if cz == 1 else row >= total - rows
    return jnp.where(lane == edge, jnp.where(clamped, value, carried), turned)


def crossed(value, cy, cs):
    if cy == 0:
        return value
    row = lax.broadcasted_iota(jnp.int32, value.shape, 0) % cs
    turned = pltpu.roll(value, 1 if cy == 1 else value.shape[0] - 1, 0)
    return jnp.where(row == (0 if cy == 1 else cs - 1), value, turned)


def turned_to(value, source, dest):
    shift = (dest - source) % value.shape[0]
    return value if shift == 0 else pltpu.roll(value, shift, 0)


def repeat(count, body, start):
    if count > 8:
        return lax.fori_loop(0, count, body, start)
    for i in range(count):
        start = body(i, start)
    return start


def plenum_kernel(sizes, relayed, room_in, plen_in, cell_in, owner_in, class_in, room_near, plen_post, *rest):
    ca, cs, blocks, n_span, per_brick = sizes
    jets = rest[:-7]
    columns, dealt, plen_buf, cells, owners, classes, sems = rest[-7:]
    copies = [pltpu.make_async_copy(src, dst, sems.at[i]) for i, (src, dst) in enumerate(
        ((plen_in, plen_buf), (cell_in, cells), (owner_in, owners), (class_in, classes), (room_in, room_near)))]
    for copy in copies:
        copy.start()
    dealt[...] = jnp.zeros_like(dealt)
    copies[0].wait()
    for r in range(0, ca * cs, 8):
        post = collide([plen_buf[q, r : r + 8] for q in range(19)])
        for q in range(19):
            plen_post[q, r : r + 8] = post[q]
        for k, q in enumerate(UPWARD):
            for y in range(8):
                columns[r + y, :, k * LANES : (k + 1) * LANES] = post[q][y : y + 1]
    for copy in copies[1:4]:
        copy.wait()
    here = lax.axis_index("span")
    first = here * per_brick

    def send_jet(i, carry):
        t = first + i
        owner = owners[t]
        share = 0.15 * (classes[t].astype(F32) + 1.0)
        same = lambda j, n: n + (owners[first + j] == owner).astype(jnp.int32)
        slot = repeat(i, same, 0) if relayed else lax.fori_loop(0, i, same, 0)
        to = (owner ^ here if relayed else owner) * CAP + slot
        dealt[to] = share * columns[cells[t]]
        return carry

    if relayed:
        for i in range(per_brick):
            send_jet(i, 0)
    else:
        lax.fori_loop(0, per_brick, send_jet, 0)
    for part, jet in enumerate(jets):
        many = jet.shape[0]
        jet[...] = dealt[part * many : (part + 1) * many]
    copies[4].wait()


def room_kernel(sizes, room_near, plen_post, room_post, swap_a, swap_b):
    ca, cs, blocks, n_span, per_brick = sizes
    rows = blocks * cs

    def plane(x, carry):
        for r in range(0, rows, 8):
            post = collide([room_near[q, x, r : r + 8] for q in range(19)])
            for q in range(19):
                room_post[q, x, r : r + 8] = post[q]
        return carry

    lax.fori_loop(0, ca, plane, 0)
    even = lax.axis_index("aisle") % 2 == 0
    for k in range(5):
        up, down = X_UP[k], X_DOWN[k]
        rising = raised(room_post[up, ca - 1], VELOCITIES[up][2], cs)
        falling = raised(room_post[down, 0], VELOCITIES[down][2], cs)
        swap_a[k * rows : (k + 1) * rows] = jnp.where(even, rising, falling)
        swap_b[k * rows : (k + 1) * rows] = jnp.where(even, falling, rising)
        rising = raised(plen_post[up, (ca - 1) * cs : ca * cs], VELOCITIES[up][2], cs)
        falling = raised(plen_post[down, 0:cs], VELOCITIES[down][2], cs)
        low = 5 * rows + k * cs
        swap_a[low : low + cs] = jnp.where(even, rising, falling)
        swap_b[low : low + cs] = jnp.where(even, falling, rising)


def jet_sums(start, places, bricks):
    sums = [start(k) for k in range(5)]
    for b, jet in bricks:
        for s in range(CAP):
            marks = places[b * CAP + s]
            sums = [total + marks * jet(s, k) for k, total in enumerate(sums)]
    return sums


def local_kernel(sizes, relayed, room_post, plen_post, jets, got_jets, cell_in, owner_in, room_part, plen_part, span_up,
                 span_down, places, inflow, cells, owners, sems):
    ca, cs, blocks, n_span, per_brick = sizes
    rows = blocks * cs
    copies = [pltpu.make_async_copy(src, dst, sems.at[i]) for i, (src, dst) in enumerate(
        ((cell_in, cells), (owner_in, owners)))]
    for copy in copies:
        copy.start()
    group = lax.broadcasted_iota(jnp.int32, (rows, LANES), 0) % cs
    for q in range(19):
        cx, cy, cz = VELOCITIES[q]
        edge = cs - 1 if cy == 1 else 0
        span, planes = (span_up, Y_UP) if cy == 1 else (span_down, Y_DOWN)
        packed = None
        for x in range(ca):
            if not 0 <= x - cx < ca:
                continue
            value = raised(room_post[q, x - cx], cz, cs)
            room_part[q, x] = crossed(value, cy, cs)
            if cy:
                ready = turned_to(value, edge, x)
                packed = ready if packed is None else jnp.where(group == x, ready, packed)
        value = raised(plen_post[q], cz, ca * cs)
        if cx == 1:
            value = pltpu.roll(value, cs, 0)
        elif cx == -1:
            value = pltpu.roll(value, ca * cs - cs, 0)
        plen_part[q] = crossed(value, cy, cs)
        if cy:
            k = planes.index(q)
            span[k * rows : (k + 1) * rows] = packed
            for x in range(ca):
                to = 5 * rows + k * ca + x
                span[to : to + 1] = value[x * cs + edge : x * cs + edge + 1]
    places[0 : n_span * CAP] = jnp.zeros((n_span * CAP, ca * cs, LANES), F32)
    here = lax.axis_index("span")
    row = lax.broadcasted_iota(jnp.int32, (ca * cs, LANES), 0)
    for copy in copies:
        copy.wait()

    def brick(b, carry):
        def place(i, slot):
            t = b * per_brick + i
            mine = owners[t] == here
            places[jnp.where(mine, b * CAP + slot, n_span * CAP)] = (row == cells[t]).astype(F32)
            return slot + mine.astype(jnp.int32)

        repeat(per_brick, place, 0)
        return carry

    repeat(n_span, brick, 0)

    def put(sums):
        for k in range(5):
            inflow[k] = sums[k]

    def reader(source, b):
        return lambda s, k: source[b * CAP + s, :, k * LANES : (k + 1) * LANES]

    if relayed:
        put(jet_sums(lambda k: jnp.zeros((ca * cs, LANES), F32), places,
                     [(here, reader(jets, 0)), (here ^ 2, reader(got_jets, 0))]))
    else:
        inflow[...] = jnp.zeros_like(inflow)

        def add_brick(b, carry):
            put(jet_sums(lambda k: inflow[k], places, [(b, reader(got_jets, b))]))
            return carry

        lax.fori_loop(0, n_span, add_brick, 0)


def pack_kernel(sizes, relayed, got_a, got_b, span_up, span_down, *rest):
    ca, cs, blocks, n_span, per_brick = sizes
    rows = blocks * cs
    if relayed:
        jets, got_jets, cross_a, cross_b = rest
    else:
        cross_a, cross_b = rest
    even = lax.axis_index("aisle") % 2 == 0
    low = lax.axis_index("span") % 2 == 0
    halo = span_up.shape[0]
    group = lax.broadcasted_iota(jnp.int32, (rows, LANES), 0) % cs

    def corner(q, low, high):
        if VELOCITIES[q][0] == 1:
            k = X_UP.index(q)
            return jnp.where(even, got_b[low(k) : high(k)], got_a[low(k) : high(k)])
        k = X_DOWN.index(q)
        return jnp.where(even, got_a[low(k) : high(k)], got_b[low(k) : high(k)])

    for k in range(5):
        sides = []
        for span, planes, edge in ((span_up, Y_UP, cs - 1), (span_down, Y_DOWN, 0)):
            q = planes[k]
            value = span[k * rows : (k + 1) * rows]
            if VELOCITIES[q][0]:
                x = 0 if VELOCITIES[q][0] == 1 else ca - 1
                came = corner(q, lambda k: k * rows, lambda k: (k + 1) * rows)
                value = jnp.where(group == x, turned_to(came, edge, x), value)
            sides.append(value)
        cross_a[k * rows : (k + 1) * rows] = jnp.where(low, sides[0], sides[1])
        cross_b[k * rows : (k + 1) * rows] = jnp.where(low, sides[1], sides[0])
    for r in range(5 * rows, halo, 8):
        rising, falling = span_up[r : r + 8], span_down[r : r + 8]
        cross_a[r : r + 8] = jnp.where(low, rising, falling)
        cross_b[r : r + 8] = jnp.where(low, falling, rising)
    for planes, edge in ((Y_UP, cs - 1), (Y_DOWN, 0)):
        for k, q in enumerate(planes):
            if VELOCITIES[q][0]:
                x = 0 if VELOCITIES[q][0] == 1 else ca - 1
                at = lambda k: 5 * rows + k * cs + edge
                came = corner(q, at, lambda k: at(k) + 1)
                to = 5 * rows + k * ca + x

                @pl.when(low == (planes is Y_UP))
                def _():
                    cross_a[to : to + 1] = came

                @pl.when(low != (planes is Y_UP))
                def _():
                    cross_b[to : to + 1] = came

    if relayed:
        for b, source in enumerate((jets, got_jets)):
            for s in range(CAP):
                for k in range(5):
                    to = halo + (b * CAP + s) * 5 + k
                    cross_a[to : to + 1] = source[CAP + s, :, k * LANES : (k + 1) * LANES]


def aisle_kernel(sizes, room_in, plen_in, got_a, got_b, room, plen):
    ca, cs, blocks, n_span, per_brick = sizes
    rows = blocks * cs
    even = lax.axis_index("aisle") % 2 == 0
    for k in range(5):
        for q, x, first, second in ((X_UP[k], 0, got_b, got_a), (X_DOWN[k], ca - 1, got_a, got_b)):
            cy = VELOCITIES[q][1]
            low, high = k * rows, (k + 1) * rows
            room[q, x] = crossed(jnp.where(even, first[low:high], second[low:high]), cy, cs)
            low = 5 * rows + k * cs
            value = jnp.where(even, first[low : low + cs], second[low : low + cs])
            at = x * cs
            if cy == 1:
                plen[q, at : at + 1] = value[0:1]
                plen[q, at + 1 : at + cs] = value[: cs - 1]
            elif cy == -1:
                plen[q, at + cs - 1 : at + cs] = value[cs - 1 : cs]
                plen[q, at : at + cs - 1] = value[1:cs]
            else:
                plen[q, at : at + cs] = value


def finish_kernel(sizes, relayed, room_in, plen_in, got_a, got_b, places, inflow, room, plen, room_out, plen_out, sems):
    ca, cs, blocks, n_span, per_brick = sizes
    rows = blocks * cs
    here = lax.axis_index("span")
    low = here % 2 == 0
    halo = 5 * (rows + cs)
    halo = halo + -halo % 8
    group = lax.broadcasted_iota(jnp.int32, (rows, LANES), 0) % cs
    spans = [[], [], []]
    for q in range(19):
        stage = 2 if q in UPWARD else 1 if VELOCITIES[q][1] else 0
        if spans[stage] and spans[stage][-1][1] == q:
            spans[stage][-1][1] = q + 1
        else:
            spans[stage].append([q, q + 1])
    copies, sem = [], 1
    for stage in spans:
        copies.append([])
        for low_q, high_q in stage:
            copies[-1].append(pltpu.make_async_copy(room.at[low_q:high_q], room_out.at[low_q:high_q], sems.at[sem]))
            sem = sem + 1
    copies[1].append(pltpu.make_async_copy(plen, plen_out, sems.at[0]))

    def put_out(stage):
        for copy in copies[stage]:
            copy.start()

    def enter(got, up):
        planes, y = (Y_UP, 0) if up else (Y_DOWN, cs - 1)
        for k, q in enumerate(planes):
            came = got[k * rows : (k + 1) * rows]
            for x in range(ca):
                room[q, x] = jnp.where(group == y, turned_to(came, x, y), room[q, x])
                at = 5 * rows + k * ca + x
                plen[q, x * cs + y : x * cs + y + 1] = got[at : at + 1]

    put_out(0)

    @pl.when(low)
    def _():
        enter(got_a, False)

    @pl.when(jnp.logical_not(low))
    def _():
        enter(got_a, True)

    @pl.when(jnp.logical_and(low, here > 0))
    def _():
        enter(got_b, True)

    @pl.when(jnp.logical_and(jnp.logical_not(low), here < n_span - 1))
    def _():
        enter(got_b, False)

    put_out(1)
    bricks = []
    if relayed:
        def reader(b):
            return lambda s, k: got_a[halo + (b * CAP + s) * 5 + k : halo + (b * CAP + s) * 5 + k + 1]

        bricks = [(here ^ 1, reader(0)), (here ^ 3, reader(1))]
    sums = jet_sums(lambda k: inflow[k], places, bricks)
    for k, q in enumerate(UPWARD):
        for x in range(ca):
            room[q, x, 0:cs] = room[q, x, 0:cs] + sums[k][x * cs : (x + 1) * cs]
    put_out(2)
    for group in copies:
        for copy in group:
            copy.wait()


def call(kernel, outs, in_specs, out_specs=None, scratch=(), aliases={}, flops=100_000, moved=1_000_000):
    return pl.pallas_call(
        kernel,
        out_shape=outs,
        in_specs=in_specs,
        out_specs=[VMEM] * len(outs) if out_specs is None else out_specs,
        scratch_shapes=list(scratch),
        input_output_aliases=aliases,
        cost_estimate=pl.CostEstimate(flops=flops, bytes_accessed=moved, transcendentals=0),
        compiler_params=pltpu.CompilerParams(vmem_limit_bytes=40 * 2**20),
    )


def swap(value, axis, odd, wraps):
    count = lax.axis_size(axis)
    pairs = []
    for i in range(count):
        j = (i ^ 1) if not odd else (i + 1 if i % 2 else i - 1)
        if wraps or 0 <= j < count:
            pairs.append((i, j % count))
    return lax.ppermute(value, axis, pairs)


def shards(room_pops, plenum_pops, tile_cell, tile_owner, tile_class):
    n_span = lax.axis_size("span")
    _, ca, cs, hr = room_pops.shape
    hp = plenum_pops.shape[3]
    blocks = hr // LANES
    rows = blocks * cs
    tiles = tile_cell.shape[0]
    sizes = (ca, cs, blocks, n_span, tiles // n_span)
    relayed = n_span == 4
    near = lambda shape: pltpu.VMEM(shape, F32)
    far = lambda value: pltpu.with_memory_space_constraint(value, pltpu.HBM)
    room_shape, plen_shape = (19, ca, rows, LANES), (19, ca * cs, LANES)
    halo = 5 * (rows + cs)
    halo = halo + -halo % 8
    room = far(room_pops.reshape(19, ca, cs, blocks, LANES).transpose(0, 1, 3, 2, 4).reshape(room_shape))
    plen = far(plenum_pops.reshape(plen_shape))
    tile_cell, tile_owner, tile_class = far(tile_cell), far(tile_owner.reshape(tiles)), far(tile_class)
    numbers = pltpu.SMEM((tiles,), jnp.int32)

    jets_shape = ((2 if relayed else n_span) * CAP, 1, 5 * hp)
    room_near, plen_post, *jets = call(
        functools.partial(plenum_kernel, sizes, relayed),
        [near(room_shape), near(plen_shape)] + [near(jets_shape)] * (2 if relayed else 1),
        [HBM] * 5,
        scratch=[pltpu.VMEM((ca * cs, 1, 5 * hp), F32), near((n_span * CAP, 1, 5 * hp)), near(plen_shape), numbers, numbers, numbers,
                 pltpu.SemaphoreType.DMA((5,))],
    )(room, plen, tile_cell, tile_owner, tile_class)
    if relayed:
        got_jets = lax.ppermute(jets[1], "span", [(i, i ^ 2) for i in range(4)])
    else:
        got_jets = lax.all_to_all(jets[0], "span", 0, 0, tiled=True)

    room_post, swap_a, swap_b = call(
        functools.partial(room_kernel, sizes),
        [near(room_shape), near((halo, LANES)), near((halo, LANES))],
        [VMEM] * 2,
    )(room_near, plen_post)
    got_a = swap(swap_a, "aisle", False, True)
    got_b = swap(swap_b, "aisle", True, True)

    room_part, plen_part, span_up, span_down, places, inflow = call(
        functools.partial(local_kernel, sizes, relayed),
        [near(room_shape), near(plen_shape), near((halo, LANES)), near((halo, LANES)),
         near((n_span * CAP + 1, ca * cs, LANES)), near((5, ca * cs, LANES))],
        [VMEM, VMEM, VMEM, VMEM, HBM, HBM],
        scratch=[numbers, numbers, pltpu.SemaphoreType.DMA((2,))],
        flops=10**9,
    )(room_post, plen_post, jets[0], got_jets, tile_cell, tile_owner)

    cross_shape = (halo + 2 * CAP * 5, LANES) if relayed else (halo, LANES)
    cross_a, cross_b = call(
        functools.partial(pack_kernel, sizes, relayed),
        [near(cross_shape), near((halo, LANES))],
        [VMEM] * (6 if relayed else 4),
    )(got_a, got_b, span_up, span_down, *((jets[0], got_jets) if relayed else ()))

    in_b = swap(cross_b, "span", True, False)
    in_a = swap(cross_a, "span", False, False)
    room_part, plen_part = call(
        functools.partial(aisle_kernel, sizes),
        [near(room_shape), near(plen_shape)],
        [VMEM] * 4,
        aliases={0: 0, 1: 1},
    )(room_part, plen_part, got_a, got_b)

    _, _, room_next, plenum_next = call(
        functools.partial(finish_kernel, sizes, relayed),
        [near(room_shape), near(plen_shape), jax.ShapeDtypeStruct(room_shape, F32),
         jax.ShapeDtypeStruct(plen_shape, F32)],
        [VMEM] * 6,
        out_specs=[VMEM, VMEM, HBM, HBM],
        scratch=[pltpu.SemaphoreType.DMA((20,))],
        aliases={0: 0, 1: 1},
    )(room_part, plen_part, in_a, in_b, places, inflow)
    room_next = room_next.reshape(19, ca, blocks, cs, LANES).transpose(0, 1, 3, 2, 4).reshape(room_pops.shape)
    return room_next, plenum_next.reshape(plenum_pops.shape)


def solution(mesh):
    return jax.shard_map(
        shards,
        mesh=mesh,
        in_specs=(
            P(None, "aisle", "span", None),
            P(None, "aisle", "span", None),
            P("aisle"),
            P("aisle", None),
            P("aisle"),
        ),
        out_specs=(P(None, "aisle", "span", None), P(None, "aisle", "span", None)),
        check_vma=False,
    )
```

```python
import functools

import jax
import jax.numpy as jnp
from jax import lax
from jax.experimental import pallas as pl
from jax.experimental.pallas import tpu as pltpu
from jax.sharding import PartitionSpec as P

VELOCITIES = [
    (0, 0, 0),
    (1, 0, 0),
    (-1, 0, 0),
    (0, 1, 0),
    (0, -1, 0),
    (0, 0, 1),
    (0, 0, -1),
    (1, 1, 0),
    (-1, -1, 0),
    (1, -1, 0),
    (-1, 1, 0),
    (1, 0, 1),
    (-1, 0, -1),
    (1, 0, -1),
    (-1, 0, 1),
    (0, 1, 1),
    (0, -1, -1),
    (0, 1, -1),
    (0, -1, 1),
]
UPWARD = [5, 11, 14, 15, 18]
OMEGA = 1.25
CAP = 4
X_UP = [q for q in range(19) if VELOCITIES[q][0] == 1]
X_DOWN = [q for q in range(19) if VELOCITIES[q][0] == -1]
Y_UP = [q for q in range(19) if VELOCITIES[q][1] == 1]
Y_DOWN = [q for q in range(19) if VELOCITIES[q][1] == -1]
F32 = jnp.float32
LANES = 128
VMEM = pl.BlockSpec(memory_space=pltpu.VMEM)
HBM = pl.BlockSpec(memory_space=pltpu.HBM)


def collide(g):
    total = lambda i: g[i] + g[i + 1]
    apart = lambda i: g[i] - g[i + 1]
    dx, dy, dz = apart(1), apart(3), apart(5)
    d7, d9, d11, d13, d15, d17 = (apart(i) for i in (7, 9, 11, 13, 15, 17))
    edges = (total(7) + total(9)) + (total(11) + total(13)) + (total(15) + total(17))
    faces = total(1) + total(3) + total(5)
    rho = g[0] * (1.0 / 3.0) + faces * (1.0 / 18.0) + edges * (1.0 / 36.0)
    mx = dx * (1.0 / 18.0) + ((d7 + d9) + (d11 + d13)) * (1.0 / 36.0)
    my = dy * (1.0 / 18.0) + ((d7 - d9) + (d15 + d17)) * (1.0 / 36.0)
    mz = dz * (1.0 / 18.0) + ((d11 - d13) + (d15 - d17)) * (1.0 / 36.0)
    inv = 1.0 / rho
    base = OMEGA * rho - (1.5 * OMEGA) * inv * (mx * mx + my * my + mz * mz)
    square = (4.5 * OMEGA) * inv
    out = [None] * 19
    out[0] = base + (1.0 - OMEGA) * g[0]
    along = {1: mx, 3: my, 5: mz, 7: mx + my, 9: mx - my, 11: mx + mz, 13: mx - mz, 15: my + mz, 17: my - mz}
    for i, c in along.items():
        even = base + square * c * c
        odd = (3.0 * OMEGA) * c
        out[i] = (even + odd) + (1.0 - OMEGA) * g[i]
        out[i + 1] = (even - odd) + (1.0 - OMEGA) * g[i + 1]
    return out


def raised(value, cz, rows):
    if cz == 0:
        return value
    lane = lax.broadcasted_iota(jnp.int32, value.shape, 1)
    row = lax.broadcasted_iota(jnp.int32, value.shape, 0)
    total = value.shape[0]
    shift, edge = (1, 0) if cz == 1 else (LANES - 1, LANES - 1)
    turned = pltpu.roll(value, shift, 1)
    if rows == total:
        return jnp.where(lane == edge, value, turned)
    carried = pltpu.roll(turned, rows if cz == 1 else total - rows, 0)
    clamped = row < rows if cz == 1 else row >= total - rows
    return jnp.where(lane == edge, jnp.where(clamped, value, carried), turned)


def crossed(value, cy, cs):
    if cy == 0:
        return value
    row = lax.broadcasted_iota(jnp.int32, value.shape, 0) % cs
    turned = pltpu.roll(value, 1 if cy == 1 else value.shape[0] - 1, 0)
    return jnp.where(row == (0 if cy == 1 else cs - 1), value, turned)


def turned_to(value, source, dest):
    shift = (dest - source) % value.shape[0]
    return value if shift == 0 else pltpu.roll(value, shift, 0)


def repeat(count, body, start):
    if count > 8:
        return lax.fori_loop(0, count, body, start)
    for i in range(count):
        start = body(i, start)
    return start


def plenum_kernel(sizes, relayed, room_in, plen_in, cell_in, owner_in, class_in, room_near, plen_post, *rest):
    ca, cs, blocks, n_span, per_brick = sizes
    jets = rest[:-7]
    columns, dealt, plen_buf, cells, owners, classes, sems = rest[-7:]
    copies = [pltpu.make_async_copy(src, dst, sems.at[i]) for i, (src, dst) in enumerate(
        ((plen_in, plen_buf), (cell_in, cells), (owner_in, owners), (class_in, classes), (room_in, room_near)))]
    for copy in copies:
        copy.start()
    dealt[...] = jnp.zeros_like(dealt)
    copies[0].wait()
    for r in range(0, ca * cs, 8):
        post = collide([plen_buf[q, r : r + 8] for q in range(19)])
        for q in range(19):
            plen_post[q, r : r + 8] = post[q]
        for k, q in enumerate(UPWARD):
            for y in range(8):
                columns[r + y, :, k * LANES : (k + 1) * LANES] = post[q][y : y + 1]
    for copy in copies[1:4]:
        copy.wait()
    here = lax.axis_index("span")
    first = here * per_brick

    def send_jet(i, carry):
        t = first + i
        owner = owners[t]
        share = 0.15 * (classes[t].astype(F32) + 1.0)
        same = lambda j, n: n + (owners[first + j] == owner).astype(jnp.int32)
        slot = repeat(i, same, 0) if relayed else lax.fori_loop(0, i, same, 0)
        to = (owner ^ here if relayed else owner) * CAP + slot
        dealt[to] = share * columns[cells[t]]
        return carry

    if relayed:
        for i in range(per_brick):
            send_jet(i, 0)
    else:
        lax.fori_loop(0, per_brick, send_jet, 0)
    for part, jet in enumerate(jets):
        many = jet.shape[0]
        jet[...] = dealt[part * many : (part + 1) * many]
    copies[4].wait()


def room_kernel(sizes, room_near, plen_post, room_post, swap_a, swap_b):
    ca, cs, blocks, n_span, per_brick = sizes
    rows = blocks * cs

    def plane(x, carry):
        for r in range(0, rows, 8):
            post = collide([room_near[q, x, r : r + 8] for q in range(19)])
            for q in range(19):
                room_post[q, x, r : r + 8] = post[q]
        return carry

    lax.fori_loop(0, ca, plane, 0)
    even = lax.axis_index("aisle") % 2 == 0
    for k in range(5):
        up, down = X_UP[k], X_DOWN[k]
        rising = raised(room_post[up, ca - 1], VELOCITIES[up][2], cs)
        falling = raised(room_post[down, 0], VELOCITIES[down][2], cs)
        swap_a[k * rows : (k + 1) * rows] = jnp.where(even, rising, falling)
        swap_b[k * rows : (k + 1) * rows] = jnp.where(even, falling, rising)
        rising = raised(plen_post[up, (ca - 1) * cs : ca * cs], VELOCITIES[up][2], cs)
        falling = raised(plen_post[down, 0:cs], VELOCITIES[down][2], cs)
        low = 5 * rows + k * cs
        swap_a[low : low + cs] = jnp.where(even, rising, falling)
        swap_b[low : low + cs] = jnp.where(even, falling, rising)


def jet_sums(start, places, bricks):
    sums = [start(k) for k in range(5)]
    for b, jet in bricks:
        for s in range(CAP):
            marks = places[b * CAP + s]
            sums = [total + marks * jet(s, k) for k, total in enumerate(sums)]
    return sums


def local_kernel(sizes, room_post, plen_post, cell_in, owner_in, room_part, plen_part, span_up, span_down, places,
                 cells, owners, sems):
    ca, cs, blocks, n_span, per_brick = sizes
    rows = blocks * cs
    copies = [pltpu.make_async_copy(src, dst, sems.at[i]) for i, (src, dst) in enumerate(
        ((cell_in, cells), (owner_in, owners)))]
    for copy in copies:
        copy.start()
    group = lax.broadcasted_iota(jnp.int32, (rows, LANES), 0) % cs
    for q in range(19):
        cx, cy, cz = VELOCITIES[q]
        edge = cs - 1 if cy == 1 else 0
        span, planes = (span_up, Y_UP) if cy == 1 else (span_down, Y_DOWN)
        packed = None
        for x in range(ca):
            if not 0 <= x - cx < ca:
                continue
            value = raised(room_post[q, x - cx], cz, cs)
            room_part[q, x] = crossed(value, cy, cs)
            if cy:
                ready = turned_to(value, edge, x)
                packed = ready if packed is None else jnp.where(group == x, ready, packed)
        value = raised(plen_post[q], cz, ca * cs)
        if cx == 1:
            value = pltpu.roll(value, cs, 0)
        elif cx == -1:
            value = pltpu.roll(value, ca * cs - cs, 0)
        plen_part[q] = crossed(value, cy, cs)
        if cy:
            k = planes.index(q)
            span[k * rows : (k + 1) * rows] = packed
            for x in range(ca):
                to = 5 * rows + k * ca + x
                span[to : to + 1] = value[x * cs + edge : x * cs + edge + 1]
    places[0 : n_span * CAP] = jnp.zeros((n_span * CAP, ca * cs, LANES), F32)
    here = lax.axis_index("span")
    row = lax.broadcasted_iota(jnp.int32, (ca * cs, LANES), 0)
    for copy in copies:
        copy.wait()

    def brick(b, carry):
        def place(i, slot):
            t = b * per_brick + i
            mine = owners[t] == here
            places[jnp.where(mine, b * CAP + slot, n_span * CAP)] = (row == cells[t]).astype(F32)
            return slot + mine.astype(jnp.int32)

        repeat(per_brick, place, 0)
        return carry

    repeat(n_span, brick, 0)


def pack_kernel(sizes, relayed, got_a, got_b, span_up, span_down, *rest):
    ca, cs, blocks, n_span, per_brick = sizes
    rows = blocks * cs
    if relayed:
        jets, got_jets, cross_a, cross_b = rest
    else:
        cross_a, cross_b = rest
    even = lax.axis_index("aisle") % 2 == 0
    low = lax.axis_index("span") % 2 == 0
    halo = span_up.shape[0]
    group = lax.broadcasted_iota(jnp.int32, (rows, LANES), 0) % cs

    def corner(q, low, high):
        if VELOCITIES[q][0] == 1:
            k = X_UP.index(q)
            return jnp.where(even, got_b[low(k) : high(k)], got_a[low(k) : high(k)])
        k = X_DOWN.index(q)
        return jnp.where(even, got_a[low(k) : high(k)], got_b[low(k) : high(k)])

    for k in range(5):
        sides = []
        for span, planes, edge in ((span_up, Y_UP, cs - 1), (span_down, Y_DOWN, 0)):
            q = planes[k]
            value = span[k * rows : (k + 1) * rows]
            if VELOCITIES[q][0]:
                x = 0 if VELOCITIES[q][0] == 1 else ca - 1
                came = corner(q, lambda k: k * rows, lambda k: (k + 1) * rows)
                value = jnp.where(group == x, turned_to(came, edge, x), value)
            sides.append(value)
        cross_a[k * rows : (k + 1) * rows] = jnp.where(low, sides[0], sides[1])
        cross_b[k * rows : (k + 1) * rows] = jnp.where(low, sides[1], sides[0])
    for r in range(5 * rows, halo, 8):
        rising, falling = span_up[r : r + 8], span_down[r : r + 8]
        cross_a[r : r + 8] = jnp.where(low, rising, falling)
        cross_b[r : r + 8] = jnp.where(low, falling, rising)
    for planes, edge in ((Y_UP, cs - 1), (Y_DOWN, 0)):
        for k, q in enumerate(planes):
            if VELOCITIES[q][0]:
                x = 0 if VELOCITIES[q][0] == 1 else ca - 1
                at = lambda k: 5 * rows + k * cs + edge
                came = corner(q, at, lambda k: at(k) + 1)
                to = 5 * rows + k * ca + x

                @pl.when(low == (planes is Y_UP))
                def _():
                    cross_a[to : to + 1] = came

                @pl.when(low != (planes is Y_UP))
                def _():
                    cross_b[to : to + 1] = came

    if relayed:
        for b, source in enumerate((jets, got_jets)):
            for s in range(CAP):
                for k in range(5):
                    to = halo + (b * CAP + s) * 5 + k
                    cross_a[to : to + 1] = source[CAP + s, :, k * LANES : (k + 1) * LANES]


def aisle_kernel(sizes, relayed, room_in, plen_in, got_a, got_b, jets, got_jets, places, room, plen, inflow):
    ca, cs, blocks, n_span, per_brick = sizes
    rows = blocks * cs
    even = lax.axis_index("aisle") % 2 == 0
    for k in range(5):
        for q, x, first, second in ((X_UP[k], 0, got_b, got_a), (X_DOWN[k], ca - 1, got_a, got_b)):
            cy = VELOCITIES[q][1]
            low, high = k * rows, (k + 1) * rows
            room[q, x] = crossed(jnp.where(even, first[low:high], second[low:high]), cy, cs)
            low = 5 * rows + k * cs
            value = jnp.where(even, first[low : low + cs], second[low : low + cs])
            at = x * cs
            if cy == 1:
                plen[q, at : at + 1] = value[0:1]
                plen[q, at + 1 : at + cs] = value[: cs - 1]
            elif cy == -1:
                plen[q, at + cs - 1 : at + cs] = value[cs - 1 : cs]
                plen[q, at : at + cs - 1] = value[1:cs]
            else:
                plen[q, at : at + cs] = value
    here = lax.axis_index("span")

    def put(sums):
        for k in range(5):
            inflow[k] = sums[k]

    def reader(source, b):
        return lambda s, k: source[b * CAP + s, :, k * LANES : (k + 1) * LANES]

    if relayed:
        put(jet_sums(lambda k: jnp.zeros((ca * cs, LANES), F32), places,
                     [(here, reader(jets, 0)), (here ^ 2, reader(got_jets, 0))]))
    else:
        inflow[...] = jnp.zeros_like(inflow)

        def add_brick(b, carry):
            put(jet_sums(lambda k: inflow[k], places, [(b, reader(got_jets, b))]))
            return carry

        lax.fori_loop(0, n_span, add_brick, 0)


def finish_kernel(sizes, relayed, room_in, plen_in, got_a, got_b, places, inflow, room, plen, room_out, plen_out, sems):
    ca, cs, blocks, n_span, per_brick = sizes
    rows = blocks * cs
    here = lax.axis_index("span")
    low = here % 2 == 0
    halo = 5 * (rows + cs)
    halo = halo + -halo % 8
    group = lax.broadcasted_iota(jnp.int32, (rows, LANES), 0) % cs
    def enter(got, up):
        planes, y = (Y_UP, 0) if up else (Y_DOWN, cs - 1)
        for k, q in enumerate(planes):
            came = got[k * rows : (k + 1) * rows]
            for x in range(ca):
                room[q, x] = jnp.where(group == y, turned_to(came, x, y), room[q, x])
                at = 5 * rows + k * ca + x
                plen[q, x * cs + y : x * cs + y + 1] = got[at : at + 1]

    @pl.when(low)
    def _():
        enter(got_a, False)

    @pl.when(jnp.logical_not(low))
    def _():
        enter(got_a, True)

    @pl.when(jnp.logical_and(low, here > 0))
    def _():
        enter(got_b, True)

    @pl.when(jnp.logical_and(jnp.logical_not(low), here < n_span - 1))
    def _():
        enter(got_b, False)

    plen_copy = pltpu.make_async_copy(plen, plen_out, sems.at[0])
    plen_copy.start()
    bricks = []
    if relayed:
        def reader(b):
            return lambda s, k: got_a[halo + (b * CAP + s) * 5 + k : halo + (b * CAP + s) * 5 + k + 1]

        bricks = [(here ^ 1, reader(0)), (here ^ 3, reader(1))]
    sums = jet_sums(lambda k: inflow[k], places, bricks)
    for k, q in enumerate(UPWARD):
        for x in range(ca):
            room[q, x, 0:cs] = room[q, x, 0:cs] + sums[k][x * cs : (x + 1) * cs]
    room_copy = pltpu.make_async_copy(room, room_out, sems.at[1])
    room_copy.start()
    plen_copy.wait()
    room_copy.wait()


def call(kernel, outs, in_specs, out_specs=None, scratch=(), aliases={}, flops=100_000, moved=1_000_000):
    return pl.pallas_call(
        kernel,
        out_shape=outs,
        in_specs=in_specs,
        out_specs=[VMEM] * len(outs) if out_specs is None else out_specs,
        scratch_shapes=list(scratch),
        input_output_aliases=aliases,
        cost_estimate=pl.CostEstimate(flops=flops, bytes_accessed=moved, transcendentals=0),
        compiler_params=pltpu.CompilerParams(vmem_limit_bytes=40 * 2**20),
    )


def swap(value, axis, odd, wraps):
    count = lax.axis_size(axis)
    pairs = []
    for i in range(count):
        j = (i ^ 1) if not odd else (i + 1 if i % 2 else i - 1)
        if wraps or 0 <= j < count:
            pairs.append((i, j % count))
    return lax.ppermute(value, axis, pairs)


def shards(room_pops, plenum_pops, tile_cell, tile_owner, tile_class):
    n_span = lax.axis_size("span")
    _, ca, cs, hr = room_pops.shape
    hp = plenum_pops.shape[3]
    blocks = hr // LANES
    rows = blocks * cs
    tiles = tile_cell.shape[0]
    sizes = (ca, cs, blocks, n_span, tiles // n_span)
    relayed = n_span == 4
    near = lambda shape: pltpu.VMEM(shape, F32)
    far = lambda value: pltpu.with_memory_space_constraint(value, pltpu.HBM)
    room_shape, plen_shape = (19, ca, rows, LANES), (19, ca * cs, LANES)
    halo = 5 * (rows + cs)
    halo = halo + -halo % 8
    room = far(room_pops.reshape(19, ca, cs, blocks, LANES).transpose(0, 1, 3, 2, 4).reshape(room_shape))
    plen = far(plenum_pops.reshape(plen_shape))
    tile_cell, tile_owner, tile_class = far(tile_cell), far(tile_owner.reshape(tiles)), far(tile_class)
    numbers = pltpu.SMEM((tiles,), jnp.int32)

    jets_shape = ((2 if relayed else n_span) * CAP, 1, 5 * hp)
    room_near, plen_post, *jets = call(
        functools.partial(plenum_kernel, sizes, relayed),
        [near(room_shape), near(plen_shape)] + [near(jets_shape)] * (2 if relayed else 1),
        [HBM] * 5,
        scratch=[pltpu.VMEM((ca * cs, 1, 5 * hp), F32), near((n_span * CAP, 1, 5 * hp)), near(plen_shape), numbers, numbers, numbers,
                 pltpu.SemaphoreType.DMA((5,))],
    )(room, plen, tile_cell, tile_owner, tile_class)
    if relayed:
        got_jets = lax.ppermute(jets[1], "span", [(i, i ^ 2) for i in range(4)])
    else:
        got_jets = lax.all_to_all(jets[0], "span", 0, 0, tiled=True)

    room_post, swap_a, swap_b = call(
        functools.partial(room_kernel, sizes),
        [near(room_shape), near((halo + 8, LANES)), near((halo, LANES))],
        [VMEM] * 2,
    )(room_near, plen_post)
    got_b = swap(swap_b, "aisle", True, True)
    got_a = swap(swap_a, "aisle", False, True)

    room_part, plen_part, span_up, span_down, places = call(
        functools.partial(local_kernel, sizes),
        [near(room_shape), near(plen_shape), near((halo, LANES)), near((halo, LANES)),
         near((n_span * CAP + 1, ca * cs, LANES))],
        [VMEM, VMEM, HBM, HBM],
        scratch=[numbers, numbers, pltpu.SemaphoreType.DMA((2,))],
        flops=10**9,
    )(room_post, plen_post, tile_cell, tile_owner)

    cross_shape = (halo + 2 * CAP * 5, LANES) if relayed else (halo, LANES)
    cross_a, cross_b = call(
        functools.partial(pack_kernel, sizes, relayed),
        [near(cross_shape), near((halo, LANES))],
        [VMEM] * (6 if relayed else 4),
    )(got_a, got_b, span_up, span_down, *((jets[0], got_jets) if relayed else ()))

    in_b = swap(cross_b, "span", True, False)
    in_a = swap(cross_a, "span", False, False)
    room_part, plen_part, inflow = call(
        functools.partial(aisle_kernel, sizes, relayed),
        [near(room_shape), near(plen_shape), near((5, ca * cs, LANES))],
        [VMEM] * 7,
        aliases={0: 0, 1: 1},
        flops=10**9,
    )(room_part, plen_part, got_a, got_b, jets[0], got_jets, places)

    _, _, room_next, plenum_next = call(
        functools.partial(finish_kernel, sizes, relayed),
        [near(room_shape), near(plen_shape), jax.ShapeDtypeStruct(room_shape, F32),
         jax.ShapeDtypeStruct(plen_shape, F32)],
        [VMEM] * 6,
        out_specs=[VMEM, VMEM, HBM, HBM],
        scratch=[pltpu.SemaphoreType.DMA((2,))],
        aliases={0: 0, 1: 1},
    )(room_part, plen_part, in_a, in_b, places, inflow)
    room_next = room_next.reshape(19, ca, blocks, cs, LANES).transpose(0, 1, 3, 2, 4).reshape(room_pops.shape)
    return room_next, plenum_next.reshape(plenum_pops.shape)


def solution(mesh):
    return jax.shard_map(
        shards,
        mesh=mesh,
        in_specs=(
            P(None, "aisle", "span", None),
            P(None, "aisle", "span", None),
            P("aisle"),
            P("aisle", None),
            P("aisle"),
        ),
        out_specs=(P(None, "aisle", "span", None), P(None, "aisle", "span", None)),
        check_vma=False,
    )
```

```python
import functools

import jax
import jax.numpy as jnp
from jax import lax
from jax.experimental import pallas as pl
from jax.experimental.pallas import tpu as pltpu
from jax.sharding import PartitionSpec as P

VELOCITIES = [
    (0, 0, 0),
    (1, 0, 0),
    (-1, 0, 0),
    (0, 1, 0),
    (0, -1, 0),
    (0, 0, 1),
    (0, 0, -1),
    (1, 1, 0),
    (-1, -1, 0),
    (1, -1, 0),
    (-1, 1, 0),
    (1, 0, 1),
    (-1, 0, -1),
    (1, 0, -1),
    (-1, 0, 1),
    (0, 1, 1),
    (0, -1, -1),
    (0, 1, -1),
    (0, -1, 1),
]
UPWARD = [5, 11, 14, 15, 18]
OMEGA = 1.25
CAP = 4
X_UP = [q for q in range(19) if VELOCITIES[q][0] == 1]
X_DOWN = [q for q in range(19) if VELOCITIES[q][0] == -1]
Y_UP = [q for q in range(19) if VELOCITIES[q][1] == 1]
Y_DOWN = [q for q in range(19) if VELOCITIES[q][1] == -1]
F32 = jnp.float32
LANES = 128
VMEM = pl.BlockSpec(memory_space=pltpu.VMEM)
HBM = pl.BlockSpec(memory_space=pltpu.HBM)


def collide(g):
    total = lambda i: g[i] + g[i + 1]
    apart = lambda i: g[i] - g[i + 1]
    dx, dy, dz = apart(1), apart(3), apart(5)
    d7, d9, d11, d13, d15, d17 = (apart(i) for i in (7, 9, 11, 13, 15, 17))
    edges = (total(7) + total(9)) + (total(11) + total(13)) + (total(15) + total(17))
    faces = total(1) + total(3) + total(5)
    rho = g[0] * (1.0 / 3.0) + faces * (1.0 / 18.0) + edges * (1.0 / 36.0)
    mx = dx * (1.0 / 18.0) + ((d7 + d9) + (d11 + d13)) * (1.0 / 36.0)
    my = dy * (1.0 / 18.0) + ((d7 - d9) + (d15 + d17)) * (1.0 / 36.0)
    mz = dz * (1.0 / 18.0) + ((d11 - d13) + (d15 - d17)) * (1.0 / 36.0)
    inv = 1.0 / rho
    base = OMEGA * rho - (1.5 * OMEGA) * inv * (mx * mx + my * my + mz * mz)
    square = (4.5 * OMEGA) * inv
    out = [None] * 19
    out[0] = base + (1.0 - OMEGA) * g[0]
    along = {1: mx, 3: my, 5: mz, 7: mx + my, 9: mx - my, 11: mx + mz, 13: mx - mz, 15: my + mz, 17: my - mz}
    for i, c in along.items():
        even = base + square * c * c
        odd = (3.0 * OMEGA) * c
        out[i] = (even + odd) + (1.0 - OMEGA) * g[i]
        out[i + 1] = (even - odd) + (1.0 - OMEGA) * g[i + 1]
    return out


def raised(value, cz, rows):
    if cz == 0:
        return value
    lane = lax.broadcasted_iota(jnp.int32, value.shape, 1)
    row = lax.broadcasted_iota(jnp.int32, value.shape, 0)
    total = value.shape[0]
    shift, edge = (1, 0) if cz == 1 else (LANES - 1, LANES - 1)
    turned = pltpu.roll(value, shift, 1)
    if rows == total:
        return jnp.where(lane == edge, value, turned)
    carried = pltpu.roll(turned, rows if cz == 1 else total - rows, 0)
    clamped = row < rows if cz == 1 else row >= total - rows
    return jnp.where(lane == edge, jnp.where(clamped, value, carried), turned)


def crossed(value, cy, cs):
    if cy == 0:
        return value
    row = lax.broadcasted_iota(jnp.int32, value.shape, 0) % cs
    turned = pltpu.roll(value, 1 if cy == 1 else value.shape[0] - 1, 0)
    return jnp.where(row == (0 if cy == 1 else cs - 1), value, turned)


def turned_to(value, source, dest):
    shift = (dest - source) % value.shape[0]
    return value if shift == 0 else pltpu.roll(value, shift, 0)


def repeat(count, body, start):
    if count > 8:
        return lax.fori_loop(0, count, body, start)
    for i in range(count):
        start = body(i, start)
    return start


def plenum_kernel(sizes, relayed, room_in, plen_in, cell_in, owner_in, class_in, room_near, plen_post, *rest):
    ca, cs, blocks, n_span, per_brick = sizes
    jets = rest[:-7]
    columns, dealt, plen_buf, cells, owners, classes, sems = rest[-7:]
    copies = [pltpu.make_async_copy(src, dst, sems.at[i]) for i, (src, dst) in enumerate(
        ((plen_in, plen_buf), (cell_in, cells), (owner_in, owners), (class_in, classes), (room_in, room_near)))]
    for copy in copies:
        copy.start()
    dealt[...] = jnp.zeros_like(dealt)
    copies[0].wait()
    for r in range(0, ca * cs, 8):
        post = collide([plen_buf[q, r : r + 8] for q in range(19)])
        for q in range(19):
            plen_post[q, r : r + 8] = post[q]
        for k, q in enumerate(UPWARD):
            for y in range(8):
                columns[r + y, :, k * LANES : (k + 1) * LANES] = post[q][y : y + 1]
    for copy in copies[1:4]:
        copy.wait()
    here = lax.axis_index("span")
    first = here * per_brick

    def send_jet(i, carry):
        t = first + i
        owner = owners[t]
        share = 0.15 * (classes[t].astype(F32) + 1.0)
        same = lambda j, n: n + (owners[first + j] == owner).astype(jnp.int32)
        slot = repeat(i, same, 0) if relayed else lax.fori_loop(0, i, same, 0)
        to = (owner ^ here if relayed else owner) * CAP + slot
        dealt[to] = share * columns[cells[t]]
        return carry

    if relayed:
        for i in range(per_brick):
            send_jet(i, 0)
    else:
        lax.fori_loop(0, per_brick, send_jet, 0)
    for part, jet in enumerate(jets):
        many = jet.shape[0]
        jet[...] = dealt[part * many : (part + 1) * many]
    copies[4].wait()


def room_kernel(sizes, room_near, plen_post, room_post, swap_a, swap_b):
    ca, cs, blocks, n_span, per_brick = sizes
    rows = blocks * cs

    def plane(x, carry):
        for r in range(0, rows, 8):
            post = collide([room_near[q, x, r : r + 8] for q in range(19)])
            for q in range(19):
                room_post[q, x, r : r + 8] = post[q]
        return carry

    lax.fori_loop(0, ca, plane, 0)
    even = lax.axis_index("aisle") % 2 == 0
    for k in range(5):
        up, down = X_UP[k], X_DOWN[k]
        rising = raised(room_post[up, ca - 1], VELOCITIES[up][2], cs)
        falling = raised(room_post[down, 0], VELOCITIES[down][2], cs)
        swap_a[k * rows : (k + 1) * rows] = jnp.where(even, rising, falling)
        swap_b[k * rows : (k + 1) * rows] = jnp.where(even, falling, rising)
        rising = raised(plen_post[up, (ca - 1) * cs : ca * cs], VELOCITIES[up][2], cs)
        falling = raised(plen_post[down, 0:cs], VELOCITIES[down][2], cs)
        low = 5 * rows + k * cs
        swap_a[low : low + cs] = jnp.where(even, rising, falling)
        swap_b[low : low + cs] = jnp.where(even, falling, rising)


def jet_sums(start, places, bricks):
    sums = [start(k) for k in range(5)]
    for b, jet in bricks:
        for s in range(CAP):
            marks = places[b * CAP + s]
            sums = [total + marks * jet(s, k) for k, total in enumerate(sums)]
    return sums


def local_kernel(sizes, room_post, plen_post, cell_in, owner_in, room_part, plen_part, span_up, span_down, places,
                 cells, owners, sems):
    ca, cs, blocks, n_span, per_brick = sizes
    rows = blocks * cs
    copies = [pltpu.make_async_copy(src, dst, sems.at[i]) for i, (src, dst) in enumerate(
        ((cell_in, cells), (owner_in, owners)))]
    for copy in copies:
        copy.start()
    group = lax.broadcasted_iota(jnp.int32, (rows, LANES), 0) % cs
    for q in range(19):
        cx, cy, cz = VELOCITIES[q]
        edge = cs - 1 if cy == 1 else 0
        span, planes = (span_up, Y_UP) if cy == 1 else (span_down, Y_DOWN)
        packed = None
        for x in range(ca):
            if not 0 <= x - cx < ca:
                continue
            value = raised(room_post[q, x - cx], cz, cs)
            room_part[q, x] = crossed(value, cy, cs)
            if cy:
                ready = turned_to(value, edge, x)
                packed = ready if packed is None else jnp.where(group == x, ready, packed)
        value = raised(plen_post[q], cz, ca * cs)
        if cx == 1:
            value = pltpu.roll(value, cs, 0)
        elif cx == -1:
            value = pltpu.roll(value, ca * cs - cs, 0)
        plen_part[q] = crossed(value, cy, cs)
        if cy:
            k = planes.index(q)
            span[k * rows : (k + 1) * rows] = packed
            for x in range(ca):
                to = 5 * rows + k * ca + x
                span[to : to + 1] = value[x * cs + edge : x * cs + edge + 1]
    places[0 : n_span * CAP] = jnp.zeros((n_span * CAP, ca * cs, LANES), F32)
    here = lax.axis_index("span")
    row = lax.broadcasted_iota(jnp.int32, (ca * cs, LANES), 0)
    for copy in copies:
        copy.wait()

    def brick(b, carry):
        def place(i, slot):
            t = b * per_brick + i
            mine = owners[t] == here
            places[jnp.where(mine, b * CAP + slot, n_span * CAP)] = (row == cells[t]).astype(F32)
            return slot + mine.astype(jnp.int32)

        repeat(per_brick, place, 0)
        return carry

    repeat(n_span, brick, 0)


def pack_kernel(sizes, relayed, got_a, got_b, span_up, span_down, *rest):
    ca, cs, blocks, n_span, per_brick = sizes
    rows = blocks * cs
    if relayed:
        jets, got_jets, cross_a, cross_b = rest
    else:
        cross_a, cross_b = rest
    even = lax.axis_index("aisle") % 2 == 0
    low = lax.axis_index("span") % 2 == 0
    halo = span_up.shape[0]
    group = lax.broadcasted_iota(jnp.int32, (rows, LANES), 0) % cs

    def corner(q, low, high):
        if VELOCITIES[q][0] == 1:
            k = X_UP.index(q)
            return jnp.where(even, got_b[low(k) : high(k)], got_a[low(k) : high(k)])
        k = X_DOWN.index(q)
        return jnp.where(even, got_a[low(k) : high(k)], got_b[low(k) : high(k)])

    for k in range(5):
        sides = []
        for span, planes, edge in ((span_up, Y_UP, cs - 1), (span_down, Y_DOWN, 0)):
            q = planes[k]
            value = span[k * rows : (k + 1) * rows]
            if VELOCITIES[q][0]:
                x = 0 if VELOCITIES[q][0] == 1 else ca - 1
                came = corner(q, lambda k: k * rows, lambda k: (k + 1) * rows)
                value = jnp.where(group == x, turned_to(came, edge, x), value)
            sides.append(value)
        cross_a[k * rows : (k + 1) * rows] = jnp.where(low, sides[0], sides[1])
        cross_b[k * rows : (k + 1) * rows] = jnp.where(low, sides[1], sides[0])
    for r in range(5 * rows, halo, 8):
        rising, falling = span_up[r : r + 8], span_down[r : r + 8]
        cross_a[r : r + 8] = jnp.where(low, rising, falling)
        cross_b[r : r + 8] = jnp.where(low, falling, rising)
    for planes, edge in ((Y_UP, cs - 1), (Y_DOWN, 0)):
        for k, q in enumerate(planes):
            if VELOCITIES[q][0]:
                x = 0 if VELOCITIES[q][0] == 1 else ca - 1
                at = lambda k: 5 * rows + k * cs + edge
                came = corner(q, at, lambda k: at(k) + 1)
                to = 5 * rows + k * ca + x

                @pl.when(low == (planes is Y_UP))
                def _():
                    cross_a[to : to + 1] = came

                @pl.when(low != (planes is Y_UP))
                def _():
                    cross_b[to : to + 1] = came

    if relayed:
        for b, source in enumerate((jets, got_jets)):
            for s in range(CAP):
                for k in range(5):
                    to = halo + (b * CAP + s) * 5 + k
                    cross_a[to : to + 1] = source[CAP + s, :, k * LANES : (k + 1) * LANES]


def aisle_kernel(sizes, relayed, room_in, plen_in, got_a, got_b, jets, got_jets, places, room, plen, inflow):
    ca, cs, blocks, n_span, per_brick = sizes
    rows = blocks * cs
    even = lax.axis_index("aisle") % 2 == 0
    for k in range(5):
        for q, x, first, second in ((X_UP[k], 0, got_b, got_a), (X_DOWN[k], ca - 1, got_a, got_b)):
            cy = VELOCITIES[q][1]
            low, high = k * rows, (k + 1) * rows
            room[q, x] = crossed(jnp.where(even, first[low:high], second[low:high]), cy, cs)
            low = 5 * rows + k * cs
            value = jnp.where(even, first[low : low + cs], second[low : low + cs])
            at = x * cs
            if cy == 1:
                plen[q, at : at + 1] = value[0:1]
                plen[q, at + 1 : at + cs] = value[: cs - 1]
            elif cy == -1:
                plen[q, at + cs - 1 : at + cs] = value[cs - 1 : cs]
                plen[q, at : at + cs - 1] = value[1:cs]
            else:
                plen[q, at : at + cs] = value
    here = lax.axis_index("span")

    def put(sums):
        for k in range(5):
            inflow[k] = sums[k]

    def reader(source, b):
        return lambda s, k: source[b * CAP + s, :, k * LANES : (k + 1) * LANES]

    if relayed:
        put(jet_sums(lambda k: jnp.zeros((ca * cs, LANES), F32), places,
                     [(here, reader(jets, 0)), (here ^ 2, reader(got_jets, 0))]))
    else:
        inflow[...] = jnp.zeros_like(inflow)

        def add_brick(b, carry):
            put(jet_sums(lambda k: inflow[k], places, [(b, reader(got_jets, b))]))
            return carry

        lax.fori_loop(0, n_span, add_brick, 0)


def finish_kernel(sizes, relayed, room_in, plen_in, got_a, got_b, places, inflow, room, plen, room_out, plen_out, sems):
    ca, cs, blocks, n_span, per_brick = sizes
    rows = blocks * cs
    here = lax.axis_index("span")
    low = here % 2 == 0
    halo = 5 * (rows + cs)
    halo = halo + -halo % 8
    group = lax.broadcasted_iota(jnp.int32, (rows, LANES), 0) % cs
    def enter(got, up):
        planes, y = (Y_UP, 0) if up else (Y_DOWN, cs - 1)
        for k, q in enumerate(planes):
            came = got[k * rows : (k + 1) * rows]
            for x in range(ca):
                room[q, x] = jnp.where(group == y, turned_to(came, x, y), room[q, x])
                at = 5 * rows + k * ca + x
                plen[q, x * cs + y : x * cs + y + 1] = got[at : at + 1]

    @pl.when(low)
    def _():
        enter(got_a, False)

    @pl.when(jnp.logical_not(low))
    def _():
        enter(got_a, True)

    @pl.when(jnp.logical_and(low, here > 0))
    def _():
        enter(got_b, True)

    @pl.when(jnp.logical_and(jnp.logical_not(low), here < n_span - 1))
    def _():
        enter(got_b, False)

    plen_copy = pltpu.make_async_copy(plen, plen_out, sems.at[0])
    plen_copy.start()
    bricks = []
    if relayed:
        def reader(b):
            return lambda s, k: got_a[halo + (b * CAP + s) * 5 + k : halo + (b * CAP + s) * 5 + k + 1]

        bricks = [(here ^ 1, reader(0)), (here ^ 3, reader(1))]
    sums = jet_sums(lambda k: inflow[k], places, bricks)
    for k, q in enumerate(UPWARD):
        for x in range(ca):
            room[q, x, 0:cs] = room[q, x, 0:cs] + sums[k][x * cs : (x + 1) * cs]
    room_copy = pltpu.make_async_copy(room, room_out, sems.at[1])
    room_copy.start()
    plen_copy.wait()
    room_copy.wait()


def call(kernel, outs, in_specs, out_specs=None, scratch=(), aliases={}, flops=100_000, moved=1_000_000):
    return pl.pallas_call(
        kernel,
        out_shape=outs,
        in_specs=in_specs,
        out_specs=[VMEM] * len(outs) if out_specs is None else out_specs,
        scratch_shapes=list(scratch),
        input_output_aliases=aliases,
        cost_estimate=pl.CostEstimate(flops=flops, bytes_accessed=moved, transcendentals=0),
        compiler_params=pltpu.CompilerParams(vmem_limit_bytes=40 * 2**20),
    )


def swap(value, axis, odd, wraps):
    count = lax.axis_size(axis)
    pairs = []
    for i in range(count):
        j = (i ^ 1) if not odd else (i + 1 if i % 2 else i - 1)
        pairs.append((i, j % count if wraps or 0 <= j < count else i))
    return lax.ppermute(value, axis, pairs)


def shards(room_pops, plenum_pops, tile_cell, tile_owner, tile_class):
    n_span = lax.axis_size("span")
    _, ca, cs, hr = room_pops.shape
    hp = plenum_pops.shape[3]
    blocks = hr // LANES
    rows = blocks * cs
    tiles = tile_cell.shape[0]
    sizes = (ca, cs, blocks, n_span, tiles // n_span)
    relayed = n_span == 4
    near = lambda shape: pltpu.VMEM(shape, F32)
    far = lambda value: pltpu.with_memory_space_constraint(value, pltpu.HBM)
    room_shape, plen_shape = (19, ca, rows, LANES), (19, ca * cs, LANES)
    halo = 5 * (rows + cs)
    halo = halo + -halo % 8
    room = far(room_pops.reshape(19, ca, cs, blocks, LANES).transpose(0, 1, 3, 2, 4).reshape(room_shape))
    plen = far(plenum_pops.reshape(plen_shape))
    tile_cell, tile_owner, tile_class = far(tile_cell), far(tile_owner.reshape(tiles)), far(tile_class)
    numbers = pltpu.SMEM((tiles,), jnp.int32)

    jets_shape = ((2 if relayed else n_span) * CAP, 1, 5 * hp)
    room_near, plen_post, *jets = call(
        functools.partial(plenum_kernel, sizes, relayed),
        [near(room_shape), near(plen_shape)] + [near(jets_shape)] * (2 if relayed else 1),
        [HBM] * 5,
        scratch=[pltpu.VMEM((ca * cs, 1, 5 * hp), F32), near((n_span * CAP, 1, 5 * hp)), near(plen_shape), numbers, numbers, numbers,
                 pltpu.SemaphoreType.DMA((5,))],
    )(room, plen, tile_cell, tile_owner, tile_class)
    if relayed:
        got_jets = lax.ppermute(jets[1], "span", [(i, i ^ 2) for i in range(4)])
    else:
        got_jets = lax.all_to_all(jets[0], "span", 0, 0, tiled=True)

    room_post, swap_a, swap_b = call(
        functools.partial(room_kernel, sizes),
        [near(room_shape), near((halo + 8, LANES)), near((halo, LANES))],
        [VMEM] * 2,
    )(room_near, plen_post)
    got_b = swap(swap_b, "aisle", True, True)
    got_a = swap(swap_a, "aisle", False, True)

    room_part, plen_part, span_up, span_down, places = call(
        functools.partial(local_kernel, sizes),
        [near(room_shape), near(plen_shape), near((halo, LANES)), near((halo, LANES)),
         near((n_span * CAP + 1, ca * cs, LANES))],
        [VMEM, VMEM, HBM, HBM],
        scratch=[numbers, numbers, pltpu.SemaphoreType.DMA((2,))],
        flops=10**9,
    )(room_post, plen_post, tile_cell, tile_owner)

    cross_shape = (halo + 2 * CAP * 5, LANES) if relayed else (halo, LANES)
    cross_a, cross_b = call(
        functools.partial(pack_kernel, sizes, relayed),
        [near(cross_shape), near((halo, LANES))],
        [VMEM] * (6 if relayed else 4),
    )(got_a, got_b, span_up, span_down, *((jets[0], got_jets) if relayed else ()))

    in_b = swap(cross_b, "span", True, False)
    in_a = swap(cross_a, "span", False, False)
    room_part, plen_part, inflow = call(
        functools.partial(aisle_kernel, sizes, relayed),
        [near(room_shape), near(plen_shape), near((5, ca * cs, LANES))],
        [VMEM] * 7,
        aliases={0: 0, 1: 1},
        flops=10**9,
    )(room_part, plen_part, got_a, got_b, jets[0], got_jets, places)

    _, _, room_next, plenum_next = call(
        functools.partial(finish_kernel, sizes, relayed),
        [near(room_shape), near(plen_shape), jax.ShapeDtypeStruct(room_shape, F32),
         jax.ShapeDtypeStruct(plen_shape, F32)],
        [VMEM] * 6,
        out_specs=[VMEM, VMEM, HBM, HBM],
        scratch=[pltpu.SemaphoreType.DMA((2,))],
        aliases={0: 0, 1: 1},
    )(room_part, plen_part, in_a, in_b, places, inflow)
    room_next = room_next.reshape(19, ca, blocks, cs, LANES).transpose(0, 1, 3, 2, 4).reshape(room_pops.shape)
    return room_next, plenum_next.reshape(plenum_pops.shape)


def solution(mesh):
    return jax.shard_map(
        shards,
        mesh=mesh,
        in_specs=(
            P(None, "aisle", "span", None),
            P(None, "aisle", "span", None),
            P("aisle"),
            P("aisle", None),
            P("aisle"),
        ),
        out_specs=(P(None, "aisle", "span", None), P(None, "aisle", "span", None)),
        check_vma=False,
    )
```

```python
import functools

import jax
import jax.numpy as jnp
from jax import lax
from jax.experimental import pallas as pl
from jax.experimental.pallas import tpu as pltpu
from jax.sharding import PartitionSpec as P

VELOCITIES = [
    (0, 0, 0),
    (1, 0, 0),
    (-1, 0, 0),
    (0, 1, 0),
    (0, -1, 0),
    (0, 0, 1),
    (0, 0, -1),
    (1, 1, 0),
    (-1, -1, 0),
    (1, -1, 0),
    (-1, 1, 0),
    (1, 0, 1),
    (-1, 0, -1),
    (1, 0, -1),
    (-1, 0, 1),
    (0, 1, 1),
    (0, -1, -1),
    (0, 1, -1),
    (0, -1, 1),
]
UPWARD = [5, 11, 14, 15, 18]
OMEGA = 1.25
CAP = 4
X_UP = [q for q in range(19) if VELOCITIES[q][0] == 1]
X_DOWN = [q for q in range(19) if VELOCITIES[q][0] == -1]
Y_UP = [q for q in range(19) if VELOCITIES[q][1] == 1]
Y_DOWN = [q for q in range(19) if VELOCITIES[q][1] == -1]
F32 = jnp.float32
LANES = 128
VMEM = pl.BlockSpec(memory_space=pltpu.VMEM)
HBM = pl.BlockSpec(memory_space=pltpu.HBM)


def collide(g):
    total = lambda i: g[i] + g[i + 1]
    apart = lambda i: g[i] - g[i + 1]
    dx, dy, dz = apart(1), apart(3), apart(5)
    d7, d9, d11, d13, d15, d17 = (apart(i) for i in (7, 9, 11, 13, 15, 17))
    edges = (total(7) + total(9)) + (total(11) + total(13)) + (total(15) + total(17))
    faces = total(1) + total(3) + total(5)
    rho = g[0] * (1.0 / 3.0) + faces * (1.0 / 18.0) + edges * (1.0 / 36.0)
    mx = dx * (1.0 / 18.0) + ((d7 + d9) + (d11 + d13)) * (1.0 / 36.0)
    my = dy * (1.0 / 18.0) + ((d7 - d9) + (d15 + d17)) * (1.0 / 36.0)
    mz = dz * (1.0 / 18.0) + ((d11 - d13) + (d15 - d17)) * (1.0 / 36.0)
    inv = 1.0 / rho
    base = OMEGA * rho - (1.5 * OMEGA) * inv * (mx * mx + my * my + mz * mz)
    square = (4.5 * OMEGA) * inv
    out = [None] * 19
    out[0] = base + (1.0 - OMEGA) * g[0]
    along = {1: mx, 3: my, 5: mz, 7: mx + my, 9: mx - my, 11: mx + mz, 13: mx - mz, 15: my + mz, 17: my - mz}
    for i, c in along.items():
        even = base + square * c * c
        odd = (3.0 * OMEGA) * c
        out[i] = (even + odd) + (1.0 - OMEGA) * g[i]
        out[i + 1] = (even - odd) + (1.0 - OMEGA) * g[i + 1]
    return out


def raised(value, cz, rows):
    if cz == 0:
        return value
    lane = lax.broadcasted_iota(jnp.int32, value.shape, 1)
    row = lax.broadcasted_iota(jnp.int32, value.shape, 0)
    total = value.shape[0]
    shift, edge = (1, 0) if cz == 1 else (LANES - 1, LANES - 1)
    turned = pltpu.roll(value, shift, 1)
    if rows == total:
        return jnp.where(lane == edge, value, turned)
    carried = pltpu.roll(turned, rows if cz == 1 else total - rows, 0)
    clamped = row < rows if cz == 1 else row >= total - rows
    return jnp.where(lane == edge, jnp.where(clamped, value, carried), turned)


def crossed(value, cy, cs):
    if cy == 0:
        return value
    row = lax.broadcasted_iota(jnp.int32, value.shape, 0) % cs
    turned = pltpu.roll(value, 1 if cy == 1 else value.shape[0] - 1, 0)
    return jnp.where(row == (0 if cy == 1 else cs - 1), value, turned)


def turned_to(value, source, dest):
    shift = (dest - source) % value.shape[0]
    return value if shift == 0 else pltpu.roll(value, shift, 0)


def repeat(count, body, start):
    if count > 8:
        return lax.fori_loop(0, count, body, start)
    for i in range(count):
        start = body(i, start)
    return start


def plenum_kernel(sizes, relayed, room_in, plen_in, cell_in, owner_in, class_in, room_near, plen_post, *rest):
    ca, cs, blocks, n_span, per_brick = sizes
    jets = rest[:-7]
    columns, dealt, plen_buf, cells, owners, classes, sems = rest[-7:]
    copies = [pltpu.make_async_copy(src, dst, sems.at[i]) for i, (src, dst) in enumerate(
        ((plen_in, plen_buf), (cell_in, cells), (owner_in, owners), (class_in, classes), (room_in, room_near)))]
    for copy in copies:
        copy.start()
    dealt[...] = jnp.zeros_like(dealt)
    copies[0].wait()
    for r in range(0, ca * cs, 8):
        post = collide([plen_buf[q, r : r + 8] for q in range(19)])
        for q in range(19):
            plen_post[q, r : r + 8] = post[q]
        for k, q in enumerate(UPWARD):
            for y in range(8):
                columns[r + y, :, k * LANES : (k + 1) * LANES] = post[q][y : y + 1]
    for copy in copies[1:4]:
        copy.wait()
    here = lax.axis_index("span")
    first = here * per_brick

    def send_jet(i, carry):
        t = first + i
        owner = owners[t]
        share = 0.15 * (classes[t].astype(F32) + 1.0)
        same = lambda j, n: n + (owners[first + j] == owner).astype(jnp.int32)
        slot = repeat(i, same, 0) if relayed else lax.fori_loop(0, i, same, 0)
        to = (owner ^ here if relayed else owner) * CAP + slot
        dealt[to] = share * columns[cells[t]]
        return carry

    if relayed:
        for i in range(per_brick):
            send_jet(i, 0)
    else:
        lax.fori_loop(0, per_brick, send_jet, 0)
    for part, jet in enumerate(jets):
        many = jet.shape[0]
        jet[...] = dealt[part * many : (part + 1) * many]
    copies[4].wait()


def room_kernel(sizes, room_near, plen_post, room_post, swap_a, swap_b):
    ca, cs, blocks, n_span, per_brick = sizes
    rows = blocks * cs

    def plane(x, carry):
        for r in range(0, rows, 8):
            post = collide([room_near[q, x, r : r + 8] for q in range(19)])
            for q in range(19):
                room_post[q, x, r : r + 8] = post[q]
        return carry

    lax.fori_loop(0, ca, plane, 0)
    even = lax.axis_index("aisle") % 2 == 0
    for k in range(5):
        up, down = X_UP[k], X_DOWN[k]
        rising = raised(room_post[up, ca - 1], VELOCITIES[up][2], cs)
        falling = raised(room_post[down, 0], VELOCITIES[down][2], cs)
        swap_a[k * rows : (k + 1) * rows] = jnp.where(even, rising, falling)
        swap_b[k * rows : (k + 1) * rows] = jnp.where(even, falling, rising)
        rising = raised(plen_post[up, (ca - 1) * cs : ca * cs], VELOCITIES[up][2], cs)
        falling = raised(plen_post[down, 0:cs], VELOCITIES[down][2], cs)
        low = 5 * rows + k * cs
        swap_a[low : low + cs] = jnp.where(even, rising, falling)
        swap_b[low : low + cs] = jnp.where(even, falling, rising)


def jet_sums(start, places, bricks):
    sums = [start(k) for k in range(5)]
    for b, jet in bricks:
        for s in range(CAP):
            marks = places[b * CAP + s]
            sums = [total + marks * jet(s, k) for k, total in enumerate(sums)]
    return sums


def local_kernel(sizes, room_post, plen_post, cell_in, owner_in, room_part, plen_part, span_up, span_down, places,
                 cells, owners, sems):
    ca, cs, blocks, n_span, per_brick = sizes
    rows = blocks * cs
    copies = [pltpu.make_async_copy(src, dst, sems.at[i]) for i, (src, dst) in enumerate(
        ((cell_in, cells), (owner_in, owners)))]
    for copy in copies:
        copy.start()
    group = lax.broadcasted_iota(jnp.int32, (rows, LANES), 0) % cs
    for q in range(19):
        cx, cy, cz = VELOCITIES[q]
        edge = cs - 1 if cy == 1 else 0
        span, planes = (span_up, Y_UP) if cy == 1 else (span_down, Y_DOWN)
        packed = None
        for x in range(ca):
            if not 0 <= x - cx < ca:
                continue
            value = raised(room_post[q, x - cx], cz, cs)
            room_part[q, x] = crossed(value, cy, cs)
            if cy:
                ready = turned_to(value, edge, x)
                packed = ready if packed is None else jnp.where(group == x, ready, packed)
        value = raised(plen_post[q], cz, ca * cs)
        if cx == 1:
            value = pltpu.roll(value, cs, 0)
        elif cx == -1:
            value = pltpu.roll(value, ca * cs - cs, 0)
        plen_part[q] = crossed(value, cy, cs)
        if cy:
            k = planes.index(q)
            span[k * rows : (k + 1) * rows] = packed
            for x in range(ca):
                to = 5 * rows + k * ca + x
                span[to : to + 1] = value[x * cs + edge : x * cs + edge + 1]
    places[0 : n_span * CAP] = jnp.zeros((n_span * CAP, ca * cs, LANES), F32)
    here = lax.axis_index("span")
    row = lax.broadcasted_iota(jnp.int32, (ca * cs, LANES), 0)
    for copy in copies:
        copy.wait()

    def brick(b, carry):
        def place(i, slot):
            t = b * per_brick + i
            mine = owners[t] == here
            places[jnp.where(mine, b * CAP + slot, n_span * CAP)] = (row == cells[t]).astype(F32)
            return slot + mine.astype(jnp.int32)

        repeat(per_brick, place, 0)
        return carry

    repeat(n_span, brick, 0)


def pack_kernel(sizes, relayed, got_a, got_b, span_up, span_down, *rest):
    ca, cs, blocks, n_span, per_brick = sizes
    rows = blocks * cs
    if relayed:
        jets, got_jets, cross_a, cross_b = rest
    else:
        cross_a, cross_b = rest
    even = lax.axis_index("aisle") % 2 == 0
    low = lax.axis_index("span") % 2 == 0
    halo = span_up.shape[0]
    group = lax.broadcasted_iota(jnp.int32, (rows, LANES), 0) % cs

    def corner(q, low, high):
        if VELOCITIES[q][0] == 1:
            k = X_UP.index(q)
            return jnp.where(even, got_b[low(k) : high(k)], got_a[low(k) : high(k)])
        k = X_DOWN.index(q)
        return jnp.where(even, got_a[low(k) : high(k)], got_b[low(k) : high(k)])

    for k in range(5):
        sides = []
        for span, planes, edge in ((span_up, Y_UP, cs - 1), (span_down, Y_DOWN, 0)):
            q = planes[k]
            value = span[k * rows : (k + 1) * rows]
            if VELOCITIES[q][0]:
                x = 0 if VELOCITIES[q][0] == 1 else ca - 1
                came = corner(q, lambda k: k * rows, lambda k: (k + 1) * rows)
                value = jnp.where(group == x, turned_to(came, edge, x), value)
            sides.append(value)
        cross_a[k * rows : (k + 1) * rows] = jnp.where(low, sides[0], sides[1])
        cross_b[k * rows : (k + 1) * rows] = jnp.where(low, sides[1], sides[0])
    for r in range(5 * rows, halo, 8):
        rising, falling = span_up[r : r + 8], span_down[r : r + 8]
        cross_a[r : r + 8] = jnp.where(low, rising, falling)
        cross_b[r : r + 8] = jnp.where(low, falling, rising)
    for planes, edge in ((Y_UP, cs - 1), (Y_DOWN, 0)):
        for k, q in enumerate(planes):
            if VELOCITIES[q][0]:
                x = 0 if VELOCITIES[q][0] == 1 else ca - 1
                at = lambda k: 5 * rows + k * cs + edge
                came = corner(q, at, lambda k: at(k) + 1)
                to = 5 * rows + k * ca + x

                @pl.when(low == (planes is Y_UP))
                def _():
                    cross_a[to : to + 1] = came

                @pl.when(low != (planes is Y_UP))
                def _():
                    cross_b[to : to + 1] = came

    if relayed:
        for b, source in enumerate((jets, got_jets)):
            for s in range(CAP):
                for k in range(5):
                    to = halo + (b * CAP + s) * 5 + k
                    cross_a[to : to + 1] = source[CAP + s, :, k * LANES : (k + 1) * LANES]


def aisle_kernel(sizes, relayed, room_in, plen_in, got_a, got_b, jets, got_jets, places, room, plen, inflow):
    ca, cs, blocks, n_span, per_brick = sizes
    rows = blocks * cs
    even = lax.axis_index("aisle") % 2 == 0
    for k in range(5):
        for q, x, first, second in ((X_UP[k], 0, got_b, got_a), (X_DOWN[k], ca - 1, got_a, got_b)):
            cy = VELOCITIES[q][1]
            low, high = k * rows, (k + 1) * rows
            room[q, x] = crossed(jnp.where(even, first[low:high], second[low:high]), cy, cs)
            low = 5 * rows + k * cs
            value = jnp.where(even, first[low : low + cs], second[low : low + cs])
            at = x * cs
            if cy == 1:
                plen[q, at : at + 1] = value[0:1]
                plen[q, at + 1 : at + cs] = value[: cs - 1]
            elif cy == -1:
                plen[q, at + cs - 1 : at + cs] = value[cs - 1 : cs]
                plen[q, at : at + cs - 1] = value[1:cs]
            else:
                plen[q, at : at + cs] = value
    here = lax.axis_index("span")

    def put(sums):
        for k in range(5):
            inflow[k] = sums[k]

    def reader(source, b):
        return lambda s, k: source[b * CAP + s, :, k * LANES : (k + 1) * LANES]

    if relayed:
        put(jet_sums(lambda k: jnp.zeros((ca * cs, LANES), F32), places,
                     [(here, reader(jets, 0)), (here ^ 2, reader(got_jets, 0))]))
    else:
        inflow[...] = jnp.zeros_like(inflow)

        def add_brick(b, carry):
            put(jet_sums(lambda k: inflow[k], places, [(b, reader(got_jets, b))]))
            return carry

        lax.fori_loop(0, n_span, add_brick, 0)


def finish_kernel(sizes, relayed, room_in, plen_in, got_a, got_b, places, inflow, room, plen, room_out, plen_out, sems):
    ca, cs, blocks, n_span, per_brick = sizes
    rows = blocks * cs
    here = lax.axis_index("span")
    low = here % 2 == 0
    halo = 5 * (rows + cs)
    halo = halo + -halo % 8
    group = lax.broadcasted_iota(jnp.int32, (rows, LANES), 0) % cs
    def enter(got, up):
        planes, y = (Y_UP, 0) if up else (Y_DOWN, cs - 1)
        for k, q in enumerate(planes):
            came = got[k * rows : (k + 1) * rows]
            for x in range(ca):
                room[q, x] = jnp.where(group == y, turned_to(came, x, y), room[q, x])
                at = 5 * rows + k * ca + x
                plen[q, x * cs + y : x * cs + y + 1] = got[at : at + 1]

    @pl.when(low)
    def _():
        enter(got_a, False)

    @pl.when(jnp.logical_not(low))
    def _():
        enter(got_a, True)

    @pl.when(jnp.logical_and(low, here > 0))
    def _():
        enter(got_b, True)

    @pl.when(jnp.logical_and(jnp.logical_not(low), here < n_span - 1))
    def _():
        enter(got_b, False)

    plen_copy = pltpu.make_async_copy(plen, plen_out, sems.at[0])
    plen_copy.start()
    bricks = []
    if relayed:
        def reader(b):
            return lambda s, k: got_a[halo + (b * CAP + s) * 5 + k : halo + (b * CAP + s) * 5 + k + 1]

        bricks = [(here ^ 1, reader(0)), (here ^ 3, reader(1))]
    sums = jet_sums(lambda k: inflow[k], places, bricks)
    for k, q in enumerate(UPWARD):
        for x in range(ca):
            room[q, x, 0:cs] = room[q, x, 0:cs] + sums[k][x * cs : (x + 1) * cs]
    room_copy = pltpu.make_async_copy(room, room_out, sems.at[1])
    room_copy.start()
    plen_copy.wait()
    room_copy.wait()


def call(kernel, outs, in_specs, out_specs=None, scratch=(), aliases={}, flops=100_000, moved=1_000_000):
    return pl.pallas_call(
        kernel,
        out_shape=outs,
        in_specs=in_specs,
        out_specs=[VMEM] * len(outs) if out_specs is None else out_specs,
        scratch_shapes=list(scratch),
        input_output_aliases=aliases,
        cost_estimate=pl.CostEstimate(flops=flops, bytes_accessed=moved, transcendentals=0),
        compiler_params=pltpu.CompilerParams(vmem_limit_bytes=40 * 2**20),
    )


def swap_aisle(value, odd):
    count = lax.axis_size("aisle")
    pairs = [(i, (i ^ 1 if not odd else i + 1 if i % 2 else i - 1) % count) for i in range(count)]
    return lax.ppermute(value, "aisle", pairs)


def swap_span(value, odd):
    count = lax.axis_size("span")
    pairs = []
    for a in range(lax.axis_size("aisle")):
        for s in range(count):
            t = s ^ 1 if not odd else s + 1 if s % 2 else s - 1
            b, t = (a, t) if 0 <= t < count else (a ^ 1, s)
            pairs.append((a * count + s, b * count + t))
    return lax.ppermute(value, ("aisle", "span"), pairs)


def shards(room_pops, plenum_pops, tile_cell, tile_owner, tile_class):
    n_span = lax.axis_size("span")
    _, ca, cs, hr = room_pops.shape
    hp = plenum_pops.shape[3]
    blocks = hr // LANES
    rows = blocks * cs
    tiles = tile_cell.shape[0]
    sizes = (ca, cs, blocks, n_span, tiles // n_span)
    relayed = n_span == 4
    near = lambda shape: pltpu.VMEM(shape, F32)
    far = lambda value: pltpu.with_memory_space_constraint(value, pltpu.HBM)
    room_shape, plen_shape = (19, ca, rows, LANES), (19, ca * cs, LANES)
    halo = 5 * (rows + cs)
    halo = halo + -halo % 8
    room = far(room_pops.reshape(19, ca, cs, blocks, LANES).transpose(0, 1, 3, 2, 4).reshape(room_shape))
    plen = far(plenum_pops.reshape(plen_shape))
    tile_cell, tile_owner, tile_class = far(tile_cell), far(tile_owner.reshape(tiles)), far(tile_class)
    numbers = pltpu.SMEM((tiles,), jnp.int32)

    jets_shape = ((2 if relayed else n_span) * CAP, 1, 5 * hp)
    room_near, plen_post, *jets = call(
        functools.partial(plenum_kernel, sizes, relayed),
        [near(room_shape), near(plen_shape)] + [near(jets_shape)] * (2 if relayed else 1),
        [HBM] * 5,
        scratch=[pltpu.VMEM((ca * cs, 1, 5 * hp), F32), near((n_span * CAP, 1, 5 * hp)), near(plen_shape), numbers, numbers, numbers,
                 pltpu.SemaphoreType.DMA((5,))],
    )(room, plen, tile_cell, tile_owner, tile_class)
    if relayed:
        got_jets = lax.ppermute(jets[1], "span", [(i, i ^ 2) for i in range(4)])
    else:
        got_jets = lax.all_to_all(jets[0], "span", 0, 0, tiled=True)

    room_post, swap_a, swap_b = call(
        functools.partial(room_kernel, sizes),
        [near(room_shape), near((halo + 8, LANES)), near((halo, LANES))],
        [VMEM] * 2,
    )(room_near, plen_post)
    got_b = swap_aisle(swap_b, True)
    got_a = swap_aisle(swap_a, False)

    room_part, plen_part, span_up, span_down, places = call(
        functools.partial(local_kernel, sizes),
        [near(room_shape), near(plen_shape), near((halo, LANES)), near((halo, LANES)),
         near((n_span * CAP + 1, ca * cs, LANES))],
        [VMEM, VMEM, HBM, HBM],
        scratch=[numbers, numbers, pltpu.SemaphoreType.DMA((2,))],
        flops=10**9,
    )(room_post, plen_post, tile_cell, tile_owner)

    cross_shape = (halo + 2 * CAP * 5, LANES) if relayed else (halo, LANES)
    cross_a, cross_b = call(
        functools.partial(pack_kernel, sizes, relayed),
        [near(cross_shape), near((halo, LANES))],
        [VMEM] * (6 if relayed else 4),
    )(got_a, got_b, span_up, span_down, *((jets[0], got_jets) if relayed else ()))

    in_b = swap_span(cross_b, True)
    in_a = swap_span(cross_a, False)
    room_part, plen_part, inflow = call(
        functools.partial(aisle_kernel, sizes, relayed),
        [near(room_shape), near(plen_shape), near((5, ca * cs, LANES))],
        [VMEM] * 7,
        aliases={0: 0, 1: 1},
        flops=10**9,
    )(room_part, plen_part, got_a, got_b, jets[0], got_jets, places)

    _, _, room_next, plenum_next = call(
        functools.partial(finish_kernel, sizes, relayed),
        [near(room_shape), near(plen_shape), jax.ShapeDtypeStruct(room_shape, F32),
         jax.ShapeDtypeStruct(plen_shape, F32)],
        [VMEM] * 6,
        out_specs=[VMEM, VMEM, HBM, HBM],
        scratch=[pltpu.SemaphoreType.DMA((2,))],
        aliases={0: 0, 1: 1},
    )(room_part, plen_part, in_a, in_b, places, inflow)
    room_next = room_next.reshape(19, ca, blocks, cs, LANES).transpose(0, 1, 3, 2, 4).reshape(room_pops.shape)
    return room_next, plenum_next.reshape(plenum_pops.shape)


def solution(mesh):
    return jax.shard_map(
        shards,
        mesh=mesh,
        in_specs=(
            P(None, "aisle", "span", None),
            P(None, "aisle", "span", None),
            P("aisle"),
            P("aisle", None),
            P("aisle"),
        ),
        out_specs=(P(None, "aisle", "span", None), P(None, "aisle", "span", None)),
        check_vma=False,
    )
```

```python
import functools

import jax
import jax.numpy as jnp
from jax import lax
from jax.experimental import pallas as pl
from jax.experimental.pallas import tpu as pltpu
from jax.sharding import PartitionSpec as P

VELOCITIES = [
    (0, 0, 0),
    (1, 0, 0),
    (-1, 0, 0),
    (0, 1, 0),
    (0, -1, 0),
    (0, 0, 1),
    (0, 0, -1),
    (1, 1, 0),
    (-1, -1, 0),
    (1, -1, 0),
    (-1, 1, 0),
    (1, 0, 1),
    (-1, 0, -1),
    (1, 0, -1),
    (-1, 0, 1),
    (0, 1, 1),
    (0, -1, -1),
    (0, 1, -1),
    (0, -1, 1),
]
UPWARD = [5, 11, 14, 15, 18]
OMEGA = 1.25
CAP = 4
X_UP = [q for q in range(19) if VELOCITIES[q][0] == 1]
X_DOWN = [q for q in range(19) if VELOCITIES[q][0] == -1]
Y_UP = [q for q in range(19) if VELOCITIES[q][1] == 1]
Y_DOWN = [q for q in range(19) if VELOCITIES[q][1] == -1]
F32 = jnp.float32
LANES = 128
VMEM = pl.BlockSpec(memory_space=pltpu.VMEM)
HBM = pl.BlockSpec(memory_space=pltpu.HBM)


def collide(g):
    total = lambda i: g[i] + g[i + 1]
    apart = lambda i: g[i] - g[i + 1]
    dx, dy, dz = apart(1), apart(3), apart(5)
    d7, d9, d11, d13, d15, d17 = (apart(i) for i in (7, 9, 11, 13, 15, 17))
    edges = (total(7) + total(9)) + (total(11) + total(13)) + (total(15) + total(17))
    faces = total(1) + total(3) + total(5)
    rho = g[0] * (1.0 / 3.0) + faces * (1.0 / 18.0) + edges * (1.0 / 36.0)
    mx = dx * (1.0 / 18.0) + ((d7 + d9) + (d11 + d13)) * (1.0 / 36.0)
    my = dy * (1.0 / 18.0) + ((d7 - d9) + (d15 + d17)) * (1.0 / 36.0)
    mz = dz * (1.0 / 18.0) + ((d11 - d13) + (d15 - d17)) * (1.0 / 36.0)
    inv = 1.0 / rho
    base = OMEGA * rho - (1.5 * OMEGA) * inv * (mx * mx + my * my + mz * mz)
    square = (4.5 * OMEGA) * inv
    out = [None] * 19
    out[0] = base + (1.0 - OMEGA) * g[0]
    along = {1: mx, 3: my, 5: mz, 7: mx + my, 9: mx - my, 11: mx + mz, 13: mx - mz, 15: my + mz, 17: my - mz}
    for i, c in along.items():
        even = base + square * c * c
        odd = (3.0 * OMEGA) * c
        out[i] = (even + odd) + (1.0 - OMEGA) * g[i]
        out[i + 1] = (even - odd) + (1.0 - OMEGA) * g[i + 1]
    return out


def raised(value, cz, rows):
    if cz == 0:
        return value
    lane = lax.broadcasted_iota(jnp.int32, value.shape, 1)
    row = lax.broadcasted_iota(jnp.int32, value.shape, 0)
    total = value.shape[0]
    shift, edge = (1, 0) if cz == 1 else (LANES - 1, LANES - 1)
    turned = pltpu.roll(value, shift, 1)
    if rows == total:
        return jnp.where(lane == edge, value, turned)
    carried = pltpu.roll(turned, rows if cz == 1 else total - rows, 0)
    clamped = row < rows if cz == 1 else row >= total - rows
    return jnp.where(lane == edge, jnp.where(clamped, value, carried), turned)


def crossed(value, cy, cs):
    if cy == 0:
        return value
    row = lax.broadcasted_iota(jnp.int32, value.shape, 0) % cs
    turned = pltpu.roll(value, 1 if cy == 1 else value.shape[0] - 1, 0)
    return jnp.where(row == (0 if cy == 1 else cs - 1), value, turned)


def turned_to(value, source, dest):
    shift = (dest - source) % value.shape[0]
    return value if shift == 0 else pltpu.roll(value, shift, 0)


def repeat(count, body, start):
    if count > 8:
        return lax.fori_loop(0, count, body, start)
    for i in range(count):
        start = body(i, start)
    return start


def plenum_kernel(sizes, relayed, room_in, plen_in, cell_in, owner_in, class_in, room_near, plen_post, *rest):
    ca, cs, blocks, n_span, per_brick = sizes
    jets = rest[:-7]
    columns, dealt, plen_buf, cells, owners, classes, sems = rest[-7:]
    copies = [pltpu.make_async_copy(src, dst, sems.at[i]) for i, (src, dst) in enumerate(
        ((plen_in, plen_buf), (cell_in, cells), (owner_in, owners), (class_in, classes), (room_in, room_near)))]
    for copy in copies:
        copy.start()
    dealt[...] = jnp.zeros_like(dealt)
    copies[0].wait()
    for r in range(0, ca * cs, 8):
        post = collide([plen_buf[q, r : r + 8] for q in range(19)])
        for q in range(19):
            plen_post[q, r : r + 8] = post[q]
        for k, q in enumerate(UPWARD):
            for y in range(8):
                columns[r + y, :, k * LANES : (k + 1) * LANES] = post[q][y : y + 1]
    for copy in copies[1:4]:
        copy.wait()
    here = lax.axis_index("span")
    first = here * per_brick

    def send_jet(i, carry):
        t = first + i
        owner = owners[t]
        share = 0.15 * (classes[t].astype(F32) + 1.0)
        same = lambda j, n: n + (owners[first + j] == owner).astype(jnp.int32)
        slot = repeat(i, same, 0) if relayed else lax.fori_loop(0, i, same, 0)
        to = (owner ^ here if relayed else owner) * CAP + slot
        dealt[to] = share * columns[cells[t]]
        return carry

    if relayed:
        for i in range(per_brick):
            send_jet(i, 0)
    else:
        lax.fori_loop(0, per_brick, send_jet, 0)
    for part, jet in enumerate(jets):
        many = jet.shape[0]
        jet[...] = dealt[part * many : (part + 1) * many]
    copies[4].wait()


def room_kernel(sizes, room_near, plen_post, room_post, swap_a, swap_b):
    ca, cs, blocks, n_span, per_brick = sizes
    rows = blocks * cs

    def plane(x, carry):
        for r in range(0, rows, 8):
            post = collide([room_near[q, x, r : r + 8] for q in range(19)])
            for q in range(19):
                room_post[q, x, r : r + 8] = post[q]
        return carry

    lax.fori_loop(0, ca, plane, 0)
    even = lax.axis_index("aisle") % 2 == 0
    for k in range(5):
        up, down = X_UP[k], X_DOWN[k]
        rising = raised(room_post[up, ca - 1], VELOCITIES[up][2], cs)
        falling = raised(room_post[down, 0], VELOCITIES[down][2], cs)
        swap_a[k * rows : (k + 1) * rows] = jnp.where(even, rising, falling)
        swap_b[k * rows : (k + 1) * rows] = jnp.where(even, falling, rising)
        rising = raised(plen_post[up, (ca - 1) * cs : ca * cs], VELOCITIES[up][2], cs)
        falling = raised(plen_post[down, 0:cs], VELOCITIES[down][2], cs)
        low = 5 * rows + k * cs
        swap_a[low : low + cs] = jnp.where(even, rising, falling)
        swap_b[low : low + cs] = jnp.where(even, falling, rising)


def jet_sums(start, places, bricks):
    sums = [start(k) for k in range(5)]
    for b, jet in bricks:
        for s in range(CAP):
            marks = places[b * CAP + s]
            sums = [total + marks * jet(s, k) for k, total in enumerate(sums)]
    return sums


def local_kernel(sizes, room_post, plen_post, cell_in, owner_in, room_part, plen_part, span_up, span_down, places,
                 cells, owners, sems):
    ca, cs, blocks, n_span, per_brick = sizes
    rows = blocks * cs
    copies = [pltpu.make_async_copy(src, dst, sems.at[i]) for i, (src, dst) in enumerate(
        ((cell_in, cells), (owner_in, owners)))]
    for copy in copies:
        copy.start()
    group = lax.broadcasted_iota(jnp.int32, (rows, LANES), 0) % cs
    for q in range(19):
        cx, cy, cz = VELOCITIES[q]
        edge = cs - 1 if cy == 1 else 0
        span, planes = (span_up, Y_UP) if cy == 1 else (span_down, Y_DOWN)
        packed = None
        for x in range(ca):
            if not 0 <= x - cx < ca:
                continue
            value = raised(room_post[q, x - cx], cz, cs)
            room_part[q, x] = crossed(value, cy, cs)
            if cy:
                ready = turned_to(value, edge, x)
                packed = ready if packed is None else jnp.where(group == x, ready, packed)
        value = raised(plen_post[q], cz, ca * cs)
        if cx == 1:
            value = pltpu.roll(value, cs, 0)
        elif cx == -1:
            value = pltpu.roll(value, ca * cs - cs, 0)
        plen_part[q] = crossed(value, cy, cs)
        if cy:
            k = planes.index(q)
            span[k * rows : (k + 1) * rows] = packed
            for x in range(ca):
                to = 5 * rows + k * ca + x
                span[to : to + 1] = value[x * cs + edge : x * cs + edge + 1]
    places[0 : n_span * CAP] = jnp.zeros((n_span * CAP, ca * cs, LANES), F32)
    here = lax.axis_index("span")
    row = lax.broadcasted_iota(jnp.int32, (ca * cs, LANES), 0)
    for copy in copies:
        copy.wait()

    def brick(b, carry):
        def place(i, slot):
            t = b * per_brick + i
            mine = owners[t] == here
            places[jnp.where(mine, b * CAP + slot, n_span * CAP)] = (row == cells[t]).astype(F32)
            return slot + mine.astype(jnp.int32)

        repeat(per_brick, place, 0)
        return carry

    repeat(n_span, brick, 0)


def pack_kernel(sizes, relayed, got_a, got_b, span_up, span_down, *rest):
    ca, cs, blocks, n_span, per_brick = sizes
    rows = blocks * cs
    if relayed:
        jets, got_jets, cross_a, cross_b = rest
    else:
        cross_a, cross_b = rest
    even = lax.axis_index("aisle") % 2 == 0
    low = lax.axis_index("span") % 2 == 0
    halo = span_up.shape[0]
    group = lax.broadcasted_iota(jnp.int32, (rows, LANES), 0) % cs

    def corner(q, low, high):
        if VELOCITIES[q][0] == 1:
            k = X_UP.index(q)
            return jnp.where(even, got_b[low(k) : high(k)], got_a[low(k) : high(k)])
        k = X_DOWN.index(q)
        return jnp.where(even, got_a[low(k) : high(k)], got_b[low(k) : high(k)])

    for k in range(5):
        sides = []
        for span, planes, edge in ((span_up, Y_UP, cs - 1), (span_down, Y_DOWN, 0)):
            q = planes[k]
            value = span[k * rows : (k + 1) * rows]
            if VELOCITIES[q][0]:
                x = 0 if VELOCITIES[q][0] == 1 else ca - 1
                came = corner(q, lambda k: k * rows, lambda k: (k + 1) * rows)
                value = jnp.where(group == x, turned_to(came, edge, x), value)
            sides.append(value)
        cross_a[k * rows : (k + 1) * rows] = jnp.where(low, sides[0], sides[1])
        cross_b[k * rows : (k + 1) * rows] = jnp.where(low, sides[1], sides[0])
    for r in range(5 * rows, halo, 8):
        rising, falling = span_up[r : r + 8], span_down[r : r + 8]
        cross_a[r : r + 8] = jnp.where(low, rising, falling)
        cross_b[r : r + 8] = jnp.where(low, falling, rising)
    for planes, edge in ((Y_UP, cs - 1), (Y_DOWN, 0)):
        for k, q in enumerate(planes):
            if VELOCITIES[q][0]:
                x = 0 if VELOCITIES[q][0] == 1 else ca - 1
                at = lambda k: 5 * rows + k * cs + edge
                came = corner(q, at, lambda k: at(k) + 1)
                to = 5 * rows + k * ca + x

                @pl.when(low == (planes is Y_UP))
                def _():
                    cross_a[to : to + 1] = came

                @pl.when(low != (planes is Y_UP))
                def _():
                    cross_b[to : to + 1] = came

    if relayed:
        for b, source in enumerate((jets, got_jets)):
            for s in range(CAP):
                for k in range(5):
                    to = halo + (b * CAP + s) * 5 + k
                    cross_a[to : to + 1] = source[CAP + s, :, k * LANES : (k + 1) * LANES]


def aisle_kernel(sizes, relayed, room_in, plen_in, got_a, got_b, jets, got_jets, places, room, plen, inflow):
    ca, cs, blocks, n_span, per_brick = sizes
    rows = blocks * cs
    even = lax.axis_index("aisle") % 2 == 0
    for k in range(5):
        for q, x, first, second in ((X_UP[k], 0, got_b, got_a), (X_DOWN[k], ca - 1, got_a, got_b)):
            cy = VELOCITIES[q][1]
            low, high = k * rows, (k + 1) * rows
            room[q, x] = crossed(jnp.where(even, first[low:high], second[low:high]), cy, cs)
            low = 5 * rows + k * cs
            value = jnp.where(even, first[low : low + cs], second[low : low + cs])
            at = x * cs
            if cy == 1:
                plen[q, at : at + 1] = value[0:1]
                plen[q, at + 1 : at + cs] = value[: cs - 1]
            elif cy == -1:
                plen[q, at + cs - 1 : at + cs] = value[cs - 1 : cs]
                plen[q, at : at + cs - 1] = value[1:cs]
            else:
                plen[q, at : at + cs] = value
    here = lax.axis_index("span")

    def put(sums):
        for k in range(5):
            inflow[k] = sums[k]

    def reader(source, b):
        return lambda s, k: source[b * CAP + s, :, k * LANES : (k + 1) * LANES]

    if relayed:
        put(jet_sums(lambda k: jnp.zeros((ca * cs, LANES), F32), places,
                     [(here, reader(jets, 0)), (here ^ 2, reader(got_jets, 0))]))
    else:
        inflow[...] = jnp.zeros_like(inflow)

        def add_brick(b, carry):
            put(jet_sums(lambda k: inflow[k], places, [(b, reader(got_jets, b))]))
            return carry

        lax.fori_loop(0, n_span, add_brick, 0)


def finish_kernel(sizes, relayed, room_in, plen_in, got_a, got_b, places, inflow, room, plen, room_out, plen_out, sems):
    ca, cs, blocks, n_span, per_brick = sizes
    rows = blocks * cs
    here = lax.axis_index("span")
    low = here % 2 == 0
    halo = 5 * (rows + cs)
    halo = halo + -halo % 8
    group = lax.broadcasted_iota(jnp.int32, (rows, LANES), 0) % cs
    def enter(got, up):
        planes, y = (Y_UP, 0) if up else (Y_DOWN, cs - 1)
        for k, q in enumerate(planes):
            came = got[k * rows : (k + 1) * rows]
            for x in range(ca):
                room[q, x] = jnp.where(group == y, turned_to(came, x, y), room[q, x])
                at = 5 * rows + k * ca + x
                plen[q, x * cs + y : x * cs + y + 1] = got[at : at + 1]

    @pl.when(low)
    def _():
        enter(got_a, False)

    @pl.when(jnp.logical_not(low))
    def _():
        enter(got_a, True)

    @pl.when(jnp.logical_and(low, here > 0))
    def _():
        enter(got_b, True)

    @pl.when(jnp.logical_and(jnp.logical_not(low), here < n_span - 1))
    def _():
        enter(got_b, False)

    plen_copy = pltpu.make_async_copy(plen, plen_out, sems.at[0])
    plen_copy.start()
    bricks = []
    if relayed:
        def reader(b):
            return lambda s, k: got_a[halo + (b * CAP + s) * 5 + k : halo + (b * CAP + s) * 5 + k + 1]

        bricks = [(here ^ 1, reader(0)), (here ^ 3, reader(1))]
    sums = jet_sums(lambda k: inflow[k], places, bricks)
    for k, q in enumerate(UPWARD):
        for x in range(ca):
            room[q, x, 0:cs] = room[q, x, 0:cs] + sums[k][x * cs : (x + 1) * cs]
    room_copy = pltpu.make_async_copy(room, room_out, sems.at[1])
    room_copy.start()
    plen_copy.wait()
    room_copy.wait()


def call(kernel, outs, in_specs, out_specs=None, scratch=(), aliases={}, flops=100_000, moved=1_000_000):
    return pl.pallas_call(
        kernel,
        out_shape=outs,
        in_specs=in_specs,
        out_specs=[VMEM] * len(outs) if out_specs is None else out_specs,
        scratch_shapes=list(scratch),
        input_output_aliases=aliases,
        cost_estimate=pl.CostEstimate(flops=flops, bytes_accessed=moved, transcendentals=0),
        compiler_params=pltpu.CompilerParams(vmem_limit_bytes=40 * 2**20),
    )


def swap_aisle(value, odd):
    count = lax.axis_size("aisle")
    pairs = [(i, (i ^ 1 if not odd else i + 1 if i % 2 else i - 1) % count) for i in range(count)]
    return lax.ppermute(value, "aisle", pairs)


def swap_span(value, odd):
    count = lax.axis_size("span")
    pairs = []
    for a in range(lax.axis_size("aisle")):
        for s in range(count):
            t = s ^ 1 if not odd else s + 1 if s % 2 else s - 1
            b, t = (a, t) if 0 <= t < count else (a ^ 1, s)
            pairs.append((a * count + s, b * count + t))
    return lax.ppermute(value, ("aisle", "span"), pairs)


def shards(room_pops, plenum_pops, tile_cell, tile_owner, tile_class):
    n_span = lax.axis_size("span")
    _, ca, cs, hr = room_pops.shape
    hp = plenum_pops.shape[3]
    blocks = hr // LANES
    rows = blocks * cs
    tiles = tile_cell.shape[0]
    sizes = (ca, cs, blocks, n_span, tiles // n_span)
    relayed = n_span == 4
    near = lambda shape: pltpu.VMEM(shape, F32)
    far = lambda value: pltpu.with_memory_space_constraint(value, pltpu.HBM)
    room_shape, plen_shape = (19, ca, rows, LANES), (19, ca * cs, LANES)
    halo = 5 * (rows + cs)
    halo = halo + -halo % 8
    room = far(room_pops.reshape(19, ca, cs, blocks, LANES).transpose(0, 1, 3, 2, 4).reshape(room_shape))
    plen = far(plenum_pops.reshape(plen_shape))
    tile_cell, tile_owner, tile_class = far(tile_cell), far(tile_owner.reshape(tiles)), far(tile_class)
    numbers = pltpu.SMEM((tiles,), jnp.int32)

    jets_shape = ((2 if relayed else n_span) * CAP, 1, 5 * hp)
    room_near, plen_post, *jets = call(
        functools.partial(plenum_kernel, sizes, relayed),
        [near(room_shape), near(plen_shape)] + [near(jets_shape)] * (2 if relayed else 1),
        [HBM] * 5,
        scratch=[pltpu.VMEM((ca * cs, 1, 5 * hp), F32), near((n_span * CAP, 1, 5 * hp)), near(plen_shape), numbers, numbers, numbers,
                 pltpu.SemaphoreType.DMA((5,))],
    )(room, plen, tile_cell, tile_owner, tile_class)
    if relayed:
        got_jets = lax.ppermute(jets[1], "span", [(i, i ^ 2) for i in range(4)])
    else:
        got_jets = lax.all_to_all(jets[0], "span", 0, 0, tiled=True)

    room_post, swap_a, swap_b = call(
        functools.partial(room_kernel, sizes),
        [near(room_shape), near((halo + 8, LANES)), near((halo, LANES))],
        [VMEM] * 2,
    )(room_near, plen_post)
    got_b = swap_aisle(swap_b, True)
    got_a = swap_aisle(swap_a, False)

    room_part, plen_part, span_up, span_down, places = call(
        functools.partial(local_kernel, sizes),
        [near(room_shape), near(plen_shape), near((halo, LANES)), near((halo, LANES)),
         near((n_span * CAP + 1, ca * cs, LANES))],
        [VMEM, VMEM, HBM, HBM],
        scratch=[numbers, numbers, pltpu.SemaphoreType.DMA((2,))],
        flops=10**9,
    )(room_post, plen_post, tile_cell, tile_owner)

    cross_shape = (halo + 2 * CAP * 5, LANES) if relayed else (halo, LANES)
    cross_a, cross_b = call(
        functools.partial(pack_kernel, sizes, relayed),
        [near(cross_shape), near((halo, LANES))],
        [VMEM] * (6 if relayed else 4),
    )(got_a, got_b, span_up, span_down, *((jets[0], got_jets) if relayed else ()))

    in_b = swap_span(cross_b, True)
    in_a = swap_span(cross_a, False)
    room_part, plen_part, inflow = call(
        functools.partial(aisle_kernel, sizes, relayed),
        [near(room_shape), near(plen_shape), near((5, ca * cs, LANES))],
        [VMEM] * 7,
        aliases={0: 0, 1: 1},
    )(room_part, plen_part, got_a, got_b, jets[0], got_jets, places)

    _, _, room_next, plenum_next = call(
        functools.partial(finish_kernel, sizes, relayed),
        [near(room_shape), near(plen_shape), jax.ShapeDtypeStruct(room_shape, F32),
         jax.ShapeDtypeStruct(plen_shape, F32)],
        [VMEM] * 6,
        out_specs=[VMEM, VMEM, HBM, HBM],
        scratch=[pltpu.SemaphoreType.DMA((2,))],
        aliases={0: 0, 1: 1},
    )(room_part, plen_part, in_a, in_b, places, inflow)
    room_next = room_next.reshape(19, ca, blocks, cs, LANES).transpose(0, 1, 3, 2, 4).reshape(room_pops.shape)
    return room_next, plenum_next.reshape(plenum_pops.shape)


def solution(mesh):
    return jax.shard_map(
        shards,
        mesh=mesh,
        in_specs=(
            P(None, "aisle", "span", None),
            P(None, "aisle", "span", None),
            P("aisle"),
            P("aisle", None),
            P("aisle"),
        ),
        out_specs=(P(None, "aisle", "span", None), P(None, "aisle", "span", None)),
        check_vma=False,
    )
```

```python
import functools

import jax
import jax.numpy as jnp
from jax import lax
from jax.experimental import pallas as pl
from jax.experimental.pallas import tpu as pltpu
from jax.sharding import PartitionSpec as P

VELOCITIES = [
    (0, 0, 0),
    (1, 0, 0),
    (-1, 0, 0),
    (0, 1, 0),
    (0, -1, 0),
    (0, 0, 1),
    (0, 0, -1),
    (1, 1, 0),
    (-1, -1, 0),
    (1, -1, 0),
    (-1, 1, 0),
    (1, 0, 1),
    (-1, 0, -1),
    (1, 0, -1),
    (-1, 0, 1),
    (0, 1, 1),
    (0, -1, -1),
    (0, 1, -1),
    (0, -1, 1),
]
UPWARD = [5, 11, 14, 15, 18]
OMEGA = 1.25
CAP = 4
X_UP = [q for q in range(19) if VELOCITIES[q][0] == 1]
X_DOWN = [q for q in range(19) if VELOCITIES[q][0] == -1]
Y_UP = [q for q in range(19) if VELOCITIES[q][1] == 1]
Y_DOWN = [q for q in range(19) if VELOCITIES[q][1] == -1]
F32 = jnp.float32
LANES = 128
VMEM = pl.BlockSpec(memory_space=pltpu.VMEM)
HBM = pl.BlockSpec(memory_space=pltpu.HBM)


def collide(g):
    total = lambda i: g[i] + g[i + 1]
    apart = lambda i: g[i] - g[i + 1]
    dx, dy, dz = apart(1), apart(3), apart(5)
    d7, d9, d11, d13, d15, d17 = (apart(i) for i in (7, 9, 11, 13, 15, 17))
    edges = (total(7) + total(9)) + (total(11) + total(13)) + (total(15) + total(17))
    faces = total(1) + total(3) + total(5)
    rho = g[0] * (1.0 / 3.0) + faces * (1.0 / 18.0) + edges * (1.0 / 36.0)
    mx = dx * (1.0 / 18.0) + ((d7 + d9) + (d11 + d13)) * (1.0 / 36.0)
    my = dy * (1.0 / 18.0) + ((d7 - d9) + (d15 + d17)) * (1.0 / 36.0)
    mz = dz * (1.0 / 18.0) + ((d11 - d13) + (d15 - d17)) * (1.0 / 36.0)
    inv = 1.0 / rho
    base = OMEGA * rho - (1.5 * OMEGA) * inv * (mx * mx + my * my + mz * mz)
    square = (4.5 * OMEGA) * inv
    out = [None] * 19
    out[0] = base + (1.0 - OMEGA) * g[0]
    along = {1: mx, 3: my, 5: mz, 7: mx + my, 9: mx - my, 11: mx + mz, 13: mx - mz, 15: my + mz, 17: my - mz}
    for i, c in along.items():
        even = base + square * c * c
        odd = (3.0 * OMEGA) * c
        out[i] = (even + odd) + (1.0 - OMEGA) * g[i]
        out[i + 1] = (even - odd) + (1.0 - OMEGA) * g[i + 1]
    return out


def raised(value, cz, rows):
    if cz == 0:
        return value
    lane = lax.broadcasted_iota(jnp.int32, value.shape, 1)
    row = lax.broadcasted_iota(jnp.int32, value.shape, 0)
    total = value.shape[0]
    shift, edge = (1, 0) if cz == 1 else (LANES - 1, LANES - 1)
    turned = pltpu.roll(value, shift, 1)
    if rows == total:
        return jnp.where(lane == edge, value, turned)
    carried = pltpu.roll(turned, rows if cz == 1 else total - rows, 0)
    clamped = row < rows if cz == 1 else row >= total - rows
    return jnp.where(lane == edge, jnp.where(clamped, value, carried), turned)


def crossed(value, cy, cs):
    if cy == 0:
        return value
    row = lax.broadcasted_iota(jnp.int32, value.shape, 0) % cs
    turned = pltpu.roll(value, 1 if cy == 1 else value.shape[0] - 1, 0)
    return jnp.where(row == (0 if cy == 1 else cs - 1), value, turned)


def shifted(value, by):
    return pltpu.roll(value, by % value.shape[0], 0) if by else value


def turned_to(value, source, dest):
    return shifted(value, dest - source)


def repeat(count, body, start):
    if count > 8:
        return lax.fori_loop(0, count, body, start)
    for i in range(count):
        start = body(i, start)
    return start


def plenum_kernel(sizes, relayed, room_in, plen_in, cell_in, owner_in, class_in, room_near, plen_post, *rest):
    ca, cs, blocks, n_span, per_brick = sizes
    jets = rest[:-7]
    columns, dealt, plen_buf, cells, owners, classes, sems = rest[-7:]
    copies = [pltpu.make_async_copy(src, dst, sems.at[i]) for i, (src, dst) in enumerate(
        ((plen_in, plen_buf), (cell_in, cells), (owner_in, owners), (class_in, classes), (room_in, room_near)))]
    for copy in copies:
        copy.start()
    dealt[...] = jnp.zeros_like(dealt)
    copies[0].wait()
    for r in range(0, ca * cs, 8):
        post = collide([plen_buf[q, r : r + 8] for q in range(19)])
        for q in range(19):
            plen_post[q, r : r + 8] = post[q]
        for k, q in enumerate(UPWARD):
            for y in range(8):
                columns[r + y, :, k * LANES : (k + 1) * LANES] = post[q][y : y + 1]
    for copy in copies[1:4]:
        copy.wait()
    here = lax.axis_index("span")
    first = here * per_brick

    def send_jet(i, carry):
        t = first + i
        owner = owners[t]
        share = 0.15 * (classes[t].astype(F32) + 1.0)
        same = lambda j, n: n + (owners[first + j] == owner).astype(jnp.int32)
        slot = repeat(i, same, 0) if relayed else lax.fori_loop(0, i, same, 0)
        to = (owner ^ here if relayed else owner) * CAP + slot
        dealt[to] = share * columns[cells[t]]
        return carry

    if relayed:
        for i in range(per_brick):
            send_jet(i, 0)
    else:
        lax.fori_loop(0, per_brick, send_jet, 0)
    for part, jet in enumerate(jets):
        many = jet.shape[0]
        jet[...] = dealt[part * many : (part + 1) * many]
    copies[4].wait()


def room_kernel(sizes, room_near, plen_post, room_post, swap_a, swap_b):
    ca, cs, blocks, n_span, per_brick = sizes
    rows = blocks * cs

    def plane(x, carry):
        for r in range(0, rows, 8):
            post = collide([room_near[q, x, r : r + 8] for q in range(19)])
            for q in range(19):
                room_post[q, x, r : r + 8] = post[q]
        return carry

    lax.fori_loop(0, ca, plane, 0)
    even = lax.axis_index("aisle") % 2 == 0
    for k in range(5):
        up, down = X_UP[k], X_DOWN[k]
        rising = raised(room_post[up, ca - 1], VELOCITIES[up][2], cs)
        falling = raised(room_post[down, 0], VELOCITIES[down][2], cs)
        swap_a[k * rows : (k + 1) * rows] = jnp.where(even, rising, falling)
        swap_b[k * rows : (k + 1) * rows] = jnp.where(even, falling, rising)
        rising = raised(plen_post[up, (ca - 1) * cs : ca * cs], VELOCITIES[up][2], cs)
        falling = raised(plen_post[down, 0:cs], VELOCITIES[down][2], cs)
        low = 5 * rows + k * cs
        swap_a[low : low + cs] = jnp.where(even, rising, falling)
        swap_b[low : low + cs] = jnp.where(even, falling, rising)


def jet_sums(start, places, bricks):
    sums = [start(k) for k in range(5)]
    for b, jet in bricks:
        for s in range(CAP):
            marks = places[b * CAP + s]
            sums = [total + marks * jet(s, k) for k, total in enumerate(sums)]
    return sums


def local_kernel(sizes, room_post, plen_post, cell_in, owner_in, room_part, plen_part, places, cells, owners, sems):
    ca, cs, blocks, n_span, per_brick = sizes
    rows = blocks * cs
    copies = [pltpu.make_async_copy(src, dst, sems.at[i]) for i, (src, dst) in enumerate(
        ((cell_in, cells), (owner_in, owners)))]
    for copy in copies:
        copy.start()
    for q in range(19):
        cx, cy, cz = VELOCITIES[q]
        for x in range(ca):
            if 0 <= x - cx < ca:
                room_part[q, x] = crossed(raised(room_post[q, x - cx], cz, cs), cy, cs)
        plen_part[q] = crossed(shifted(raised(plen_post[q], cz, ca * cs), cx * cs), cy, cs)
    places[0 : n_span * CAP] = jnp.zeros((n_span * CAP, ca * cs, LANES), F32)
    here = lax.axis_index("span")
    row = lax.broadcasted_iota(jnp.int32, (ca * cs, LANES), 0)
    for copy in copies:
        copy.wait()

    def brick(b, carry):
        def place(i, slot):
            t = b * per_brick + i
            mine = owners[t] == here
            places[jnp.where(mine, b * CAP + slot, n_span * CAP)] = (row == cells[t]).astype(F32)
            return slot + mine.astype(jnp.int32)

        repeat(per_brick, place, 0)
        return carry

    repeat(n_span, brick, 0)


def cross_kernel(sizes, relayed, room_post, plen_post, jets, cross_a, cross_b):
    ca, cs, blocks, n_span, per_brick = sizes
    rows = blocks * cs
    low = lax.axis_index("span") % 2 == 0
    group = lax.broadcasted_iota(jnp.int32, (rows, LANES), 0) % cs
    for k in range(5):
        sides, near = [], []
        for q, edge in ((Y_UP[k], cs - 1), (Y_DOWN[k], 0)):
            cx, cy, cz = VELOCITIES[q]
            packed = None
            for x in range(max(cx, 0), ca + min(cx, 0)):
                ready = turned_to(raised(room_post[q, x - cx], cz, cs), edge, x)
                packed = ready if packed is None else jnp.where(group == x, ready, packed)
            sides.append(packed)
            near.append(shifted(raised(plen_post[q], cz, ca * cs), cx * cs - edge))
        cross_a[k * rows : (k + 1) * rows] = jnp.where(low, sides[0], sides[1])
        cross_b[k * rows : (k + 1) * rows] = jnp.where(low, sides[1], sides[0])
        first, second = jnp.where(low, near[0], near[1]), jnp.where(low, near[1], near[0])
        for x in range(ca):
            to = 5 * rows + k * ca + x
            cross_a[to : to + 1] = first[x * cs : x * cs + 1]
            cross_b[to : to + 1] = second[x * cs : x * cs + 1]
    if relayed:
        for s in range(CAP):
            for k in range(5):
                to = 5 * (rows + ca) + s * 5 + k
                cross_a[to : to + 1] = jets[CAP + s, :, k * LANES : (k + 1) * LANES]


def corners(cs, up):
    return [q for q in (Y_UP if up else Y_DOWN) if VELOCITIES[q][0]], cs - 1 if up else 0


def corner_kernel(sizes, relayed, got_a, got_b, got_jets, places, cross_a, cross_b):
    del places
    ca, cs, blocks, n_span, per_brick = sizes
    rows = blocks * cs
    even = lax.axis_index("aisle") % 2 == 0
    low = lax.axis_index("span") % 2 == 0
    group = lax.broadcasted_iota(jnp.int32, (rows, LANES), 0) % cs

    def came(q, low, high):
        if VELOCITIES[q][0] == 1:
            k = X_UP.index(q)
            return jnp.where(even, got_b[low(k) : high(k)], got_a[low(k) : high(k)])
        k = X_DOWN.index(q)
        return jnp.where(even, got_a[low(k) : high(k)], got_b[low(k) : high(k)])

    sides, near = [], []
    for up in (True, False):
        two, edge = corners(cs, up)
        parts = [turned_to(came(q, lambda k: k * rows, lambda k: (k + 1) * rows), edge, c) for c, q in enumerate(two)]
        sides.append(jnp.where(group == 0, parts[0], parts[1]))
        at = lambda k: 5 * rows + k * cs + edge
        near.append([came(q, at, lambda k: at(k) + 1) for q in two])
    cross_a[0:rows] = jnp.where(low, sides[0], sides[1])
    cross_b[0:rows] = jnp.where(low, sides[1], sides[0])
    for c in range(2):
        cross_a[rows + c : rows + c + 1] = jnp.where(low, near[0][c], near[1][c])
        cross_b[rows + c : rows + c + 1] = jnp.where(low, near[1][c], near[0][c])
    if relayed:
        for s in range(CAP):
            for k in range(5):
                to = rows + 2 + s * 5 + k
                cross_a[to : to + 1] = got_jets[CAP + s, :, k * LANES : (k + 1) * LANES]


def aisle_kernel(sizes, relayed, room_in, plen_in, got_a, got_b, jets, got_jets, places, room, plen, inflow):
    ca, cs, blocks, n_span, per_brick = sizes
    rows = blocks * cs
    even = lax.axis_index("aisle") % 2 == 0
    for k in range(5):
        for q, x, first, second in ((X_UP[k], 0, got_b, got_a), (X_DOWN[k], ca - 1, got_a, got_b)):
            cy = VELOCITIES[q][1]
            low, high = k * rows, (k + 1) * rows
            room[q, x] = crossed(jnp.where(even, first[low:high], second[low:high]), cy, cs)
            low = 5 * rows + k * cs
            value = jnp.where(even, first[low : low + cs], second[low : low + cs])
            at = x * cs
            if cy == 1:
                plen[q, at : at + 1] = value[0:1]
                plen[q, at + 1 : at + cs] = value[: cs - 1]
            elif cy == -1:
                plen[q, at + cs - 1 : at + cs] = value[cs - 1 : cs]
                plen[q, at : at + cs - 1] = value[1:cs]
            else:
                plen[q, at : at + cs] = value
    here = lax.axis_index("span")

    def put(sums):
        for k in range(5):
            inflow[k] = sums[k]

    def reader(source, b):
        return lambda s, k: source[b * CAP + s, :, k * LANES : (k + 1) * LANES]

    if relayed:
        put(jet_sums(lambda k: jnp.zeros((ca * cs, LANES), F32), places,
                     [(here, reader(jets, 0)), (here ^ 2, reader(got_jets, 0))]))
    else:
        inflow[...] = jnp.zeros_like(inflow)

        def add_brick(b, carry):
            put(jet_sums(lambda k: inflow[k], places, [(b, reader(got_jets, b))]))
            return carry

        lax.fori_loop(0, n_span, add_brick, 0)


def entering(n_span, got_a, got_b, enter):
    here = lax.axis_index("span")
    low = here % 2 == 0

    @pl.when(low)
    def _():
        enter(got_a, False)

    @pl.when(jnp.logical_not(low))
    def _():
        enter(got_a, True)

    @pl.when(jnp.logical_and(low, here > 0))
    def _():
        enter(got_b, True)

    @pl.when(jnp.logical_and(jnp.logical_not(low), here < n_span - 1))
    def _():
        enter(got_b, False)


def enter_kernel(sizes, relayed, room_in, plen_in, got_a, got_b, places, inflow_in, room, plen, inflow):
    ca, cs, blocks, n_span, per_brick = sizes
    rows = blocks * cs
    here = lax.axis_index("span")
    group = lax.broadcasted_iota(jnp.int32, (rows, LANES), 0) % cs

    def enter(got, up):
        planes, y = (Y_UP, 0) if up else (Y_DOWN, cs - 1)
        for k, q in enumerate(planes):
            came = got[k * rows : (k + 1) * rows]
            for x in range(ca):
                room[q, x] = jnp.where(group == y, turned_to(came, x, y), room[q, x])
                at = 5 * rows + k * ca + x
                plen[q, x * cs + y : x * cs + y + 1] = got[at : at + 1]

    entering(n_span, got_a, got_b, enter)
    if relayed:
        start = 5 * (rows + ca)
        jet = lambda s, k: got_a[start + s * 5 + k : start + s * 5 + k + 1]
        sums = jet_sums(lambda k: inflow_in[k], places, [(here ^ 1, jet)])
        for k in range(5):
            inflow[k] = sums[k]
    else:
        inflow[...] = inflow_in[...]


def finish_kernel(sizes, relayed, room_in, plen_in, got_a, got_b, places, inflow, room, plen, room_out, plen_out, sems):
    ca, cs, blocks, n_span, per_brick = sizes
    rows = blocks * cs
    here = lax.axis_index("span")
    group = lax.broadcasted_iota(jnp.int32, (rows, LANES), 0) % cs

    def enter(got, up):
        two, _ = corners(cs, up)
        y = 0 if up else cs - 1
        came = got[0:rows]
        for c, q in enumerate(two):
            x = 0 if VELOCITIES[q][0] == 1 else ca - 1
            room[q, x] = jnp.where(group == y, turned_to(came, c, y), room[q, x])
            plen[q, x * cs + y : x * cs + y + 1] = got[rows + c : rows + c + 1]

    entering(n_span, got_a, got_b, enter)
    plen_copy = pltpu.make_async_copy(plen, plen_out, sems.at[0])
    plen_copy.start()
    bricks = []
    if relayed:
        bricks = [(here ^ 3, lambda s, k: got_a[rows + 2 + s * 5 + k : rows + 2 + s * 5 + k + 1])]
    sums = jet_sums(lambda k: inflow[k], places, bricks)
    for k, q in enumerate(UPWARD):
        for x in range(ca):
            room[q, x, 0:cs] = room[q, x, 0:cs] + sums[k][x * cs : (x + 1) * cs]
    room_copy = pltpu.make_async_copy(room, room_out, sems.at[1])
    room_copy.start()
    plen_copy.wait()
    room_copy.wait()


def call(kernel, outs, in_specs, out_specs=None, scratch=(), aliases={}, flops=100_000, moved=1_000_000):
    return pl.pallas_call(
        kernel,
        name=kernel.func.__name__,
        out_shape=outs,
        in_specs=in_specs,
        out_specs=[VMEM] * len(outs) if out_specs is None else out_specs,
        scratch_shapes=list(scratch),
        input_output_aliases=aliases,
        cost_estimate=pl.CostEstimate(flops=flops, bytes_accessed=moved, transcendentals=0),
        compiler_params=pltpu.CompilerParams(vmem_limit_bytes=40 * 2**20),
    )


def swap_aisle(value, odd):
    count = lax.axis_size("aisle")
    pairs = [(i, (i ^ 1 if not odd else i + 1 if i % 2 else i - 1) % count) for i in range(count)]
    return lax.ppermute(value, "aisle", pairs)


def swap_span(value, odd):
    count = lax.axis_size("span")
    pairs = []
    for a in range(lax.axis_size("aisle")):
        for s in range(count):
            t = s ^ 1 if not odd else s + 1 if s % 2 else s - 1
            b, t = (a, t) if 0 <= t < count else (a ^ 1, s)
            pairs.append((a * count + s, b * count + t))
    return lax.ppermute(value, ("aisle", "span"), pairs)


def shards(room_pops, plenum_pops, tile_cell, tile_owner, tile_class):
    n_span = lax.axis_size("span")
    _, ca, cs, hr = room_pops.shape
    hp = plenum_pops.shape[3]
    blocks = hr // LANES
    rows = blocks * cs
    tiles = tile_cell.shape[0]
    sizes = (ca, cs, blocks, n_span, tiles // n_span)
    relayed = n_span == 4
    near = lambda shape: pltpu.VMEM(shape, F32)
    far = lambda value: pltpu.with_memory_space_constraint(value, pltpu.HBM)
    room_shape, plen_shape = (19, ca, rows, LANES), (19, ca * cs, LANES)
    halo = 5 * (rows + cs)
    halo = halo + -halo % 8
    room = far(room_pops.reshape(19, ca, cs, blocks, LANES).transpose(0, 1, 3, 2, 4).reshape(room_shape))
    plen = far(plenum_pops.reshape(plen_shape))
    tile_cell, tile_owner, tile_class = far(tile_cell), far(tile_owner.reshape(tiles)), far(tile_class)
    numbers = pltpu.SMEM((tiles,), jnp.int32)

    jets_shape = ((2 if relayed else n_span) * CAP, 1, 5 * hp)
    room_near, plen_post, *jets = call(
        functools.partial(plenum_kernel, sizes, relayed),
        [near(room_shape), near(plen_shape)] + [near(jets_shape)] * (2 if relayed else 1),
        [HBM] * 5,
        scratch=[pltpu.VMEM((ca * cs, 1, 5 * hp), F32), near((n_span * CAP, 1, 5 * hp)), near(plen_shape), numbers, numbers, numbers,
                 pltpu.SemaphoreType.DMA((5,))],
    )(room, plen, tile_cell, tile_owner, tile_class)
    if relayed:
        got_jets = lax.ppermute(jets[1], "span", [(i, i ^ 2) for i in range(4)])
    else:
        got_jets = lax.all_to_all(jets[0], "span", 0, 0, tiled=True)

    room_post, swap_a, swap_b = call(
        functools.partial(room_kernel, sizes),
        [near(room_shape), near((halo + 8, LANES)), near((halo, LANES))],
        [VMEM] * 2,
    )(room_near, plen_post)
    got_b = swap_aisle(swap_b, True)
    got_a = swap_aisle(swap_a, False)

    upto8 = lambda count: count + -count % 8
    cross_a, cross_b = call(
        functools.partial(cross_kernel, sizes, relayed),
        [near((upto8(5 * (rows + ca) + (5 * CAP if relayed else 0)), LANES)), near((halo, LANES))],
        [VMEM] * 3,
    )(room_post, plen_post, jets[0])
    in_a = swap_span(cross_a, False)
    in_b = swap_span(cross_b, True)

    room_part, plen_part, places = call(
        functools.partial(local_kernel, sizes),
        [near(room_shape), near(plen_shape), near((n_span * CAP + 1, ca * cs, LANES))],
        [VMEM, VMEM, HBM, HBM],
        scratch=[numbers, numbers, pltpu.SemaphoreType.DMA((2,))],
        flops=10**9,
    )(room_post, plen_post, tile_cell, tile_owner)

    corner_a, corner_b = call(
        functools.partial(corner_kernel, sizes, relayed),
        [near((upto8(rows + 2 + (5 * CAP if relayed else 0)), LANES)), near((upto8(rows + 2), LANES))],
        [VMEM] * 4,
    )(got_a, got_b, got_jets, places)
    last_a = swap_span(corner_a, False)
    last_b = swap_span(corner_b, True)

    room_part, plen_part, inflow = call(
        functools.partial(aisle_kernel, sizes, relayed),
        [near(room_shape), near(plen_shape), near((5, ca * cs, LANES))],
        [VMEM] * 7,
        aliases={0: 0, 1: 1},
    )(room_part, plen_part, got_a, got_b, jets[0], got_jets, places)
    room_part, plen_part, inflow = call(
        functools.partial(enter_kernel, sizes, relayed),
        [near(room_shape), near(plen_shape), near((5, ca * cs, LANES))],
        [VMEM] * 6,
        aliases={0: 0, 1: 1},
    )(room_part, plen_part, in_a, in_b, places, inflow)

    _, _, room_next, plenum_next = call(
        functools.partial(finish_kernel, sizes, relayed),
        [near(room_shape), near(plen_shape), jax.ShapeDtypeStruct(room_shape, F32),
         jax.ShapeDtypeStruct(plen_shape, F32)],
        [VMEM] * 6,
        out_specs=[VMEM, VMEM, HBM, HBM],
        scratch=[pltpu.SemaphoreType.DMA((2,))],
        aliases={0: 0, 1: 1},
    )(room_part, plen_part, last_a, last_b, places, inflow)
    room_next = room_next.reshape(19, ca, blocks, cs, LANES).transpose(0, 1, 3, 2, 4).reshape(room_pops.shape)
    return room_next, plenum_next.reshape(plenum_pops.shape)


def solution(mesh):
    return jax.shard_map(
        shards,
        mesh=mesh,
        in_specs=(
            P(None, "aisle", "span", None),
            P(None, "aisle", "span", None),
            P("aisle"),
            P("aisle", None),
            P("aisle"),
        ),
        out_specs=(P(None, "aisle", "span", None), P(None, "aisle", "span", None)),
        check_vma=False,
    )
```

```python
import functools

import jax
import jax.numpy as jnp
from jax import lax
from jax.experimental import pallas as pl
from jax.experimental.pallas import tpu as pltpu
from jax.sharding import PartitionSpec as P

VELOCITIES = [
    (0, 0, 0),
    (1, 0, 0),
    (-1, 0, 0),
    (0, 1, 0),
    (0, -1, 0),
    (0, 0, 1),
    (0, 0, -1),
    (1, 1, 0),
    (-1, -1, 0),
    (1, -1, 0),
    (-1, 1, 0),
    (1, 0, 1),
    (-1, 0, -1),
    (1, 0, -1),
    (-1, 0, 1),
    (0, 1, 1),
    (0, -1, -1),
    (0, 1, -1),
    (0, -1, 1),
]
UPWARD = [5, 11, 14, 15, 18]
OMEGA = 1.25
CAP = 4
X_UP = [q for q in range(19) if VELOCITIES[q][0] == 1]
X_DOWN = [q for q in range(19) if VELOCITIES[q][0] == -1]
Y_UP = [q for q in range(19) if VELOCITIES[q][1] == 1]
Y_DOWN = [q for q in range(19) if VELOCITIES[q][1] == -1]
F32 = jnp.float32
LANES = 128
VMEM = pl.BlockSpec(memory_space=pltpu.VMEM)
HBM = pl.BlockSpec(memory_space=pltpu.HBM)


def collide(g):
    total = lambda i: g[i] + g[i + 1]
    apart = lambda i: g[i] - g[i + 1]
    dx, dy, dz = apart(1), apart(3), apart(5)
    d7, d9, d11, d13, d15, d17 = (apart(i) for i in (7, 9, 11, 13, 15, 17))
    edges = (total(7) + total(9)) + (total(11) + total(13)) + (total(15) + total(17))
    faces = total(1) + total(3) + total(5)
    rho = g[0] * (1.0 / 3.0) + faces * (1.0 / 18.0) + edges * (1.0 / 36.0)
    mx = dx * (1.0 / 18.0) + ((d7 + d9) + (d11 + d13)) * (1.0 / 36.0)
    my = dy * (1.0 / 18.0) + ((d7 - d9) + (d15 + d17)) * (1.0 / 36.0)
    mz = dz * (1.0 / 18.0) + ((d11 - d13) + (d15 - d17)) * (1.0 / 36.0)
    inv = 1.0 / rho
    base = OMEGA * rho - (1.5 * OMEGA) * inv * (mx * mx + my * my + mz * mz)
    square = (4.5 * OMEGA) * inv
    out = [None] * 19
    out[0] = base + (1.0 - OMEGA) * g[0]
    along = {1: mx, 3: my, 5: mz, 7: mx + my, 9: mx - my, 11: mx + mz, 13: mx - mz, 15: my + mz, 17: my - mz}
    for i, c in along.items():
        even = base + square * c * c
        odd = (3.0 * OMEGA) * c
        out[i] = (even + odd) + (1.0 - OMEGA) * g[i]
        out[i + 1] = (even - odd) + (1.0 - OMEGA) * g[i + 1]
    return out


def raised(value, cz, rows):
    if cz == 0:
        return value
    lane = lax.broadcasted_iota(jnp.int32, value.shape, 1)
    row = lax.broadcasted_iota(jnp.int32, value.shape, 0)
    total = value.shape[0]
    shift, edge = (1, 0) if cz == 1 else (LANES - 1, LANES - 1)
    turned = pltpu.roll(value, shift, 1)
    if rows == total:
        return jnp.where(lane == edge, value, turned)
    carried = pltpu.roll(turned, rows if cz == 1 else total - rows, 0)
    clamped = row < rows if cz == 1 else row >= total - rows
    return jnp.where(lane == edge, jnp.where(clamped, value, carried), turned)


def crossed(value, cy, cs):
    if cy == 0:
        return value
    row = lax.broadcasted_iota(jnp.int32, value.shape, 0) % cs
    turned = pltpu.roll(value, 1 if cy == 1 else value.shape[0] - 1, 0)
    return jnp.where(row == (0 if cy == 1 else cs - 1), value, turned)


def shifted(value, by):
    return pltpu.roll(value, by % value.shape[0], 0) if by else value


def turned_to(value, source, dest):
    return shifted(value, dest - source)


def repeat(count, body, start):
    if count > 8:
        return lax.fori_loop(0, count, body, start)
    for i in range(count):
        start = body(i, start)
    return start


def plenum_kernel(sizes, relayed, room_in, plen_in, cell_in, owner_in, class_in, room_near, plen_post, *rest):
    ca, cs, blocks, n_span, per_brick = sizes
    jets = rest[:-7]
    columns, dealt, plen_buf, cells, owners, classes, sems = rest[-7:]
    copies = [pltpu.make_async_copy(src, dst, sems.at[i]) for i, (src, dst) in enumerate(
        ((plen_in, plen_buf), (cell_in, cells), (owner_in, owners), (class_in, classes), (room_in, room_near)))]
    for copy in copies:
        copy.start()
    dealt[...] = jnp.zeros_like(dealt)
    copies[0].wait()
    for r in range(0, ca * cs, 8):
        post = collide([plen_buf[q, r : r + 8] for q in range(19)])
        for q in range(19):
            plen_post[q, r : r + 8] = post[q]
        for k, q in enumerate(UPWARD):
            for y in range(8):
                columns[r + y, :, k * LANES : (k + 1) * LANES] = post[q][y : y + 1]
    for copy in copies[1:4]:
        copy.wait()
    here = lax.axis_index("span")
    first = here * per_brick

    def send_jet(i, carry):
        t = first + i
        owner = owners[t]
        share = 0.15 * (classes[t].astype(F32) + 1.0)
        same = lambda j, n: n + (owners[first + j] == owner).astype(jnp.int32)
        slot = repeat(i, same, 0) if relayed else lax.fori_loop(0, i, same, 0)
        to = (owner ^ here if relayed else owner) * CAP + slot
        dealt[to] = share * columns[cells[t]]
        return carry

    if relayed:
        for i in range(per_brick):
            send_jet(i, 0)
    else:
        lax.fori_loop(0, per_brick, send_jet, 0)
    for part, jet in enumerate(jets):
        many = jet.shape[0]
        jet[...] = dealt[part * many : (part + 1) * many]
    copies[4].wait()


def room_kernel(sizes, room_near, plen_post, room_post, swap_a, swap_b):
    ca, cs, blocks, n_span, per_brick = sizes
    rows = blocks * cs

    def plane(x, carry):
        for r in range(0, rows, 8):
            post = collide([room_near[q, x, r : r + 8] for q in range(19)])
            for q in range(19):
                room_post[q, x, r : r + 8] = post[q]
        return carry

    lax.fori_loop(0, ca, plane, 0)
    even = lax.axis_index("aisle") % 2 == 0
    for k in range(5):
        up, down = X_UP[k], X_DOWN[k]
        rising = raised(room_post[up, ca - 1], VELOCITIES[up][2], cs)
        falling = raised(room_post[down, 0], VELOCITIES[down][2], cs)
        swap_a[k * rows : (k + 1) * rows] = jnp.where(even, rising, falling)
        swap_b[k * rows : (k + 1) * rows] = jnp.where(even, falling, rising)
        rising = raised(plen_post[up, (ca - 1) * cs : ca * cs], VELOCITIES[up][2], cs)
        falling = raised(plen_post[down, 0:cs], VELOCITIES[down][2], cs)
        low = 5 * rows + k * cs
        swap_a[low : low + cs] = jnp.where(even, rising, falling)
        swap_b[low : low + cs] = jnp.where(even, falling, rising)


def jet_sums(start, places, bricks):
    sums = [start(k) for k in range(5)]
    for b, jet in bricks:
        for s in range(CAP):
            marks = places[b * CAP + s]
            sums = [total + marks * jet(s, k) for k, total in enumerate(sums)]
    return sums


def local_kernel(sizes, room_post, plen_post, corner, cell_in, owner_in, room_part, plen_part, places, cells, owners, sems):
    del corner
    ca, cs, blocks, n_span, per_brick = sizes
    rows = blocks * cs
    copies = [pltpu.make_async_copy(src, dst, sems.at[i]) for i, (src, dst) in enumerate(
        ((cell_in, cells), (owner_in, owners)))]
    for copy in copies:
        copy.start()
    for q in range(19):
        cx, cy, cz = VELOCITIES[q]
        for x in range(ca):
            if 0 <= x - cx < ca:
                room_part[q, x] = crossed(raised(room_post[q, x - cx], cz, cs), cy, cs)
        plen_part[q] = crossed(shifted(raised(plen_post[q], cz, ca * cs), cx * cs), cy, cs)
    places[0 : n_span * CAP] = jnp.zeros((n_span * CAP, ca * cs, LANES), F32)
    here = lax.axis_index("span")
    row = lax.broadcasted_iota(jnp.int32, (ca * cs, LANES), 0)
    for copy in copies:
        copy.wait()

    def brick(b, carry):
        def place(i, slot):
            t = b * per_brick + i
            mine = owners[t] == here
            places[jnp.where(mine, b * CAP + slot, n_span * CAP)] = (row == cells[t]).astype(F32)
            return slot + mine.astype(jnp.int32)

        repeat(per_brick, place, 0)
        return carry

    repeat(n_span, brick, 0)


def cross_kernel(sizes, relayed, room_post, plen_post, jets, cross_a, cross_b):
    ca, cs, blocks, n_span, per_brick = sizes
    rows = blocks * cs
    low = lax.axis_index("span") % 2 == 0
    group = lax.broadcasted_iota(jnp.int32, (rows, LANES), 0) % cs
    for k in range(5):
        sides, near = [], []
        for q, edge in ((Y_UP[k], cs - 1), (Y_DOWN[k], 0)):
            cx, cy, cz = VELOCITIES[q]
            packed = None
            for x in range(max(cx, 0), ca + min(cx, 0)):
                ready = turned_to(raised(room_post[q, x - cx], cz, cs), edge, x)
                packed = ready if packed is None else jnp.where(group == x, ready, packed)
            sides.append(packed)
            near.append(shifted(raised(plen_post[q], cz, ca * cs), cx * cs - edge))
        cross_a[k * rows : (k + 1) * rows] = jnp.where(low, sides[0], sides[1])
        cross_b[k * rows : (k + 1) * rows] = jnp.where(low, sides[1], sides[0])
        first, second = jnp.where(low, near[0], near[1]), jnp.where(low, near[1], near[0])
        for x in range(ca):
            to = 5 * rows + k * ca + x
            cross_a[to : to + 1] = first[x * cs : x * cs + 1]
            cross_b[to : to + 1] = second[x * cs : x * cs + 1]
    if relayed:
        for s in range(CAP):
            for k in range(5):
                to = 5 * (rows + ca) + s * 5 + k
                cross_a[to : to + 1] = jets[CAP + s, :, k * LANES : (k + 1) * LANES]


def corners(cs, up):
    return [q for q in (Y_UP if up else Y_DOWN) if VELOCITIES[q][0]], cs - 1 if up else 0


def corner_kernel(sizes, relayed, got_a, got_b, got_jets, cross_a, cross_b):
    ca, cs, blocks, n_span, per_brick = sizes
    rows = blocks * cs
    even = lax.axis_index("aisle") % 2 == 0
    low = lax.axis_index("span") % 2 == 0
    group = lax.broadcasted_iota(jnp.int32, (rows, LANES), 0) % cs

    def came(q, low, high):
        if VELOCITIES[q][0] == 1:
            k = X_UP.index(q)
            return jnp.where(even, got_b[low(k) : high(k)], got_a[low(k) : high(k)])
        k = X_DOWN.index(q)
        return jnp.where(even, got_a[low(k) : high(k)], got_b[low(k) : high(k)])

    sides, near = [], []
    for up in (True, False):
        two, edge = corners(cs, up)
        parts = [turned_to(came(q, lambda k: k * rows, lambda k: (k + 1) * rows), edge, c) for c, q in enumerate(two)]
        sides.append(jnp.where(group == 0, parts[0], parts[1]))
        at = lambda k: 5 * rows + k * cs + edge
        near.append([came(q, at, lambda k: at(k) + 1) for q in two])
    cross_a[0:rows] = jnp.where(low, sides[0], sides[1])
    cross_b[0:rows] = jnp.where(low, sides[1], sides[0])
    for c in range(2):
        cross_a[rows + c : rows + c + 1] = jnp.where(low, near[0][c], near[1][c])
        cross_b[rows + c : rows + c + 1] = jnp.where(low, near[1][c], near[0][c])
    if relayed:
        for s in range(CAP):
            for k in range(5):
                to = rows + 2 + s * 5 + k
                cross_a[to : to + 1] = got_jets[CAP + s, :, k * LANES : (k + 1) * LANES]


def aisle_kernel(sizes, relayed, room_in, plen_in, got_a, got_b, jets, got_jets, places, room, plen, inflow):
    ca, cs, blocks, n_span, per_brick = sizes
    rows = blocks * cs
    even = lax.axis_index("aisle") % 2 == 0
    for k in range(5):
        for q, x, first, second in ((X_UP[k], 0, got_b, got_a), (X_DOWN[k], ca - 1, got_a, got_b)):
            cy = VELOCITIES[q][1]
            low, high = k * rows, (k + 1) * rows
            room[q, x] = crossed(jnp.where(even, first[low:high], second[low:high]), cy, cs)
            low = 5 * rows + k * cs
            value = jnp.where(even, first[low : low + cs], second[low : low + cs])
            at = x * cs
            if cy == 1:
                plen[q, at : at + 1] = value[0:1]
                plen[q, at + 1 : at + cs] = value[: cs - 1]
            elif cy == -1:
                plen[q, at + cs - 1 : at + cs] = value[cs - 1 : cs]
                plen[q, at : at + cs - 1] = value[1:cs]
            else:
                plen[q, at : at + cs] = value
    here = lax.axis_index("span")

    def put(sums):
        for k in range(5):
            inflow[k] = sums[k]

    def reader(source, b):
        return lambda s, k: source[b * CAP + s, :, k * LANES : (k + 1) * LANES]

    if relayed:
        put(jet_sums(lambda k: jnp.zeros((ca * cs, LANES), F32), places,
                     [(here, reader(jets, 0)), (here ^ 2, reader(got_jets, 0))]))
    else:
        inflow[...] = jnp.zeros_like(inflow)

        def add_brick(b, carry):
            put(jet_sums(lambda k: inflow[k], places, [(b, reader(got_jets, b))]))
            return carry

        lax.fori_loop(0, n_span, add_brick, 0)


def entering(n_span, got_a, got_b, enter):
    here = lax.axis_index("span")
    low = here % 2 == 0

    @pl.when(low)
    def _():
        enter(got_a, False)

    @pl.when(jnp.logical_not(low))
    def _():
        enter(got_a, True)

    @pl.when(jnp.logical_and(low, here > 0))
    def _():
        enter(got_b, True)

    @pl.when(jnp.logical_and(jnp.logical_not(low), here < n_span - 1))
    def _():
        enter(got_b, False)


def enter_kernel(sizes, relayed, room_in, plen_in, got_a, got_b, places, inflow_in, room, plen, inflow):
    ca, cs, blocks, n_span, per_brick = sizes
    rows = blocks * cs
    here = lax.axis_index("span")
    group = lax.broadcasted_iota(jnp.int32, (rows, LANES), 0) % cs

    def enter(got, up):
        planes, y = (Y_UP, 0) if up else (Y_DOWN, cs - 1)
        for k, q in enumerate(planes):
            came = got[k * rows : (k + 1) * rows]
            for x in range(ca):
                room[q, x] = jnp.where(group == y, turned_to(came, x, y), room[q, x])
                at = 5 * rows + k * ca + x
                plen[q, x * cs + y : x * cs + y + 1] = got[at : at + 1]

    entering(n_span, got_a, got_b, enter)
    if relayed:
        start = 5 * (rows + ca)
        jet = lambda s, k: got_a[start + s * 5 + k : start + s * 5 + k + 1]
        sums = jet_sums(lambda k: inflow_in[k], places, [(here ^ 1, jet)])
        for k in range(5):
            inflow[k] = sums[k]
    else:
        inflow[...] = inflow_in[...]


def finish_kernel(sizes, relayed, room_in, plen_in, got_a, got_b, places, inflow, room, plen, room_out, plen_out, sems):
    ca, cs, blocks, n_span, per_brick = sizes
    rows = blocks * cs
    here = lax.axis_index("span")
    group = lax.broadcasted_iota(jnp.int32, (rows, LANES), 0) % cs

    def enter(got, up):
        two, _ = corners(cs, up)
        y = 0 if up else cs - 1
        came = got[0:rows]
        for c, q in enumerate(two):
            x = 0 if VELOCITIES[q][0] == 1 else ca - 1
            room[q, x] = jnp.where(group == y, turned_to(came, c, y), room[q, x])
            plen[q, x * cs + y : x * cs + y + 1] = got[rows + c : rows + c + 1]

    entering(n_span, got_a, got_b, enter)
    plen_copy = pltpu.make_async_copy(plen, plen_out, sems.at[0])
    plen_copy.start()
    bricks = []
    if relayed:
        bricks = [(here ^ 3, lambda s, k: got_a[rows + 2 + s * 5 + k : rows + 2 + s * 5 + k + 1])]
    sums = jet_sums(lambda k: inflow[k], places, bricks)
    for k, q in enumerate(UPWARD):
        for x in range(ca):
            room[q, x, 0:cs] = room[q, x, 0:cs] + sums[k][x * cs : (x + 1) * cs]
    room_copy = pltpu.make_async_copy(room, room_out, sems.at[1])
    room_copy.start()
    plen_copy.wait()
    room_copy.wait()


def call(kernel, outs, in_specs, out_specs=None, scratch=(), aliases={}, flops=100_000, moved=1_000_000):
    return pl.pallas_call(
        kernel,
        name=kernel.func.__name__,
        out_shape=outs,
        in_specs=in_specs,
        out_specs=[VMEM] * len(outs) if out_specs is None else out_specs,
        scratch_shapes=list(scratch),
        input_output_aliases=aliases,
        cost_estimate=pl.CostEstimate(flops=flops, bytes_accessed=moved, transcendentals=0),
        compiler_params=pltpu.CompilerParams(vmem_limit_bytes=40 * 2**20),
    )


def swap_aisle(value, odd):
    count = lax.axis_size("aisle")
    pairs = [(i, (i ^ 1 if not odd else i + 1 if i % 2 else i - 1) % count) for i in range(count)]
    return lax.ppermute(value, "aisle", pairs)


def swap_span(value, odd):
    count = lax.axis_size("span")
    pairs = []
    for a in range(lax.axis_size("aisle")):
        for s in range(count):
            t = s ^ 1 if not odd else s + 1 if s % 2 else s - 1
            b, t = (a, t) if 0 <= t < count else (a ^ 1, s)
            pairs.append((a * count + s, b * count + t))
    return lax.ppermute(value, ("aisle", "span"), pairs)


def shards(room_pops, plenum_pops, tile_cell, tile_owner, tile_class):
    n_span = lax.axis_size("span")
    _, ca, cs, hr = room_pops.shape
    hp = plenum_pops.shape[3]
    blocks = hr // LANES
    rows = blocks * cs
    tiles = tile_cell.shape[0]
    sizes = (ca, cs, blocks, n_span, tiles // n_span)
    relayed = n_span == 4
    near = lambda shape: pltpu.VMEM(shape, F32)
    far = lambda value: pltpu.with_memory_space_constraint(value, pltpu.HBM)
    room_shape, plen_shape = (19, ca, rows, LANES), (19, ca * cs, LANES)
    halo = 5 * (rows + cs)
    halo = halo + -halo % 8
    room = far(room_pops.reshape(19, ca, cs, blocks, LANES).transpose(0, 1, 3, 2, 4).reshape(room_shape))
    plen = far(plenum_pops.reshape(plen_shape))
    tile_cell, tile_owner, tile_class = far(tile_cell), far(tile_owner.reshape(tiles)), far(tile_class)
    numbers = pltpu.SMEM((tiles,), jnp.int32)

    jets_shape = ((2 if relayed else n_span) * CAP, 1, 5 * hp)
    room_near, plen_post, *jets = call(
        functools.partial(plenum_kernel, sizes, relayed),
        [near(room_shape), near(plen_shape)] + [near(jets_shape)] * (2 if relayed else 1),
        [HBM] * 5,
        scratch=[pltpu.VMEM((ca * cs, 1, 5 * hp), F32), near((n_span * CAP, 1, 5 * hp)), near(plen_shape), numbers, numbers, numbers,
                 pltpu.SemaphoreType.DMA((5,))],
    )(room, plen, tile_cell, tile_owner, tile_class)
    if relayed:
        got_jets = lax.ppermute(jets[1], "span", [(i, i ^ 2) for i in range(4)])
    else:
        got_jets = lax.all_to_all(jets[0], "span", 0, 0, tiled=True)

    room_post, swap_a, swap_b = call(
        functools.partial(room_kernel, sizes),
        [near(room_shape), near((halo + 8, LANES)), near((halo, LANES))],
        [VMEM] * 2,
    )(room_near, plen_post)
    got_b = swap_aisle(swap_b, True)
    got_a = swap_aisle(swap_a, False)

    upto8 = lambda count: count + -count % 8
    cross_a, cross_b = call(
        functools.partial(cross_kernel, sizes, relayed),
        [near((upto8(5 * (rows + ca) + (5 * CAP if relayed else 0)), LANES)), near((halo, LANES))],
        [VMEM] * 3,
        flops=10**9,
    )(room_post, plen_post, jets[0])
    in_a = swap_span(cross_a, False)
    in_b = swap_span(cross_b, True)

    last = upto8(rows + 2 + (5 * CAP if relayed else 0))
    corner_a, corner_b = call(
        functools.partial(corner_kernel, sizes, relayed),
        [near((last, LANES)), near((last + 8, LANES))],
        [VMEM] * 3,
    )(got_a, got_b, got_jets)
    last_a = swap_span(corner_a, False)
    last_b = swap_span(corner_b, True)

    room_part, plen_part, places = call(
        functools.partial(local_kernel, sizes),
        [near(room_shape), near(plen_shape), near((n_span * CAP + 1, ca * cs, LANES))],
        [VMEM, VMEM, VMEM, HBM, HBM],
        scratch=[numbers, numbers, pltpu.SemaphoreType.DMA((2,))],
        flops=10**9,
    )(room_post, plen_post, corner_a, tile_cell, tile_owner)

    room_part, plen_part, inflow = call(
        functools.partial(aisle_kernel, sizes, relayed),
        [near(room_shape), near(plen_shape), near((5, ca * cs, LANES))],
        [VMEM] * 7,
        aliases={0: 0, 1: 1},
    )(room_part, plen_part, got_a, got_b, jets[0], got_jets, places)
    room_part, plen_part, inflow = call(
        functools.partial(enter_kernel, sizes, relayed),
        [near(room_shape), near(plen_shape), near((5, ca * cs, LANES))],
        [VMEM] * 6,
        aliases={0: 0, 1: 1},
    )(room_part, plen_part, in_a, in_b, places, inflow)

    _, _, room_next, plenum_next = call(
        functools.partial(finish_kernel, sizes, relayed),
        [near(room_shape), near(plen_shape), jax.ShapeDtypeStruct(room_shape, F32),
         jax.ShapeDtypeStruct(plen_shape, F32)],
        [VMEM] * 6,
        out_specs=[VMEM, VMEM, HBM, HBM],
        scratch=[pltpu.SemaphoreType.DMA((2,))],
        aliases={0: 0, 1: 1},
    )(room_part, plen_part, last_a, last_b, places, inflow)
    room_next = room_next.reshape(19, ca, blocks, cs, LANES).transpose(0, 1, 3, 2, 4).reshape(room_pops.shape)
    return room_next, plenum_next.reshape(plenum_pops.shape)


def solution(mesh):
    return jax.shard_map(
        shards,
        mesh=mesh,
        in_specs=(
            P(None, "aisle", "span", None),
            P(None, "aisle", "span", None),
            P("aisle"),
            P("aisle", None),
            P("aisle"),
        ),
        out_specs=(P(None, "aisle", "span", None), P(None, "aisle", "span", None)),
        check_vma=False,
    )
```

```python
import functools

import jax
import jax.numpy as jnp
from jax import lax
from jax.experimental import pallas as pl
from jax.experimental.pallas import tpu as pltpu
from jax.sharding import PartitionSpec as P

VELOCITIES = [
    (0, 0, 0),
    (1, 0, 0),
    (-1, 0, 0),
    (0, 1, 0),
    (0, -1, 0),
    (0, 0, 1),
    (0, 0, -1),
    (1, 1, 0),
    (-1, -1, 0),
    (1, -1, 0),
    (-1, 1, 0),
    (1, 0, 1),
    (-1, 0, -1),
    (1, 0, -1),
    (-1, 0, 1),
    (0, 1, 1),
    (0, -1, -1),
    (0, 1, -1),
    (0, -1, 1),
]
UPWARD = [5, 11, 14, 15, 18]
OMEGA = 1.25
CAP = 4
X_UP = [q for q in range(19) if VELOCITIES[q][0] == 1]
X_DOWN = [q for q in range(19) if VELOCITIES[q][0] == -1]
Y_UP = [q for q in range(19) if VELOCITIES[q][1] == 1]
Y_DOWN = [q for q in range(19) if VELOCITIES[q][1] == -1]
F32 = jnp.float32
LANES = 128
VMEM = pl.BlockSpec(memory_space=pltpu.VMEM)
HBM = pl.BlockSpec(memory_space=pltpu.HBM)


def collide(g):
    total = lambda i: g[i] + g[i + 1]
    apart = lambda i: g[i] - g[i + 1]
    dx, dy, dz = apart(1), apart(3), apart(5)
    d7, d9, d11, d13, d15, d17 = (apart(i) for i in (7, 9, 11, 13, 15, 17))
    edges = (total(7) + total(9)) + (total(11) + total(13)) + (total(15) + total(17))
    faces = total(1) + total(3) + total(5)
    rho = g[0] * (1.0 / 3.0) + faces * (1.0 / 18.0) + edges * (1.0 / 36.0)
    mx = dx * (1.0 / 18.0) + ((d7 + d9) + (d11 + d13)) * (1.0 / 36.0)
    my = dy * (1.0 / 18.0) + ((d7 - d9) + (d15 + d17)) * (1.0 / 36.0)
    mz = dz * (1.0 / 18.0) + ((d11 - d13) + (d15 - d17)) * (1.0 / 36.0)
    inv = 1.0 / rho
    base = OMEGA * rho - (1.5 * OMEGA) * inv * (mx * mx + my * my + mz * mz)
    square = (4.5 * OMEGA) * inv
    out = [None] * 19
    out[0] = base + (1.0 - OMEGA) * g[0]
    along = {1: mx, 3: my, 5: mz, 7: mx + my, 9: mx - my, 11: mx + mz, 13: mx - mz, 15: my + mz, 17: my - mz}
    for i, c in along.items():
        even = base + square * c * c
        odd = (3.0 * OMEGA) * c
        out[i] = (even + odd) + (1.0 - OMEGA) * g[i]
        out[i + 1] = (even - odd) + (1.0 - OMEGA) * g[i + 1]
    return out


def raised(value, cz, rows):
    if cz == 0:
        return value
    lane = lax.broadcasted_iota(jnp.int32, value.shape, 1)
    row = lax.broadcasted_iota(jnp.int32, value.shape, 0)
    total = value.shape[0]
    shift, edge = (1, 0) if cz == 1 else (LANES - 1, LANES - 1)
    turned = pltpu.roll(value, shift, 1)
    if rows == total:
        return jnp.where(lane == edge, value, turned)
    carried = pltpu.roll(turned, rows if cz == 1 else total - rows, 0)
    clamped = row < rows if cz == 1 else row >= total - rows
    return jnp.where(lane == edge, jnp.where(clamped, value, carried), turned)


def crossed(value, cy, cs):
    if cy == 0:
        return value
    row = lax.broadcasted_iota(jnp.int32, value.shape, 0) % cs
    turned = pltpu.roll(value, 1 if cy == 1 else value.shape[0] - 1, 0)
    return jnp.where(row == (0 if cy == 1 else cs - 1), value, turned)


def turned_to(value, source, dest):
    shift = (dest - source) % value.shape[0]
    return value if shift == 0 else pltpu.roll(value, shift, 0)


def repeat(count, body, start):
    if count > 8:
        return lax.fori_loop(0, count, body, start)
    for i in range(count):
        start = body(i, start)
    return start


def collide_kernel(sizes, room_in, plen_in, room_post, plen_post, swap_a, swap_b, room_buf, plen_buf, sems):
    ca, cs, blocks, n_span, per_brick = sizes
    rows = blocks * cs
    copies = [pltpu.make_async_copy(src, dst, sems.at[i]) for i, (src, dst) in enumerate(
        ((plen_in, plen_buf), (room_in, room_buf)))]
    for copy in copies:
        copy.start()
    copies[0].wait()
    for r in range(0, ca * cs, 8):
        post = collide([plen_buf[q, r : r + 8] for q in range(19)])
        for q in range(19):
            plen_post[q, r : r + 8] = post[q]
    copies[1].wait()

    def plane(x, carry):
        for r in range(0, rows, 8):
            post = collide([room_buf[q, x, r : r + 8] for q in range(19)])
            for q in range(19):
                room_post[q, x, r : r + 8] = post[q]
        return carry

    lax.fori_loop(0, ca, plane, 0)
    even = lax.axis_index("aisle") % 2 == 0
    for k in range(5):
        up, down = X_UP[k], X_DOWN[k]
        rising = raised(room_post[up, ca - 1], VELOCITIES[up][2], cs)
        falling = raised(room_post[down, 0], VELOCITIES[down][2], cs)
        swap_a[k * rows : (k + 1) * rows] = jnp.where(even, rising, falling)
        swap_b[k * rows : (k + 1) * rows] = jnp.where(even, falling, rising)
        rising = raised(plen_post[up, (ca - 1) * cs : ca * cs], VELOCITIES[up][2], cs)
        falling = raised(plen_post[down, 0:cs], VELOCITIES[down][2], cs)
        low = 5 * rows + k * cs
        swap_a[low : low + cs] = jnp.where(even, rising, falling)
        swap_b[low : low + cs] = jnp.where(even, falling, rising)


def jet_sums(start, places, bricks):
    sums = [start(k) for k in range(5)]
    for b, jet in bricks:
        for s in range(CAP):
            marks = places[b * CAP + s]
            sums = [total + marks * jet(s, k) for k, total in enumerate(sums)]
    return sums


def local_kernel(sizes, direct, room_post, plen_post, cell_in, owner_in, class_in, room_part, plen_part, span_up, span_down,
                 places, *rest):
    ca, cs, blocks, n_span, per_brick = sizes
    rows = blocks * cs
    jets = rest[:-6]
    columns, dealt, cells, owners, classes, sems = rest[-6:]
    copies = [pltpu.make_async_copy(src, dst, sems.at[i]) for i, (src, dst) in enumerate(
        ((cell_in, cells), (owner_in, owners), (class_in, classes)))]
    for copy in copies:
        copy.start()
    dealt[...] = jnp.zeros_like(dealt)
    for k, q in enumerate(UPWARD):
        post = plen_post[q]
        for cell in range(ca * cs):
            columns[cell, :, k * LANES : (k + 1) * LANES] = post[cell : cell + 1]
    group = lax.broadcasted_iota(jnp.int32, (rows, LANES), 0) % cs
    for q in range(19):
        cx, cy, cz = VELOCITIES[q]
        edge = cs - 1 if cy == 1 else 0
        span, planes = (span_up, Y_UP) if cy == 1 else (span_down, Y_DOWN)
        packed = None
        for x in range(ca):
            if not 0 <= x - cx < ca:
                continue
            value = raised(room_post[q, x - cx], cz, cs)
            room_part[q, x] = crossed(value, cy, cs)
            if cy:
                ready = turned_to(value, edge, x)
                packed = ready if packed is None else jnp.where(group == x, ready, packed)
        value = raised(plen_post[q], cz, ca * cs)
        if cx == 1:
            value = pltpu.roll(value, cs, 0)
        elif cx == -1:
            value = pltpu.roll(value, ca * cs - cs, 0)
        plen_part[q] = crossed(value, cy, cs)
        if cy:
            k = planes.index(q)
            span[k * rows : (k + 1) * rows] = packed
            for x in range(ca):
                to = 5 * rows + k * ca + x
                span[to : to + 1] = value[x * cs + edge : x * cs + edge + 1]
    places[0 : n_span * CAP] = jnp.zeros((n_span * CAP, ca * cs, LANES), F32)
    here = lax.axis_index("span")
    row = lax.broadcasted_iota(jnp.int32, (ca * cs, LANES), 0)
    for copy in copies:
        copy.wait()
    first = here * per_brick

    def send_jet(i, carry):
        t = first + i
        owner = owners[t]
        share = 0.15 * (classes[t].astype(F32) + 1.0)
        same = lambda j, n: n + (owners[first + j] == owner).astype(jnp.int32)
        slot = repeat(i, same, 0) if direct else lax.fori_loop(0, i, same, 0)
        to = (owner ^ here if direct else owner) * CAP + slot
        dealt[to] = share * columns[cells[t]]
        return carry

    if direct:
        for i in range(per_brick):
            send_jet(i, 0)
    else:
        lax.fori_loop(0, per_brick, send_jet, 0)
    start = 0
    for jet in jets:
        jet[...] = dealt[start : start + jet.shape[0]]
        start = start + jet.shape[0]

    def brick(b, carry):
        def place(i, slot):
            t = b * per_brick + i
            mine = owners[t] == here
            places[jnp.where(mine, b * CAP + slot, n_span * CAP)] = (row == cells[t]).astype(F32)
            return slot + mine.astype(jnp.int32)

        repeat(per_brick, place, 0)
        return carry

    repeat(n_span, brick, 0)


def pack_kernel(sizes, direct, got_a, got_b, span_up, span_down, *rest):
    ca, cs, blocks, n_span, per_brick = sizes
    rows = blocks * cs
    if direct:
        jets, cross_a, cross_b = rest
    else:
        cross_a, cross_b = rest
    even = lax.axis_index("aisle") % 2 == 0
    low = lax.axis_index("span") % 2 == 0
    halo = span_up.shape[0]
    group = lax.broadcasted_iota(jnp.int32, (rows, LANES), 0) % cs

    def corner(q, low, high):
        if VELOCITIES[q][0] == 1:
            k = X_UP.index(q)
            return jnp.where(even, got_b[low(k) : high(k)], got_a[low(k) : high(k)])
        k = X_DOWN.index(q)
        return jnp.where(even, got_a[low(k) : high(k)], got_b[low(k) : high(k)])

    for k in range(5):
        sides = []
        for span, planes, edge in ((span_up, Y_UP, cs - 1), (span_down, Y_DOWN, 0)):
            q = planes[k]
            value = span[k * rows : (k + 1) * rows]
            if VELOCITIES[q][0]:
                x = 0 if VELOCITIES[q][0] == 1 else ca - 1
                came = corner(q, lambda k: k * rows, lambda k: (k + 1) * rows)
                value = jnp.where(group == x, turned_to(came, edge, x), value)
            sides.append(value)
        cross_a[k * rows : (k + 1) * rows] = jnp.where(low, sides[0], sides[1])
        cross_b[k * rows : (k + 1) * rows] = jnp.where(low, sides[1], sides[0])
    for r in range(5 * rows, halo, 8):
        rising, falling = span_up[r : r + 8], span_down[r : r + 8]
        cross_a[r : r + 8] = jnp.where(low, rising, falling)
        cross_b[r : r + 8] = jnp.where(low, falling, rising)
    for planes, edge in ((Y_UP, cs - 1), (Y_DOWN, 0)):
        for k, q in enumerate(planes):
            if VELOCITIES[q][0]:
                x = 0 if VELOCITIES[q][0] == 1 else ca - 1
                at = lambda k: 5 * rows + k * cs + edge
                came = corner(q, at, lambda k: at(k) + 1)
                to = 5 * rows + k * ca + x

                @pl.when(low == (planes is Y_UP))
                def _():
                    cross_a[to : to + 1] = came

                @pl.when(low != (planes is Y_UP))
                def _():
                    cross_b[to : to + 1] = came

    if direct:
        for s in range(CAP):
            for k in range(5):
                to = 5 * (rows + cs) + s * 5 + k
                cross_a[to : to + 1] = jets[CAP + s, :, k * LANES : (k + 1) * LANES]


def aisle_kernel(sizes, direct, room_in, plen_in, got_a, got_b, jets, places, room, plen, inflow):
    ca, cs, blocks, n_span, per_brick = sizes
    rows = blocks * cs
    even = lax.axis_index("aisle") % 2 == 0
    for k in range(5):
        for q, x, first, second in ((X_UP[k], 0, got_b, got_a), (X_DOWN[k], ca - 1, got_a, got_b)):
            cy = VELOCITIES[q][1]
            low, high = k * rows, (k + 1) * rows
            room[q, x] = crossed(jnp.where(even, first[low:high], second[low:high]), cy, cs)
            low = 5 * rows + k * cs
            value = jnp.where(even, first[low : low + cs], second[low : low + cs])
            at = x * cs
            if cy == 1:
                plen[q, at : at + 1] = value[0:1]
                plen[q, at + 1 : at + cs] = value[: cs - 1]
            elif cy == -1:
                plen[q, at + cs - 1 : at + cs] = value[cs - 1 : cs]
                plen[q, at : at + cs - 1] = value[1:cs]
            else:
                plen[q, at : at + cs] = value
    here = lax.axis_index("span")

    def put(sums):
        for k in range(5):
            inflow[k] = sums[k]

    def reader(source, b):
        return lambda s, k: source[b * CAP + s, :, k * LANES : (k + 1) * LANES]

    if direct:
        put(jet_sums(lambda k: jnp.zeros((ca * cs, LANES), F32), places,
                     [(here, reader(jets, 0))]))
    else:
        inflow[...] = jnp.zeros_like(inflow)

        def add_brick(b, carry):
            put(jet_sums(lambda k: inflow[k], places, [(b, reader(jets, b))]))
            return carry

        lax.fori_loop(0, n_span, add_brick, 0)


def finish_kernel(sizes, direct, room_in, plen_in, got_a, got_b, places, inflow, *rest):
    *got_jets, room, plen, room_out, plen_out, sems = rest
    ca, cs, blocks, n_span, per_brick = sizes
    rows = blocks * cs
    here = lax.axis_index("span")
    low = here % 2 == 0
    group = lax.broadcasted_iota(jnp.int32, (rows, LANES), 0) % cs

    def enter(got, up):
        planes, y = (Y_UP, 0) if up else (Y_DOWN, cs - 1)
        for k, q in enumerate(planes):
            came = got[k * rows : (k + 1) * rows]
            for x in range(ca):
                room[q, x] = jnp.where(group == y, turned_to(came, x, y), room[q, x])
                at = 5 * rows + k * ca + x
                plen[q, x * cs + y : x * cs + y + 1] = got[at : at + 1]

    @pl.when(low)
    def _():
        enter(got_a, False)

    @pl.when(jnp.logical_not(low))
    def _():
        enter(got_a, True)

    @pl.when(jnp.logical_and(low, here > 0))
    def _():
        enter(got_b, True)

    @pl.when(jnp.logical_and(jnp.logical_not(low), here < n_span - 1))
    def _():
        enter(got_b, False)

    plen_copy = pltpu.make_async_copy(plen, plen_out, sems.at[0])
    plen_copy.start()
    bricks = []
    if direct:
        start = 5 * (rows + cs)
        bricks = [(here ^ 1, lambda s, k: got_a[start + s * 5 + k : start + s * 5 + k + 1])]
        for apart, got in zip((2, 3), got_jets):
            bricks.append((here ^ apart, lambda s, k, got=got: got[s, :, k * LANES : (k + 1) * LANES]))
    sums = jet_sums(lambda k: inflow[k], places, bricks)
    for k, q in enumerate(UPWARD):
        for x in range(ca):
            room[q, x, 0:cs] = room[q, x, 0:cs] + sums[k][x * cs : (x + 1) * cs]
    room_copy = pltpu.make_async_copy(room, room_out, sems.at[1])
    room_copy.start()
    plen_copy.wait()
    room_copy.wait()


def call(kernel, outs, in_specs, out_specs=None, scratch=(), aliases={}, flops=100_000, moved=1_000_000):
    return pl.pallas_call(
        kernel,
        name=kernel.func.__name__,
        out_shape=outs,
        in_specs=in_specs,
        out_specs=[VMEM] * len(outs) if out_specs is None else out_specs,
        scratch_shapes=list(scratch),
        input_output_aliases=aliases,
        cost_estimate=pl.CostEstimate(flops=flops, bytes_accessed=moved, transcendentals=0),
        compiler_params=pltpu.CompilerParams(vmem_limit_bytes=40 * 2**20),
    )


def swap_aisle(value, odd):
    count = lax.axis_size("aisle")
    pairs = [(i, (i ^ 1 if not odd else i + 1 if i % 2 else i - 1) % count) for i in range(count)]
    return lax.ppermute(value, "aisle", pairs)


def swap_span(value, odd):
    count = lax.axis_size("span")
    pairs = []
    for a in range(lax.axis_size("aisle")):
        for s in range(count):
            t = s ^ 1 if not odd else s + 1 if s % 2 else s - 1
            b, t = (a, t) if 0 <= t < count else (a ^ 1, s)
            pairs.append((a * count + s, b * count + t))
    return lax.ppermute(value, ("aisle", "span"), pairs)


def shards(room_pops, plenum_pops, tile_cell, tile_owner, tile_class):
    n_span = lax.axis_size("span")
    _, ca, cs, hr = room_pops.shape
    hp = plenum_pops.shape[3]
    blocks = hr // LANES
    rows = blocks * cs
    tiles = tile_cell.shape[0]
    sizes = (ca, cs, blocks, n_span, tiles // n_span)
    direct = n_span == 4
    near = lambda shape: pltpu.VMEM(shape, F32)
    far = lambda value: pltpu.with_memory_space_constraint(value, pltpu.HBM)
    room_shape, plen_shape = (19, ca, rows, LANES), (19, ca * cs, LANES)
    halo = 5 * (rows + cs)
    halo = halo + -halo % 8
    room = far(room_pops.reshape(19, ca, cs, blocks, LANES).transpose(0, 1, 3, 2, 4).reshape(room_shape))
    plen = far(plenum_pops.reshape(plen_shape))
    tile_cell, tile_owner, tile_class = far(tile_cell), far(tile_owner.reshape(tiles)), far(tile_class)
    numbers = pltpu.SMEM((tiles,), jnp.int32)

    jet_shapes = [(count * CAP, 1, 5 * hp) for count in ((2, 1, 1) if direct else (n_span,))]
    room_post, plen_post, swap_a, swap_b = call(
        functools.partial(collide_kernel, sizes),
        [near(room_shape), near(plen_shape), near((halo + 8, LANES)), near((halo, LANES))],
        [HBM] * 2,
        scratch=[near(room_shape), near(plen_shape), pltpu.SemaphoreType.DMA((2,))],
    )(room, plen)
    got_b = swap_aisle(swap_b, True)
    got_a = swap_aisle(swap_a, False)

    room_part, plen_part, span_up, span_down, places, *jets = call(
        functools.partial(local_kernel, sizes, direct),
        [near(room_shape), near(plen_shape), near((halo, LANES)), near((halo, LANES)),
         near((n_span * CAP + 1, ca * cs, LANES))] + [near(shape) for shape in jet_shapes],
        [VMEM, VMEM, HBM, HBM, HBM],
        scratch=[near((ca * cs, 1, 5 * hp)), near((n_span * CAP, 1, 5 * hp)), numbers, numbers, numbers,
                 pltpu.SemaphoreType.DMA((3,))],
        flops=10**9,
    )(room_post, plen_post, tile_cell, tile_owner, tile_class)
    if direct:
        got_jets = [lax.ppermute(jets[apart - 1], "span", [(i, i ^ apart) for i in range(4)]) for apart in (2, 3)]
    else:
        jets = [lax.all_to_all(jets[0], "span", 0, 0, tiled=True)]
        got_jets = []

    upto8 = lambda count: count + -count % 8
    cross_shape = (upto8(5 * (rows + cs) + 5 * CAP), LANES) if direct else (halo, LANES)
    cross_a, cross_b = call(
        functools.partial(pack_kernel, sizes, direct),
        [near(cross_shape), near((cross_shape[0] + 8, LANES))],
        [VMEM] * (5 if direct else 4),
    )(got_a, got_b, span_up, span_down, *(jets[:1] if direct else ()))

    in_b = swap_span(cross_b, True)
    in_a = swap_span(cross_a, False)
    room_part, plen_part, inflow = call(
        functools.partial(aisle_kernel, sizes, direct),
        [near(room_shape), near(plen_shape), near((5, ca * cs, LANES))],
        [VMEM] * 6,
        aliases={0: 0, 1: 1},
        flops=10**9,
    )(room_part, plen_part, got_a, got_b, jets[0], places)

    _, _, room_next, plenum_next = call(
        functools.partial(finish_kernel, sizes, direct),
        [near(room_shape), near(plen_shape), jax.ShapeDtypeStruct(room_shape, F32),
         jax.ShapeDtypeStruct(plen_shape, F32)],
        [VMEM] * (6 + len(got_jets)),
        out_specs=[VMEM, VMEM, HBM, HBM],
        scratch=[pltpu.SemaphoreType.DMA((2,))],
        aliases={0: 0, 1: 1},
    )(room_part, plen_part, in_a, in_b, places, inflow, *got_jets)
    room_next = room_next.reshape(19, ca, blocks, cs, LANES).transpose(0, 1, 3, 2, 4).reshape(room_pops.shape)
    return room_next, plenum_next.reshape(plenum_pops.shape)


def solution(mesh):
    return jax.shard_map(
        shards,
        mesh=mesh,
        in_specs=(
            P(None, "aisle", "span", None),
            P(None, "aisle", "span", None),
            P("aisle"),
            P("aisle", None),
            P("aisle"),
        ),
        out_specs=(P(None, "aisle", "span", None), P(None, "aisle", "span", None)),
        check_vma=False,
    )
```

```python
import functools

import jax
import jax.numpy as jnp
from jax import lax
from jax.experimental import pallas as pl
from jax.experimental.pallas import tpu as pltpu
from jax.sharding import PartitionSpec as P

VELOCITIES = [
    (0, 0, 0),
    (1, 0, 0),
    (-1, 0, 0),
    (0, 1, 0),
    (0, -1, 0),
    (0, 0, 1),
    (0, 0, -1),
    (1, 1, 0),
    (-1, -1, 0),
    (1, -1, 0),
    (-1, 1, 0),
    (1, 0, 1),
    (-1, 0, -1),
    (1, 0, -1),
    (-1, 0, 1),
    (0, 1, 1),
    (0, -1, -1),
    (0, 1, -1),
    (0, -1, 1),
]
UPWARD = [5, 11, 14, 15, 18]
OMEGA = 1.25
CAP = 4
X_UP = [q for q in range(19) if VELOCITIES[q][0] == 1]
X_DOWN = [q for q in range(19) if VELOCITIES[q][0] == -1]
Y_UP = [q for q in range(19) if VELOCITIES[q][1] == 1]
Y_DOWN = [q for q in range(19) if VELOCITIES[q][1] == -1]
F32 = jnp.float32
LANES = 128
VMEM = pl.BlockSpec(memory_space=pltpu.VMEM)
HBM = pl.BlockSpec(memory_space=pltpu.HBM)


def collide(g):
    total = lambda i: g[i] + g[i + 1]
    apart = lambda i: g[i] - g[i + 1]
    dx, dy, dz = apart(1), apart(3), apart(5)
    d7, d9, d11, d13, d15, d17 = (apart(i) for i in (7, 9, 11, 13, 15, 17))
    edges = (total(7) + total(9)) + (total(11) + total(13)) + (total(15) + total(17))
    faces = total(1) + total(3) + total(5)
    rho = g[0] * (1.0 / 3.0) + faces * (1.0 / 18.0) + edges * (1.0 / 36.0)
    mx = dx * (1.0 / 18.0) + ((d7 + d9) + (d11 + d13)) * (1.0 / 36.0)
    my = dy * (1.0 / 18.0) + ((d7 - d9) + (d15 + d17)) * (1.0 / 36.0)
    mz = dz * (1.0 / 18.0) + ((d11 - d13) + (d15 - d17)) * (1.0 / 36.0)
    inv = 1.0 / rho
    base = OMEGA * rho - (1.5 * OMEGA) * inv * (mx * mx + my * my + mz * mz)
    square = (4.5 * OMEGA) * inv
    out = [None] * 19
    out[0] = base + (1.0 - OMEGA) * g[0]
    along = {1: mx, 3: my, 5: mz, 7: mx + my, 9: mx - my, 11: mx + mz, 13: mx - mz, 15: my + mz, 17: my - mz}
    for i, c in along.items():
        even = base + square * c * c
        odd = (3.0 * OMEGA) * c
        out[i] = (even + odd) + (1.0 - OMEGA) * g[i]
        out[i + 1] = (even - odd) + (1.0 - OMEGA) * g[i + 1]
    return out


def raised(value, cz, rows):
    if cz == 0:
        return value
    lane = lax.broadcasted_iota(jnp.int32, value.shape, 1)
    row = lax.broadcasted_iota(jnp.int32, value.shape, 0)
    total = value.shape[0]
    shift, edge = (1, 0) if cz == 1 else (LANES - 1, LANES - 1)
    turned = pltpu.roll(value, shift, 1)
    if rows == total:
        return jnp.where(lane == edge, value, turned)
    carried = pltpu.roll(turned, rows if cz == 1 else total - rows, 0)
    clamped = row < rows if cz == 1 else row >= total - rows
    return jnp.where(lane == edge, jnp.where(clamped, value, carried), turned)


def crossed(value, cy, cs):
    if cy == 0:
        return value
    row = lax.broadcasted_iota(jnp.int32, value.shape, 0) % cs
    turned = pltpu.roll(value, 1 if cy == 1 else value.shape[0] - 1, 0)
    return jnp.where(row == (0 if cy == 1 else cs - 1), value, turned)


def shifted(value, by):
    return pltpu.roll(value, by % value.shape[0], 0) if by else value


def turned_to(value, source, dest):
    return shifted(value, dest - source)


def repeat(count, body, start):
    if count > 8:
        return lax.fori_loop(0, count, body, start)
    for i in range(count):
        start = body(i, start)
    return start


def collide_kernel(sizes, direct, room_in, plen_in, cell_in, owner_in, class_in, room_post, plen_post, swap_a, swap_b,
                   *rest):
    ca, cs, blocks, n_span, per_brick = sizes
    rows = blocks * cs
    jets = rest[:-8]
    columns, dealt, room_buf, plen_buf, cells, owners, classes, sems = rest[-8:]
    copies = [pltpu.make_async_copy(src, dst, sems.at[i]) for i, (src, dst) in enumerate(
        ((plen_in, plen_buf), (cell_in, cells), (owner_in, owners), (class_in, classes), (room_in, room_buf)))]
    for copy in copies:
        copy.start()
    dealt[...] = jnp.zeros_like(dealt)
    copies[0].wait()
    for r in range(0, ca * cs, 8):
        post = collide([plen_buf[q, r : r + 8] for q in range(19)])
        for q in range(19):
            plen_post[q, r : r + 8] = post[q]
        for k, q in enumerate(UPWARD):
            for y in range(8):
                columns[r + y, :, k * LANES : (k + 1) * LANES] = post[q][y : y + 1]
    for copy in copies[1:4]:
        copy.wait()
    here = lax.axis_index("span")
    first = here * per_brick

    def send_jet(i, carry):
        t = first + i
        owner = owners[t]
        share = 0.15 * (classes[t].astype(F32) + 1.0)
        same = lambda j, n: n + (owners[first + j] == owner).astype(jnp.int32)
        slot = repeat(i, same, 0) if direct else lax.fori_loop(0, i, same, 0)
        to = (owner ^ here if direct else owner) * CAP + slot
        dealt[to] = share * columns[cells[t]]
        return carry

    if direct:
        for i in range(per_brick):
            send_jet(i, 0)
    else:
        lax.fori_loop(0, per_brick, send_jet, 0)
    start = 0
    for jet in jets:
        jet[...] = dealt[start : start + jet.shape[0]]
        start = start + jet.shape[0]
    copies[4].wait()

    def plane(x, carry):
        for r in range(0, rows, 8):
            post = collide([room_buf[q, x, r : r + 8] for q in range(19)])
            for q in range(19):
                room_post[q, x, r : r + 8] = post[q]
        return carry

    lax.fori_loop(0, ca, plane, 0)
    even = lax.axis_index("aisle") % 2 == 0
    for k in range(5):
        up, down = X_UP[k], X_DOWN[k]
        rising = raised(room_post[up, ca - 1], VELOCITIES[up][2], cs)
        falling = raised(room_post[down, 0], VELOCITIES[down][2], cs)
        swap_a[k * rows : (k + 1) * rows] = jnp.where(even, rising, falling)
        swap_b[k * rows : (k + 1) * rows] = jnp.where(even, falling, rising)
        rising = raised(plen_post[up, (ca - 1) * cs : ca * cs], VELOCITIES[up][2], cs)
        falling = raised(plen_post[down, 0:cs], VELOCITIES[down][2], cs)
        low = 5 * rows + k * cs
        swap_a[low : low + cs] = jnp.where(even, rising, falling)
        swap_b[low : low + cs] = jnp.where(even, falling, rising)


def jet_sums(start, places, bricks):
    sums = [start(k) for k in range(5)]
    for b, jet in bricks:
        for s in range(CAP):
            marks = places[b * CAP + s]
            sums = [total + marks * jet(s, k) for k, total in enumerate(sums)]
    return sums


def local_kernel(sizes, room_post, plen_post, crossing, cell_in, owner_in, room_part, plen_part, places, cells, owners,
                 sems):
    del crossing
    ca, cs, blocks, n_span, per_brick = sizes
    rows = blocks * cs
    copies = [pltpu.make_async_copy(src, dst, sems.at[i]) for i, (src, dst) in enumerate(
        ((cell_in, cells), (owner_in, owners)))]
    for copy in copies:
        copy.start()
    for q in range(19):
        cx, cy, cz = VELOCITIES[q]
        for x in range(ca):
            if 0 <= x - cx < ca:
                room_part[q, x] = crossed(raised(room_post[q, x - cx], cz, cs), cy, cs)
        plen_part[q] = crossed(shifted(raised(plen_post[q], cz, ca * cs), cx * cs), cy, cs)
    places[0 : n_span * CAP] = jnp.zeros((n_span * CAP, ca * cs, LANES), F32)
    here = lax.axis_index("span")
    row = lax.broadcasted_iota(jnp.int32, (ca * cs, LANES), 0)
    for copy in copies:
        copy.wait()

    def brick(b, carry):
        def place(i, slot):
            t = b * per_brick + i
            mine = owners[t] == here
            places[jnp.where(mine, b * CAP + slot, n_span * CAP)] = (row == cells[t]).astype(F32)
            return slot + mine.astype(jnp.int32)

        repeat(per_brick, place, 0)
        return carry

    repeat(n_span, brick, 0)


def cross_kernel(sizes, direct, room_post, plen_post, jets, cross_a, cross_b):
    ca, cs, blocks, n_span, per_brick = sizes
    rows = blocks * cs
    low = lax.axis_index("span") % 2 == 0
    group = lax.broadcasted_iota(jnp.int32, (rows, LANES), 0) % cs
    for k in range(5):
        sides, near = [], []
        for q, edge in ((Y_UP[k], cs - 1), (Y_DOWN[k], 0)):
            cx, cy, cz = VELOCITIES[q]
            packed = None
            for x in range(max(cx, 0), ca + min(cx, 0)):
                ready = turned_to(raised(room_post[q, x - cx], cz, cs), edge, x)
                packed = ready if packed is None else jnp.where(group == x, ready, packed)
            sides.append(packed)
            near.append(shifted(raised(plen_post[q], cz, ca * cs), cx * cs - edge))
        cross_a[k * rows : (k + 1) * rows] = jnp.where(low, sides[0], sides[1])
        cross_b[k * rows : (k + 1) * rows] = jnp.where(low, sides[1], sides[0])
        first, second = jnp.where(low, near[0], near[1]), jnp.where(low, near[1], near[0])
        for x in range(ca):
            to = 5 * rows + k * ca + x
            cross_a[to : to + 1] = first[x * cs : x * cs + 1]
            cross_b[to : to + 1] = second[x * cs : x * cs + 1]
    if direct:
        for s in range(CAP):
            for k in range(5):
                to = 5 * (rows + ca) + s * 5 + k
                cross_a[to : to + 1] = jets[CAP + s, :, k * LANES : (k + 1) * LANES]


def corners(cs, up):
    return [q for q in (Y_UP if up else Y_DOWN) if VELOCITIES[q][0]], cs - 1 if up else 0


def pack_kernel(sizes, got_a, got_b, part_a, part_b, cross_a, cross_b):
    ca, cs, blocks, n_span, per_brick = sizes
    rows = blocks * cs
    even = lax.axis_index("aisle") % 2 == 0
    low = lax.axis_index("span") % 2 == 0
    group = lax.broadcasted_iota(jnp.int32, (rows, LANES), 0) % cs
    cross_a[...] = part_a[...]
    cross_b[...] = part_b[...]

    def came(q, low, high):
        if VELOCITIES[q][0] == 1:
            return jnp.where(even, got_b[low:high], got_a[low:high])
        return jnp.where(even, got_a[low:high], got_b[low:high])

    def complete(cross, up):
        two, edge = corners(cs, up)
        for q in two:
            slot = (X_UP if VELOCITIES[q][0] == 1 else X_DOWN).index(q)
            x = 0 if VELOCITIES[q][0] == 1 else ca - 1
            k = (Y_UP if up else Y_DOWN).index(q)
            column = turned_to(came(q, slot * rows, (slot + 1) * rows), edge, x)
            cross[k * rows : (k + 1) * rows] = jnp.where(group == x, column, cross[k * rows : (k + 1) * rows])
            at, to = 5 * rows + slot * cs + edge, 5 * rows + k * ca + x
            cross[to : to + 1] = came(q, at, at + 1)

    @pl.when(low)
    def _():
        complete(cross_a, True)
        complete(cross_b, False)

    @pl.when(jnp.logical_not(low))
    def _():
        complete(cross_a, False)
        complete(cross_b, True)


def aisle_kernel(sizes, direct, room_in, plen_in, got_a, got_b, jets, places, room, plen, inflow):
    ca, cs, blocks, n_span, per_brick = sizes
    rows = blocks * cs
    even = lax.axis_index("aisle") % 2 == 0
    for k in range(5):
        for q, x, first, second in ((X_UP[k], 0, got_b, got_a), (X_DOWN[k], ca - 1, got_a, got_b)):
            cy = VELOCITIES[q][1]
            low, high = k * rows, (k + 1) * rows
            room[q, x] = crossed(jnp.where(even, first[low:high], second[low:high]), cy, cs)
            low = 5 * rows + k * cs
            value = jnp.where(even, first[low : low + cs], second[low : low + cs])
            at = x * cs
            if cy == 1:
                plen[q, at : at + 1] = value[0:1]
                plen[q, at + 1 : at + cs] = value[: cs - 1]
            elif cy == -1:
                plen[q, at + cs - 1 : at + cs] = value[cs - 1 : cs]
                plen[q, at : at + cs - 1] = value[1:cs]
            else:
                plen[q, at : at + cs] = value
    here = lax.axis_index("span")

    def put(sums):
        for k in range(5):
            inflow[k] = sums[k]

    def reader(source, b):
        return lambda s, k: source[b * CAP + s, :, k * LANES : (k + 1) * LANES]

    if direct:
        put(jet_sums(lambda k: jnp.zeros((ca * cs, LANES), F32), places,
                     [(here, reader(jets, 0))]))
    else:
        inflow[...] = jnp.zeros_like(inflow)

        def add_brick(b, carry):
            put(jet_sums(lambda k: inflow[k], places, [(b, reader(jets, b))]))
            return carry

        lax.fori_loop(0, n_span, add_brick, 0)


def finish_kernel(sizes, direct, room_in, plen_in, got_a, got_b, places, inflow, *rest):
    *got_jets, room, plen, room_out, plen_out, sems = rest
    ca, cs, blocks, n_span, per_brick = sizes
    rows = blocks * cs
    here = lax.axis_index("span")
    low = here % 2 == 0
    group = lax.broadcasted_iota(jnp.int32, (rows, LANES), 0) % cs

    def enter(got, up):
        planes, y = (Y_UP, 0) if up else (Y_DOWN, cs - 1)
        for k, q in enumerate(planes):
            came = got[k * rows : (k + 1) * rows]
            for x in range(ca):
                room[q, x] = jnp.where(group == y, turned_to(came, x, y), room[q, x])
                at = 5 * rows + k * ca + x
                plen[q, x * cs + y : x * cs + y + 1] = got[at : at + 1]

    @pl.when(low)
    def _():
        enter(got_a, False)

    @pl.when(jnp.logical_not(low))
    def _():
        enter(got_a, True)

    @pl.when(jnp.logical_and(low, here > 0))
    def _():
        enter(got_b, True)

    @pl.when(jnp.logical_and(jnp.logical_not(low), here < n_span - 1))
    def _():
        enter(got_b, False)

    plen_copy = pltpu.make_async_copy(plen, plen_out, sems.at[0])
    plen_copy.start()
    bricks = []
    if direct:
        start = 5 * (rows + cs)
        bricks = [(here ^ 1, lambda s, k: got_a[start + s * 5 + k : start + s * 5 + k + 1])]
        for apart, got in zip((2, 3), got_jets):
            bricks.append((here ^ apart, lambda s, k, got=got: got[s, :, k * LANES : (k + 1) * LANES]))
    sums = jet_sums(lambda k: inflow[k], places, bricks)
    for k, q in enumerate(UPWARD):
        for x in range(ca):
            room[q, x, 0:cs] = room[q, x, 0:cs] + sums[k][x * cs : (x + 1) * cs]
    room_copy = pltpu.make_async_copy(room, room_out, sems.at[1])
    room_copy.start()
    plen_copy.wait()
    room_copy.wait()


def call(kernel, outs, in_specs, out_specs=None, scratch=(), aliases={}, flops=100_000, moved=1_000_000):
    return pl.pallas_call(
        kernel,
        name=kernel.func.__name__,
        out_shape=outs,
        in_specs=in_specs,
        out_specs=[VMEM] * len(outs) if out_specs is None else out_specs,
        scratch_shapes=list(scratch),
        input_output_aliases=aliases,
        cost_estimate=pl.CostEstimate(flops=flops, bytes_accessed=moved, transcendentals=0),
        compiler_params=pltpu.CompilerParams(vmem_limit_bytes=40 * 2**20),
    )


def swap_aisle(value, odd):
    count = lax.axis_size("aisle")
    pairs = [(i, (i ^ 1 if not odd else i + 1 if i % 2 else i - 1) % count) for i in range(count)]
    return lax.ppermute(value, "aisle", pairs)


def swap_span(value, odd):
    count = lax.axis_size("span")
    pairs = []
    for a in range(lax.axis_size("aisle")):
        for s in range(count):
            t = s ^ 1 if not odd else s + 1 if s % 2 else s - 1
            b, t = (a, t) if 0 <= t < count else (a ^ 1, s)
            pairs.append((a * count + s, b * count + t))
    return lax.ppermute(value, ("aisle", "span"), pairs)


def shards(room_pops, plenum_pops, tile_cell, tile_owner, tile_class):
    n_span = lax.axis_size("span")
    _, ca, cs, hr = room_pops.shape
    hp = plenum_pops.shape[3]
    blocks = hr // LANES
    rows = blocks * cs
    tiles = tile_cell.shape[0]
    sizes = (ca, cs, blocks, n_span, tiles // n_span)
    direct = n_span == 4
    near = lambda shape: pltpu.VMEM(shape, F32)
    far = lambda value: pltpu.with_memory_space_constraint(value, pltpu.HBM)
    room_shape, plen_shape = (19, ca, rows, LANES), (19, ca * cs, LANES)
    halo = 5 * (rows + cs)
    halo = halo + -halo % 8
    room = far(room_pops.reshape(19, ca, cs, blocks, LANES).transpose(0, 1, 3, 2, 4).reshape(room_shape))
    plen = far(plenum_pops.reshape(plen_shape))
    tile_cell, tile_owner, tile_class = far(tile_cell), far(tile_owner.reshape(tiles)), far(tile_class)
    numbers = pltpu.SMEM((tiles,), jnp.int32)

    jet_shapes = [(count * CAP, 1, 5 * hp) for count in ((2, 1, 1) if direct else (n_span,))]
    room_post, plen_post, swap_a, swap_b, *jets = call(
        functools.partial(collide_kernel, sizes, direct),
        [near(room_shape), near(plen_shape), near((halo, LANES)), near((halo + 8, LANES))]
        + [near(shape) for shape in jet_shapes],
        [HBM] * 5,
        scratch=[near((ca * cs, 1, 5 * hp)), near((n_span * CAP, 1, 5 * hp)), near(room_shape), near(plen_shape),
                 numbers, numbers, numbers, pltpu.SemaphoreType.DMA((5,))],
    )(room, plen, tile_cell, tile_owner, tile_class)
    got_b = swap_aisle(swap_b, True)
    got_a = swap_aisle(swap_a, False)
    if direct:
        got_jets = [lax.ppermute(jets[apart - 1], "span", [(i, i ^ apart) for i in range(4)]) for apart in (2, 3)]
    else:
        jets = [lax.all_to_all(jets[0], "span", 0, 0, tiled=True)]
        got_jets = []

    upto8 = lambda count: count + -count % 8
    wide = upto8(5 * (rows + ca) + (5 * CAP if direct else 0))
    cross_shapes = [near((wide, LANES)), near((wide + 8, LANES))]
    part_a, part_b = call(
        functools.partial(cross_kernel, sizes, direct),
        cross_shapes,
        [VMEM] * 3,
    )(room_post, plen_post, jets[0])
    cross_a, cross_b = call(
        functools.partial(pack_kernel, sizes),
        cross_shapes,
        [VMEM] * 4,
    )(got_a, got_b, part_a, part_b)
    in_a = swap_span(cross_a, False)
    in_b = swap_span(cross_b, True)

    room_part, plen_part, places = call(
        functools.partial(local_kernel, sizes),
        [near(room_shape), near(plen_shape), near((n_span * CAP + 1, ca * cs, LANES))],
        [VMEM, VMEM, VMEM, HBM, HBM],
        scratch=[numbers, numbers, pltpu.SemaphoreType.DMA((2,))],
        flops=10**9,
    )(room_post, plen_post, cross_a, tile_cell, tile_owner)
    room_part, plen_part, inflow = call(
        functools.partial(aisle_kernel, sizes, direct),
        [near(room_shape), near(plen_shape), near((5, ca * cs, LANES))],
        [VMEM] * 6,
        aliases={0: 0, 1: 1},
    )(room_part, plen_part, got_a, got_b, jets[0], places)

    _, _, room_next, plenum_next = call(
        functools.partial(finish_kernel, sizes, direct),
        [near(room_shape), near(plen_shape), jax.ShapeDtypeStruct(room_shape, F32),
         jax.ShapeDtypeStruct(plen_shape, F32)],
        [VMEM] * (6 + len(got_jets)),
        out_specs=[VMEM, VMEM, HBM, HBM],
        scratch=[pltpu.SemaphoreType.DMA((2,))],
        aliases={0: 0, 1: 1},
    )(room_part, plen_part, in_a, in_b, places, inflow, *got_jets)
    room_next = room_next.reshape(19, ca, blocks, cs, LANES).transpose(0, 1, 3, 2, 4).reshape(room_pops.shape)
    return room_next, plenum_next.reshape(plenum_pops.shape)


def solution(mesh):
    return jax.shard_map(
        shards,
        mesh=mesh,
        in_specs=(
            P(None, "aisle", "span", None),
            P(None, "aisle", "span", None),
            P("aisle"),
            P("aisle", None),
            P("aisle"),
        ),
        out_specs=(P(None, "aisle", "span", None), P(None, "aisle", "span", None)),
        check_vma=False,
    )
```

```python
import functools

import jax
import jax.numpy as jnp
from jax import lax
from jax.experimental import pallas as pl
from jax.experimental.pallas import tpu as pltpu
from jax.sharding import PartitionSpec as P

VELOCITIES = [
    (0, 0, 0),
    (1, 0, 0),
    (-1, 0, 0),
    (0, 1, 0),
    (0, -1, 0),
    (0, 0, 1),
    (0, 0, -1),
    (1, 1, 0),
    (-1, -1, 0),
    (1, -1, 0),
    (-1, 1, 0),
    (1, 0, 1),
    (-1, 0, -1),
    (1, 0, -1),
    (-1, 0, 1),
    (0, 1, 1),
    (0, -1, -1),
    (0, 1, -1),
    (0, -1, 1),
]
UPWARD = [5, 11, 14, 15, 18]
OMEGA = 1.25
CAP = 4
X_UP = [q for q in range(19) if VELOCITIES[q][0] == 1]
X_DOWN = [q for q in range(19) if VELOCITIES[q][0] == -1]
Y_UP = [q for q in range(19) if VELOCITIES[q][1] == 1]
Y_DOWN = [q for q in range(19) if VELOCITIES[q][1] == -1]
F32 = jnp.float32
LANES = 128
VMEM = pl.BlockSpec(memory_space=pltpu.VMEM)
HBM = pl.BlockSpec(memory_space=pltpu.HBM)


def collide(g):
    total = lambda i: g[i] + g[i + 1]
    apart = lambda i: g[i] - g[i + 1]
    dx, dy, dz = apart(1), apart(3), apart(5)
    d7, d9, d11, d13, d15, d17 = (apart(i) for i in (7, 9, 11, 13, 15, 17))
    edges = (total(7) + total(9)) + (total(11) + total(13)) + (total(15) + total(17))
    faces = total(1) + total(3) + total(5)
    rho = g[0] * (1.0 / 3.0) + faces * (1.0 / 18.0) + edges * (1.0 / 36.0)
    mx = dx * (1.0 / 18.0) + ((d7 + d9) + (d11 + d13)) * (1.0 / 36.0)
    my = dy * (1.0 / 18.0) + ((d7 - d9) + (d15 + d17)) * (1.0 / 36.0)
    mz = dz * (1.0 / 18.0) + ((d11 - d13) + (d15 - d17)) * (1.0 / 36.0)
    inv = 1.0 / rho
    base = OMEGA * rho - (1.5 * OMEGA) * inv * (mx * mx + my * my + mz * mz)
    square = (4.5 * OMEGA) * inv
    out = [None] * 19
    out[0] = base + (1.0 - OMEGA) * g[0]
    along = {1: mx, 3: my, 5: mz, 7: mx + my, 9: mx - my, 11: mx + mz, 13: mx - mz, 15: my + mz, 17: my - mz}
    for i, c in along.items():
        even = base + square * c * c
        odd = (3.0 * OMEGA) * c
        out[i] = (even + odd) + (1.0 - OMEGA) * g[i]
        out[i + 1] = (even - odd) + (1.0 - OMEGA) * g[i + 1]
    return out


def raised(value, cz, rows):
    if cz == 0:
        return value
    lane = lax.broadcasted_iota(jnp.int32, value.shape, 1)
    row = lax.broadcasted_iota(jnp.int32, value.shape, 0)
    total = value.shape[0]
    shift, edge = (1, 0) if cz == 1 else (LANES - 1, LANES - 1)
    turned = pltpu.roll(value, shift, 1)
    if rows == total:
        return jnp.where(lane == edge, value, turned)
    carried = pltpu.roll(turned, rows if cz == 1 else total - rows, 0)
    clamped = row < rows if cz == 1 else row >= total - rows
    return jnp.where(lane == edge, jnp.where(clamped, value, carried), turned)


def crossed(value, cy, cs):
    if cy == 0:
        return value
    row = lax.broadcasted_iota(jnp.int32, value.shape, 0) % cs
    turned = pltpu.roll(value, 1 if cy == 1 else value.shape[0] - 1, 0)
    return jnp.where(row == (0 if cy == 1 else cs - 1), value, turned)


def shifted(value, by):
    return pltpu.roll(value, by % value.shape[0], 0) if by else value


def turned_to(value, source, dest):
    return shifted(value, dest - source)


def repeat(count, body, start):
    if count > 8:
        return lax.fori_loop(0, count, body, start)
    for i in range(count):
        start = body(i, start)
    return start


def collide_kernel(sizes, direct, room_in, plen_in, cell_in, owner_in, class_in, room_post, plen_post, swap_a, swap_b,
                   *rest):
    ca, cs, blocks, n_span, per_brick = sizes
    rows = blocks * cs
    jets = rest[:-8]
    columns, dealt, room_buf, plen_buf, cells, owners, classes, sems = rest[-8:]
    copies = [pltpu.make_async_copy(src, dst, sems.at[i]) for i, (src, dst) in enumerate(
        ((plen_in, plen_buf), (cell_in, cells), (owner_in, owners), (class_in, classes)))]
    order = [0, ca - 1] + list(range(1, ca - 1))
    planes = [pltpu.make_async_copy(room_in.at[:, x], room_buf.at[:, x], sems.at[4 + x]) for x in order]
    for copy in copies[:1] + planes + copies[1:]:
        copy.start()
    dealt[...] = jnp.zeros_like(dealt)
    copies[0].wait()
    for r in range(0, ca * cs, 8):
        post = collide([plen_buf[q, r : r + 8] for q in range(19)])
        for q in range(19):
            plen_post[q, r : r + 8] = post[q]
        for k, q in enumerate(UPWARD):
            for y in range(8):
                columns[r + y, :, k * LANES : (k + 1) * LANES] = post[q][y : y + 1]
    for copy in copies[1:4]:
        copy.wait()
    here = lax.axis_index("span")
    first = here * per_brick

    def send_jet(i, carry):
        t = first + i
        owner = owners[t]
        share = 0.15 * (classes[t].astype(F32) + 1.0)
        same = lambda j, n: n + (owners[first + j] == owner).astype(jnp.int32)
        slot = repeat(i, same, 0) if direct else lax.fori_loop(0, i, same, 0)
        to = (owner ^ here if direct else owner) * CAP + slot
        dealt[to] = share * columns[cells[t]]
        return carry

    if direct:
        for i in range(per_brick):
            send_jet(i, 0)
    else:
        lax.fori_loop(0, per_brick, send_jet, 0)
    start = 0
    for jet in jets:
        jet[...] = dealt[start : start + jet.shape[0]]
        start = start + jet.shape[0]

    def plane(i):
        planes[i].wait()
        x = order[i]
        for r in range(0, rows, 8):
            post = collide([room_buf[q, x, r : r + 8] for q in range(19)])
            for q in range(19):
                room_post[q, x, r : r + 8] = post[q]

    plane(0)
    plane(1)
    even = lax.axis_index("aisle") % 2 == 0
    for k in range(5):
        up, down = X_UP[k], X_DOWN[k]
        rising = raised(room_post[up, ca - 1], VELOCITIES[up][2], cs)
        falling = raised(room_post[down, 0], VELOCITIES[down][2], cs)
        swap_a[k * rows : (k + 1) * rows] = jnp.where(even, rising, falling)
        swap_b[k * rows : (k + 1) * rows] = jnp.where(even, falling, rising)
        rising = raised(plen_post[up, (ca - 1) * cs : ca * cs], VELOCITIES[up][2], cs)
        falling = raised(plen_post[down, 0:cs], VELOCITIES[down][2], cs)
        low = 5 * rows + k * cs
        swap_a[low : low + cs] = jnp.where(even, rising, falling)
        swap_b[low : low + cs] = jnp.where(even, falling, rising)
    for i in range(2, ca):
        plane(i)


def jet_sums(start, places, bricks):
    sums = [start(k) for k in range(5)]
    for b, jet in bricks:
        for s in range(CAP):
            marks = places[b * CAP + s]
            sums = [total + marks * jet(s, k) for k, total in enumerate(sums)]
    return sums


def local_kernel(sizes, room_post, plen_post, crossing, cell_in, owner_in, room_part, plen_part, places, cells, owners,
                 sems):
    del crossing
    ca, cs, blocks, n_span, per_brick = sizes
    rows = blocks * cs
    copies = [pltpu.make_async_copy(src, dst, sems.at[i]) for i, (src, dst) in enumerate(
        ((cell_in, cells), (owner_in, owners)))]
    for copy in copies:
        copy.start()
    for q in range(19):
        cx, cy, cz = VELOCITIES[q]
        for x in range(ca):
            if 0 <= x - cx < ca:
                room_part[q, x] = crossed(raised(room_post[q, x - cx], cz, cs), cy, cs)
        plen_part[q] = crossed(shifted(raised(plen_post[q], cz, ca * cs), cx * cs), cy, cs)
    places[0 : n_span * CAP] = jnp.zeros((n_span * CAP, ca * cs, LANES), F32)
    here = lax.axis_index("span")
    row = lax.broadcasted_iota(jnp.int32, (ca * cs, LANES), 0)
    for copy in copies:
        copy.wait()

    def brick(b, carry):
        def place(i, slot):
            t = b * per_brick + i
            mine = owners[t] == here
            places[jnp.where(mine, b * CAP + slot, n_span * CAP)] = (row == cells[t]).astype(F32)
            return slot + mine.astype(jnp.int32)

        repeat(per_brick, place, 0)
        return carry

    repeat(n_span, brick, 0)


def cross_kernel(sizes, direct, room_post, plen_post, jets, cross_a, cross_b):
    ca, cs, blocks, n_span, per_brick = sizes
    rows = blocks * cs
    low = lax.axis_index("span") % 2 == 0
    group = lax.broadcasted_iota(jnp.int32, (rows, LANES), 0) % cs
    for k in range(5):
        sides, near = [], []
        for q, edge in ((Y_UP[k], cs - 1), (Y_DOWN[k], 0)):
            cx, cy, cz = VELOCITIES[q]
            packed = None
            for x in range(max(cx, 0), ca + min(cx, 0)):
                ready = turned_to(raised(room_post[q, x - cx], cz, cs), edge, x)
                packed = ready if packed is None else jnp.where(group == x, ready, packed)
            sides.append(packed)
            near.append(shifted(raised(plen_post[q], cz, ca * cs), cx * cs - edge))
        cross_a[k * rows : (k + 1) * rows] = jnp.where(low, sides[0], sides[1])
        cross_b[k * rows : (k + 1) * rows] = jnp.where(low, sides[1], sides[0])
        first, second = jnp.where(low, near[0], near[1]), jnp.where(low, near[1], near[0])
        for x in range(ca):
            to = 5 * rows + k * ca + x
            cross_a[to : to + 1] = first[x * cs : x * cs + 1]
            cross_b[to : to + 1] = second[x * cs : x * cs + 1]
    if direct:
        for s in range(CAP):
            for k in range(5):
                to = 5 * (rows + ca) + s * 5 + k
                cross_a[to : to + 1] = jets[CAP + s, :, k * LANES : (k + 1) * LANES]


def corners(cs, up):
    return [q for q in (Y_UP if up else Y_DOWN) if VELOCITIES[q][0]], cs - 1 if up else 0


def pack_kernel(sizes, got_a, got_b, part_a, part_b, cross_a, cross_b):
    ca, cs, blocks, n_span, per_brick = sizes
    rows = blocks * cs
    even = lax.axis_index("aisle") % 2 == 0
    low = lax.axis_index("span") % 2 == 0
    group = lax.broadcasted_iota(jnp.int32, (rows, LANES), 0) % cs
    cross_a[...] = part_a[...]
    cross_b[...] = part_b[...]

    def came(q, low, high):
        if VELOCITIES[q][0] == 1:
            return jnp.where(even, got_b[low:high], got_a[low:high])
        return jnp.where(even, got_a[low:high], got_b[low:high])

    def complete(cross, up):
        two, edge = corners(cs, up)
        for q in two:
            slot = (X_UP if VELOCITIES[q][0] == 1 else X_DOWN).index(q)
            x = 0 if VELOCITIES[q][0] == 1 else ca - 1
            k = (Y_UP if up else Y_DOWN).index(q)
            column = turned_to(came(q, slot * rows, (slot + 1) * rows), edge, x)
            cross[k * rows : (k + 1) * rows] = jnp.where(group == x, column, cross[k * rows : (k + 1) * rows])
            at, to = 5 * rows + slot * cs + edge, 5 * rows + k * ca + x
            cross[to : to + 1] = came(q, at, at + 1)

    @pl.when(low)
    def _():
        complete(cross_a, True)
        complete(cross_b, False)

    @pl.when(jnp.logical_not(low))
    def _():
        complete(cross_a, False)
        complete(cross_b, True)


def aisle_kernel(sizes, direct, room_in, plen_in, got_a, got_b, jets, places, room, plen, inflow):
    ca, cs, blocks, n_span, per_brick = sizes
    rows = blocks * cs
    even = lax.axis_index("aisle") % 2 == 0
    for k in range(5):
        for q, x, first, second in ((X_UP[k], 0, got_b, got_a), (X_DOWN[k], ca - 1, got_a, got_b)):
            cy = VELOCITIES[q][1]
            low, high = k * rows, (k + 1) * rows
            room[q, x] = crossed(jnp.where(even, first[low:high], second[low:high]), cy, cs)
            low = 5 * rows + k * cs
            value = jnp.where(even, first[low : low + cs], second[low : low + cs])
            at = x * cs
            if cy == 1:
                plen[q, at : at + 1] = value[0:1]
                plen[q, at + 1 : at + cs] = value[: cs - 1]
            elif cy == -1:
                plen[q, at + cs - 1 : at + cs] = value[cs - 1 : cs]
                plen[q, at : at + cs - 1] = value[1:cs]
            else:
                plen[q, at : at + cs] = value
    here = lax.axis_index("span")

    def put(sums):
        for k in range(5):
            inflow[k] = sums[k]

    def reader(source, b):
        return lambda s, k: source[b * CAP + s, :, k * LANES : (k + 1) * LANES]

    if direct:
        put(jet_sums(lambda k: jnp.zeros((ca * cs, LANES), F32), places,
                     [(here, reader(jets, 0))]))
    else:
        inflow[...] = jnp.zeros_like(inflow)

        def add_brick(b, carry):
            put(jet_sums(lambda k: inflow[k], places, [(b, reader(jets, b))]))
            return carry

        lax.fori_loop(0, n_span, add_brick, 0)


def finish_kernel(sizes, direct, room_in, plen_in, got_a, got_b, places, inflow, *rest):
    *got_jets, room, plen, room_out, plen_out, sems = rest
    ca, cs, blocks, n_span, per_brick = sizes
    rows = blocks * cs
    here = lax.axis_index("span")
    low = here % 2 == 0
    group = lax.broadcasted_iota(jnp.int32, (rows, LANES), 0) % cs

    def enter(got, up):
        planes, y = (Y_UP, 0) if up else (Y_DOWN, cs - 1)
        for k, q in enumerate(planes):
            came = got[k * rows : (k + 1) * rows]
            for x in range(ca):
                room[q, x] = jnp.where(group == y, turned_to(came, x, y), room[q, x])
                at = 5 * rows + k * ca + x
                plen[q, x * cs + y : x * cs + y + 1] = got[at : at + 1]

    @pl.when(low)
    def _():
        enter(got_a, False)

    @pl.when(jnp.logical_not(low))
    def _():
        enter(got_a, True)

    @pl.when(jnp.logical_and(low, here > 0))
    def _():
        enter(got_b, True)

    @pl.when(jnp.logical_and(jnp.logical_not(low), here < n_span - 1))
    def _():
        enter(got_b, False)

    plen_copy = pltpu.make_async_copy(plen, plen_out, sems.at[0])
    plen_copy.start()
    bricks = []
    if direct:
        start = 5 * (rows + cs)
        bricks = [(here ^ 1, lambda s, k: got_a[start + s * 5 + k : start + s * 5 + k + 1])]
        for apart, got in zip((2, 3), got_jets):
            bricks.append((here ^ apart, lambda s, k, got=got: got[s, :, k * LANES : (k + 1) * LANES]))
    sums = jet_sums(lambda k: inflow[k], places, bricks)
    for k, q in enumerate(UPWARD):
        for x in range(ca):
            room[q, x, 0:cs] = room[q, x, 0:cs] + sums[k][x * cs : (x + 1) * cs]
    room_copy = pltpu.make_async_copy(room, room_out, sems.at[1])
    room_copy.start()
    plen_copy.wait()
    room_copy.wait()


def call(kernel, outs, in_specs, out_specs=None, scratch=(), aliases={}, flops=100_000, moved=1_000_000):
    return pl.pallas_call(
        kernel,
        name=kernel.func.__name__,
        out_shape=outs,
        in_specs=in_specs,
        out_specs=[VMEM] * len(outs) if out_specs is None else out_specs,
        scratch_shapes=list(scratch),
        input_output_aliases=aliases,
        cost_estimate=pl.CostEstimate(flops=flops, bytes_accessed=moved, transcendentals=0),
        compiler_params=pltpu.CompilerParams(vmem_limit_bytes=40 * 2**20),
    )


def swap_aisle(value, odd):
    count = lax.axis_size("aisle")
    pairs = [(i, (i ^ 1 if not odd else i + 1 if i % 2 else i - 1) % count) for i in range(count)]
    return lax.ppermute(value, "aisle", pairs)


def swap_span(value, odd):
    count = lax.axis_size("span")
    pairs = []
    for a in range(lax.axis_size("aisle")):
        for s in range(count):
            t = s ^ 1 if not odd else s + 1 if s % 2 else s - 1
            b, t = (a, t) if 0 <= t < count else (a ^ 1, s)
            pairs.append((a * count + s, b * count + t))
    return lax.ppermute(value, ("aisle", "span"), pairs)


def shards(room_pops, plenum_pops, tile_cell, tile_owner, tile_class):
    n_span = lax.axis_size("span")
    _, ca, cs, hr = room_pops.shape
    hp = plenum_pops.shape[3]
    blocks = hr // LANES
    rows = blocks * cs
    tiles = tile_cell.shape[0]
    sizes = (ca, cs, blocks, n_span, tiles // n_span)
    direct = n_span == 4
    near = lambda shape: pltpu.VMEM(shape, F32)
    far = lambda value: pltpu.with_memory_space_constraint(value, pltpu.HBM)
    room_shape, plen_shape = (19, ca, rows, LANES), (19, ca * cs, LANES)
    halo = 5 * (rows + cs)
    halo = halo + -halo % 8
    room = far(room_pops.reshape(19, ca, cs, blocks, LANES).transpose(0, 1, 3, 2, 4).reshape(room_shape))
    plen = far(plenum_pops.reshape(plen_shape))
    tile_cell, tile_owner, tile_class = far(tile_cell), far(tile_owner.reshape(tiles)), far(tile_class)
    numbers = pltpu.SMEM((tiles,), jnp.int32)

    jet_shapes = [(count * CAP, 1, 5 * hp) for count in ((2, 1, 1) if direct else (n_span,))]
    room_post, plen_post, swap_a, swap_b, *jets = call(
        functools.partial(collide_kernel, sizes, direct),
        [near(room_shape), near(plen_shape), near((halo, LANES)), near((halo + 8, LANES))]
        + [near(shape) for shape in jet_shapes],
        [HBM] * 5,
        scratch=[near((ca * cs, 1, 5 * hp)), near((n_span * CAP, 1, 5 * hp)), near(room_shape), near(plen_shape),
                 numbers, numbers, numbers, pltpu.SemaphoreType.DMA((4 + ca,))],
    )(room, plen, tile_cell, tile_owner, tile_class)
    got_b = swap_aisle(swap_b, True)
    got_a = swap_aisle(swap_a, False)
    if direct:
        got_jets = [lax.ppermute(jets[apart - 1], "span", [(i, i ^ apart) for i in range(4)]) for apart in (2, 3)]
    else:
        jets = [lax.all_to_all(jets[0], "span", 0, 0, tiled=True)]
        got_jets = []

    upto8 = lambda count: count + -count % 8
    wide = upto8(5 * (rows + ca) + (5 * CAP if direct else 0))
    cross_shapes = [near((wide, LANES)), near((wide + 8, LANES))]
    part_a, part_b = call(
        functools.partial(cross_kernel, sizes, direct),
        cross_shapes,
        [VMEM] * 3,
    )(room_post, plen_post, jets[0])
    cross_a, cross_b = call(
        functools.partial(pack_kernel, sizes),
        cross_shapes,
        [VMEM] * 4,
    )(got_a, got_b, part_a, part_b)
    in_a = swap_span(cross_a, False)
    in_b = swap_span(cross_b, True)

    room_part, plen_part, places = call(
        functools.partial(local_kernel, sizes),
        [near(room_shape), near(plen_shape), near((n_span * CAP + 1, ca * cs, LANES))],
        [VMEM, VMEM, VMEM, HBM, HBM],
        scratch=[numbers, numbers, pltpu.SemaphoreType.DMA((2,))],
        flops=10**9,
    )(room_post, plen_post, cross_a, tile_cell, tile_owner)
    room_part, plen_part, inflow = call(
        functools.partial(aisle_kernel, sizes, direct),
        [near(room_shape), near(plen_shape), near((5, ca * cs, LANES))],
        [VMEM] * 6,
        aliases={0: 0, 1: 1},
    )(room_part, plen_part, got_a, got_b, jets[0], places)

    _, _, room_next, plenum_next = call(
        functools.partial(finish_kernel, sizes, direct),
        [near(room_shape), near(plen_shape), jax.ShapeDtypeStruct(room_shape, F32),
         jax.ShapeDtypeStruct(plen_shape, F32)],
        [VMEM] * (6 + len(got_jets)),
        out_specs=[VMEM, VMEM, HBM, HBM],
        scratch=[pltpu.SemaphoreType.DMA((2,))],
        aliases={0: 0, 1: 1},
    )(room_part, plen_part, in_a, in_b, places, inflow, *got_jets)
    room_next = room_next.reshape(19, ca, blocks, cs, LANES).transpose(0, 1, 3, 2, 4).reshape(room_pops.shape)
    return room_next, plenum_next.reshape(plenum_pops.shape)


def solution(mesh):
    return jax.shard_map(
        shards,
        mesh=mesh,
        in_specs=(
            P(None, "aisle", "span", None),
            P(None, "aisle", "span", None),
            P("aisle"),
            P("aisle", None),
            P("aisle"),
        ),
        out_specs=(P(None, "aisle", "span", None), P(None, "aisle", "span", None)),
        check_vma=False,
    )
```

```python
import functools

import jax
import jax.numpy as jnp
from jax import lax
from jax.experimental import pallas as pl
from jax.experimental.pallas import tpu as pltpu
from jax.sharding import PartitionSpec as P

VELOCITIES = [
    (0, 0, 0),
    (1, 0, 0),
    (-1, 0, 0),
    (0, 1, 0),
    (0, -1, 0),
    (0, 0, 1),
    (0, 0, -1),
    (1, 1, 0),
    (-1, -1, 0),
    (1, -1, 0),
    (-1, 1, 0),
    (1, 0, 1),
    (-1, 0, -1),
    (1, 0, -1),
    (-1, 0, 1),
    (0, 1, 1),
    (0, -1, -1),
    (0, 1, -1),
    (0, -1, 1),
]
UPWARD = [5, 11, 14, 15, 18]
OMEGA = 1.25
CAP = 4
X_UP = [q for q in range(19) if VELOCITIES[q][0] == 1]
X_DOWN = [q for q in range(19) if VELOCITIES[q][0] == -1]
Y_UP = [q for q in range(19) if VELOCITIES[q][1] == 1]
Y_DOWN = [q for q in range(19) if VELOCITIES[q][1] == -1]
F32 = jnp.float32
LANES = 128
VMEM = pl.BlockSpec(memory_space=pltpu.VMEM)
HBM = pl.BlockSpec(memory_space=pltpu.HBM)


def collide(g):
    total = lambda i: g[i] + g[i + 1]
    apart = lambda i: g[i] - g[i + 1]
    dx, dy, dz = apart(1), apart(3), apart(5)
    d7, d9, d11, d13, d15, d17 = (apart(i) for i in (7, 9, 11, 13, 15, 17))
    edges = (total(7) + total(9)) + (total(11) + total(13)) + (total(15) + total(17))
    faces = total(1) + total(3) + total(5)
    rho = g[0] * (1.0 / 3.0) + faces * (1.0 / 18.0) + edges * (1.0 / 36.0)
    mx = dx * (1.0 / 18.0) + ((d7 + d9) + (d11 + d13)) * (1.0 / 36.0)
    my = dy * (1.0 / 18.0) + ((d7 - d9) + (d15 + d17)) * (1.0 / 36.0)
    mz = dz * (1.0 / 18.0) + ((d11 - d13) + (d15 - d17)) * (1.0 / 36.0)
    inv = 1.0 / rho
    base = OMEGA * rho - (1.5 * OMEGA) * inv * (mx * mx + my * my + mz * mz)
    square = (4.5 * OMEGA) * inv
    out = [None] * 19
    out[0] = base + (1.0 - OMEGA) * g[0]
    along = {1: mx, 3: my, 5: mz, 7: mx + my, 9: mx - my, 11: mx + mz, 13: mx - mz, 15: my + mz, 17: my - mz}
    for i, c in along.items():
        even = base + square * c * c
        odd = (3.0 * OMEGA) * c
        out[i] = (even + odd) + (1.0 - OMEGA) * g[i]
        out[i + 1] = (even - odd) + (1.0 - OMEGA) * g[i + 1]
    return out


def raised(value, cz, rows):
    if cz == 0:
        return value
    lane = lax.broadcasted_iota(jnp.int32, value.shape, 1)
    row = lax.broadcasted_iota(jnp.int32, value.shape, 0)
    total = value.shape[0]
    shift, edge = (1, 0) if cz == 1 else (LANES - 1, LANES - 1)
    turned = pltpu.roll(value, shift, 1)
    if rows == total:
        return jnp.where(lane == edge, value, turned)
    carried = pltpu.roll(turned, rows if cz == 1 else total - rows, 0)
    clamped = row < rows if cz == 1 else row >= total - rows
    return jnp.where(lane == edge, jnp.where(clamped, value, carried), turned)


def crossed(value, cy, cs):
    if cy == 0:
        return value
    row = lax.broadcasted_iota(jnp.int32, value.shape, 0) % cs
    turned = pltpu.roll(value, 1 if cy == 1 else value.shape[0] - 1, 0)
    return jnp.where(row == (0 if cy == 1 else cs - 1), value, turned)


def shifted(value, by):
    return pltpu.roll(value, by % value.shape[0], 0) if by else value


def turned_to(value, source, dest):
    return shifted(value, dest - source)


def repeat(count, body, start):
    if count > 8:
        return lax.fori_loop(0, count, body, start)
    for i in range(count):
        start = body(i, start)
    return start


def collide_plane(room, x):
    for r in range(0, room.shape[2], 8):
        post = collide([room[q, x, r : r + 8] for q in range(19)])
        for q in range(19):
            room[q, x, r : r + 8] = post[q]


def collide_kernel(sizes, direct, room_in, plen_in, cell_in, owner_in, class_in, room_post, plen_post, swap_a, swap_b,
                   dealt, columns, plen_buf, cells, owners, classes, sems):
    ca, cs, blocks, n_span, per_brick = sizes
    rows = blocks * cs
    copies = [pltpu.make_async_copy(src, dst, sems.at[i]) for i, (src, dst) in enumerate(
        ((plen_in, plen_buf), (cell_in, cells), (owner_in, owners), (class_in, classes)))]
    order = [0, ca - 1] + list(range(1, ca - 1))
    planes = [pltpu.make_async_copy(room_in.at[:, x], room_post.at[:, x], sems.at[4 + x]) for x in order]
    for copy in copies[:1] + planes + copies[1:]:
        copy.start()
    dealt[...] = jnp.zeros_like(dealt)
    copies[0].wait()
    for r in range(0, ca * cs, 8):
        post = collide([plen_buf[q, r : r + 8] for q in range(19)])
        for q in range(19):
            plen_post[q, r : r + 8] = post[q]
        for k, q in enumerate(UPWARD):
            for y in range(8):
                columns[r + y, :, k * LANES : (k + 1) * LANES] = post[q][y : y + 1]
    for copy in copies[1:4]:
        copy.wait()
    here = lax.axis_index("span")
    first = here * per_brick

    def send_jet(i, carry):
        t = first + i
        owner = owners[t]
        share = 0.15 * (classes[t].astype(F32) + 1.0)
        same = lambda j, n: n + (owners[first + j] == owner).astype(jnp.int32)
        slot = repeat(i, same, 0) if direct else lax.fori_loop(0, i, same, 0)
        to = (owner ^ here if direct else owner) * CAP + slot
        dealt[to] = share * columns[cells[t]]
        return carry

    if direct:
        for i in range(per_brick):
            send_jet(i, 0)
    else:
        lax.fori_loop(0, per_brick, send_jet, 0)
    for i in range(2):
        planes[i].wait()
        collide_plane(room_post, order[i])
    even = lax.axis_index("aisle") % 2 == 0
    for k in range(5):
        up, down = X_UP[k], X_DOWN[k]
        rising = raised(room_post[up, ca - 1], VELOCITIES[up][2], cs)
        falling = raised(room_post[down, 0], VELOCITIES[down][2], cs)
        swap_a[k * rows : (k + 1) * rows] = jnp.where(even, rising, falling)
        swap_b[k * rows : (k + 1) * rows] = jnp.where(even, falling, rising)
        rising = raised(plen_post[up, (ca - 1) * cs : ca * cs], VELOCITIES[up][2], cs)
        falling = raised(plen_post[down, 0:cs], VELOCITIES[down][2], cs)
        low = 5 * rows + k * cs
        swap_a[low : low + cs] = jnp.where(even, rising, falling)
        swap_b[low : low + cs] = jnp.where(even, falling, rising)
    for i in range(2, ca):
        planes[i].wait()


def jet_sums(start, places, bricks):
    sums = [start(k) for k in range(5)]
    for b, jet in bricks:
        for s in range(CAP):
            marks = places[b * CAP + s]
            sums = [total + marks * jet(s, k) for k, total in enumerate(sums)]
    return sums


def local_kernel(sizes, room_post, plen_post, crossing, cell_in, owner_in, room_part, plen_part, places, cells, owners,
                 sems):
    del crossing
    ca, cs, blocks, n_span, per_brick = sizes
    rows = blocks * cs
    copies = [pltpu.make_async_copy(src, dst, sems.at[i]) for i, (src, dst) in enumerate(
        ((cell_in, cells), (owner_in, owners)))]
    for copy in copies:
        copy.start()
    for q in range(19):
        cx, cy, cz = VELOCITIES[q]
        for x in range(ca):
            if 0 <= x - cx < ca:
                room_part[q, x] = crossed(raised(room_post[q, x - cx], cz, cs), cy, cs)
        plen_part[q] = crossed(shifted(raised(plen_post[q], cz, ca * cs), cx * cs), cy, cs)
    places[0 : n_span * CAP] = jnp.zeros((n_span * CAP, ca * cs, LANES), F32)
    here = lax.axis_index("span")
    row = lax.broadcasted_iota(jnp.int32, (ca * cs, LANES), 0)
    for copy in copies:
        copy.wait()

    def brick(b, carry):
        def place(i, slot):
            t = b * per_brick + i
            mine = owners[t] == here
            places[jnp.where(mine, b * CAP + slot, n_span * CAP)] = (row == cells[t]).astype(F32)
            return slot + mine.astype(jnp.int32)

        repeat(per_brick, place, 0)
        return carry

    repeat(n_span, brick, 0)


def inner(sizes, direct, room_post, plen_post, jets, cross_a, cross_b):
    ca, cs, blocks, n_span, per_brick = sizes
    rows = blocks * cs
    low = lax.axis_index("span") % 2 == 0
    group = lax.broadcasted_iota(jnp.int32, (rows, LANES), 0) % cs
    for x in range(1, ca - 1):
        collide_plane(room_post, x)
    for k in range(5):
        sides, near = [], []
        for q, edge in ((Y_UP[k], cs - 1), (Y_DOWN[k], 0)):
            cx, cy, cz = VELOCITIES[q]
            packed = None
            for x in range(max(cx, 0), ca + min(cx, 0)):
                ready = turned_to(raised(room_post[q, x - cx], cz, cs), edge, x)
                packed = ready if packed is None else jnp.where(group == x, ready, packed)
            sides.append(packed)
            near.append(shifted(raised(plen_post[q], cz, ca * cs), cx * cs - edge))
        cross_a[k * rows : (k + 1) * rows] = jnp.where(low, sides[0], sides[1])
        cross_b[k * rows : (k + 1) * rows] = jnp.where(low, sides[1], sides[0])
        first, second = jnp.where(low, near[0], near[1]), jnp.where(low, near[1], near[0])
        for x in range(ca):
            to = 5 * rows + k * ca + x
            cross_a[to : to + 1] = first[x * cs : x * cs + 1]
            cross_b[to : to + 1] = second[x * cs : x * cs + 1]
    if direct:
        for s in range(CAP):
            for k in range(5):
                to = 5 * (rows + ca) + s * 5 + k
                cross_a[to : to + 1] = jets[CAP + s, :, k * LANES : (k + 1) * LANES]


def early_kernel(sizes, direct, room_in, plen_post, dealt, room_post, cross_a, cross_b, *jets):
    start = 2 * CAP
    for jet in jets:
        jet[...] = dealt[start : start + CAP]
        start = start + CAP

    @pl.when(lax.axis_index("span") < sizes[3] // 2)
    def _():
        inner(sizes, direct, room_post, plen_post, dealt, cross_a, cross_b)


def late_kernel(sizes, direct, room_in, plen_post, dealt, a_in, b_in, room_post, cross_a, cross_b):
    @pl.when(lax.axis_index("span") >= sizes[3] // 2)
    def _():
        inner(sizes, direct, room_post, plen_post, dealt, cross_a, cross_b)


def corners(cs, up):
    return [q for q in (Y_UP if up else Y_DOWN) if VELOCITIES[q][0]], cs - 1 if up else 0


def pack_kernel(sizes, got_a, got_b, part_a, part_b, cross_a, cross_b):
    ca, cs, blocks, n_span, per_brick = sizes
    rows = blocks * cs
    even = lax.axis_index("aisle") % 2 == 0
    low = lax.axis_index("span") % 2 == 0
    group = lax.broadcasted_iota(jnp.int32, (rows, LANES), 0) % cs
    cross_a[...] = part_a[...]
    cross_b[...] = part_b[...]

    def came(q, low, high):
        if VELOCITIES[q][0] == 1:
            return jnp.where(even, got_b[low:high], got_a[low:high])
        return jnp.where(even, got_a[low:high], got_b[low:high])

    def complete(cross, up):
        two, edge = corners(cs, up)
        for q in two:
            slot = (X_UP if VELOCITIES[q][0] == 1 else X_DOWN).index(q)
            x = 0 if VELOCITIES[q][0] == 1 else ca - 1
            k = (Y_UP if up else Y_DOWN).index(q)
            column = turned_to(came(q, slot * rows, (slot + 1) * rows), edge, x)
            cross[k * rows : (k + 1) * rows] = jnp.where(group == x, column, cross[k * rows : (k + 1) * rows])
            at, to = 5 * rows + slot * cs + edge, 5 * rows + k * ca + x
            cross[to : to + 1] = came(q, at, at + 1)

    @pl.when(low)
    def _():
        complete(cross_a, True)
        complete(cross_b, False)

    @pl.when(jnp.logical_not(low))
    def _():
        complete(cross_a, False)
        complete(cross_b, True)


def aisle_kernel(sizes, direct, room_in, plen_in, got_a, got_b, jets, places, room, plen, inflow):
    ca, cs, blocks, n_span, per_brick = sizes
    rows = blocks * cs
    even = lax.axis_index("aisle") % 2 == 0
    for k in range(5):
        for q, x, first, second in ((X_UP[k], 0, got_b, got_a), (X_DOWN[k], ca - 1, got_a, got_b)):
            cy = VELOCITIES[q][1]
            low, high = k * rows, (k + 1) * rows
            room[q, x] = crossed(jnp.where(even, first[low:high], second[low:high]), cy, cs)
            low = 5 * rows + k * cs
            value = jnp.where(even, first[low : low + cs], second[low : low + cs])
            at = x * cs
            if cy == 1:
                plen[q, at : at + 1] = value[0:1]
                plen[q, at + 1 : at + cs] = value[: cs - 1]
            elif cy == -1:
                plen[q, at + cs - 1 : at + cs] = value[cs - 1 : cs]
                plen[q, at : at + cs - 1] = value[1:cs]
            else:
                plen[q, at : at + cs] = value
    here = lax.axis_index("span")

    def put(sums):
        for k in range(5):
            inflow[k] = sums[k]

    def reader(source, b):
        return lambda s, k: source[b * CAP + s, :, k * LANES : (k + 1) * LANES]

    if direct:
        put(jet_sums(lambda k: jnp.zeros((ca * cs, LANES), F32), places,
                     [(here, reader(jets, 0))]))
    else:
        inflow[...] = jnp.zeros_like(inflow)

        def add_brick(b, carry):
            put(jet_sums(lambda k: inflow[k], places, [(b, reader(jets, b))]))
            return carry

        lax.fori_loop(0, n_span, add_brick, 0)


def finish_kernel(sizes, direct, room_in, plen_in, got_a, got_b, places, inflow, *rest):
    *got_jets, room, plen, room_out, plen_out, sems = rest
    ca, cs, blocks, n_span, per_brick = sizes
    rows = blocks * cs
    here = lax.axis_index("span")
    low = here % 2 == 0
    group = lax.broadcasted_iota(jnp.int32, (rows, LANES), 0) % cs

    def enter(got, up):
        planes, y = (Y_UP, 0) if up else (Y_DOWN, cs - 1)
        for k, q in enumerate(planes):
            came = got[k * rows : (k + 1) * rows]
            for x in range(ca):
                room[q, x] = jnp.where(group == y, turned_to(came, x, y), room[q, x])
                at = 5 * rows + k * ca + x
                plen[q, x * cs + y : x * cs + y + 1] = got[at : at + 1]

    @pl.when(low)
    def _():
        enter(got_a, False)

    @pl.when(jnp.logical_not(low))
    def _():
        enter(got_a, True)

    @pl.when(jnp.logical_and(low, here > 0))
    def _():
        enter(got_b, True)

    @pl.when(jnp.logical_and(jnp.logical_not(low), here < n_span - 1))
    def _():
        enter(got_b, False)

    plen_copy = pltpu.make_async_copy(plen, plen_out, sems.at[0])
    plen_copy.start()
    bricks = []
    if direct:
        start = 5 * (rows + cs)
        bricks = [(here ^ 1, lambda s, k: got_a[start + s * 5 + k : start + s * 5 + k + 1])]
        for apart, got in zip((2, 3), got_jets):
            bricks.append((here ^ apart, lambda s, k, got=got: got[s, :, k * LANES : (k + 1) * LANES]))
    sums = jet_sums(lambda k: inflow[k], places, bricks)
    for k, q in enumerate(UPWARD):
        for x in range(ca):
            room[q, x, 0:cs] = room[q, x, 0:cs] + sums[k][x * cs : (x + 1) * cs]
    room_copy = pltpu.make_async_copy(room, room_out, sems.at[1])
    room_copy.start()
    plen_copy.wait()
    room_copy.wait()


def call(kernel, outs, in_specs, out_specs=None, scratch=(), aliases={}, flops=100_000, moved=1_000_000):
    return pl.pallas_call(
        kernel,
        name=kernel.func.__name__,
        out_shape=outs,
        in_specs=in_specs,
        out_specs=[VMEM] * len(outs) if out_specs is None else out_specs,
        scratch_shapes=list(scratch),
        input_output_aliases=aliases,
        cost_estimate=pl.CostEstimate(flops=flops, bytes_accessed=moved, transcendentals=0),
        compiler_params=pltpu.CompilerParams(vmem_limit_bytes=40 * 2**20),
    )


def swap_aisle(value, odd):
    count = lax.axis_size("aisle")
    pairs = [(i, (i ^ 1 if not odd else i + 1 if i % 2 else i - 1) % count) for i in range(count)]
    return lax.ppermute(value, "aisle", pairs)


def swap_span(value, odd):
    count = lax.axis_size("span")
    pairs = []
    for a in range(lax.axis_size("aisle")):
        for s in range(count):
            t = s ^ 1 if not odd else s + 1 if s % 2 else s - 1
            b, t = (a, t) if 0 <= t < count else (a ^ 1, s)
            pairs.append((a * count + s, b * count + t))
    return lax.ppermute(value, ("aisle", "span"), pairs)


def shards(room_pops, plenum_pops, tile_cell, tile_owner, tile_class):
    n_span = lax.axis_size("span")
    _, ca, cs, hr = room_pops.shape
    hp = plenum_pops.shape[3]
    blocks = hr // LANES
    rows = blocks * cs
    tiles = tile_cell.shape[0]
    sizes = (ca, cs, blocks, n_span, tiles // n_span)
    direct = n_span == 4
    near = lambda shape: pltpu.VMEM(shape, F32)
    far = lambda value: pltpu.with_memory_space_constraint(value, pltpu.HBM)
    room_shape, plen_shape = (19, ca, rows, LANES), (19, ca * cs, LANES)
    halo = 5 * (rows + cs)
    halo = halo + -halo % 8
    room = far(room_pops.reshape(19, ca, cs, blocks, LANES).transpose(0, 1, 3, 2, 4).reshape(room_shape))
    plen = far(plenum_pops.reshape(plen_shape))
    tile_cell, tile_owner, tile_class = far(tile_cell), far(tile_owner.reshape(tiles)), far(tile_class)
    numbers = pltpu.SMEM((tiles,), jnp.int32)

    dealt_shape, jet_shape = (n_span * CAP, 1, 5 * hp), (CAP, 1, 5 * hp)
    room_post, plen_post, swap_a, swap_b, dealt = call(
        functools.partial(collide_kernel, sizes, direct),
        [near(room_shape), near(plen_shape), near((halo, LANES)), near((halo + 8, LANES)),
         near(dealt_shape)],
        [HBM] * 5,
        scratch=[near((ca * cs, 1, 5 * hp)), near(plen_shape), numbers, numbers, numbers,
                 pltpu.SemaphoreType.DMA((4 + ca,))],
    )(room, plen, tile_cell, tile_owner, tile_class)
    got_b = swap_aisle(swap_b, True)
    got_a = swap_aisle(swap_a, False)

    upto8 = lambda count: count + -count % 8
    wide = upto8(5 * (rows + ca) + (5 * CAP if direct else 0))
    cross_shapes = [near((wide, LANES)), near((wide + 8, LANES))]
    room_post, part_a, part_b, *jets = call(
        functools.partial(early_kernel, sizes, direct),
        [near(room_shape)] + cross_shapes + [near(jet_shape)] * (2 if direct else 0),
        [VMEM] * 3,
        aliases={0: 0},
    )(room_post, plen_post, dealt)
    if direct:
        own_jets = dealt
        got_jets = [lax.ppermute(jets[apart - 2], "span", [(i, i ^ apart) for i in range(4)]) for apart in (2, 3)]
    else:
        own_jets = lax.all_to_all(dealt, "span", 0, 0, tiled=True)
        got_jets = []
    room_post, part_a, part_b = call(
        functools.partial(late_kernel, sizes, direct),
        [near(room_shape)] + cross_shapes,
        [VMEM] * 5,
        aliases={0: 0, 3: 1, 4: 2},
    )(room_post, plen_post, dealt, part_a, part_b)
    cross_a, cross_b = call(
        functools.partial(pack_kernel, sizes),
        cross_shapes,
        [VMEM] * 4,
    )(got_a, got_b, part_a, part_b)
    in_a = swap_span(cross_a, False)
    in_b = swap_span(cross_b, True)

    room_part, plen_part, places = call(
        functools.partial(local_kernel, sizes),
        [near(room_shape), near(plen_shape), near((n_span * CAP + 1, ca * cs, LANES))],
        [VMEM, VMEM, VMEM, HBM, HBM],
        scratch=[numbers, numbers, pltpu.SemaphoreType.DMA((2,))],
        flops=10**9,
    )(room_post, plen_post, cross_a, tile_cell, tile_owner)
    room_part, plen_part, inflow = call(
        functools.partial(aisle_kernel, sizes, direct),
        [near(room_shape), near(plen_shape), near((5, ca * cs, LANES))],
        [VMEM] * 6,
        aliases={0: 0, 1: 1},
    )(room_part, plen_part, got_a, got_b, own_jets, places)

    _, _, room_next, plenum_next = call(
        functools.partial(finish_kernel, sizes, direct),
        [near(room_shape), near(plen_shape), jax.ShapeDtypeStruct(room_shape, F32),
         jax.ShapeDtypeStruct(plen_shape, F32)],
        [VMEM] * (6 + len(got_jets)),
        out_specs=[VMEM, VMEM, HBM, HBM],
        scratch=[pltpu.SemaphoreType.DMA((2,))],
        aliases={0: 0, 1: 1},
    )(room_part, plen_part, in_a, in_b, places, inflow, *got_jets)
    room_next = room_next.reshape(19, ca, blocks, cs, LANES).transpose(0, 1, 3, 2, 4).reshape(room_pops.shape)
    return room_next, plenum_next.reshape(plenum_pops.shape)


def solution(mesh):
    return jax.shard_map(
        shards,
        mesh=mesh,
        in_specs=(
            P(None, "aisle", "span", None),
            P(None, "aisle", "span", None),
            P("aisle"),
            P("aisle", None),
            P("aisle"),
        ),
        out_specs=(P(None, "aisle", "span", None), P(None, "aisle", "span", None)),
        check_vma=False,
    )
```

```python
import functools

import jax
import jax.numpy as jnp
from jax import lax
from jax.experimental import pallas as pl
from jax.experimental.pallas import tpu as pltpu
from jax.sharding import PartitionSpec as P

VELOCITIES = [
    (0, 0, 0),
    (1, 0, 0),
    (-1, 0, 0),
    (0, 1, 0),
    (0, -1, 0),
    (0, 0, 1),
    (0, 0, -1),
    (1, 1, 0),
    (-1, -1, 0),
    (1, -1, 0),
    (-1, 1, 0),
    (1, 0, 1),
    (-1, 0, -1),
    (1, 0, -1),
    (-1, 0, 1),
    (0, 1, 1),
    (0, -1, -1),
    (0, 1, -1),
    (0, -1, 1),
]
UPWARD = [5, 11, 14, 15, 18]
OMEGA = 1.25
CAP = 4
X_UP = [q for q in range(19) if VELOCITIES[q][0] == 1]
X_DOWN = [q for q in range(19) if VELOCITIES[q][0] == -1]
Y_UP = [q for q in range(19) if VELOCITIES[q][1] == 1]
Y_DOWN = [q for q in range(19) if VELOCITIES[q][1] == -1]
F32 = jnp.float32
LANES = 128
VMEM = pl.BlockSpec(memory_space=pltpu.VMEM)
HBM = pl.BlockSpec(memory_space=pltpu.HBM)


def collide(g):
    total = lambda i: g[i] + g[i + 1]
    apart = lambda i: g[i] - g[i + 1]
    dx, dy, dz = apart(1), apart(3), apart(5)
    d7, d9, d11, d13, d15, d17 = (apart(i) for i in (7, 9, 11, 13, 15, 17))
    edges = (total(7) + total(9)) + (total(11) + total(13)) + (total(15) + total(17))
    faces = total(1) + total(3) + total(5)
    rho = g[0] * (1.0 / 3.0) + faces * (1.0 / 18.0) + edges * (1.0 / 36.0)
    mx = dx * (1.0 / 18.0) + ((d7 + d9) + (d11 + d13)) * (1.0 / 36.0)
    my = dy * (1.0 / 18.0) + ((d7 - d9) + (d15 + d17)) * (1.0 / 36.0)
    mz = dz * (1.0 / 18.0) + ((d11 - d13) + (d15 - d17)) * (1.0 / 36.0)
    inv = 1.0 / rho
    base = OMEGA * rho - (1.5 * OMEGA) * inv * (mx * mx + my * my + mz * mz)
    square = (4.5 * OMEGA) * inv
    out = [None] * 19
    out[0] = base + (1.0 - OMEGA) * g[0]
    along = {1: mx, 3: my, 5: mz, 7: mx + my, 9: mx - my, 11: mx + mz, 13: mx - mz, 15: my + mz, 17: my - mz}
    for i, c in along.items():
        even = base + square * c * c
        odd = (3.0 * OMEGA) * c
        out[i] = (even + odd) + (1.0 - OMEGA) * g[i]
        out[i + 1] = (even - odd) + (1.0 - OMEGA) * g[i + 1]
    return out


def raised(value, cz, rows):
    if cz == 0:
        return value
    lane = lax.broadcasted_iota(jnp.int32, value.shape, 1)
    row = lax.broadcasted_iota(jnp.int32, value.shape, 0)
    total = value.shape[0]
    shift, edge = (1, 0) if cz == 1 else (LANES - 1, LANES - 1)
    turned = pltpu.roll(value, shift, 1)
    if rows == total:
        return jnp.where(lane == edge, value, turned)
    carried = pltpu.roll(turned, rows if cz == 1 else total - rows, 0)
    clamped = row < rows if cz == 1 else row >= total - rows
    return jnp.where(lane == edge, jnp.where(clamped, value, carried), turned)


def crossed(value, cy, cs):
    if cy == 0:
        return value
    row = lax.broadcasted_iota(jnp.int32, value.shape, 0) % cs
    turned = pltpu.roll(value, 1 if cy == 1 else value.shape[0] - 1, 0)
    return jnp.where(row == (0 if cy == 1 else cs - 1), value, turned)


def shifted(value, by):
    return pltpu.roll(value, by % value.shape[0], 0) if by else value


def turned_to(value, source, dest):
    return shifted(value, dest - source)


def repeat(count, body, start):
    if count > 8:
        return lax.fori_loop(0, count, body, start)
    for i in range(count):
        start = body(i, start)
    return start


def collide_plane(room, x):
    for r in range(0, room.shape[2], 8):
        post = collide([room[q, x, r : r + 8] for q in range(19)])
        for q in range(19):
            room[q, x, r : r + 8] = post[q]


def collide_kernel(sizes, direct, room_in, plen_in, cell_in, owner_in, class_in, room_post, plen_post, swap_a, swap_b,
                   dealt, columns, plen_buf, cells, owners, classes, sems):
    ca, cs, blocks, n_span, per_brick = sizes
    rows = blocks * cs
    copies = [pltpu.make_async_copy(src, dst, sems.at[i]) for i, (src, dst) in enumerate(
        ((plen_in, plen_buf), (cell_in, cells), (owner_in, owners), (class_in, classes)))]
    order = [0, ca - 1] + list(range(1, ca - 1))
    planes = [pltpu.make_async_copy(room_in.at[:, x], room_post.at[:, x], sems.at[4 + x]) for x in order]
    for copy in copies[:1] + planes + copies[1:]:
        copy.start()
    dealt[...] = jnp.zeros_like(dealt)
    copies[0].wait()
    for r in range(0, ca * cs, 8):
        post = collide([plen_buf[q, r : r + 8] for q in range(19)])
        for q in range(19):
            plen_post[q, r : r + 8] = post[q]
        for k, q in enumerate(UPWARD):
            for y in range(8):
                columns[r + y, :, k * LANES : (k + 1) * LANES] = post[q][y : y + 1]
    for copy in copies[1:4]:
        copy.wait()
    here = lax.axis_index("span")
    first = here * per_brick

    def send_jet(i, carry):
        t = first + i
        owner = owners[t]
        share = 0.15 * (classes[t].astype(F32) + 1.0)
        same = lambda j, n: n + (owners[first + j] == owner).astype(jnp.int32)
        slot = repeat(i, same, 0) if direct else lax.fori_loop(0, i, same, 0)
        to = (owner ^ here if direct else owner) * CAP + slot
        dealt[to] = share * columns[cells[t]]
        return carry

    if direct:
        for i in range(per_brick):
            send_jet(i, 0)
    else:
        lax.fori_loop(0, per_brick, send_jet, 0)
    for i in range(2):
        planes[i].wait()
        collide_plane(room_post, order[i])
    even = lax.axis_index("aisle") % 2 == 0
    for k in range(5):
        up, down = X_UP[k], X_DOWN[k]
        rising = raised(room_post[up, ca - 1], VELOCITIES[up][2], cs)
        falling = raised(room_post[down, 0], VELOCITIES[down][2], cs)
        swap_a[k * rows : (k + 1) * rows] = jnp.where(even, rising, falling)
        swap_b[k * rows : (k + 1) * rows] = jnp.where(even, falling, rising)
        rising = raised(plen_post[up, (ca - 1) * cs : ca * cs], VELOCITIES[up][2], cs)
        falling = raised(plen_post[down, 0:cs], VELOCITIES[down][2], cs)
        low = 5 * rows + k * cs
        swap_a[low : low + cs] = jnp.where(even, rising, falling)
        swap_b[low : low + cs] = jnp.where(even, falling, rising)
    for i in range(2, ca):
        planes[i].wait()


def jet_sums(start, places, bricks):
    sums = [start(k) for k in range(5)]
    for b, jet in bricks:
        for s in range(CAP):
            marks = places[b * CAP + s]
            sums = [total + marks * jet(s, k) for k, total in enumerate(sums)]
    return sums


def local_kernel(sizes, room_post, plen_post, crossing, cell_in, owner_in, room_part, plen_part, places, cells, owners,
                 sems):
    del crossing
    ca, cs, blocks, n_span, per_brick = sizes
    rows = blocks * cs
    copies = [pltpu.make_async_copy(src, dst, sems.at[i]) for i, (src, dst) in enumerate(
        ((cell_in, cells), (owner_in, owners)))]
    for copy in copies:
        copy.start()
    for q in range(19):
        cx, cy, cz = VELOCITIES[q]
        for x in range(ca):
            if 0 <= x - cx < ca:
                room_part[q, x] = crossed(raised(room_post[q, x - cx], cz, cs), cy, cs)
        plen_part[q] = crossed(shifted(raised(plen_post[q], cz, ca * cs), cx * cs), cy, cs)
    places[0 : n_span * CAP] = jnp.zeros((n_span * CAP, ca * cs, LANES), F32)
    here = lax.axis_index("span")
    row = lax.broadcasted_iota(jnp.int32, (ca * cs, LANES), 0)
    for copy in copies:
        copy.wait()

    def brick(b, carry):
        def place(i, slot):
            t = b * per_brick + i
            mine = owners[t] == here
            places[jnp.where(mine, b * CAP + slot, n_span * CAP)] = (row == cells[t]).astype(F32)
            return slot + mine.astype(jnp.int32)

        repeat(per_brick, place, 0)
        return carry

    repeat(n_span, brick, 0)


def inner(sizes, direct, room_post, plen_post, jets, cross_a, cross_b):
    ca, cs, blocks, n_span, per_brick = sizes
    rows = blocks * cs
    low = lax.axis_index("span") % 2 == 0
    group = lax.broadcasted_iota(jnp.int32, (rows, LANES), 0) % cs
    for x in range(1, ca - 1):
        collide_plane(room_post, x)
    for k in range(5):
        sides, near = [], []
        for q, edge in ((Y_UP[k], cs - 1), (Y_DOWN[k], 0)):
            cx, cy, cz = VELOCITIES[q]
            packed = None
            for x in range(max(cx, 0), ca + min(cx, 0)):
                ready = turned_to(raised(room_post[q, x - cx], cz, cs), edge, x)
                packed = ready if packed is None else jnp.where(group == x, ready, packed)
            sides.append(packed)
            near.append(shifted(raised(plen_post[q], cz, ca * cs), cx * cs - edge))
        cross_a[k * rows : (k + 1) * rows] = jnp.where(low, sides[0], sides[1])
        cross_b[k * rows : (k + 1) * rows] = jnp.where(low, sides[1], sides[0])
        first, second = jnp.where(low, near[0], near[1]), jnp.where(low, near[1], near[0])
        for x in range(ca):
            to = 5 * rows + k * ca + x
            cross_a[to : to + 1] = first[x * cs : x * cs + 1]
            cross_b[to : to + 1] = second[x * cs : x * cs + 1]
    if direct:
        for s in range(CAP):
            for k in range(5):
                to = 5 * (rows + ca) + s * 5 + k
                cross_a[to : to + 1] = jets[CAP + s, :, k * LANES : (k + 1) * LANES]


def early_kernel(sizes, direct, room_in, plen_post, dealt, room_post, cross_a, cross_b, *jets):
    start = 2 * CAP
    for jet in jets:
        jet[...] = dealt[start : start + CAP]
        start = start + CAP

    @pl.when(lax.axis_index("span") == 0)
    def _():
        inner(sizes, direct, room_post, plen_post, dealt, cross_a, cross_b)


def late_kernel(sizes, direct, room_in, plen_post, dealt, a_in, b_in, room_post, cross_a, cross_b):
    @pl.when(lax.axis_index("span") > 0)
    def _():
        inner(sizes, direct, room_post, plen_post, dealt, cross_a, cross_b)


def corners(cs, up):
    return [q for q in (Y_UP if up else Y_DOWN) if VELOCITIES[q][0]], cs - 1 if up else 0


def pack_kernel(sizes, got_a, got_b, part_a, part_b, cross_a, cross_b):
    ca, cs, blocks, n_span, per_brick = sizes
    rows = blocks * cs
    even = lax.axis_index("aisle") % 2 == 0
    low = lax.axis_index("span") % 2 == 0
    group = lax.broadcasted_iota(jnp.int32, (rows, LANES), 0) % cs
    cross_a[...] = part_a[...]
    cross_b[...] = part_b[...]

    def came(q, low, high):
        if VELOCITIES[q][0] == 1:
            return jnp.where(even, got_b[low:high], got_a[low:high])
        return jnp.where(even, got_a[low:high], got_b[low:high])

    def complete(cross, up):
        two, edge = corners(cs, up)
        for q in two:
            slot = (X_UP if VELOCITIES[q][0] == 1 else X_DOWN).index(q)
            x = 0 if VELOCITIES[q][0] == 1 else ca - 1
            k = (Y_UP if up else Y_DOWN).index(q)
            column = turned_to(came(q, slot * rows, (slot + 1) * rows), edge, x)
            cross[k * rows : (k + 1) * rows] = jnp.where(group == x, column, cross[k * rows : (k + 1) * rows])
            at, to = 5 * rows + slot * cs + edge, 5 * rows + k * ca + x
            cross[to : to + 1] = came(q, at, at + 1)

    @pl.when(low)
    def _():
        complete(cross_a, True)
        complete(cross_b, False)

    @pl.when(jnp.logical_not(low))
    def _():
        complete(cross_a, False)
        complete(cross_b, True)


def aisle_kernel(sizes, direct, room_in, plen_in, got_a, got_b, jets, places, room, plen, inflow):
    ca, cs, blocks, n_span, per_brick = sizes
    rows = blocks * cs
    even = lax.axis_index("aisle") % 2 == 0
    for k in range(5):
        for q, x, first, second in ((X_UP[k], 0, got_b, got_a), (X_DOWN[k], ca - 1, got_a, got_b)):
            cy = VELOCITIES[q][1]
            low, high = k * rows, (k + 1) * rows
            room[q, x] = crossed(jnp.where(even, first[low:high], second[low:high]), cy, cs)
            low = 5 * rows + k * cs
            value = jnp.where(even, first[low : low + cs], second[low : low + cs])
            at = x * cs
            if cy == 1:
                plen[q, at : at + 1] = value[0:1]
                plen[q, at + 1 : at + cs] = value[: cs - 1]
            elif cy == -1:
                plen[q, at + cs - 1 : at + cs] = value[cs - 1 : cs]
                plen[q, at : at + cs - 1] = value[1:cs]
            else:
                plen[q, at : at + cs] = value
    here = lax.axis_index("span")

    def put(sums):
        for k in range(5):
            inflow[k] = sums[k]

    def reader(source, b):
        return lambda s, k: source[b * CAP + s, :, k * LANES : (k + 1) * LANES]

    if direct:
        put(jet_sums(lambda k: jnp.zeros((ca * cs, LANES), F32), places,
                     [(here, reader(jets, 0))]))
    else:
        inflow[...] = jnp.zeros_like(inflow)

        def add_brick(b, carry):
            put(jet_sums(lambda k: inflow[k], places, [(b, reader(jets, b))]))
            return carry

        lax.fori_loop(0, n_span, add_brick, 0)


def finish_kernel(sizes, direct, room_in, plen_in, got_a, got_b, places, inflow, *rest):
    *got_jets, room, plen, room_out, plen_out, sems = rest
    ca, cs, blocks, n_span, per_brick = sizes
    rows = blocks * cs
    here = lax.axis_index("span")
    low = here % 2 == 0
    group = lax.broadcasted_iota(jnp.int32, (rows, LANES), 0) % cs

    def enter(got, up):
        planes, y = (Y_UP, 0) if up else (Y_DOWN, cs - 1)
        for k, q in enumerate(planes):
            came = got[k * rows : (k + 1) * rows]
            for x in range(ca):
                room[q, x] = jnp.where(group == y, turned_to(came, x, y), room[q, x])
                at = 5 * rows + k * ca + x
                plen[q, x * cs + y : x * cs + y + 1] = got[at : at + 1]

    @pl.when(low)
    def _():
        enter(got_a, False)

    @pl.when(jnp.logical_not(low))
    def _():
        enter(got_a, True)

    @pl.when(jnp.logical_and(low, here > 0))
    def _():
        enter(got_b, True)

    @pl.when(jnp.logical_and(jnp.logical_not(low), here < n_span - 1))
    def _():
        enter(got_b, False)

    plen_copy = pltpu.make_async_copy(plen, plen_out, sems.at[0])
    plen_copy.start()
    bricks = []
    if direct:
        start = 5 * (rows + cs)
        bricks = [(here ^ 1, lambda s, k: got_a[start + s * 5 + k : start + s * 5 + k + 1])]
        for apart, got in zip((2, 3), got_jets):
            bricks.append((here ^ apart, lambda s, k, got=got: got[s, :, k * LANES : (k + 1) * LANES]))
    sums = jet_sums(lambda k: inflow[k], places, bricks)
    for k, q in enumerate(UPWARD):
        for x in range(ca):
            room[q, x, 0:cs] = room[q, x, 0:cs] + sums[k][x * cs : (x + 1) * cs]
    room_copy = pltpu.make_async_copy(room, room_out, sems.at[1])
    room_copy.start()
    plen_copy.wait()
    room_copy.wait()


def call(kernel, outs, in_specs, out_specs=None, scratch=(), aliases={}, flops=100_000, moved=1_000_000):
    return pl.pallas_call(
        kernel,
        name=kernel.func.__name__,
        out_shape=outs,
        in_specs=in_specs,
        out_specs=[VMEM] * len(outs) if out_specs is None else out_specs,
        scratch_shapes=list(scratch),
        input_output_aliases=aliases,
        cost_estimate=pl.CostEstimate(flops=flops, bytes_accessed=moved, transcendentals=0),
        compiler_params=pltpu.CompilerParams(vmem_limit_bytes=40 * 2**20),
    )


def swap_aisle(value, odd):
    count = lax.axis_size("aisle")
    pairs = [(i, (i ^ 1 if not odd else i + 1 if i % 2 else i - 1) % count) for i in range(count)]
    return lax.ppermute(value, "aisle", pairs)


def swap_span(value, odd):
    count = lax.axis_size("span")
    pairs = []
    for a in range(lax.axis_size("aisle")):
        for s in range(count):
            t = s ^ 1 if not odd else s + 1 if s % 2 else s - 1
            b, t = (a, t) if 0 <= t < count else (a ^ 1, s)
            pairs.append((a * count + s, b * count + t))
    return lax.ppermute(value, ("aisle", "span"), pairs)


def shards(room_pops, plenum_pops, tile_cell, tile_owner, tile_class):
    n_span = lax.axis_size("span")
    _, ca, cs, hr = room_pops.shape
    hp = plenum_pops.shape[3]
    blocks = hr // LANES
    rows = blocks * cs
    tiles = tile_cell.shape[0]
    sizes = (ca, cs, blocks, n_span, tiles // n_span)
    direct = n_span == 4
    near = lambda shape: pltpu.VMEM(shape, F32)
    far = lambda value: pltpu.with_memory_space_constraint(value, pltpu.HBM)
    room_shape, plen_shape = (19, ca, rows, LANES), (19, ca * cs, LANES)
    halo = 5 * (rows + cs)
    halo = halo + -halo % 8
    room = far(room_pops.reshape(19, ca, cs, blocks, LANES).transpose(0, 1, 3, 2, 4).reshape(room_shape))
    plen = far(plenum_pops.reshape(plen_shape))
    tile_cell, tile_owner, tile_class = far(tile_cell), far(tile_owner.reshape(tiles)), far(tile_class)
    numbers = pltpu.SMEM((tiles,), jnp.int32)

    dealt_shape, jet_shape = (n_span * CAP, 1, 5 * hp), (CAP, 1, 5 * hp)
    room_post, plen_post, swap_a, swap_b, dealt = call(
        functools.partial(collide_kernel, sizes, direct),
        [near(room_shape), near(plen_shape), near((halo, LANES)), near((halo + 8, LANES)),
         near(dealt_shape)],
        [HBM] * 5,
        scratch=[near((ca * cs, 1, 5 * hp)), near(plen_shape), numbers, numbers, numbers,
                 pltpu.SemaphoreType.DMA((4 + ca,))],
    )(room, plen, tile_cell, tile_owner, tile_class)
    got_b = swap_aisle(swap_b, True)
    got_a = swap_aisle(swap_a, False)

    upto8 = lambda count: count + -count % 8
    wide = upto8(5 * (rows + ca) + (5 * CAP if direct else 0))
    cross_shapes = [near((wide, LANES)), near((wide + 8, LANES))]
    room_post, part_a, part_b, *jets = call(
        functools.partial(early_kernel, sizes, direct),
        [near(room_shape)] + cross_shapes + [near(jet_shape)] * (2 if direct else 0),
        [VMEM] * 3,
        aliases={0: 0},
    )(room_post, plen_post, dealt)
    if direct:
        own_jets = dealt
        got_jets = [lax.ppermute(jets[apart - 2], "span", [(i, i ^ apart) for i in range(4)]) for apart in (2, 3)]
    else:
        own_jets = lax.all_to_all(dealt, "span", 0, 0, tiled=True)
        got_jets = []
    room_post, part_a, part_b = call(
        functools.partial(late_kernel, sizes, direct),
        [near(room_shape)] + cross_shapes,
        [VMEM] * 5,
        aliases={0: 0, 3: 1, 4: 2},
    )(room_post, plen_post, dealt, part_a, part_b)
    cross_a, cross_b = call(
        functools.partial(pack_kernel, sizes),
        cross_shapes,
        [VMEM] * 4,
    )(got_a, got_b, part_a, part_b)
    in_a = swap_span(cross_a, False)
    in_b = swap_span(cross_b, True)

    room_part, plen_part, places = call(
        functools.partial(local_kernel, sizes),
        [near(room_shape), near(plen_shape), near((n_span * CAP + 1, ca * cs, LANES))],
        [VMEM, VMEM, VMEM, HBM, HBM],
        scratch=[numbers, numbers, pltpu.SemaphoreType.DMA((2,))],
        flops=10**9,
    )(room_post, plen_post, cross_a, tile_cell, tile_owner)
    room_part, plen_part, inflow = call(
        functools.partial(aisle_kernel, sizes, direct),
        [near(room_shape), near(plen_shape), near((5, ca * cs, LANES))],
        [VMEM] * 6,
        aliases={0: 0, 1: 1},
    )(room_part, plen_part, got_a, got_b, own_jets, places)

    _, _, room_next, plenum_next = call(
        functools.partial(finish_kernel, sizes, direct),
        [near(room_shape), near(plen_shape), jax.ShapeDtypeStruct(room_shape, F32),
         jax.ShapeDtypeStruct(plen_shape, F32)],
        [VMEM] * (6 + len(got_jets)),
        out_specs=[VMEM, VMEM, HBM, HBM],
        scratch=[pltpu.SemaphoreType.DMA((2,))],
        aliases={0: 0, 1: 1},
    )(room_part, plen_part, in_a, in_b, places, inflow, *got_jets)
    room_next = room_next.reshape(19, ca, blocks, cs, LANES).transpose(0, 1, 3, 2, 4).reshape(room_pops.shape)
    return room_next, plenum_next.reshape(plenum_pops.shape)


def solution(mesh):
    return jax.shard_map(
        shards,
        mesh=mesh,
        in_specs=(
            P(None, "aisle", "span", None),
            P(None, "aisle", "span", None),
            P("aisle"),
            P("aisle", None),
            P("aisle"),
        ),
        out_specs=(P(None, "aisle", "span", None), P(None, "aisle", "span", None)),
        check_vma=False,
    )
```

```python
import functools

import jax
import jax.numpy as jnp
from jax import lax
from jax.experimental import pallas as pl
from jax.experimental.pallas import tpu as pltpu
from jax.sharding import PartitionSpec as P

VELOCITIES = [
    (0, 0, 0),
    (1, 0, 0),
    (-1, 0, 0),
    (0, 1, 0),
    (0, -1, 0),
    (0, 0, 1),
    (0, 0, -1),
    (1, 1, 0),
    (-1, -1, 0),
    (1, -1, 0),
    (-1, 1, 0),
    (1, 0, 1),
    (-1, 0, -1),
    (1, 0, -1),
    (-1, 0, 1),
    (0, 1, 1),
    (0, -1, -1),
    (0, 1, -1),
    (0, -1, 1),
]
UPWARD = [5, 11, 14, 15, 18]
OMEGA = 1.25
CAP = 4
X_UP = [q for q in range(19) if VELOCITIES[q][0] == 1]
X_DOWN = [q for q in range(19) if VELOCITIES[q][0] == -1]
Y_UP = [q for q in range(19) if VELOCITIES[q][1] == 1]
Y_DOWN = [q for q in range(19) if VELOCITIES[q][1] == -1]
F32 = jnp.float32
LANES = 128
VMEM = pl.BlockSpec(memory_space=pltpu.VMEM)
HBM = pl.BlockSpec(memory_space=pltpu.HBM)


def collide(g):
    total = lambda i: g[i] + g[i + 1]
    apart = lambda i: g[i] - g[i + 1]
    dx, dy, dz = apart(1), apart(3), apart(5)
    d7, d9, d11, d13, d15, d17 = (apart(i) for i in (7, 9, 11, 13, 15, 17))
    edges = (total(7) + total(9)) + (total(11) + total(13)) + (total(15) + total(17))
    faces = total(1) + total(3) + total(5)
    rho = g[0] * (1.0 / 3.0) + faces * (1.0 / 18.0) + edges * (1.0 / 36.0)
    mx = dx * (1.0 / 18.0) + ((d7 + d9) + (d11 + d13)) * (1.0 / 36.0)
    my = dy * (1.0 / 18.0) + ((d7 - d9) + (d15 + d17)) * (1.0 / 36.0)
    mz = dz * (1.0 / 18.0) + ((d11 - d13) + (d15 - d17)) * (1.0 / 36.0)
    inv = 1.0 / rho
    base = OMEGA * rho - (1.5 * OMEGA) * inv * (mx * mx + my * my + mz * mz)
    square = (4.5 * OMEGA) * inv
    out = [None] * 19
    out[0] = base + (1.0 - OMEGA) * g[0]
    along = {1: mx, 3: my, 5: mz, 7: mx + my, 9: mx - my, 11: mx + mz, 13: mx - mz, 15: my + mz, 17: my - mz}
    for i, c in along.items():
        even = base + square * c * c
        odd = (3.0 * OMEGA) * c
        out[i] = (even + odd) + (1.0 - OMEGA) * g[i]
        out[i + 1] = (even - odd) + (1.0 - OMEGA) * g[i + 1]
    return out


def raised(value, cz, rows):
    if cz == 0:
        return value
    lane = lax.broadcasted_iota(jnp.int32, value.shape, 1)
    row = lax.broadcasted_iota(jnp.int32, value.shape, 0)
    total = value.shape[0]
    shift, edge = (1, 0) if cz == 1 else (LANES - 1, LANES - 1)
    turned = pltpu.roll(value, shift, 1)
    if rows == total:
        return jnp.where(lane == edge, value, turned)
    carried = pltpu.roll(turned, rows if cz == 1 else total - rows, 0)
    clamped = row < rows if cz == 1 else row >= total - rows
    return jnp.where(lane == edge, jnp.where(clamped, value, carried), turned)


def crossed(value, cy, cs):
    if cy == 0:
        return value
    row = lax.broadcasted_iota(jnp.int32, value.shape, 0) % cs
    turned = pltpu.roll(value, 1 if cy == 1 else value.shape[0] - 1, 0)
    return jnp.where(row == (0 if cy == 1 else cs - 1), value, turned)


def shifted(value, by):
    return pltpu.roll(value, by % value.shape[0], 0) if by else value


def turned_to(value, source, dest):
    return shifted(value, dest - source)


def repeat(count, body, start):
    if count > 8:
        return lax.fori_loop(0, count, body, start)
    for i in range(count):
        start = body(i, start)
    return start


def collide_plane(room, x):
    for r in range(0, room.shape[2], 8):
        post = collide([room[q, x, r : r + 8] for q in range(19)])
        for q in range(19):
            room[q, x, r : r + 8] = post[q]


def collide_kernel(sizes, direct, room_in, plen_in, cell_in, owner_in, class_in, room_post, plen_post, swap_a, swap_b,
                   dealt, columns, plen_buf, cells, owners, classes, sems):
    ca, cs, blocks, n_span, per_brick = sizes
    rows = blocks * cs
    copies = [pltpu.make_async_copy(src, dst, sems.at[i]) for i, (src, dst) in enumerate(
        ((plen_in, plen_buf), (cell_in, cells), (owner_in, owners), (class_in, classes)))]
    order = [0, ca - 1] + list(range(1, ca - 1))
    planes = [pltpu.make_async_copy(room_in.at[:, x], room_post.at[:, x], sems.at[4 + x]) for x in order]
    for copy in copies[1:] + copies[:1] + planes:
        copy.start()
    dealt[...] = jnp.zeros_like(dealt)
    copies[0].wait()
    for r in range(0, ca * cs, 8):
        post = collide([plen_buf[q, r : r + 8] for q in range(19)])
        for q in range(19):
            plen_post[q, r : r + 8] = post[q]
        for k, q in enumerate(UPWARD):
            for y in range(8):
                columns[r + y, :, k * LANES : (k + 1) * LANES] = post[q][y : y + 1]
    for copy in copies[1:4]:
        copy.wait()
    here = lax.axis_index("span")
    first = here * per_brick

    def send_jet(i, carry):
        t = first + i
        owner = owners[t]
        share = 0.15 * (classes[t].astype(F32) + 1.0)
        same = lambda j, n: n + (owners[first + j] == owner).astype(jnp.int32)
        slot = repeat(i, same, 0) if direct else lax.fori_loop(0, i, same, 0)
        to = (owner ^ here if direct else owner) * CAP + slot
        dealt[to] = share * columns[cells[t]]
        return carry

    if direct:
        for i in range(per_brick):
            send_jet(i, 0)
    else:
        lax.fori_loop(0, per_brick, send_jet, 0)
    for i in range(2):
        planes[i].wait()
        collide_plane(room_post, order[i])
    even = lax.axis_index("aisle") % 2 == 0
    for k in range(5):
        up, down = X_UP[k], X_DOWN[k]
        rising = raised(room_post[up, ca - 1], VELOCITIES[up][2], cs)
        falling = raised(room_post[down, 0], VELOCITIES[down][2], cs)
        swap_a[k * rows : (k + 1) * rows] = jnp.where(even, rising, falling)
        swap_b[k * rows : (k + 1) * rows] = jnp.where(even, falling, rising)
        rising = raised(plen_post[up, (ca - 1) * cs : ca * cs], VELOCITIES[up][2], cs)
        falling = raised(plen_post[down, 0:cs], VELOCITIES[down][2], cs)
        low = 5 * rows + k * cs
        swap_a[low : low + cs] = jnp.where(even, rising, falling)
        swap_b[low : low + cs] = jnp.where(even, falling, rising)
    for i in range(2, ca):
        planes[i].wait()


def jet_sums(start, places, bricks):
    sums = [start(k) for k in range(5)]
    for b, jet in bricks:
        for s in range(CAP):
            marks = places[b * CAP + s]
            sums = [total + marks * jet(s, k) for k, total in enumerate(sums)]
    return sums


def local_kernel(sizes, room_post, plen_post, crossing, cell_in, owner_in, room_part, plen_part, places, cells, owners,
                 sems):
    del crossing
    ca, cs, blocks, n_span, per_brick = sizes
    rows = blocks * cs
    copies = [pltpu.make_async_copy(src, dst, sems.at[i]) for i, (src, dst) in enumerate(
        ((cell_in, cells), (owner_in, owners)))]
    for copy in copies:
        copy.start()
    for q in range(19):
        cx, cy, cz = VELOCITIES[q]
        for x in range(ca):
            if 0 <= x - cx < ca:
                room_part[q, x] = crossed(raised(room_post[q, x - cx], cz, cs), cy, cs)
        plen_part[q] = crossed(shifted(raised(plen_post[q], cz, ca * cs), cx * cs), cy, cs)
    places[0 : n_span * CAP] = jnp.zeros((n_span * CAP, ca * cs, LANES), F32)
    here = lax.axis_index("span")
    row = lax.broadcasted_iota(jnp.int32, (ca * cs, LANES), 0)
    for copy in copies:
        copy.wait()

    def brick(b, carry):
        def place(i, slot):
            t = b * per_brick + i
            mine = owners[t] == here
            places[jnp.where(mine, b * CAP + slot, n_span * CAP)] = (row == cells[t]).astype(F32)
            return slot + mine.astype(jnp.int32)

        repeat(per_brick, place, 0)
        return carry

    repeat(n_span, brick, 0)


def inner(sizes, direct, room_post, plen_post, jets, cross_a, cross_b):
    ca, cs, blocks, n_span, per_brick = sizes
    rows = blocks * cs
    low = lax.axis_index("span") % 2 == 0
    group = lax.broadcasted_iota(jnp.int32, (rows, LANES), 0) % cs
    for x in range(1, ca - 1):
        collide_plane(room_post, x)
    for k in range(5):
        sides, near = [], []
        for q, edge in ((Y_UP[k], cs - 1), (Y_DOWN[k], 0)):
            cx, cy, cz = VELOCITIES[q]
            packed = None
            for x in range(max(cx, 0), ca + min(cx, 0)):
                ready = turned_to(raised(room_post[q, x - cx], cz, cs), edge, x)
                packed = ready if packed is None else jnp.where(group == x, ready, packed)
            sides.append(packed)
            near.append(shifted(raised(plen_post[q], cz, ca * cs), cx * cs - edge))
        cross_a[k * rows : (k + 1) * rows] = jnp.where(low, sides[0], sides[1])
        cross_b[k * rows : (k + 1) * rows] = jnp.where(low, sides[1], sides[0])
        first, second = jnp.where(low, near[0], near[1]), jnp.where(low, near[1], near[0])
        for x in range(ca):
            to = 5 * rows + k * ca + x
            cross_a[to : to + 1] = first[x * cs : x * cs + 1]
            cross_b[to : to + 1] = second[x * cs : x * cs + 1]
    if direct:
        for s in range(CAP):
            for k in range(5):
                to = 5 * (rows + ca) + s * 5 + k
                cross_a[to : to + 1] = jets[CAP + s, :, k * LANES : (k + 1) * LANES]


def early_kernel(sizes, direct, room_in, plen_post, dealt, room_post, cross_a, cross_b, *jets):
    start = 2 * CAP
    for jet in jets:
        jet[...] = dealt[start : start + CAP]
        start = start + CAP

    @pl.when(lax.axis_index("span") == 0)
    def _():
        inner(sizes, direct, room_post, plen_post, dealt, cross_a, cross_b)


def late_kernel(sizes, direct, room_in, plen_post, dealt, a_in, b_in, room_post, cross_a, cross_b):
    @pl.when(lax.axis_index("span") > 0)
    def _():
        inner(sizes, direct, room_post, plen_post, dealt, cross_a, cross_b)


def corners(cs, up):
    return [q for q in (Y_UP if up else Y_DOWN) if VELOCITIES[q][0]], cs - 1 if up else 0


def pack_kernel(sizes, got_a, got_b, part_a, part_b, cross_a, cross_b):
    ca, cs, blocks, n_span, per_brick = sizes
    rows = blocks * cs
    even = lax.axis_index("aisle") % 2 == 0
    low = lax.axis_index("span") % 2 == 0
    group = lax.broadcasted_iota(jnp.int32, (rows, LANES), 0) % cs
    cross_a[...] = part_a[...]
    cross_b[...] = part_b[...]

    def came(q, low, high):
        if VELOCITIES[q][0] == 1:
            return jnp.where(even, got_b[low:high], got_a[low:high])
        return jnp.where(even, got_a[low:high], got_b[low:high])

    def complete(cross, up):
        two, edge = corners(cs, up)
        for q in two:
            slot = (X_UP if VELOCITIES[q][0] == 1 else X_DOWN).index(q)
            x = 0 if VELOCITIES[q][0] == 1 else ca - 1
            k = (Y_UP if up else Y_DOWN).index(q)
            column = turned_to(came(q, slot * rows, (slot + 1) * rows), edge, x)
            cross[k * rows : (k + 1) * rows] = jnp.where(group == x, column, cross[k * rows : (k + 1) * rows])
            at, to = 5 * rows + slot * cs + edge, 5 * rows + k * ca + x
            cross[to : to + 1] = came(q, at, at + 1)

    @pl.when(low)
    def _():
        complete(cross_a, True)
        complete(cross_b, False)

    @pl.when(jnp.logical_not(low))
    def _():
        complete(cross_a, False)
        complete(cross_b, True)


def aisle_kernel(sizes, direct, room_in, plen_in, got_a, got_b, jets, places, room, plen, inflow):
    ca, cs, blocks, n_span, per_brick = sizes
    rows = blocks * cs
    even = lax.axis_index("aisle") % 2 == 0
    for k in range(5):
        for q, x, first, second in ((X_UP[k], 0, got_b, got_a), (X_DOWN[k], ca - 1, got_a, got_b)):
            cy = VELOCITIES[q][1]
            low, high = k * rows, (k + 1) * rows
            room[q, x] = crossed(jnp.where(even, first[low:high], second[low:high]), cy, cs)
            low = 5 * rows + k * cs
            value = jnp.where(even, first[low : low + cs], second[low : low + cs])
            at = x * cs
            if cy == 1:
                plen[q, at : at + 1] = value[0:1]
                plen[q, at + 1 : at + cs] = value[: cs - 1]
            elif cy == -1:
                plen[q, at + cs - 1 : at + cs] = value[cs - 1 : cs]
                plen[q, at : at + cs - 1] = value[1:cs]
            else:
                plen[q, at : at + cs] = value
    here = lax.axis_index("span")

    def put(sums):
        for k in range(5):
            inflow[k] = sums[k]

    def reader(source, b):
        return lambda s, k: source[b * CAP + s, :, k * LANES : (k + 1) * LANES]

    if direct:
        put(jet_sums(lambda k: jnp.zeros((ca * cs, LANES), F32), places,
                     [(here, reader(jets, 0))]))
    else:
        inflow[...] = jnp.zeros_like(inflow)

        def add_brick(b, carry):
            put(jet_sums(lambda k: inflow[k], places, [(b, reader(jets, b))]))
            return carry

        lax.fori_loop(0, n_span, add_brick, 0)


def finish_kernel(sizes, direct, room_in, plen_in, got_a, got_b, places, inflow, *rest):
    *got_jets, room, plen, room_out, plen_out, sems = rest
    ca, cs, blocks, n_span, per_brick = sizes
    rows = blocks * cs
    here = lax.axis_index("span")
    low = here % 2 == 0
    group = lax.broadcasted_iota(jnp.int32, (rows, LANES), 0) % cs

    def enter(got, up):
        planes, y = (Y_UP, 0) if up else (Y_DOWN, cs - 1)
        for k, q in enumerate(planes):
            came = got[k * rows : (k + 1) * rows]
            for x in range(ca):
                room[q, x] = jnp.where(group == y, turned_to(came, x, y), room[q, x])
                at = 5 * rows + k * ca + x
                plen[q, x * cs + y : x * cs + y + 1] = got[at : at + 1]

    @pl.when(low)
    def _():
        enter(got_a, False)

    @pl.when(jnp.logical_not(low))
    def _():
        enter(got_a, True)

    @pl.when(jnp.logical_and(low, here > 0))
    def _():
        enter(got_b, True)

    @pl.when(jnp.logical_and(jnp.logical_not(low), here < n_span - 1))
    def _():
        enter(got_b, False)

    parts = [pltpu.make_async_copy(room.at[low_q:high_q], room_out.at[low_q:high_q], sems.at[1 + i])
             for i, (low_q, high_q) in enumerate(((0, 5), (6, 11), (11, 19), (5, 6)))]
    parts.append(pltpu.make_async_copy(plen, plen_out, sems.at[0]))
    for part in parts[:2] + parts[4:]:
        part.start()
    bricks = []
    if direct:
        start = 5 * (rows + cs)
        bricks = [(here ^ 1, lambda s, k: got_a[start + s * 5 + k : start + s * 5 + k + 1])]
        for apart, got in zip((2, 3), got_jets):
            bricks.append((here ^ apart, lambda s, k, got=got: got[s, :, k * LANES : (k + 1) * LANES]))
    sums = jet_sums(lambda k: inflow[k], places, bricks)
    for k, q in enumerate(UPWARD):
        for x in range(ca):
            room[q, x, 0:cs] = room[q, x, 0:cs] + sums[k][x * cs : (x + 1) * cs]
    for part in parts[2:4]:
        part.start()
    for part in parts:
        part.wait()


def call(kernel, outs, in_specs, out_specs=None, scratch=(), aliases={}, flops=100_000, moved=1_000_000):
    return pl.pallas_call(
        kernel,
        name=kernel.func.__name__,
        out_shape=outs,
        in_specs=in_specs,
        out_specs=[VMEM] * len(outs) if out_specs is None else out_specs,
        scratch_shapes=list(scratch),
        input_output_aliases=aliases,
        cost_estimate=pl.CostEstimate(flops=flops, bytes_accessed=moved, transcendentals=0),
        compiler_params=pltpu.CompilerParams(vmem_limit_bytes=40 * 2**20),
    )


def swap_aisle(value, odd):
    count = lax.axis_size("aisle")
    pairs = [(i, (i ^ 1 if not odd else i + 1 if i % 2 else i - 1) % count) for i in range(count)]
    return lax.ppermute(value, "aisle", pairs)


def swap_span(value, odd):
    count = lax.axis_size("span")
    pairs = []
    for a in range(lax.axis_size("aisle")):
        for s in range(count):
            t = s ^ 1 if not odd else s + 1 if s % 2 else s - 1
            b, t = (a, t) if 0 <= t < count else (a ^ 1, s)
            pairs.append((a * count + s, b * count + t))
    return lax.ppermute(value, ("aisle", "span"), pairs)


def shards(room_pops, plenum_pops, tile_cell, tile_owner, tile_class):
    n_span = lax.axis_size("span")
    _, ca, cs, hr = room_pops.shape
    hp = plenum_pops.shape[3]
    blocks = hr // LANES
    rows = blocks * cs
    tiles = tile_cell.shape[0]
    sizes = (ca, cs, blocks, n_span, tiles // n_span)
    direct = n_span == 4
    near = lambda shape: pltpu.VMEM(shape, F32)
    far = lambda value: pltpu.with_memory_space_constraint(value, pltpu.HBM)
    room_shape, plen_shape = (19, ca, rows, LANES), (19, ca * cs, LANES)
    halo = 5 * (rows + cs)
    halo = halo + -halo % 8
    room = far(room_pops.reshape(19, ca, cs, blocks, LANES).transpose(0, 1, 3, 2, 4).reshape(room_shape))
    plen = far(plenum_pops.reshape(plen_shape))
    tile_cell, tile_owner, tile_class = far(tile_cell), far(tile_owner.reshape(tiles)), far(tile_class)
    numbers = pltpu.SMEM((tiles,), jnp.int32)

    dealt_shape, jet_shape = (n_span * CAP, 1, 5 * hp), (CAP, 1, 5 * hp)
    room_post, plen_post, swap_a, swap_b, dealt = call(
        functools.partial(collide_kernel, sizes, direct),
        [near(room_shape), near(plen_shape), near((halo, LANES)), near((halo + 8, LANES)),
         near(dealt_shape)],
        [HBM] * 5,
        scratch=[near((ca * cs, 1, 5 * hp)), near(plen_shape), numbers, numbers, numbers,
                 pltpu.SemaphoreType.DMA((4 + ca,))],
    )(room, plen, tile_cell, tile_owner, tile_class)
    got_b = swap_aisle(swap_b, True)
    got_a = swap_aisle(swap_a, False)

    upto8 = lambda count: count + -count % 8
    wide = upto8(5 * (rows + ca) + (5 * CAP if direct else 0))
    cross_shapes = [near((wide, LANES)), near((wide + 8, LANES))]
    room_post, part_a, part_b, *jets = call(
        functools.partial(early_kernel, sizes, direct),
        [near(room_shape)] + cross_shapes + [near(jet_shape)] * (2 if direct else 0),
        [VMEM] * 3,
        aliases={0: 0},
    )(room_post, plen_post, dealt)
    if direct:
        own_jets = dealt
        got_jets = [lax.ppermute(jets[apart - 2], "span", [(i, i ^ apart) for i in range(4)]) for apart in (2, 3)]
    else:
        own_jets = lax.all_to_all(dealt, "span", 0, 0, tiled=True)
        got_jets = []
    room_post, part_a, part_b = call(
        functools.partial(late_kernel, sizes, direct),
        [near(room_shape)] + cross_shapes,
        [VMEM] * 5,
        aliases={0: 0, 3: 1, 4: 2},
    )(room_post, plen_post, dealt, part_a, part_b)
    cross_a, cross_b = call(
        functools.partial(pack_kernel, sizes),
        cross_shapes,
        [VMEM] * 4,
    )(got_a, got_b, part_a, part_b)
    in_a = swap_span(cross_a, False)
    in_b = swap_span(cross_b, True)

    room_part, plen_part, places = call(
        functools.partial(local_kernel, sizes),
        [near(room_shape), near(plen_shape), near((n_span * CAP + 1, ca * cs, LANES))],
        [VMEM, VMEM, VMEM, HBM, HBM],
        scratch=[numbers, numbers, pltpu.SemaphoreType.DMA((2,))],
        flops=10**9,
    )(room_post, plen_post, cross_a, tile_cell, tile_owner)
    room_part, plen_part, inflow = call(
        functools.partial(aisle_kernel, sizes, direct),
        [near(room_shape), near(plen_shape), near((5, ca * cs, LANES))],
        [VMEM] * 6,
        aliases={0: 0, 1: 1},
    )(room_part, plen_part, got_a, got_b, own_jets, places)

    _, _, room_next, plenum_next = call(
        functools.partial(finish_kernel, sizes, direct),
        [near(room_shape), near(plen_shape), jax.ShapeDtypeStruct(room_shape, F32),
         jax.ShapeDtypeStruct(plen_shape, F32)],
        [VMEM] * (6 + len(got_jets)),
        out_specs=[VMEM, VMEM, HBM, HBM],
        scratch=[pltpu.SemaphoreType.DMA((5,))],
        aliases={0: 0, 1: 1},
    )(room_part, plen_part, in_a, in_b, places, inflow, *got_jets)
    room_next = room_next.reshape(19, ca, blocks, cs, LANES).transpose(0, 1, 3, 2, 4).reshape(room_pops.shape)
    return room_next, plenum_next.reshape(plenum_pops.shape)


def solution(mesh):
    return jax.shard_map(
        shards,
        mesh=mesh,
        in_specs=(
            P(None, "aisle", "span", None),
            P(None, "aisle", "span", None),
            P("aisle"),
            P("aisle", None),
            P("aisle"),
        ),
        out_specs=(P(None, "aisle", "span", None), P(None, "aisle", "span", None)),
        check_vma=False,
    )
```

```python
import functools

import jax
import jax.numpy as jnp
from jax import lax
from jax.experimental import pallas as pl
from jax.experimental.pallas import tpu as pltpu
from jax.sharding import PartitionSpec as P

VELOCITIES = [
    (0, 0, 0),
    (1, 0, 0),
    (-1, 0, 0),
    (0, 1, 0),
    (0, -1, 0),
    (0, 0, 1),
    (0, 0, -1),
    (1, 1, 0),
    (-1, -1, 0),
    (1, -1, 0),
    (-1, 1, 0),
    (1, 0, 1),
    (-1, 0, -1),
    (1, 0, -1),
    (-1, 0, 1),
    (0, 1, 1),
    (0, -1, -1),
    (0, 1, -1),
    (0, -1, 1),
]
UPWARD = [5, 11, 14, 15, 18]
OMEGA = 1.25
CAP = 4
X_UP = [q for q in range(19) if VELOCITIES[q][0] == 1]
X_DOWN = [q for q in range(19) if VELOCITIES[q][0] == -1]
Y_UP = [q for q in range(19) if VELOCITIES[q][1] == 1]
Y_DOWN = [q for q in range(19) if VELOCITIES[q][1] == -1]
F32 = jnp.float32
LANES = 128
VMEM = pl.BlockSpec(memory_space=pltpu.VMEM)
HBM = pl.BlockSpec(memory_space=pltpu.HBM)


def collide(g):
    total = lambda i: g[i] + g[i + 1]
    apart = lambda i: g[i] - g[i + 1]
    dx, dy, dz = apart(1), apart(3), apart(5)
    d7, d9, d11, d13, d15, d17 = (apart(i) for i in (7, 9, 11, 13, 15, 17))
    edges = (total(7) + total(9)) + (total(11) + total(13)) + (total(15) + total(17))
    faces = total(1) + total(3) + total(5)
    rho = g[0] * (1.0 / 3.0) + faces * (1.0 / 18.0) + edges * (1.0 / 36.0)
    mx = dx * (1.0 / 18.0) + ((d7 + d9) + (d11 + d13)) * (1.0 / 36.0)
    my = dy * (1.0 / 18.0) + ((d7 - d9) + (d15 + d17)) * (1.0 / 36.0)
    mz = dz * (1.0 / 18.0) + ((d11 - d13) + (d15 - d17)) * (1.0 / 36.0)
    inv = 1.0 / rho
    base = OMEGA * rho - (1.5 * OMEGA) * inv * (mx * mx + my * my + mz * mz)
    square = (4.5 * OMEGA) * inv
    out = [None] * 19
    out[0] = base + (1.0 - OMEGA) * g[0]
    along = {1: mx, 3: my, 5: mz, 7: mx + my, 9: mx - my, 11: mx + mz, 13: mx - mz, 15: my + mz, 17: my - mz}
    for i, c in along.items():
        even = base + square * c * c
        odd = (3.0 * OMEGA) * c
        out[i] = (even + odd) + (1.0 - OMEGA) * g[i]
        out[i + 1] = (even - odd) + (1.0 - OMEGA) * g[i + 1]
    return out


def raised(value, cz, rows):
    if cz == 0:
        return value
    lane = lax.broadcasted_iota(jnp.int32, value.shape, 1)
    row = lax.broadcasted_iota(jnp.int32, value.shape, 0)
    total = value.shape[0]
    shift, edge = (1, 0) if cz == 1 else (LANES - 1, LANES - 1)
    turned = pltpu.roll(value, shift, 1)
    if rows == total:
        return jnp.where(lane == edge, value, turned)
    carried = pltpu.roll(turned, rows if cz == 1 else total - rows, 0)
    clamped = row < rows if cz == 1 else row >= total - rows
    return jnp.where(lane == edge, jnp.where(clamped, value, carried), turned)


def crossed(value, cy, cs):
    if cy == 0:
        return value
    row = lax.broadcasted_iota(jnp.int32, value.shape, 0) % cs
    turned = pltpu.roll(value, 1 if cy == 1 else value.shape[0] - 1, 0)
    return jnp.where(row == (0 if cy == 1 else cs - 1), value, turned)


def shifted(value, by):
    return pltpu.roll(value, by % value.shape[0], 0) if by else value


def turned_to(value, source, dest):
    return shifted(value, dest - source)


def repeat(count, body, start):
    if count > 8:
        return lax.fori_loop(0, count, body, start)
    for i in range(count):
        start = body(i, start)
    return start


def first_up(n_span):
    return (lax.axis_index("aisle") % 2 == 0) == (lax.axis_index("span") == n_span - 1)


def collide_plane(room, x):
    for r in range(0, room.shape[2], 8):
        post = collide([room[q, x, r : r + 8] for q in range(19)])
        for q in range(19):
            room[q, x, r : r + 8] = post[q]


def collide_kernel(sizes, direct, room_in, plen_in, cell_in, owner_in, class_in, room_post, plen_post, swap_a, swap_b,
                   dealt, columns, plen_buf, cells, owners, classes, sems):
    ca, cs, blocks, n_span, per_brick = sizes
    rows = blocks * cs
    copies = [pltpu.make_async_copy(src, dst, sems.at[i]) for i, (src, dst) in enumerate(
        ((plen_in, plen_buf), (cell_in, cells), (owner_in, owners), (class_in, classes)))]
    order = [0, ca - 1] + list(range(1, ca - 1))
    planes = [pltpu.make_async_copy(room_in.at[:, x], room_post.at[:, x], sems.at[4 + x]) for x in order]
    for copy in copies[:1] + planes + copies[1:]:
        copy.start()
    dealt[...] = jnp.zeros_like(dealt)
    copies[0].wait()
    for r in range(0, ca * cs, 8):
        post = collide([plen_buf[q, r : r + 8] for q in range(19)])
        for q in range(19):
            plen_post[q, r : r + 8] = post[q]
        for k, q in enumerate(UPWARD):
            for y in range(8):
                columns[r + y, :, k * LANES : (k + 1) * LANES] = post[q][y : y + 1]
    for copy in copies[1:4]:
        copy.wait()
    here = lax.axis_index("span")
    first = here * per_brick

    def send_jet(i, carry):
        t = first + i
        owner = owners[t]
        share = 0.15 * (classes[t].astype(F32) + 1.0)
        same = lambda j, n: n + (owners[first + j] == owner).astype(jnp.int32)
        slot = repeat(i, same, 0) if direct else lax.fori_loop(0, i, same, 0)
        to = (owner ^ here if direct else owner) * CAP + slot
        dealt[to] = share * columns[cells[t]]
        return carry

    if direct:
        for i in range(per_brick):
            send_jet(i, 0)
    else:
        lax.fori_loop(0, per_brick, send_jet, 0)
    for i in range(2):
        planes[i].wait()
        collide_plane(room_post, order[i])
    even = first_up(n_span)
    for k in range(5):
        up, down = X_UP[k], X_DOWN[k]
        rising = raised(room_post[up, ca - 1], VELOCITIES[up][2], cs)
        falling = raised(room_post[down, 0], VELOCITIES[down][2], cs)
        swap_a[k * rows : (k + 1) * rows] = jnp.where(even, rising, falling)
        swap_b[k * rows : (k + 1) * rows] = jnp.where(even, falling, rising)
        rising = raised(plen_post[up, (ca - 1) * cs : ca * cs], VELOCITIES[up][2], cs)
        falling = raised(plen_post[down, 0:cs], VELOCITIES[down][2], cs)
        low = 5 * rows + k * cs
        swap_a[low : low + cs] = jnp.where(even, rising, falling)
        swap_b[low : low + cs] = jnp.where(even, falling, rising)
    for i in range(2, ca):
        planes[i].wait()


def jet_sums(start, places, bricks):
    sums = [start(k) for k in range(5)]
    for b, jet in bricks:
        for s in range(CAP):
            marks = places[b * CAP + s]
            sums = [total + marks * jet(s, k) for k, total in enumerate(sums)]
    return sums


def local_kernel(sizes, room_post, plen_post, crossing, *rest):
    cell_in, owner_in, room_part, plen_part, places, cells, owners, sems = rest[-8:]
    del crossing
    ca, cs, blocks, n_span, per_brick = sizes
    rows = blocks * cs
    copies = [pltpu.make_async_copy(src, dst, sems.at[i]) for i, (src, dst) in enumerate(
        ((cell_in, cells), (owner_in, owners)))]
    for copy in copies:
        copy.start()
    for q in range(19):
        cx, cy, cz = VELOCITIES[q]
        for x in range(ca):
            if 0 <= x - cx < ca:
                room_part[q, x] = crossed(raised(room_post[q, x - cx], cz, cs), cy, cs)
        plen_part[q] = crossed(shifted(raised(plen_post[q], cz, ca * cs), cx * cs), cy, cs)
    places[0 : n_span * CAP] = jnp.zeros((n_span * CAP, ca * cs, LANES), F32)
    here = lax.axis_index("span")
    row = lax.broadcasted_iota(jnp.int32, (ca * cs, LANES), 0)
    for copy in copies:
        copy.wait()

    def brick(b, carry):
        def place(i, slot):
            t = b * per_brick + i
            mine = owners[t] == here
            places[jnp.where(mine, b * CAP + slot, n_span * CAP)] = (row == cells[t]).astype(F32)
            return slot + mine.astype(jnp.int32)

        repeat(per_brick, place, 0)
        return carry

    repeat(n_span, brick, 0)


def inner(sizes, direct, room_post, plen_post, jets, cross_a, cross_b):
    ca, cs, blocks, n_span, per_brick = sizes
    rows = blocks * cs
    low = lax.axis_index("span") % 2 == 0
    group = lax.broadcasted_iota(jnp.int32, (rows, LANES), 0) % cs
    for x in range(1, ca - 1):
        collide_plane(room_post, x)
    for k in range(5):
        sides, near = [], []
        for q, edge in ((Y_UP[k], cs - 1), (Y_DOWN[k], 0)):
            cx, cy, cz = VELOCITIES[q]
            packed = None
            for x in range(max(cx, 0), ca + min(cx, 0)):
                ready = turned_to(raised(room_post[q, x - cx], cz, cs), edge, x)
                packed = ready if packed is None else jnp.where(group == x, ready, packed)
            sides.append(packed)
            near.append(shifted(raised(plen_post[q], cz, ca * cs), cx * cs - edge))
        cross_a[k * rows : (k + 1) * rows] = jnp.where(low, sides[0], sides[1])
        cross_b[k * rows : (k + 1) * rows] = jnp.where(low, sides[1], sides[0])
        first, second = jnp.where(low, near[0], near[1]), jnp.where(low, near[1], near[0])
        for x in range(ca):
            to = 5 * rows + k * ca + x
            cross_a[to : to + 1] = first[x * cs : x * cs + 1]
            cross_b[to : to + 1] = second[x * cs : x * cs + 1]
    if direct:
        for s in range(CAP):
            for k in range(5):
                to = 5 * (rows + ca) + s * 5 + k
                cross_a[to : to + 1] = jets[CAP + s, :, k * LANES : (k + 1) * LANES]


def early_kernel(sizes, direct, room_in, plen_post, dealt, room_post, cross_a, cross_b, *jets):
    start = 2 * CAP
    for jet in jets:
        jet[0:CAP] = dealt[start : start + CAP]
        start = start + CAP

    @pl.when(lax.axis_index("span") == 0)
    def _():
        inner(sizes, direct, room_post, plen_post, dealt, cross_a, cross_b)


def late_kernel(sizes, direct, room_in, plen_post, dealt, a_in, b_in, room_post, cross_a, cross_b):
    @pl.when(lax.axis_index("span") > 0)
    def _():
        inner(sizes, direct, room_post, plen_post, dealt, cross_a, cross_b)


def corners(cs, up):
    return [q for q in (Y_UP if up else Y_DOWN) if VELOCITIES[q][0]], cs - 1 if up else 0


def pack_kernel(sizes, got_a, got_b, part_a, part_b, cross_a, cross_b):
    ca, cs, blocks, n_span, per_brick = sizes
    rows = blocks * cs
    even = first_up(n_span)
    low = lax.axis_index("span") % 2 == 0
    group = lax.broadcasted_iota(jnp.int32, (rows, LANES), 0) % cs
    cross_a[...] = part_a[...]
    cross_b[...] = part_b[...]

    def came(q, low, high):
        if VELOCITIES[q][0] == 1:
            return jnp.where(even, got_b[low:high], got_a[low:high])
        return jnp.where(even, got_a[low:high], got_b[low:high])

    def complete(cross, up):
        two, edge = corners(cs, up)
        for q in two:
            slot = (X_UP if VELOCITIES[q][0] == 1 else X_DOWN).index(q)
            x = 0 if VELOCITIES[q][0] == 1 else ca - 1
            k = (Y_UP if up else Y_DOWN).index(q)
            column = turned_to(came(q, slot * rows, (slot + 1) * rows), edge, x)
            cross[k * rows : (k + 1) * rows] = jnp.where(group == x, column, cross[k * rows : (k + 1) * rows])
            at, to = 5 * rows + slot * cs + edge, 5 * rows + k * ca + x
            cross[to : to + 1] = came(q, at, at + 1)

    @pl.when(low)
    def _():
        complete(cross_a, True)
        complete(cross_b, False)

    @pl.when(jnp.logical_not(low))
    def _():
        complete(cross_a, False)
        complete(cross_b, True)


def aisle_kernel(sizes, direct, room_in, plen_in, got_a, got_b, jets, places, room, plen, inflow):
    ca, cs, blocks, n_span, per_brick = sizes
    rows = blocks * cs
    even = first_up(n_span)
    for k in range(5):
        for q, x, first, second in ((X_UP[k], 0, got_b, got_a), (X_DOWN[k], ca - 1, got_a, got_b)):
            cy = VELOCITIES[q][1]
            low, high = k * rows, (k + 1) * rows
            room[q, x] = crossed(jnp.where(even, first[low:high], second[low:high]), cy, cs)
            low = 5 * rows + k * cs
            value = jnp.where(even, first[low : low + cs], second[low : low + cs])
            at = x * cs
            if cy == 1:
                plen[q, at : at + 1] = value[0:1]
                plen[q, at + 1 : at + cs] = value[: cs - 1]
            elif cy == -1:
                plen[q, at + cs - 1 : at + cs] = value[cs - 1 : cs]
                plen[q, at : at + cs - 1] = value[1:cs]
            else:
                plen[q, at : at + cs] = value
    here = lax.axis_index("span")

    def put(sums):
        for k in range(5):
            inflow[k] = sums[k]

    def reader(source, b):
        return lambda s, k: source[b * CAP + s, :, k * LANES : (k + 1) * LANES]

    if direct:
        put(jet_sums(lambda k: jnp.zeros((ca * cs, LANES), F32), places,
                     [(here, reader(jets, 0))]))
    else:
        inflow[...] = jnp.zeros_like(inflow)

        def add_brick(b, carry):
            put(jet_sums(lambda k: inflow[k], places, [(b, reader(jets, b))]))
            return carry

        lax.fori_loop(0, n_span, add_brick, 0)


def finish_kernel(sizes, direct, room_in, plen_in, got_a, got_b, places, inflow, *rest):
    *got_jets, room, plen, room_out, plen_out, sems = rest
    ca, cs, blocks, n_span, per_brick = sizes
    rows = blocks * cs
    here = lax.axis_index("span")
    low = here % 2 == 0
    group = lax.broadcasted_iota(jnp.int32, (rows, LANES), 0) % cs

    def enter(got, up):
        planes, y = (Y_UP, 0) if up else (Y_DOWN, cs - 1)
        for k, q in enumerate(planes):
            came = got[k * rows : (k + 1) * rows]
            for x in range(ca):
                room[q, x] = jnp.where(group == y, turned_to(came, x, y), room[q, x])
                at = 5 * rows + k * ca + x
                plen[q, x * cs + y : x * cs + y + 1] = got[at : at + 1]

    @pl.when(low)
    def _():
        enter(got_a, False)

    @pl.when(jnp.logical_not(low))
    def _():
        enter(got_a, True)

    @pl.when(jnp.logical_and(low, here > 0))
    def _():
        enter(got_b, True)

    @pl.when(jnp.logical_and(jnp.logical_not(low), here < n_span - 1))
    def _():
        enter(got_b, False)

    plen_copy = pltpu.make_async_copy(plen, plen_out, sems.at[0])
    plen_copy.start()
    bricks = []
    if direct:
        start = 5 * (rows + cs)
        bricks = [(here ^ 1, lambda s, k: got_a[start + s * 5 + k : start + s * 5 + k + 1])]
        for apart, got in zip((2, 3), got_jets):
            bricks.append((here ^ apart, lambda s, k, got=got: got[s, :, k * LANES : (k + 1) * LANES]))
    sums = jet_sums(lambda k: inflow[k], places, bricks)
    for k, q in enumerate(UPWARD):
        for x in range(ca):
            room[q, x, 0:cs] = room[q, x, 0:cs] + sums[k][x * cs : (x + 1) * cs]
    room_copy = pltpu.make_async_copy(room, room_out, sems.at[1])
    room_copy.start()
    plen_copy.wait()
    room_copy.wait()


def call(kernel, outs, in_specs, out_specs=None, scratch=(), aliases={}, flops=100_000, moved=1_000_000):
    return pl.pallas_call(
        kernel,
        name=kernel.func.__name__,
        out_shape=outs,
        in_specs=in_specs,
        out_specs=[VMEM] * len(outs) if out_specs is None else out_specs,
        scratch_shapes=list(scratch),
        input_output_aliases=aliases,
        cost_estimate=pl.CostEstimate(flops=flops, bytes_accessed=moved, transcendentals=0),
        compiler_params=pltpu.CompilerParams(vmem_limit_bytes=40 * 2**20),
    )


def swap_aisle(value, second):
    count, across = lax.axis_size("aisle"), lax.axis_size("span")
    pairs = []
    for a in range(count):
        for s in range(across):
            b = a ^ 1 if second != (s == across - 1) else (a + 1 if a % 2 else a - 1) % count
            pairs.append((a * across + s, b * across + s))
    return lax.ppermute(value, ("aisle", "span"), pairs)


def swap_span(value, odd):
    count = lax.axis_size("span")
    pairs = []
    for a in range(lax.axis_size("aisle")):
        for s in range(count):
            t = s ^ 1 if not odd else s + 1 if s % 2 else s - 1
            b, t = (a, t) if 0 <= t < count else (a ^ 1, s)
            pairs.append((a * count + s, b * count + t))
    return lax.ppermute(value, ("aisle", "span"), pairs)


def shards(room_pops, plenum_pops, tile_cell, tile_owner, tile_class):
    n_span = lax.axis_size("span")
    _, ca, cs, hr = room_pops.shape
    hp = plenum_pops.shape[3]
    blocks = hr // LANES
    rows = blocks * cs
    tiles = tile_cell.shape[0]
    sizes = (ca, cs, blocks, n_span, tiles // n_span)
    direct = n_span == 4
    near = lambda shape: pltpu.VMEM(shape, F32)
    far = lambda value: pltpu.with_memory_space_constraint(value, pltpu.HBM)
    room_shape, plen_shape = (19, ca, rows, LANES), (19, ca * cs, LANES)
    halo = 5 * (rows + cs)
    halo = halo + -halo % 8
    room = far(room_pops.reshape(19, ca, cs, blocks, LANES).transpose(0, 1, 3, 2, 4).reshape(room_shape))
    plen = far(plenum_pops.reshape(plen_shape))
    tile_cell, tile_owner, tile_class = far(tile_cell), far(tile_owner.reshape(tiles)), far(tile_class)
    numbers = pltpu.SMEM((tiles,), jnp.int32)

    dealt_shape = (n_span * CAP, 1, 5 * hp)
    between = -(-(halo + 4) * LANES // (5 * hp))
    jet_shapes = [near((CAP, 1, 5 * hp)), near((between, 1, 5 * hp))] if direct else []
    room_post, plen_post, swap_a, swap_b, dealt = call(
        functools.partial(collide_kernel, sizes, direct),
        [near(room_shape), near(plen_shape), near((halo + 8, LANES)), near((halo, LANES)),
         near(dealt_shape)],
        [HBM] * 5,
        scratch=[near((ca * cs, 1, 5 * hp)), near(plen_shape), numbers, numbers, numbers,
                 pltpu.SemaphoreType.DMA((4 + ca,))],
    )(room, plen, tile_cell, tile_owner, tile_class)
    got_a = swap_aisle(swap_a, False)
    got_b = swap_aisle(swap_b, True)

    upto8 = lambda count: count + -count % 8
    wide = upto8(5 * (rows + ca) + (5 * CAP if direct else 0))
    cross_shapes = [near((wide + 8, LANES)), near((wide, LANES))]
    room_post, part_a, part_b, *jets = call(
        functools.partial(early_kernel, sizes, direct),
        [near(room_shape)] + cross_shapes + jet_shapes,
        [VMEM] * 3,
        aliases={0: 0},
    )(room_post, plen_post, dealt)
    if direct:
        own_jets = dealt
        got_jets = [lax.ppermute(jets[apart - 2], "span", [(i, i ^ apart) for i in range(4)]) for apart in (2, 3)]
    else:
        own_jets = lax.all_to_all(dealt, "span", 0, 0, tiled=True)
        got_jets = []
    room_post, part_a, part_b = call(
        functools.partial(late_kernel, sizes, direct),
        [near(room_shape)] + cross_shapes,
        [VMEM] * 5,
        aliases={0: 0, 3: 1, 4: 2},
    )(room_post, plen_post, dealt, part_a, part_b)
    cross_a, cross_b = call(
        functools.partial(pack_kernel, sizes),
        cross_shapes,
        [VMEM] * 4,
    )(got_a, got_b, part_a, part_b)
    in_a = swap_span(cross_a, False)
    in_b = swap_span(cross_b, True)

    room_part, plen_part, places = call(
        functools.partial(local_kernel, sizes),
        [near(room_shape), near(plen_shape), near((n_span * CAP + 1, ca * cs, LANES))],
        [VMEM] * (3 + len(got_jets[1:])) + [HBM, HBM],
        scratch=[numbers, numbers, pltpu.SemaphoreType.DMA((2,))],
        flops=10**9,
    )(room_post, plen_post, cross_a, *got_jets[1:], tile_cell, tile_owner)
    room_part, plen_part, inflow = call(
        functools.partial(aisle_kernel, sizes, direct),
        [near(room_shape), near(plen_shape), near((5, ca * cs, LANES))],
        [VMEM] * 6,
        aliases={0: 0, 1: 1},
    )(room_part, plen_part, got_a, got_b, own_jets, places)

    _, _, room_next, plenum_next = call(
        functools.partial(finish_kernel, sizes, direct),
        [near(room_shape), near(plen_shape), jax.ShapeDtypeStruct(room_shape, F32),
         jax.ShapeDtypeStruct(plen_shape, F32)],
        [VMEM] * (6 + len(got_jets)),
        out_specs=[VMEM, VMEM, HBM, HBM],
        scratch=[pltpu.SemaphoreType.DMA((2,))],
        aliases={0: 0, 1: 1},
    )(room_part, plen_part, in_a, in_b, places, inflow, *got_jets)
    room_next = room_next.reshape(19, ca, blocks, cs, LANES).transpose(0, 1, 3, 2, 4).reshape(room_pops.shape)
    return room_next, plenum_next.reshape(plenum_pops.shape)


def solution(mesh):
    return jax.shard_map(
        shards,
        mesh=mesh,
        in_specs=(
            P(None, "aisle", "span", None),
            P(None, "aisle", "span", None),
            P("aisle"),
            P("aisle", None),
            P("aisle"),
        ),
        out_specs=(P(None, "aisle", "span", None), P(None, "aisle", "span", None)),
        check_vma=False,
    )
```

```python
import functools

import jax
import jax.numpy as jnp
from jax import lax
from jax.experimental import pallas as pl
from jax.experimental.pallas import tpu as pltpu
from jax.sharding import PartitionSpec as P

VELOCITIES = [
    (0, 0, 0),
    (1, 0, 0),
    (-1, 0, 0),
    (0, 1, 0),
    (0, -1, 0),
    (0, 0, 1),
    (0, 0, -1),
    (1, 1, 0),
    (-1, -1, 0),
    (1, -1, 0),
    (-1, 1, 0),
    (1, 0, 1),
    (-1, 0, -1),
    (1, 0, -1),
    (-1, 0, 1),
    (0, 1, 1),
    (0, -1, -1),
    (0, 1, -1),
    (0, -1, 1),
]
UPWARD = [5, 11, 14, 15, 18]
OMEGA = 1.25
CAP = 4
X_UP = [q for q in range(19) if VELOCITIES[q][0] == 1]
X_DOWN = [q for q in range(19) if VELOCITIES[q][0] == -1]
Y_UP = [q for q in range(19) if VELOCITIES[q][1] == 1]
Y_DOWN = [q for q in range(19) if VELOCITIES[q][1] == -1]
F32 = jnp.float32
LANES = 128
VMEM = pl.BlockSpec(memory_space=pltpu.VMEM)
HBM = pl.BlockSpec(memory_space=pltpu.HBM)


def collide(g):
    total = lambda i: g[i] + g[i + 1]
    apart = lambda i: g[i] - g[i + 1]
    dx, dy, dz = apart(1), apart(3), apart(5)
    d7, d9, d11, d13, d15, d17 = (apart(i) for i in (7, 9, 11, 13, 15, 17))
    edges = (total(7) + total(9)) + (total(11) + total(13)) + (total(15) + total(17))
    faces = total(1) + total(3) + total(5)
    rho = g[0] * (1.0 / 3.0) + faces * (1.0 / 18.0) + edges * (1.0 / 36.0)
    mx = dx * (1.0 / 18.0) + ((d7 + d9) + (d11 + d13)) * (1.0 / 36.0)
    my = dy * (1.0 / 18.0) + ((d7 - d9) + (d15 + d17)) * (1.0 / 36.0)
    mz = dz * (1.0 / 18.0) + ((d11 - d13) + (d15 - d17)) * (1.0 / 36.0)
    inv = 1.0 / rho
    base = OMEGA * rho - (1.5 * OMEGA) * inv * (mx * mx + my * my + mz * mz)
    square = (4.5 * OMEGA) * inv
    out = [None] * 19
    out[0] = base + (1.0 - OMEGA) * g[0]
    along = {1: mx, 3: my, 5: mz, 7: mx + my, 9: mx - my, 11: mx + mz, 13: mx - mz, 15: my + mz, 17: my - mz}
    for i, c in along.items():
        even = base + square * c * c
        odd = (3.0 * OMEGA) * c
        out[i] = (even + odd) + (1.0 - OMEGA) * g[i]
        out[i + 1] = (even - odd) + (1.0 - OMEGA) * g[i + 1]
    return out


def raised(value, cz, rows):
    if cz == 0:
        return value
    lane = lax.broadcasted_iota(jnp.int32, value.shape, 1)
    row = lax.broadcasted_iota(jnp.int32, value.shape, 0)
    total = value.shape[0]
    shift, edge = (1, 0) if cz == 1 else (LANES - 1, LANES - 1)
    turned = pltpu.roll(value, shift, 1)
    if rows == total:
        return jnp.where(lane == edge, value, turned)
    carried = pltpu.roll(turned, rows if cz == 1 else total - rows, 0)
    clamped = row < rows if cz == 1 else row >= total - rows
    return jnp.where(lane == edge, jnp.where(clamped, value, carried), turned)


def crossed(value, cy, cs):
    if cy == 0:
        return value
    row = lax.broadcasted_iota(jnp.int32, value.shape, 0) % cs
    turned = pltpu.roll(value, 1 if cy == 1 else value.shape[0] - 1, 0)
    return jnp.where(row == (0 if cy == 1 else cs - 1), value, turned)


def shifted(value, by):
    return pltpu.roll(value, by % value.shape[0], 0) if by else value


def turned_to(value, source, dest):
    return shifted(value, dest - source)


def repeat(count, body, start):
    if count > 8:
        return lax.fori_loop(0, count, body, start)
    for i in range(count):
        start = body(i, start)
    return start


def first_up(n_span):
    return (lax.axis_index("aisle") % 2 == 0) == (lax.axis_index("span") == n_span - 1)


def collide_plane(room, x):
    for r in range(0, room.shape[2], 8):
        post = collide([room[q, x, r : r + 8] for q in range(19)])
        for q in range(19):
            room[q, x, r : r + 8] = post[q]


def collide_kernel(sizes, direct, room_in, plen_in, cell_in, owner_in, class_in, room_post, plen_post, swap_a, swap_b,
                   dealt, columns, plen_buf, cells, owners, classes, sems):
    ca, cs, blocks, n_span, per_brick = sizes
    rows = blocks * cs
    copies = [pltpu.make_async_copy(src, dst, sems.at[i]) for i, (src, dst) in enumerate(
        ((plen_in, plen_buf), (cell_in, cells), (owner_in, owners), (class_in, classes)))]
    order = [0, ca - 1] + list(range(1, ca - 1))
    planes = [pltpu.make_async_copy(room_in.at[:, x], room_post.at[:, x], sems.at[4 + x]) for x in order]
    for copy in copies[:1] + planes + copies[1:]:
        copy.start()
    dealt[...] = jnp.zeros_like(dealt)
    copies[0].wait()
    for r in range(0, ca * cs, 8):
        post = collide([plen_buf[q, r : r + 8] for q in range(19)])
        for q in range(19):
            plen_post[q, r : r + 8] = post[q]
        for k, q in enumerate(UPWARD):
            for y in range(8):
                columns[r + y, :, k * LANES : (k + 1) * LANES] = post[q][y : y + 1]
    for copy in copies[1:4]:
        copy.wait()
    here = lax.axis_index("span")
    first = here * per_brick

    def send_jet(i, carry):
        t = first + i
        owner = owners[t]
        share = 0.15 * (classes[t].astype(F32) + 1.0)
        same = lambda j, n: n + (owners[first + j] == owner).astype(jnp.int32)
        slot = repeat(i, same, 0) if direct else lax.fori_loop(0, i, same, 0)
        to = (owner ^ here if direct else owner) * CAP + slot
        dealt[to] = share * columns[cells[t]]
        return carry

    if direct:
        for i in range(per_brick):
            send_jet(i, 0)
    else:
        lax.fori_loop(0, per_brick, send_jet, 0)
    for i in range(2):
        planes[i].wait()
        collide_plane(room_post, order[i])
    even = first_up(n_span)
    for k in range(5):
        up, down = X_UP[k], X_DOWN[k]
        rising = raised(room_post[up, ca - 1], VELOCITIES[up][2], cs)
        falling = raised(room_post[down, 0], VELOCITIES[down][2], cs)
        swap_a[k * rows : (k + 1) * rows] = jnp.where(even, rising, falling)
        swap_b[k * rows : (k + 1) * rows] = jnp.where(even, falling, rising)
        rising = raised(plen_post[up, (ca - 1) * cs : ca * cs], VELOCITIES[up][2], cs)
        falling = raised(plen_post[down, 0:cs], VELOCITIES[down][2], cs)
        low = 5 * rows + k * cs
        swap_a[low : low + cs] = jnp.where(even, rising, falling)
        swap_b[low : low + cs] = jnp.where(even, falling, rising)
    for i in range(2, ca):
        planes[i].wait()


def jet_sums(start, places, bricks):
    sums = [start(k) for k in range(5)]
    for b, jet in bricks:
        for s in range(CAP):
            marks = places[b * CAP + s]
            sums = [total + marks * jet(s, k) for k, total in enumerate(sums)]
    return sums


def local_kernel(sizes, room_post, plen_post, crossing, *rest):
    cell_in, owner_in, room_part, plen_part, places, cells, owners, sems = rest[-8:]
    del crossing
    ca, cs, blocks, n_span, per_brick = sizes
    rows = blocks * cs
    copies = [pltpu.make_async_copy(src, dst, sems.at[i]) for i, (src, dst) in enumerate(
        ((cell_in, cells), (owner_in, owners)))]
    for copy in copies:
        copy.start()
    for q in range(19):
        cx, cy, cz = VELOCITIES[q]
        for x in range(ca):
            if 0 <= x - cx < ca:
                room_part[q, x] = crossed(raised(room_post[q, x - cx], cz, cs), cy, cs)
        plen_part[q] = crossed(shifted(raised(plen_post[q], cz, ca * cs), cx * cs), cy, cs)
    places[0 : n_span * CAP] = jnp.zeros((n_span * CAP, ca * cs, LANES), F32)
    here = lax.axis_index("span")
    row = lax.broadcasted_iota(jnp.int32, (ca * cs, LANES), 0)
    for copy in copies:
        copy.wait()

    def brick(b, carry):
        def place(i, slot):
            t = b * per_brick + i
            mine = owners[t] == here
            places[jnp.where(mine, b * CAP + slot, n_span * CAP)] = (row == cells[t]).astype(F32)
            return slot + mine.astype(jnp.int32)

        repeat(per_brick, place, 0)
        return carry

    repeat(n_span, brick, 0)


def inner(sizes, direct, room_post, plen_post, jets, cross_a, cross_b):
    ca, cs, blocks, n_span, per_brick = sizes
    rows = blocks * cs
    low = lax.axis_index("span") % 2 == 0
    group = lax.broadcasted_iota(jnp.int32, (rows, LANES), 0) % cs
    for x in range(1, ca - 1):
        collide_plane(room_post, x)
    for k in range(5):
        sides, near = [], []
        for q, edge in ((Y_UP[k], cs - 1), (Y_DOWN[k], 0)):
            cx, cy, cz = VELOCITIES[q]
            packed = None
            for x in range(max(cx, 0), ca + min(cx, 0)):
                ready = turned_to(raised(room_post[q, x - cx], cz, cs), edge, x)
                packed = ready if packed is None else jnp.where(group == x, ready, packed)
            sides.append(packed)
            near.append(shifted(raised(plen_post[q], cz, ca * cs), cx * cs - edge))
        cross_a[k * rows : (k + 1) * rows] = jnp.where(low, sides[0], sides[1])
        cross_b[k * rows : (k + 1) * rows] = jnp.where(low, sides[1], sides[0])
        first, second = jnp.where(low, near[0], near[1]), jnp.where(low, near[1], near[0])
        for x in range(ca):
            to = 5 * rows + k * ca + x
            cross_a[to : to + 1] = first[x * cs : x * cs + 1]
            cross_b[to : to + 1] = second[x * cs : x * cs + 1]
    if direct:
        for s in range(CAP):
            for k in range(5):
                to = 5 * (rows + ca) + s * 5 + k
                cross_a[to : to + 1] = jets[CAP + s, :, k * LANES : (k + 1) * LANES]


def early_kernel(sizes, direct, room_in, plen_post, dealt, room_post, cross_a, cross_b, *jets):
    start = 2 * CAP
    for jet in jets:
        jet[0:CAP] = dealt[start : start + CAP]
        start = start + CAP

    @pl.when(lax.axis_index("span") == 0)
    def _():
        inner(sizes, direct, room_post, plen_post, dealt, cross_a, cross_b)


def late_kernel(sizes, direct, room_in, plen_post, dealt, a_in, b_in, room_post, cross_a, cross_b):
    @pl.when(lax.axis_index("span") > 0)
    def _():
        inner(sizes, direct, room_post, plen_post, dealt, cross_a, cross_b)


def corners(cs, up):
    return [q for q in (Y_UP if up else Y_DOWN) if VELOCITIES[q][0]], cs - 1 if up else 0


def pack_kernel(sizes, got_a, got_b, part_a, part_b, cross_a, cross_b, *copies):
    ca, cs, blocks, n_span, per_brick = sizes
    rows = blocks * cs
    even = first_up(n_span)
    low = lax.axis_index("span") % 2 == 0
    group = lax.broadcasted_iota(jnp.int32, (rows, LANES), 0) % cs
    cross_a[...] = part_a[...]
    cross_b[...] = part_b[...]

    def came(q, low, high):
        if VELOCITIES[q][0] == 1:
            return jnp.where(even, got_b[low:high], got_a[low:high])
        return jnp.where(even, got_a[low:high], got_b[low:high])

    def complete(cross, up):
        two, edge = corners(cs, up)
        for q in two:
            slot = (X_UP if VELOCITIES[q][0] == 1 else X_DOWN).index(q)
            x = 0 if VELOCITIES[q][0] == 1 else ca - 1
            k = (Y_UP if up else Y_DOWN).index(q)
            column = turned_to(came(q, slot * rows, (slot + 1) * rows), edge, x)
            cross[k * rows : (k + 1) * rows] = jnp.where(group == x, column, cross[k * rows : (k + 1) * rows])
            at, to = 5 * rows + slot * cs + edge, 5 * rows + k * ca + x
            cross[to : to + 1] = came(q, at, at + 1)

    @pl.when(low)
    def _():
        complete(cross_a, True)
        complete(cross_b, False)

    @pl.when(jnp.logical_not(low))
    def _():
        complete(cross_a, False)
        complete(cross_b, True)

    for copy in copies:
        copy[0 : cross_a.shape[0]] = cross_a[...]


def aisle_kernel(sizes, direct, room_in, plen_in, got_a, got_b, jets, places, room, plen, inflow):
    ca, cs, blocks, n_span, per_brick = sizes
    rows = blocks * cs
    even = first_up(n_span)
    for k in range(5):
        for q, x, first, second in ((X_UP[k], 0, got_b, got_a), (X_DOWN[k], ca - 1, got_a, got_b)):
            cy = VELOCITIES[q][1]
            low, high = k * rows, (k + 1) * rows
            room[q, x] = crossed(jnp.where(even, first[low:high], second[low:high]), cy, cs)
            low = 5 * rows + k * cs
            value = jnp.where(even, first[low : low + cs], second[low : low + cs])
            at = x * cs
            if cy == 1:
                plen[q, at : at + 1] = value[0:1]
                plen[q, at + 1 : at + cs] = value[: cs - 1]
            elif cy == -1:
                plen[q, at + cs - 1 : at + cs] = value[cs - 1 : cs]
                plen[q, at : at + cs - 1] = value[1:cs]
            else:
                plen[q, at : at + cs] = value
    here = lax.axis_index("span")

    def put(sums):
        for k in range(5):
            inflow[k] = sums[k]

    def reader(source, b):
        return lambda s, k: source[b * CAP + s, :, k * LANES : (k + 1) * LANES]

    if direct:
        put(jet_sums(lambda k: jnp.zeros((ca * cs, LANES), F32), places,
                     [(here, reader(jets, 0))]))
    else:
        inflow[...] = jnp.zeros_like(inflow)

        def add_brick(b, carry):
            put(jet_sums(lambda k: inflow[k], places, [(b, reader(jets, b))]))
            return carry

        lax.fori_loop(0, n_span, add_brick, 0)


def finish_kernel(sizes, direct, room_in, plen_in, got_b, places, inflow, *rest):
    *got_jets, room, plen, room_out, plen_out, sems = rest
    many = 2 if direct else 1
    got_a, got_jets = got_jets[:many], got_jets[many:]
    ca, cs, blocks, n_span, per_brick = sizes
    rows = blocks * cs
    here = lax.axis_index("span")
    low = here % 2 == 0
    group = lax.broadcasted_iota(jnp.int32, (rows, LANES), 0) % cs

    def enter(got, up):
        planes, y = (Y_UP, 0) if up else (Y_DOWN, cs - 1)
        for k, q in enumerate(planes):
            came = got[k * rows : (k + 1) * rows]
            for x in range(ca):
                room[q, x] = jnp.where(group == y, turned_to(came, x, y), room[q, x])
                at = 5 * rows + k * ca + x
                plen[q, x * cs + y : x * cs + y + 1] = got[at : at + 1]

    for half, got in enumerate(got_a):
        inside = jnp.logical_and(here >= 2 * half, here < (2 * half + 2 if direct else n_span))

        @pl.when(jnp.logical_and(low, inside))
        def _(got=got):
            enter(got, False)

        @pl.when(jnp.logical_and(jnp.logical_not(low), inside))
        def _(got=got):
            enter(got, True)

    @pl.when(jnp.logical_and(low, here > 0))
    def _():
        enter(got_b, True)

    @pl.when(jnp.logical_and(jnp.logical_not(low), here < n_span - 1))
    def _():
        enter(got_b, False)

    plen_copy = pltpu.make_async_copy(plen, plen_out, sems.at[0])
    plen_copy.start()
    bricks = []
    if direct:
        start = 5 * (rows + cs)
        near_jet = lambda s, k: jnp.where(here < 2, *[got[start + s * 5 + k : start + s * 5 + k + 1] for got in got_a])
        bricks = [(here ^ 1, near_jet)]
        for apart, got in zip((2, 3), got_jets):
            bricks.append((here ^ apart, lambda s, k, got=got: got[s, :, k * LANES : (k + 1) * LANES]))
    sums = jet_sums(lambda k: inflow[k], places, bricks)
    for k, q in enumerate(UPWARD):
        for x in range(ca):
            room[q, x, 0:cs] = room[q, x, 0:cs] + sums[k][x * cs : (x + 1) * cs]
    room_copy = pltpu.make_async_copy(room, room_out, sems.at[1])
    room_copy.start()
    plen_copy.wait()
    room_copy.wait()


def call(kernel, outs, in_specs, out_specs=None, scratch=(), aliases={}, flops=100_000, moved=1_000_000):
    return pl.pallas_call(
        kernel,
        name=kernel.func.__name__,
        out_shape=outs,
        in_specs=in_specs,
        out_specs=[VMEM] * len(outs) if out_specs is None else out_specs,
        scratch_shapes=list(scratch),
        input_output_aliases=aliases,
        cost_estimate=pl.CostEstimate(flops=flops, bytes_accessed=moved, transcendentals=0),
        compiler_params=pltpu.CompilerParams(vmem_limit_bytes=40 * 2**20),
    )


def swap_aisle(value, second):
    count, across = lax.axis_size("aisle"), lax.axis_size("span")
    pairs = []
    for a in range(count):
        for s in range(across):
            b = a ^ 1 if second != (s == across - 1) else (a + 1 if a % 2 else a - 1) % count
            pairs.append((a * across + s, b * across + s))
    return lax.ppermute(value, ("aisle", "span"), pairs)


def swap_span(value, odd, bricks):
    count = lax.axis_size("span")
    pairs = []
    for a in range(lax.axis_size("aisle")):
        for s in range(count):
            t = s ^ 1 if not odd else s + 1 if s % 2 else s - 1
            b, t = (a, t) if 0 <= t < count and s in bricks else (a ^ 1, s)
            pairs.append((a * count + s, b * count + t))
    return lax.ppermute(value, ("aisle", "span"), pairs)


def shards(room_pops, plenum_pops, tile_cell, tile_owner, tile_class):
    n_span = lax.axis_size("span")
    _, ca, cs, hr = room_pops.shape
    hp = plenum_pops.shape[3]
    blocks = hr // LANES
    rows = blocks * cs
    tiles = tile_cell.shape[0]
    sizes = (ca, cs, blocks, n_span, tiles // n_span)
    direct = n_span == 4
    near = lambda shape: pltpu.VMEM(shape, F32)
    far = lambda value: pltpu.with_memory_space_constraint(value, pltpu.HBM)
    room_shape, plen_shape = (19, ca, rows, LANES), (19, ca * cs, LANES)
    halo = 5 * (rows + cs)
    halo = halo + -halo % 8
    room = far(room_pops.reshape(19, ca, cs, blocks, LANES).transpose(0, 1, 3, 2, 4).reshape(room_shape))
    plen = far(plenum_pops.reshape(plen_shape))
    tile_cell, tile_owner, tile_class = far(tile_cell), far(tile_owner.reshape(tiles)), far(tile_class)
    numbers = pltpu.SMEM((tiles,), jnp.int32)

    dealt_shape = (n_span * CAP, 1, 5 * hp)
    between = -(-(halo + 4) * LANES // (5 * hp))
    jet_shapes = [near((CAP, 1, 5 * hp)), near((between, 1, 5 * hp))] if direct else []
    room_post, plen_post, swap_a, swap_b, dealt = call(
        functools.partial(collide_kernel, sizes, direct),
        [near(room_shape), near(plen_shape), near((halo + 8, LANES)), near((halo, LANES)),
         near(dealt_shape)],
        [HBM] * 5,
        scratch=[near((ca * cs, 1, 5 * hp)), near(plen_shape), numbers, numbers, numbers,
                 pltpu.SemaphoreType.DMA((4 + ca,))],
    )(room, plen, tile_cell, tile_owner, tile_class)
    got_a = swap_aisle(swap_a, False)
    got_b = swap_aisle(swap_b, True)

    upto8 = lambda count: count + -count % 8
    wide = upto8(5 * (rows + ca) + (5 * CAP if direct else 0))
    cross_shapes = [near((wide, LANES)), near((wide + 8, LANES))]
    room_post, part_a, part_b, *jets = call(
        functools.partial(early_kernel, sizes, direct),
        [near(room_shape)] + cross_shapes + jet_shapes,
        [VMEM] * 3,
        aliases={0: 0},
    )(room_post, plen_post, dealt)
    if direct:
        own_jets = dealt
        got_jets = [lax.ppermute(jets[apart - 2], "span", [(i, i ^ apart) for i in range(4)]) for apart in (2, 3)]
    else:
        own_jets = lax.all_to_all(dealt, "span", 0, 0, tiled=True)
        got_jets = []
    room_post, part_a, part_b = call(
        functools.partial(late_kernel, sizes, direct),
        [near(room_shape)] + cross_shapes,
        [VMEM] * 5,
        aliases={0: 0, 3: 1, 4: 2},
    )(room_post, plen_post, dealt, part_a, part_b)
    cross_a, cross_b, *cross_c = call(
        functools.partial(pack_kernel, sizes),
        cross_shapes + [near((wide + 16, LANES))] * (1 if direct else 0),
        [VMEM] * 4,
    )(got_a, got_b, part_a, part_b)
    halves = (range(2), range(2, 4)) if direct else (range(n_span),)
    in_a = [swap_span(value, False, half) for value, half in zip((cross_a, *cross_c), halves)]
    in_b = swap_span(cross_b, True, range(n_span))

    room_part, plen_part, places = call(
        functools.partial(local_kernel, sizes),
        [near(room_shape), near(plen_shape), near((n_span * CAP + 1, ca * cs, LANES))],
        [VMEM] * (3 + len(got_jets[1:])) + [HBM, HBM],
        scratch=[numbers, numbers, pltpu.SemaphoreType.DMA((2,))],
        flops=10**9,
    )(room_post, plen_post, cross_a, *got_jets[1:], tile_cell, tile_owner)
    room_part, plen_part, inflow = call(
        functools.partial(aisle_kernel, sizes, direct),
        [near(room_shape), near(plen_shape), near((5, ca * cs, LANES))],
        [VMEM] * 6,
        aliases={0: 0, 1: 1},
    )(room_part, plen_part, got_a, got_b, own_jets, places)

    _, _, room_next, plenum_next = call(
        functools.partial(finish_kernel, sizes, direct),
        [near(room_shape), near(plen_shape), jax.ShapeDtypeStruct(room_shape, F32),
         jax.ShapeDtypeStruct(plen_shape, F32)],
        [VMEM] * (5 + len(in_a) + len(got_jets)),
        out_specs=[VMEM, VMEM, HBM, HBM],
        scratch=[pltpu.SemaphoreType.DMA((2,))],
        aliases={0: 0, 1: 1},
    )(room_part, plen_part, in_b, places, inflow, *in_a, *got_jets)
    room_next = room_next.reshape(19, ca, blocks, cs, LANES).transpose(0, 1, 3, 2, 4).reshape(room_pops.shape)
    return room_next, plenum_next.reshape(plenum_pops.shape)


def solution(mesh):
    return jax.shard_map(
        shards,
        mesh=mesh,
        in_specs=(
            P(None, "aisle", "span", None),
            P(None, "aisle", "span", None),
            P("aisle"),
            P("aisle", None),
            P("aisle"),
        ),
        out_specs=(P(None, "aisle", "span", None), P(None, "aisle", "span", None)),
        check_vma=False,
    )
```

```python
import functools

import jax
import jax.numpy as jnp
from jax import lax
from jax.experimental import pallas as pl
from jax.experimental.pallas import tpu as pltpu
from jax.sharding import PartitionSpec as P

VELOCITIES = [
    (0, 0, 0),
    (1, 0, 0),
    (-1, 0, 0),
    (0, 1, 0),
    (0, -1, 0),
    (0, 0, 1),
    (0, 0, -1),
    (1, 1, 0),
    (-1, -1, 0),
    (1, -1, 0),
    (-1, 1, 0),
    (1, 0, 1),
    (-1, 0, -1),
    (1, 0, -1),
    (-1, 0, 1),
    (0, 1, 1),
    (0, -1, -1),
    (0, 1, -1),
    (0, -1, 1),
]
UPWARD = [5, 11, 14, 15, 18]
OMEGA = 1.25
CAP = 4
X_UP = [q for q in range(19) if VELOCITIES[q][0] == 1]
X_DOWN = [q for q in range(19) if VELOCITIES[q][0] == -1]
Y_UP = [q for q in range(19) if VELOCITIES[q][1] == 1]
Y_DOWN = [q for q in range(19) if VELOCITIES[q][1] == -1]
F32 = jnp.float32
LANES = 128
VMEM = pl.BlockSpec(memory_space=pltpu.VMEM)
HBM = pl.BlockSpec(memory_space=pltpu.HBM)


def collide(g):
    total = lambda i: g[i] + g[i + 1]
    apart = lambda i: g[i] - g[i + 1]
    dx, dy, dz = apart(1), apart(3), apart(5)
    d7, d9, d11, d13, d15, d17 = (apart(i) for i in (7, 9, 11, 13, 15, 17))
    edges = (total(7) + total(9)) + (total(11) + total(13)) + (total(15) + total(17))
    faces = total(1) + total(3) + total(5)
    rho = g[0] * (1.0 / 3.0) + faces * (1.0 / 18.0) + edges * (1.0 / 36.0)
    mx = dx * (1.0 / 18.0) + ((d7 + d9) + (d11 + d13)) * (1.0 / 36.0)
    my = dy * (1.0 / 18.0) + ((d7 - d9) + (d15 + d17)) * (1.0 / 36.0)
    mz = dz * (1.0 / 18.0) + ((d11 - d13) + (d15 - d17)) * (1.0 / 36.0)
    inv = 1.0 / rho
    base = OMEGA * rho - (1.5 * OMEGA) * inv * (mx * mx + my * my + mz * mz)
    square = (4.5 * OMEGA) * inv
    out = [None] * 19
    out[0] = base + (1.0 - OMEGA) * g[0]
    along = {1: mx, 3: my, 5: mz, 7: mx + my, 9: mx - my, 11: mx + mz, 13: mx - mz, 15: my + mz, 17: my - mz}
    for i, c in along.items():
        even = base + square * c * c
        odd = (3.0 * OMEGA) * c
        out[i] = (even + odd) + (1.0 - OMEGA) * g[i]
        out[i + 1] = (even - odd) + (1.0 - OMEGA) * g[i + 1]
    return out


def raised(value, cz, rows):
    if cz == 0:
        return value
    lane = lax.broadcasted_iota(jnp.int32, value.shape, 1)
    row = lax.broadcasted_iota(jnp.int32, value.shape, 0)
    total = value.shape[0]
    shift, edge = (1, 0) if cz == 1 else (LANES - 1, LANES - 1)
    turned = pltpu.roll(value, shift, 1)
    if rows == total:
        return jnp.where(lane == edge, value, turned)
    carried = pltpu.roll(turned, rows if cz == 1 else total - rows, 0)
    clamped = row < rows if cz == 1 else row >= total - rows
    return jnp.where(lane == edge, jnp.where(clamped, value, carried), turned)


def crossed(value, cy, cs):
    if cy == 0:
        return value
    row = lax.broadcasted_iota(jnp.int32, value.shape, 0) % cs
    turned = pltpu.roll(value, 1 if cy == 1 else value.shape[0] - 1, 0)
    return jnp.where(row == (0 if cy == 1 else cs - 1), value, turned)


def shifted(value, by):
    return pltpu.roll(value, by % value.shape[0], 0) if by else value


def turned_to(value, source, dest):
    return shifted(value, dest - source)


def repeat(count, body, start):
    if count > 8:
        return lax.fori_loop(0, count, body, start)
    for i in range(count):
        start = body(i, start)
    return start


def collide_plane(room, x):
    for r in range(0, room.shape[2], 8):
        post = collide([room[q, x, r : r + 8] for q in range(19)])
        for q in range(19):
            room[q, x, r : r + 8] = post[q]


def collide_kernel(sizes, direct, room_in, plen_in, cell_in, owner_in, class_in, room_post, plen_post, swap_a, swap_b,
                   dealt, columns, plen_buf, cells, owners, classes, sems):
    ca, cs, blocks, n_span, per_brick = sizes
    rows = blocks * cs
    copies = [pltpu.make_async_copy(src, dst, sems.at[i]) for i, (src, dst) in enumerate(
        ((plen_in, plen_buf), (cell_in, cells), (owner_in, owners), (class_in, classes)))]
    order = [0, ca - 1] + list(range(1, ca - 1))
    planes = [pltpu.make_async_copy(room_in.at[:, x], room_post.at[:, x], sems.at[4 + x]) for x in order]
    for copy in copies[:1] + planes + copies[1:]:
        copy.start()
    dealt[...] = jnp.zeros_like(dealt)
    copies[0].wait()
    for r in range(0, ca * cs, 8):
        post = collide([plen_buf[q, r : r + 8] for q in range(19)])
        for q in range(19):
            plen_post[q, r : r + 8] = post[q]
        for k, q in enumerate(UPWARD):
            for y in range(8):
                columns[r + y, :, k * LANES : (k + 1) * LANES] = post[q][y : y + 1]
    for copy in copies[1:4]:
        copy.wait()
    here = lax.axis_index("span")
    first = here * per_brick

    def send_jet(i, carry):
        t = first + i
        owner = owners[t]
        share = 0.15 * (classes[t].astype(F32) + 1.0)
        same = lambda j, n: n + (owners[first + j] == owner).astype(jnp.int32)
        slot = repeat(i, same, 0) if direct else lax.fori_loop(0, i, same, 0)
        to = (owner ^ here if direct else owner) * CAP + slot
        dealt[to] = share * columns[cells[t]]
        return carry

    if direct:
        for i in range(per_brick):
            send_jet(i, 0)
    else:
        lax.fori_loop(0, per_brick, send_jet, 0)
    for i in range(2):
        planes[i].wait()
        collide_plane(room_post, order[i])
    even = lax.axis_index("aisle") % 2 == 0
    for k in range(5):
        up, down = X_UP[k], X_DOWN[k]
        rising = raised(room_post[up, ca - 1], VELOCITIES[up][2], cs)
        falling = raised(room_post[down, 0], VELOCITIES[down][2], cs)
        swap_a[k * rows : (k + 1) * rows] = jnp.where(even, rising, falling)
        swap_b[k * rows : (k + 1) * rows] = jnp.where(even, falling, rising)
        rising = raised(plen_post[up, (ca - 1) * cs : ca * cs], VELOCITIES[up][2], cs)
        falling = raised(plen_post[down, 0:cs], VELOCITIES[down][2], cs)
        low = 5 * rows + k * cs
        swap_a[low : low + cs] = jnp.where(even, rising, falling)
        swap_b[low : low + cs] = jnp.where(even, falling, rising)
    for i in range(2, ca):
        planes[i].wait()


def jet_sums(start, places, bricks):
    sums = [start(k) for k in range(5)]
    for b, jet in bricks:
        for s in range(CAP):
            marks = places[b * CAP + s]
            sums = [total + marks * jet(s, k) for k, total in enumerate(sums)]
    return sums


def local_kernel(sizes, room_post, plen_post, crossing, cell_in, owner_in, room_part, plen_part, places, cells, owners,
                 sems):
    del crossing
    ca, cs, blocks, n_span, per_brick = sizes
    rows = blocks * cs
    copies = [pltpu.make_async_copy(src, dst, sems.at[i]) for i, (src, dst) in enumerate(
        ((cell_in, cells), (owner_in, owners)))]
    for copy in copies:
        copy.start()
    for q in range(19):
        cx, cy, cz = VELOCITIES[q]
        for x in range(ca):
            if 0 <= x - cx < ca:
                room_part[q, x] = crossed(raised(room_post[q, x - cx], cz, cs), cy, cs)
        plen_part[q] = crossed(shifted(raised(plen_post[q], cz, ca * cs), cx * cs), cy, cs)
    places[0 : n_span * CAP] = jnp.zeros((n_span * CAP, ca * cs, LANES), F32)
    here = lax.axis_index("span")
    row = lax.broadcasted_iota(jnp.int32, (ca * cs, LANES), 0)
    for copy in copies:
        copy.wait()

    def brick(b, carry):
        def place(i, slot):
            t = b * per_brick + i
            mine = owners[t] == here
            places[jnp.where(mine, b * CAP + slot, n_span * CAP)] = (row == cells[t]).astype(F32)
            return slot + mine.astype(jnp.int32)

        repeat(per_brick, place, 0)
        return carry

    repeat(n_span, brick, 0)


def inner(sizes, direct, room_post, plen_post, jets, cross_a, cross_b):
    ca, cs, blocks, n_span, per_brick = sizes
    rows = blocks * cs
    low = lax.axis_index("span") % 2 == 0
    group = lax.broadcasted_iota(jnp.int32, (rows, LANES), 0) % cs
    for x in range(1, ca - 1):
        collide_plane(room_post, x)
    for k in range(5):
        sides, near = [], []
        for q, edge in ((Y_UP[k], cs - 1), (Y_DOWN[k], 0)):
            cx, cy, cz = VELOCITIES[q]
            packed = None
            for x in range(max(cx, 0), ca + min(cx, 0)):
                ready = turned_to(raised(room_post[q, x - cx], cz, cs), edge, x)
                packed = ready if packed is None else jnp.where(group == x, ready, packed)
            sides.append(packed)
            near.append(shifted(raised(plen_post[q], cz, ca * cs), cx * cs - edge))
        cross_a[k * rows : (k + 1) * rows] = jnp.where(low, sides[0], sides[1])
        cross_b[k * rows : (k + 1) * rows] = jnp.where(low, sides[1], sides[0])
        first, second = jnp.where(low, near[0], near[1]), jnp.where(low, near[1], near[0])
        for x in range(ca):
            to = 5 * rows + k * ca + x
            cross_a[to : to + 1] = first[x * cs : x * cs + 1]
            cross_b[to : to + 1] = second[x * cs : x * cs + 1]
    if direct:
        for s in range(CAP):
            for k in range(5):
                to = 5 * (rows + ca) + s * 5 + k
                cross_a[to : to + 1] = jets[CAP + s, :, k * LANES : (k + 1) * LANES]


def early_kernel(sizes, direct, room_in, plen_post, dealt, room_post, cross_a, cross_b, *jets):
    start = 2 * CAP
    for jet in jets:
        jet[0:CAP] = dealt[start : start + CAP]
        start = start + CAP

    @pl.when(lax.axis_index("span") == 0)
    def _():
        inner(sizes, direct, room_post, plen_post, dealt, cross_a, cross_b)


def late_kernel(sizes, direct, room_in, plen_post, dealt, a_in, b_in, room_post, cross_a, cross_b):
    @pl.when(lax.axis_index("span") > 0)
    def _():
        inner(sizes, direct, room_post, plen_post, dealt, cross_a, cross_b)


def corners(cs, up):
    return [q for q in (Y_UP if up else Y_DOWN) if VELOCITIES[q][0]], cs - 1 if up else 0


def pack_kernel(sizes, got_a, got_b, part_a, part_b, cross_a, cross_b):
    ca, cs, blocks, n_span, per_brick = sizes
    rows = blocks * cs
    even = lax.axis_index("aisle") % 2 == 0
    low = lax.axis_index("span") % 2 == 0
    group = lax.broadcasted_iota(jnp.int32, (rows, LANES), 0) % cs
    cross_a[...] = part_a[...]
    cross_b[...] = part_b[...]

    def came(q, low, high):
        if VELOCITIES[q][0] == 1:
            return jnp.where(even, got_b[low:high], got_a[low:high])
        return jnp.where(even, got_a[low:high], got_b[low:high])

    def complete(cross, up):
        two, edge = corners(cs, up)
        for q in two:
            slot = (X_UP if VELOCITIES[q][0] == 1 else X_DOWN).index(q)
            x = 0 if VELOCITIES[q][0] == 1 else ca - 1
            k = (Y_UP if up else Y_DOWN).index(q)
            column = turned_to(came(q, slot * rows, (slot + 1) * rows), edge, x)
            cross[k * rows : (k + 1) * rows] = jnp.where(group == x, column, cross[k * rows : (k + 1) * rows])
            at, to = 5 * rows + slot * cs + edge, 5 * rows + k * ca + x
            cross[to : to + 1] = came(q, at, at + 1)

    @pl.when(low)
    def _():
        complete(cross_a, True)
        complete(cross_b, False)

    @pl.when(jnp.logical_not(low))
    def _():
        complete(cross_a, False)
        complete(cross_b, True)


def aisle_kernel(sizes, direct, room_in, plen_in, got_a, got_b, jets, places, room, plen, inflow):
    ca, cs, blocks, n_span, per_brick = sizes
    rows = blocks * cs
    even = lax.axis_index("aisle") % 2 == 0
    for k in range(5):
        for q, x, first, second in ((X_UP[k], 0, got_b, got_a), (X_DOWN[k], ca - 1, got_a, got_b)):
            cy = VELOCITIES[q][1]
            low, high = k * rows, (k + 1) * rows
            room[q, x] = crossed(jnp.where(even, first[low:high], second[low:high]), cy, cs)
            low = 5 * rows + k * cs
            value = jnp.where(even, first[low : low + cs], second[low : low + cs])
            at = x * cs
            if cy == 1:
                plen[q, at : at + 1] = value[0:1]
                plen[q, at + 1 : at + cs] = value[: cs - 1]
            elif cy == -1:
                plen[q, at + cs - 1 : at + cs] = value[cs - 1 : cs]
                plen[q, at : at + cs - 1] = value[1:cs]
            else:
                plen[q, at : at + cs] = value
    here = lax.axis_index("span")

    def put(sums):
        for k in range(5):
            inflow[k] = sums[k]

    def reader(source, b):
        return lambda s, k: source[b * CAP + s, :, k * LANES : (k + 1) * LANES]

    if direct:
        put(jet_sums(lambda k: jnp.zeros((ca * cs, LANES), F32), places,
                     [(here, reader(jets, 0))]))
    else:
        inflow[...] = jnp.zeros_like(inflow)

        def add_brick(b, carry):
            put(jet_sums(lambda k: inflow[k], places, [(b, reader(jets, b))]))
            return carry

        lax.fori_loop(0, n_span, add_brick, 0)


def finish_kernel(sizes, direct, room_in, plen_in, got_a, got_b, places, inflow, *rest):
    *got_jets, room, plen, room_out, plen_out, sems = rest
    ca, cs, blocks, n_span, per_brick = sizes
    rows = blocks * cs
    here = lax.axis_index("span")
    low = here % 2 == 0
    group = lax.broadcasted_iota(jnp.int32, (rows, LANES), 0) % cs

    def enter(got, up):
        planes, y = (Y_UP, 0) if up else (Y_DOWN, cs - 1)
        for k, q in enumerate(planes):
            came = got[k * rows : (k + 1) * rows]
            for x in range(ca):
                room[q, x] = jnp.where(group == y, turned_to(came, x, y), room[q, x])
                at = 5 * rows + k * ca + x
                plen[q, x * cs + y : x * cs + y + 1] = got[at : at + 1]

    @pl.when(low)
    def _():
        enter(got_a, False)

    @pl.when(jnp.logical_not(low))
    def _():
        enter(got_a, True)

    @pl.when(jnp.logical_and(low, here > 0))
    def _():
        enter(got_b, True)

    @pl.when(jnp.logical_and(jnp.logical_not(low), here < n_span - 1))
    def _():
        enter(got_b, False)

    plen_copy = pltpu.make_async_copy(plen, plen_out, sems.at[0])
    plen_copy.start()
    bricks = []
    if direct:
        start = 5 * (rows + cs)
        bricks = [(here ^ 1, lambda s, k: got_a[start + s * 5 + k : start + s * 5 + k + 1])]
        for apart, got in zip((2, 3), got_jets):
            bricks.append((here ^ apart, lambda s, k, got=got: got[s, :, k * LANES : (k + 1) * LANES]))
    sums = jet_sums(lambda k: inflow[k], places, bricks)
    for k, q in enumerate(UPWARD):
        for x in range(ca):
            room[q, x, 0:cs] = room[q, x, 0:cs] + sums[k][x * cs : (x + 1) * cs]
    room_copy = pltpu.make_async_copy(room, room_out, sems.at[1])
    room_copy.start()
    plen_copy.wait()
    room_copy.wait()


def call(kernel, outs, in_specs, out_specs=None, scratch=(), aliases={}, flops=100_000, moved=1_000_000):
    return pl.pallas_call(
        kernel,
        name=kernel.func.__name__,
        out_shape=outs,
        in_specs=in_specs,
        out_specs=[VMEM] * len(outs) if out_specs is None else out_specs,
        scratch_shapes=list(scratch),
        input_output_aliases=aliases,
        cost_estimate=pl.CostEstimate(flops=flops, bytes_accessed=moved, transcendentals=0),
        compiler_params=pltpu.CompilerParams(vmem_limit_bytes=40 * 2**20),
    )


def swap_aisle(value, odd):
    count = lax.axis_size("aisle")
    pairs = [(i, (i ^ 1 if not odd else i + 1 if i % 2 else i - 1) % count) for i in range(count)]
    return lax.ppermute(value, "aisle", pairs)


def swap_span(value, odd):
    count = lax.axis_size("span")
    pairs = []
    for a in range(lax.axis_size("aisle")):
        for s in range(count):
            t = s ^ 1 if not odd else s + 1 if s % 2 else s - 1
            b, t = (a, t) if 0 <= t < count else (a ^ 1, s)
            pairs.append((a * count + s, b * count + t))
    return lax.ppermute(value, ("aisle", "span"), pairs)


def shards(room_pops, plenum_pops, tile_cell, tile_owner, tile_class):
    n_span = lax.axis_size("span")
    _, ca, cs, hr = room_pops.shape
    hp = plenum_pops.shape[3]
    blocks = hr // LANES
    rows = blocks * cs
    tiles = tile_cell.shape[0]
    sizes = (ca, cs, blocks, n_span, tiles // n_span)
    direct = n_span == 4
    near = lambda shape: pltpu.VMEM(shape, F32)
    far = lambda value: pltpu.with_memory_space_constraint(value, pltpu.HBM)
    room_shape, plen_shape = (19, ca, rows, LANES), (19, ca * cs, LANES)
    halo = 5 * (rows + cs)
    halo = halo + -halo % 8
    room = far(room_pops.reshape(19, ca, cs, blocks, LANES).transpose(0, 1, 3, 2, 4).reshape(room_shape))
    plen = far(plenum_pops.reshape(plen_shape))
    tile_cell, tile_owner, tile_class = far(tile_cell), far(tile_owner.reshape(tiles)), far(tile_class)
    numbers = pltpu.SMEM((tiles,), jnp.int32)

    dealt_shape = (n_span * CAP, 1, 5 * hp)
    jet_shapes = [near((count, 1, 5 * hp)) for count in ((CAP + 1, CAP) if direct else ())]
    room_post, plen_post, swap_a, swap_b, dealt = call(
        functools.partial(collide_kernel, sizes, direct),
        [near(room_shape), near(plen_shape), near((halo, LANES)), near((halo + 8, LANES)),
         near(dealt_shape)],
        [HBM] * 5,
        scratch=[near((ca * cs, 1, 5 * hp)), near(plen_shape), numbers, numbers, numbers,
                 pltpu.SemaphoreType.DMA((4 + ca,))],
    )(room, plen, tile_cell, tile_owner, tile_class)
    got_b = swap_aisle(swap_b, True)
    got_a = swap_aisle(swap_a, False)

    upto8 = lambda count: count + -count % 8
    wide = upto8(5 * (rows + ca) + (5 * CAP if direct else 0))
    cross_shapes = [near((wide, LANES)), near((wide + 8, LANES))]
    room_post, part_a, part_b, *jets = call(
        functools.partial(early_kernel, sizes, direct),
        [near(room_shape)] + cross_shapes + jet_shapes,
        [VMEM] * 3,
        aliases={0: 0},
    )(room_post, plen_post, dealt)
    if direct:
        own_jets = dealt
        got_jets = [lax.ppermute(jets[apart - 2], "span", [(i, i ^ apart) for i in range(4)]) for apart in (2, 3)]
    else:
        own_jets = lax.all_to_all(dealt, "span", 0, 0, tiled=True)
        got_jets = []
    room_post, part_a, part_b = call(
        functools.partial(late_kernel, sizes, direct),
        [near(room_shape)] + cross_shapes,
        [VMEM] * 5,
        aliases={0: 0, 3: 1, 4: 2},
    )(room_post, plen_post, dealt, part_a, part_b)
    cross_a, cross_b = call(
        functools.partial(pack_kernel, sizes),
        cross_shapes,
        [VMEM] * 4,
    )(got_a, got_b, part_a, part_b)
    in_a = swap_span(cross_a, False)
    in_b = swap_span(cross_b, True)

    room_part, plen_part, places = call(
        functools.partial(local_kernel, sizes),
        [near(room_shape), near(plen_shape), near((n_span * CAP + 1, ca * cs, LANES))],
        [VMEM, VMEM, VMEM, HBM, HBM],
        scratch=[numbers, numbers, pltpu.SemaphoreType.DMA((2,))],
        flops=10**9,
    )(room_post, plen_post, cross_a, tile_cell, tile_owner)
    room_part, plen_part, inflow = call(
        functools.partial(aisle_kernel, sizes, direct),
        [near(room_shape), near(plen_shape), near((5, ca * cs, LANES))],
        [VMEM] * 6,
        aliases={0: 0, 1: 1},
    )(room_part, plen_part, got_a, got_b, own_jets, places)

    _, _, room_next, plenum_next = call(
        functools.partial(finish_kernel, sizes, direct),
        [near(room_shape), near(plen_shape), jax.ShapeDtypeStruct(room_shape, F32),
         jax.ShapeDtypeStruct(plen_shape, F32)],
        [VMEM] * (6 + len(got_jets)),
        out_specs=[VMEM, VMEM, HBM, HBM],
        scratch=[pltpu.SemaphoreType.DMA((2,))],
        aliases={0: 0, 1: 1},
    )(room_part, plen_part, in_a, in_b, places, inflow, *got_jets)
    room_next = room_next.reshape(19, ca, blocks, cs, LANES).transpose(0, 1, 3, 2, 4).reshape(room_pops.shape)
    return room_next, plenum_next.reshape(plenum_pops.shape)


def solution(mesh):
    return jax.shard_map(
        shards,
        mesh=mesh,
        in_specs=(
            P(None, "aisle", "span", None),
            P(None, "aisle", "span", None),
            P("aisle"),
            P("aisle", None),
            P("aisle"),
        ),
        out_specs=(P(None, "aisle", "span", None), P(None, "aisle", "span", None)),
        check_vma=False,
    )
```

```python
import functools

import jax
import jax.numpy as jnp
from jax import lax
from jax.experimental import pallas as pl
from jax.experimental.pallas import tpu as pltpu
from jax.sharding import PartitionSpec as P

VELOCITIES = [
    (0, 0, 0),
    (1, 0, 0),
    (-1, 0, 0),
    (0, 1, 0),
    (0, -1, 0),
    (0, 0, 1),
    (0, 0, -1),
    (1, 1, 0),
    (-1, -1, 0),
    (1, -1, 0),
    (-1, 1, 0),
    (1, 0, 1),
    (-1, 0, -1),
    (1, 0, -1),
    (-1, 0, 1),
    (0, 1, 1),
    (0, -1, -1),
    (0, 1, -1),
    (0, -1, 1),
]
UPWARD = [5, 11, 14, 15, 18]
OMEGA = 1.25
CAP = 4
X_UP = [q for q in range(19) if VELOCITIES[q][0] == 1]
X_DOWN = [q for q in range(19) if VELOCITIES[q][0] == -1]
Y_UP = [q for q in range(19) if VELOCITIES[q][1] == 1]
Y_DOWN = [q for q in range(19) if VELOCITIES[q][1] == -1]
F32 = jnp.float32
LANES = 128
VMEM = pl.BlockSpec(memory_space=pltpu.VMEM)
HBM = pl.BlockSpec(memory_space=pltpu.HBM)


def collide(g):
    total = lambda i: g[i] + g[i + 1]
    apart = lambda i: g[i] - g[i + 1]
    dx, dy, dz = apart(1), apart(3), apart(5)
    d7, d9, d11, d13, d15, d17 = (apart(i) for i in (7, 9, 11, 13, 15, 17))
    edges = (total(7) + total(9)) + (total(11) + total(13)) + (total(15) + total(17))
    faces = total(1) + total(3) + total(5)
    rho = g[0] * (1.0 / 3.0) + faces * (1.0 / 18.0) + edges * (1.0 / 36.0)
    mx = dx * (1.0 / 18.0) + ((d7 + d9) + (d11 + d13)) * (1.0 / 36.0)
    my = dy * (1.0 / 18.0) + ((d7 - d9) + (d15 + d17)) * (1.0 / 36.0)
    mz = dz * (1.0 / 18.0) + ((d11 - d13) + (d15 - d17)) * (1.0 / 36.0)
    inv = 1.0 / rho
    base = OMEGA * rho - (1.5 * OMEGA) * inv * (mx * mx + my * my + mz * mz)
    square = (4.5 * OMEGA) * inv
    out = [None] * 19
    out[0] = base + (1.0 - OMEGA) * g[0]
    along = {1: mx, 3: my, 5: mz, 7: mx + my, 9: mx - my, 11: mx + mz, 13: mx - mz, 15: my + mz, 17: my - mz}
    for i, c in along.items():
        even = base + square * c * c
        odd = (3.0 * OMEGA) * c
        out[i] = (even + odd) + (1.0 - OMEGA) * g[i]
        out[i + 1] = (even - odd) + (1.0 - OMEGA) * g[i + 1]
    return out


def raised(value, cz, rows):
    if cz == 0:
        return value
    lane = lax.broadcasted_iota(jnp.int32, value.shape, 1)
    row = lax.broadcasted_iota(jnp.int32, value.shape, 0)
    total = value.shape[0]
    shift, edge = (1, 0) if cz == 1 else (LANES - 1, LANES - 1)
    turned = pltpu.roll(value, shift, 1)
    if rows == total:
        return jnp.where(lane == edge, value, turned)
    carried = pltpu.roll(turned, rows if cz == 1 else total - rows, 0)
    clamped = row < rows if cz == 1 else row >= total - rows
    return jnp.where(lane == edge, jnp.where(clamped, value, carried), turned)


def crossed(value, cy, cs):
    if cy == 0:
        return value
    row = lax.broadcasted_iota(jnp.int32, value.shape, 0) % cs
    turned = pltpu.roll(value, 1 if cy == 1 else value.shape[0] - 1, 0)
    return jnp.where(row == (0 if cy == 1 else cs - 1), value, turned)


def shifted(value, by):
    return pltpu.roll(value, by % value.shape[0], 0) if by else value


def turned_to(value, source, dest):
    return shifted(value, dest - source)


def repeat(count, body, start):
    if count > 8:
        return lax.fori_loop(0, count, body, start)
    for i in range(count):
        start = body(i, start)
    return start


def collide_plane(room, x):
    for r in range(0, room.shape[2], 8):
        post = collide([room[q, x, r : r + 8] for q in range(19)])
        for q in range(19):
            room[q, x, r : r + 8] = post[q]


def collide_kernel(sizes, direct, room_in, plen_in, cell_in, owner_in, class_in, room_post, plen_post, swap_a, swap_b,
                   dealt, columns, plen_buf, cells, owners, classes, sems):
    ca, cs, blocks, n_span, per_brick = sizes
    rows = blocks * cs
    copies = [pltpu.make_async_copy(src, dst, sems.at[i]) for i, (src, dst) in enumerate(
        ((plen_in, plen_buf), (cell_in, cells), (owner_in, owners), (class_in, classes)))]
    order = [0, ca - 1] + list(range(1, ca - 1))
    planes = [pltpu.make_async_copy(room_in.at[:, x], room_post.at[:, x], sems.at[4 + x]) for x in order]
    for copy in copies[1:] + copies[:1] + planes:
        copy.start()
    dealt[...] = jnp.zeros_like(dealt)
    for copy in copies[1:4]:
        copy.wait()
    here = lax.axis_index("span")
    first = here * per_brick

    def deal(i, slot):
        owner = owners[first + i]
        to = (owner ^ here if direct else owner) * CAP + slot
        return to, 0.15 * (classes[first + i].astype(F32) + 1.0), cells[first + i]

    tiles = []
    if direct:
        named = [owners[first + i] for i in range(per_brick)]
        for i in range(per_brick):
            tiles.append(deal(i, sum([(named[j] == named[i]).astype(jnp.int32) for j in range(i)], jnp.int32(0))))
    copies[0].wait()
    for r in range(0, ca * cs, 8):
        post = collide([plen_buf[q, r : r + 8] for q in range(19)])
        for q in range(19):
            plen_post[q, r : r + 8] = post[q]
        for k, q in enumerate(UPWARD):
            for y in range(8):
                columns[r + y, :, k * LANES : (k + 1) * LANES] = post[q][y : y + 1]
    for to, share, cell in tiles:
        dealt[to] = share * columns[cell]

    def send_jet(i, carry):
        same = lambda j, n: n + (owners[first + j] == owners[first + i]).astype(jnp.int32)
        to, share, cell = deal(i, lax.fori_loop(0, i, same, 0))
        dealt[to] = share * columns[cell]
        return carry

    if not direct:
        lax.fori_loop(0, per_brick, send_jet, 0)

    for i in range(2):
        planes[i].wait()
        collide_plane(room_post, order[i])
    even = lax.axis_index("aisle") % 2 == 0
    for k in range(5):
        up, down = X_UP[k], X_DOWN[k]
        rising = raised(room_post[up, ca - 1], VELOCITIES[up][2], cs)
        falling = raised(room_post[down, 0], VELOCITIES[down][2], cs)
        swap_a[k * rows : (k + 1) * rows] = jnp.where(even, rising, falling)
        swap_b[k * rows : (k + 1) * rows] = jnp.where(even, falling, rising)
        rising = raised(plen_post[up, (ca - 1) * cs : ca * cs], VELOCITIES[up][2], cs)
        falling = raised(plen_post[down, 0:cs], VELOCITIES[down][2], cs)
        low = 5 * rows + k * cs
        swap_a[low : low + cs] = jnp.where(even, rising, falling)
        swap_b[low : low + cs] = jnp.where(even, falling, rising)
    for i in range(2, ca):
        planes[i].wait()


def jet_sums(start, places, bricks):
    sums = [start(k) for k in range(5)]
    for b, jet in bricks:
        for s in range(CAP):
            marks = places[b * CAP + s]
            sums = [total + marks * jet(s, k) for k, total in enumerate(sums)]
    return sums


def local_kernel(sizes, room_post, plen_post, crossing, cell_in, owner_in, room_part, plen_part, places, cells, owners,
                 sems):
    del crossing
    ca, cs, blocks, n_span, per_brick = sizes
    rows = blocks * cs
    copies = [pltpu.make_async_copy(src, dst, sems.at[i]) for i, (src, dst) in enumerate(
        ((cell_in, cells), (owner_in, owners)))]
    for copy in copies:
        copy.start()
    for q in range(19):
        cx, cy, cz = VELOCITIES[q]
        for x in range(ca):
            if 0 <= x - cx < ca:
                room_part[q, x] = crossed(raised(room_post[q, x - cx], cz, cs), cy, cs)
        plen_part[q] = crossed(shifted(raised(plen_post[q], cz, ca * cs), cx * cs), cy, cs)
    places[0 : n_span * CAP] = jnp.zeros((n_span * CAP, ca * cs, LANES), F32)
    here = lax.axis_index("span")
    row = lax.broadcasted_iota(jnp.int32, (ca * cs, LANES), 0)
    for copy in copies:
        copy.wait()

    def brick(b, carry):
        def place(i, slot):
            t = b * per_brick + i
            mine = owners[t] == here
            places[jnp.where(mine, b * CAP + slot, n_span * CAP)] = (row == cells[t]).astype(F32)
            return slot + mine.astype(jnp.int32)

        repeat(per_brick, place, 0)
        return carry

    repeat(n_span, brick, 0)


def inner(sizes, direct, room_post, plen_post, jets, cross_a, cross_b):
    ca, cs, blocks, n_span, per_brick = sizes
    rows = blocks * cs
    low = lax.axis_index("span") % 2 == 0
    group = lax.broadcasted_iota(jnp.int32, (rows, LANES), 0) % cs
    for x in range(1, ca - 1):
        collide_plane(room_post, x)
    for k in range(5):
        sides, near = [], []
        for q, edge in ((Y_UP[k], cs - 1), (Y_DOWN[k], 0)):
            cx, cy, cz = VELOCITIES[q]
            packed = None
            for x in range(max(cx, 0), ca + min(cx, 0)):
                ready = turned_to(raised(room_post[q, x - cx], cz, cs), edge, x)
                packed = ready if packed is None else jnp.where(group == x, ready, packed)
            sides.append(packed)
            near.append(shifted(raised(plen_post[q], cz, ca * cs), cx * cs - edge))
        cross_a[k * rows : (k + 1) * rows] = jnp.where(low, sides[0], sides[1])
        cross_b[k * rows : (k + 1) * rows] = jnp.where(low, sides[1], sides[0])
        first, second = jnp.where(low, near[0], near[1]), jnp.where(low, near[1], near[0])
        for x in range(ca):
            to = 5 * rows + k * ca + x
            cross_a[to : to + 1] = first[x * cs : x * cs + 1]
            cross_b[to : to + 1] = second[x * cs : x * cs + 1]
    if direct:
        for s in range(CAP):
            for k in range(5):
                to = 5 * (rows + ca) + s * 5 + k
                cross_a[to : to + 1] = jets[CAP + s, :, k * LANES : (k + 1) * LANES]


def early_kernel(sizes, direct, room_in, plen_post, dealt, room_post, cross_a, cross_b, *jets):
    start = 2 * CAP
    for jet in jets:
        jet[0:CAP] = dealt[start : start + CAP]
        start = start + CAP

    @pl.when(lax.axis_index("span") == 0)
    def _():
        inner(sizes, direct, room_post, plen_post, dealt, cross_a, cross_b)


def late_kernel(sizes, direct, room_in, plen_post, dealt, a_in, b_in, room_post, cross_a, cross_b):
    @pl.when(lax.axis_index("span") > 0)
    def _():
        inner(sizes, direct, room_post, plen_post, dealt, cross_a, cross_b)


def corners(cs, up):
    return [q for q in (Y_UP if up else Y_DOWN) if VELOCITIES[q][0]], cs - 1 if up else 0


def pack_kernel(sizes, got_a, got_b, part_a, part_b, cross_a, cross_b):
    ca, cs, blocks, n_span, per_brick = sizes
    rows = blocks * cs
    even = lax.axis_index("aisle") % 2 == 0
    low = lax.axis_index("span") % 2 == 0
    group = lax.broadcasted_iota(jnp.int32, (rows, LANES), 0) % cs
    cross_a[...] = part_a[...]
    cross_b[...] = part_b[...]

    def came(q, low, high):
        if VELOCITIES[q][0] == 1:
            return jnp.where(even, got_b[low:high], got_a[low:high])
        return jnp.where(even, got_a[low:high], got_b[low:high])

    def complete(cross, up):
        two, edge = corners(cs, up)
        for q in two:
            slot = (X_UP if VELOCITIES[q][0] == 1 else X_DOWN).index(q)
            x = 0 if VELOCITIES[q][0] == 1 else ca - 1
            k = (Y_UP if up else Y_DOWN).index(q)
            column = turned_to(came(q, slot * rows, (slot + 1) * rows), edge, x)
            cross[k * rows : (k + 1) * rows] = jnp.where(group == x, column, cross[k * rows : (k + 1) * rows])
            at, to = 5 * rows + slot * cs + edge, 5 * rows + k * ca + x
            cross[to : to + 1] = came(q, at, at + 1)

    @pl.when(low)
    def _():
        complete(cross_a, True)
        complete(cross_b, False)

    @pl.when(jnp.logical_not(low))
    def _():
        complete(cross_a, False)
        complete(cross_b, True)


def aisle_kernel(sizes, direct, room_in, plen_in, got_a, got_b, jets, places, room, plen, inflow):
    ca, cs, blocks, n_span, per_brick = sizes
    rows = blocks * cs
    even = lax.axis_index("aisle") % 2 == 0
    for k in range(5):
        for q, x, first, second in ((X_UP[k], 0, got_b, got_a), (X_DOWN[k], ca - 1, got_a, got_b)):
            cy = VELOCITIES[q][1]
            low, high = k * rows, (k + 1) * rows
            room[q, x] = crossed(jnp.where(even, first[low:high], second[low:high]), cy, cs)
            low = 5 * rows + k * cs
            value = jnp.where(even, first[low : low + cs], second[low : low + cs])
            at = x * cs
            if cy == 1:
                plen[q, at : at + 1] = value[0:1]
                plen[q, at + 1 : at + cs] = value[: cs - 1]
            elif cy == -1:
                plen[q, at + cs - 1 : at + cs] = value[cs - 1 : cs]
                plen[q, at : at + cs - 1] = value[1:cs]
            else:
                plen[q, at : at + cs] = value
    here = lax.axis_index("span")

    def put(sums):
        for k in range(5):
            inflow[k] = sums[k]

    def reader(source, b):
        return lambda s, k: source[b * CAP + s, :, k * LANES : (k + 1) * LANES]

    if direct:
        put(jet_sums(lambda k: jnp.zeros((ca * cs, LANES), F32), places,
                     [(here, reader(jets, 0))]))
    else:
        inflow[...] = jnp.zeros_like(inflow)

        def add_brick(b, carry):
            put(jet_sums(lambda k: inflow[k], places, [(b, reader(jets, b))]))
            return carry

        lax.fori_loop(0, n_span, add_brick, 0)


def finish_kernel(sizes, direct, room_in, plen_in, got_a, got_b, places, inflow, *rest):
    *got_jets, room, plen, room_out, plen_out, sems = rest
    ca, cs, blocks, n_span, per_brick = sizes
    rows = blocks * cs
    here = lax.axis_index("span")
    low = here % 2 == 0
    group = lax.broadcasted_iota(jnp.int32, (rows, LANES), 0) % cs

    def enter(got, up):
        planes, y = (Y_UP, 0) if up else (Y_DOWN, cs - 1)
        for k, q in enumerate(planes):
            came = got[k * rows : (k + 1) * rows]
            for x in range(ca):
                room[q, x] = jnp.where(group == y, turned_to(came, x, y), room[q, x])
                at = 5 * rows + k * ca + x
                plen[q, x * cs + y : x * cs + y + 1] = got[at : at + 1]

    @pl.when(low)
    def _():
        enter(got_a, False)

    @pl.when(jnp.logical_not(low))
    def _():
        enter(got_a, True)

    @pl.when(jnp.logical_and(low, here > 0))
    def _():
        enter(got_b, True)

    @pl.when(jnp.logical_and(jnp.logical_not(low), here < n_span - 1))
    def _():
        enter(got_b, False)

    plen_copy = pltpu.make_async_copy(plen, plen_out, sems.at[0])
    plen_copy.start()
    bricks = []
    if direct:
        start = 5 * (rows + cs)
        bricks = [(here ^ 1, lambda s, k: got_a[start + s * 5 + k : start + s * 5 + k + 1])]
        for apart, got in zip((2, 3), got_jets):
            bricks.append((here ^ apart, lambda s, k, got=got: got[s, :, k * LANES : (k + 1) * LANES]))
    sums = jet_sums(lambda k: inflow[k], places, bricks)
    for k, q in enumerate(UPWARD):
        for x in range(ca):
            room[q, x, 0:cs] = room[q, x, 0:cs] + sums[k][x * cs : (x + 1) * cs]
    room_copy = pltpu.make_async_copy(room, room_out, sems.at[1])
    room_copy.start()
    plen_copy.wait()
    room_copy.wait()


def call(kernel, outs, in_specs, out_specs=None, scratch=(), aliases={}, flops=100_000, moved=1_000_000):
    return pl.pallas_call(
        kernel,
        name=kernel.func.__name__,
        out_shape=outs,
        in_specs=in_specs,
        out_specs=[VMEM] * len(outs) if out_specs is None else out_specs,
        scratch_shapes=list(scratch),
        input_output_aliases=aliases,
        cost_estimate=pl.CostEstimate(flops=flops, bytes_accessed=moved, transcendentals=0),
        compiler_params=pltpu.CompilerParams(vmem_limit_bytes=40 * 2**20),
    )


def swap_aisle(value, odd):
    count = lax.axis_size("aisle")
    pairs = [(i, (i ^ 1 if not odd else i + 1 if i % 2 else i - 1) % count) for i in range(count)]
    return lax.ppermute(value, "aisle", pairs)


def swap_span(value, odd):
    count = lax.axis_size("span")
    pairs = []
    for a in range(lax.axis_size("aisle")):
        for s in range(count):
            t = s ^ 1 if not odd else s + 1 if s % 2 else s - 1
            b, t = (a, t) if 0 <= t < count else (a ^ 1, s)
            pairs.append((a * count + s, b * count + t))
    return lax.ppermute(value, ("aisle", "span"), pairs)


def shards(room_pops, plenum_pops, tile_cell, tile_owner, tile_class):
    n_span = lax.axis_size("span")
    _, ca, cs, hr = room_pops.shape
    hp = plenum_pops.shape[3]
    blocks = hr // LANES
    rows = blocks * cs
    tiles = tile_cell.shape[0]
    sizes = (ca, cs, blocks, n_span, tiles // n_span)
    direct = n_span == 4
    near = lambda shape: pltpu.VMEM(shape, F32)
    far = lambda value: pltpu.with_memory_space_constraint(value, pltpu.HBM)
    room_shape, plen_shape = (19, ca, rows, LANES), (19, ca * cs, LANES)
    halo = 5 * (rows + cs)
    halo = halo + -halo % 8
    room = far(room_pops.reshape(19, ca, cs, blocks, LANES).transpose(0, 1, 3, 2, 4).reshape(room_shape))
    plen = far(plenum_pops.reshape(plen_shape))
    tile_cell, tile_owner, tile_class = far(tile_cell), far(tile_owner.reshape(tiles)), far(tile_class)
    numbers = pltpu.SMEM((tiles,), jnp.int32)

    dealt_shape = (n_span * CAP, 1, 5 * hp)
    jet_shapes = [near((count, 1, 5 * hp)) for count in ((CAP + 1, CAP) if direct else ())]
    room_post, plen_post, swap_a, swap_b, dealt = call(
        functools.partial(collide_kernel, sizes, direct),
        [near(room_shape), near(plen_shape), near((halo, LANES)), near((halo + 8, LANES)),
         near(dealt_shape)],
        [HBM] * 5,
        scratch=[near((ca * cs, 1, 5 * hp)), near(plen_shape), numbers, numbers, numbers,
                 pltpu.SemaphoreType.DMA((4 + ca,))],
    )(room, plen, tile_cell, tile_owner, tile_class)
    got_b = swap_aisle(swap_b, True)
    got_a = swap_aisle(swap_a, False)

    upto8 = lambda count: count + -count % 8
    wide = upto8(5 * (rows + ca) + (5 * CAP if direct else 0))
    cross_shapes = [near((wide, LANES)), near((wide + 8, LANES))]
    room_post, part_a, part_b, *jets = call(
        functools.partial(early_kernel, sizes, direct),
        [near(room_shape)] + cross_shapes + jet_shapes,
        [VMEM] * 3,
        aliases={0: 0},
    )(room_post, plen_post, dealt)
    if direct:
        own_jets = dealt
        got_jets = [lax.ppermute(jets[apart - 2], "span", [(i, i ^ apart) for i in range(4)]) for apart in (2, 3)]
    else:
        own_jets = lax.all_to_all(dealt, "span", 0, 0, tiled=True)
        got_jets = []
    room_post, part_a, part_b = call(
        functools.partial(late_kernel, sizes, direct),
        [near(room_shape)] + cross_shapes,
        [VMEM] * 5,
        aliases={0: 0, 3: 1, 4: 2},
    )(room_post, plen_post, dealt, part_a, part_b)
    cross_a, cross_b = call(
        functools.partial(pack_kernel, sizes),
        cross_shapes,
        [VMEM] * 4,
    )(got_a, got_b, part_a, part_b)
    in_a = swap_span(cross_a, False)
    in_b = swap_span(cross_b, True)

    room_part, plen_part, places = call(
        functools.partial(local_kernel, sizes),
        [near(room_shape), near(plen_shape), near((n_span * CAP + 1, ca * cs, LANES))],
        [VMEM, VMEM, VMEM, HBM, HBM],
        scratch=[numbers, numbers, pltpu.SemaphoreType.DMA((2,))],
        flops=10**9,
    )(room_post, plen_post, cross_a, tile_cell, tile_owner)
    room_part, plen_part, inflow = call(
        functools.partial(aisle_kernel, sizes, direct),
        [near(room_shape), near(plen_shape), near((5, ca * cs, LANES))],
        [VMEM] * 6,
        aliases={0: 0, 1: 1},
    )(room_part, plen_part, got_a, got_b, own_jets, places)

    _, _, room_next, plenum_next = call(
        functools.partial(finish_kernel, sizes, direct),
        [near(room_shape), near(plen_shape), jax.ShapeDtypeStruct(room_shape, F32),
         jax.ShapeDtypeStruct(plen_shape, F32)],
        [VMEM] * (6 + len(got_jets)),
        out_specs=[VMEM, VMEM, HBM, HBM],
        scratch=[pltpu.SemaphoreType.DMA((2,))],
        aliases={0: 0, 1: 1},
    )(room_part, plen_part, in_a, in_b, places, inflow, *got_jets)
    room_next = room_next.reshape(19, ca, blocks, cs, LANES).transpose(0, 1, 3, 2, 4).reshape(room_pops.shape)
    return room_next, plenum_next.reshape(plenum_pops.shape)


def solution(mesh):
    return jax.shard_map(
        shards,
        mesh=mesh,
        in_specs=(
            P(None, "aisle", "span", None),
            P(None, "aisle", "span", None),
            P("aisle"),
            P("aisle", None),
            P("aisle"),
        ),
        out_specs=(P(None, "aisle", "span", None), P(None, "aisle", "span", None)),
        check_vma=False,
    )
```

```python
import functools

import jax
import jax.numpy as jnp
from jax import lax
from jax.experimental import pallas as pl
from jax.experimental.pallas import tpu as pltpu
from jax.sharding import PartitionSpec as P

VELOCITIES = [
    (0, 0, 0),
    (1, 0, 0),
    (-1, 0, 0),
    (0, 1, 0),
    (0, -1, 0),
    (0, 0, 1),
    (0, 0, -1),
    (1, 1, 0),
    (-1, -1, 0),
    (1, -1, 0),
    (-1, 1, 0),
    (1, 0, 1),
    (-1, 0, -1),
    (1, 0, -1),
    (-1, 0, 1),
    (0, 1, 1),
    (0, -1, -1),
    (0, 1, -1),
    (0, -1, 1),
]
UPWARD = [5, 11, 14, 15, 18]
OMEGA = 1.25
CAP = 4
X_UP = [q for q in range(19) if VELOCITIES[q][0] == 1]
X_DOWN = [q for q in range(19) if VELOCITIES[q][0] == -1]
Y_UP = [q for q in range(19) if VELOCITIES[q][1] == 1]
Y_DOWN = [q for q in range(19) if VELOCITIES[q][1] == -1]
F32 = jnp.float32
LANES = 128
VMEM = pl.BlockSpec(memory_space=pltpu.VMEM)
HBM = pl.BlockSpec(memory_space=pltpu.HBM)


def collide(g):
    total = lambda i: g[i] + g[i + 1]
    apart = lambda i: g[i] - g[i + 1]
    dx, dy, dz = apart(1), apart(3), apart(5)
    d7, d9, d11, d13, d15, d17 = (apart(i) for i in (7, 9, 11, 13, 15, 17))
    edges = (total(7) + total(9)) + (total(11) + total(13)) + (total(15) + total(17))
    faces = total(1) + total(3) + total(5)
    rho = g[0] * (1.0 / 3.0) + faces * (1.0 / 18.0) + edges * (1.0 / 36.0)
    mx = dx * (1.0 / 18.0) + ((d7 + d9) + (d11 + d13)) * (1.0 / 36.0)
    my = dy * (1.0 / 18.0) + ((d7 - d9) + (d15 + d17)) * (1.0 / 36.0)
    mz = dz * (1.0 / 18.0) + ((d11 - d13) + (d15 - d17)) * (1.0 / 36.0)
    inv = 1.0 / rho
    base = OMEGA * rho - (1.5 * OMEGA) * inv * (mx * mx + my * my + mz * mz)
    square = (4.5 * OMEGA) * inv
    out = [None] * 19
    out[0] = base + (1.0 - OMEGA) * g[0]
    along = {1: mx, 3: my, 5: mz, 7: mx + my, 9: mx - my, 11: mx + mz, 13: mx - mz, 15: my + mz, 17: my - mz}
    for i, c in along.items():
        even = base + square * c * c
        odd = (3.0 * OMEGA) * c
        out[i] = (even + odd) + (1.0 - OMEGA) * g[i]
        out[i + 1] = (even - odd) + (1.0 - OMEGA) * g[i + 1]
    return out


def raised(value, cz, rows):
    if cz == 0:
        return value
    lane = lax.broadcasted_iota(jnp.int32, value.shape, 1)
    row = lax.broadcasted_iota(jnp.int32, value.shape, 0)
    total = value.shape[0]
    shift, edge = (1, 0) if cz == 1 else (LANES - 1, LANES - 1)
    turned = pltpu.roll(value, shift, 1)
    if rows == total:
        return jnp.where(lane == edge, value, turned)
    carried = pltpu.roll(turned, rows if cz == 1 else total - rows, 0)
    clamped = row < rows if cz == 1 else row >= total - rows
    return jnp.where(lane == edge, jnp.where(clamped, value, carried), turned)


def crossed(value, cy, cs):
    if cy == 0:
        return value
    row = lax.broadcasted_iota(jnp.int32, value.shape, 0) % cs
    turned = pltpu.roll(value, 1 if cy == 1 else value.shape[0] - 1, 0)
    return jnp.where(row == (0 if cy == 1 else cs - 1), value, turned)


def shifted(value, by):
    return pltpu.roll(value, by % value.shape[0], 0) if by else value


def turned_to(value, source, dest):
    return shifted(value, dest - source)


def repeat(count, body, start):
    if count > 8:
        return lax.fori_loop(0, count, body, start)
    for i in range(count):
        start = body(i, start)
    return start


def collide_plane(room, x):
    for r in range(0, room.shape[2], 8):
        post = collide([room[q, x, r : r + 8] for q in range(19)])
        for q in range(19):
            room[q, x, r : r + 8] = post[q]


def collide_kernel(sizes, direct, room_in, plen_in, cell_in, owner_in, class_in, room_post, plen_post, swap_a, swap_b,
                   dealt, plen_buf, cells, owners, classes, sems):
    ca, cs, blocks, n_span, per_brick = sizes
    rows = blocks * cs
    copies = [pltpu.make_async_copy(src, dst, sems.at[i]) for i, (src, dst) in enumerate(
        ((plen_in, plen_buf), (cell_in, cells), (owner_in, owners), (class_in, classes)))]
    order = [0, ca - 1] + list(range(1, ca - 1))
    planes = [pltpu.make_async_copy(room_in.at[:, x], room_post.at[:, x], sems.at[4 + x]) for x in order]
    for copy in copies[1:] + copies[:1] + planes:
        copy.start()
    dealt[...] = jnp.zeros_like(dealt)
    for copy in copies[1:4]:
        copy.wait()
    here = lax.axis_index("span")
    first = here * per_brick

    def deal(i, slot):
        owner = owners[first + i]
        to = (owner ^ here if direct else owner) * CAP + slot
        return to, 0.15 * (classes[first + i].astype(F32) + 1.0), cells[first + i]

    tiles = []
    if direct:
        named = [owners[first + i] for i in range(per_brick)]
        for i in range(per_brick):
            tiles.append(deal(i, sum([(named[j] == named[i]).astype(jnp.int32) for j in range(i)], jnp.int32(0))))
    copies[0].wait()
    for r in range(0, ca * cs, 8):
        post = collide([plen_buf[q, r : r + 8] for q in range(19)])
        for q in range(19):
            plen_post[q, r : r + 8] = post[q]

    def put(to, share, cell):
        for k, q in enumerate(UPWARD):
            dealt[to, :, k * LANES : (k + 1) * LANES] = share * plen_post[q, pl.ds(cell, 1), :]

    for tile in tiles:
        put(*tile)

    def send_jet(i, carry):
        same = lambda j, n: n + (owners[first + j] == owners[first + i]).astype(jnp.int32)
        put(*deal(i, lax.fori_loop(0, i, same, 0)))
        return carry

    if not direct:
        lax.fori_loop(0, per_brick, send_jet, 0)

    for i in range(2):
        planes[i].wait()
        collide_plane(room_post, order[i])
    even = lax.axis_index("aisle") % 2 == 0
    for k in range(5):
        up, down = X_UP[k], X_DOWN[k]
        rising = raised(room_post[up, ca - 1], VELOCITIES[up][2], cs)
        falling = raised(room_post[down, 0], VELOCITIES[down][2], cs)
        swap_a[k * rows : (k + 1) * rows] = jnp.where(even, rising, falling)
        swap_b[k * rows : (k + 1) * rows] = jnp.where(even, falling, rising)
        rising = raised(plen_post[up, (ca - 1) * cs : ca * cs], VELOCITIES[up][2], cs)
        falling = raised(plen_post[down, 0:cs], VELOCITIES[down][2], cs)
        low = 5 * rows + k * cs
        swap_a[low : low + cs] = jnp.where(even, rising, falling)
        swap_b[low : low + cs] = jnp.where(even, falling, rising)
    for i in range(2, ca):
        planes[i].wait()


def jet_sums(start, places, bricks):
    sums = [start(k) for k in range(5)]
    for b, jet in bricks:
        for s in range(CAP):
            marks = places[b * CAP + s]
            sums = [total + marks * jet(s, k) for k, total in enumerate(sums)]
    return sums


def local_kernel(sizes, room_post, plen_post, crossing, cell_in, owner_in, room_part, plen_part, places, cells, owners,
                 sems):
    del crossing
    ca, cs, blocks, n_span, per_brick = sizes
    rows = blocks * cs
    copies = [pltpu.make_async_copy(src, dst, sems.at[i]) for i, (src, dst) in enumerate(
        ((cell_in, cells), (owner_in, owners)))]
    for copy in copies:
        copy.start()
    for q in range(19):
        cx, cy, cz = VELOCITIES[q]
        for x in range(ca):
            if 0 <= x - cx < ca:
                room_part[q, x] = crossed(raised(room_post[q, x - cx], cz, cs), cy, cs)
        plen_part[q] = crossed(shifted(raised(plen_post[q], cz, ca * cs), cx * cs), cy, cs)
    places[0 : n_span * CAP] = jnp.zeros((n_span * CAP, ca * cs, LANES), F32)
    here = lax.axis_index("span")
    row = lax.broadcasted_iota(jnp.int32, (ca * cs, LANES), 0)
    for copy in copies:
        copy.wait()

    def brick(b, carry):
        def place(i, slot):
            t = b * per_brick + i
            mine = owners[t] == here
            places[jnp.where(mine, b * CAP + slot, n_span * CAP)] = (row == cells[t]).astype(F32)
            return slot + mine.astype(jnp.int32)

        repeat(per_brick, place, 0)
        return carry

    repeat(n_span, brick, 0)


def inner(sizes, direct, room_post, plen_post, jets, cross_a, cross_b):
    ca, cs, blocks, n_span, per_brick = sizes
    rows = blocks * cs
    low = lax.axis_index("span") % 2 == 0
    group = lax.broadcasted_iota(jnp.int32, (rows, LANES), 0) % cs
    for x in range(1, ca - 1):
        collide_plane(room_post, x)
    for k in range(5):
        sides, near = [], []
        for q, edge in ((Y_UP[k], cs - 1), (Y_DOWN[k], 0)):
            cx, cy, cz = VELOCITIES[q]
            packed = None
            for x in range(max(cx, 0), ca + min(cx, 0)):
                ready = turned_to(raised(room_post[q, x - cx], cz, cs), edge, x)
                packed = ready if packed is None else jnp.where(group == x, ready, packed)
            sides.append(packed)
            near.append(shifted(raised(plen_post[q], cz, ca * cs), cx * cs - edge))
        cross_a[k * rows : (k + 1) * rows] = jnp.where(low, sides[0], sides[1])
        cross_b[k * rows : (k + 1) * rows] = jnp.where(low, sides[1], sides[0])
        first, second = jnp.where(low, near[0], near[1]), jnp.where(low, near[1], near[0])
        for x in range(ca):
            to = 5 * rows + k * ca + x
            cross_a[to : to + 1] = first[x * cs : x * cs + 1]
            cross_b[to : to + 1] = second[x * cs : x * cs + 1]
    if direct:
        for s in range(CAP):
            for k in range(5):
                to = 5 * (rows + ca) + s * 5 + k
                cross_a[to : to + 1] = jets[CAP + s, :, k * LANES : (k + 1) * LANES]


def early_kernel(sizes, direct, room_in, plen_post, dealt, room_post, cross_a, cross_b, *jets):
    start = 2 * CAP
    for jet in jets:
        jet[0:CAP] = dealt[start : start + CAP]
        start = start + CAP

    @pl.when(lax.axis_index("span") == 0)
    def _():
        inner(sizes, direct, room_post, plen_post, dealt, cross_a, cross_b)


def late_kernel(sizes, direct, room_in, plen_post, dealt, a_in, b_in, room_post, cross_a, cross_b):
    @pl.when(lax.axis_index("span") > 0)
    def _():
        inner(sizes, direct, room_post, plen_post, dealt, cross_a, cross_b)


def corners(cs, up):
    return [q for q in (Y_UP if up else Y_DOWN) if VELOCITIES[q][0]], cs - 1 if up else 0


def pack_kernel(sizes, got_a, got_b, part_a, part_b, cross_a, cross_b):
    ca, cs, blocks, n_span, per_brick = sizes
    rows = blocks * cs
    even = lax.axis_index("aisle") % 2 == 0
    low = lax.axis_index("span") % 2 == 0
    group = lax.broadcasted_iota(jnp.int32, (rows, LANES), 0) % cs
    cross_a[...] = part_a[...]
    cross_b[...] = part_b[...]

    def came(q, low, high):
        if VELOCITIES[q][0] == 1:
            return jnp.where(even, got_b[low:high], got_a[low:high])
        return jnp.where(even, got_a[low:high], got_b[low:high])

    def complete(cross, up):
        two, edge = corners(cs, up)
        for q in two:
            slot = (X_UP if VELOCITIES[q][0] == 1 else X_DOWN).index(q)
            x = 0 if VELOCITIES[q][0] == 1 else ca - 1
            k = (Y_UP if up else Y_DOWN).index(q)
            column = turned_to(came(q, slot * rows, (slot + 1) * rows), edge, x)
            cross[k * rows : (k + 1) * rows] = jnp.where(group == x, column, cross[k * rows : (k + 1) * rows])
            at, to = 5 * rows + slot * cs + edge, 5 * rows + k * ca + x
            cross[to : to + 1] = came(q, at, at + 1)

    @pl.when(low)
    def _():
        complete(cross_a, True)
        complete(cross_b, False)

    @pl.when(jnp.logical_not(low))
    def _():
        complete(cross_a, False)
        complete(cross_b, True)


def aisle_kernel(sizes, direct, room_in, plen_in, got_a, got_b, jets, places, room, plen, inflow):
    ca, cs, blocks, n_span, per_brick = sizes
    rows = blocks * cs
    even = lax.axis_index("aisle") % 2 == 0
    for k in range(5):
        for q, x, first, second in ((X_UP[k], 0, got_b, got_a), (X_DOWN[k], ca - 1, got_a, got_b)):
            cy = VELOCITIES[q][1]
            low, high = k * rows, (k + 1) * rows
            room[q, x] = crossed(jnp.where(even, first[low:high], second[low:high]), cy, cs)
            low = 5 * rows + k * cs
            value = jnp.where(even, first[low : low + cs], second[low : low + cs])
            at = x * cs
            if cy == 1:
                plen[q, at : at + 1] = value[0:1]
                plen[q, at + 1 : at + cs] = value[: cs - 1]
            elif cy == -1:
                plen[q, at + cs - 1 : at + cs] = value[cs - 1 : cs]
                plen[q, at : at + cs - 1] = value[1:cs]
            else:
                plen[q, at : at + cs] = value
    here = lax.axis_index("span")

    def put(sums):
        for k in range(5):
            inflow[k] = sums[k]

    def reader(source, b):
        return lambda s, k: source[b * CAP + s, :, k * LANES : (k + 1) * LANES]

    if direct:
        put(jet_sums(lambda k: jnp.zeros((ca * cs, LANES), F32), places,
                     [(here, reader(jets, 0))]))
    else:
        inflow[...] = jnp.zeros_like(inflow)

        def add_brick(b, carry):
            put(jet_sums(lambda k: inflow[k], places, [(b, reader(jets, b))]))
            return carry

        lax.fori_loop(0, n_span, add_brick, 0)


def finish_kernel(sizes, direct, room_in, plen_in, got_a, got_b, places, inflow, *rest):
    *got_jets, room, plen, room_out, plen_out, sems = rest
    ca, cs, blocks, n_span, per_brick = sizes
    rows = blocks * cs
    here = lax.axis_index("span")
    low = here % 2 == 0
    group = lax.broadcasted_iota(jnp.int32, (rows, LANES), 0) % cs

    def enter(got, up):
        planes, y = (Y_UP, 0) if up else (Y_DOWN, cs - 1)
        for k, q in enumerate(planes):
            came = got[k * rows : (k + 1) * rows]
            for x in range(ca):
                room[q, x] = jnp.where(group == y, turned_to(came, x, y), room[q, x])
                at = 5 * rows + k * ca + x
                plen[q, x * cs + y : x * cs + y + 1] = got[at : at + 1]

    @pl.when(low)
    def _():
        enter(got_a, False)

    @pl.when(jnp.logical_not(low))
    def _():
        enter(got_a, True)

    @pl.when(jnp.logical_and(low, here > 0))
    def _():
        enter(got_b, True)

    @pl.when(jnp.logical_and(jnp.logical_not(low), here < n_span - 1))
    def _():
        enter(got_b, False)

    plen_copy = pltpu.make_async_copy(plen, plen_out, sems.at[0])
    plen_copy.start()
    bricks = []
    if direct:
        start = 5 * (rows + cs)
        bricks = [(here ^ 1, lambda s, k: got_a[start + s * 5 + k : start + s * 5 + k + 1])]
        for apart, got in zip((2, 3), got_jets):
            bricks.append((here ^ apart, lambda s, k, got=got: got[s, :, k * LANES : (k + 1) * LANES]))
    sums = jet_sums(lambda k: inflow[k], places, bricks)
    for k, q in enumerate(UPWARD):
        for x in range(ca):
            room[q, x, 0:cs] = room[q, x, 0:cs] + sums[k][x * cs : (x + 1) * cs]
    room_copy = pltpu.make_async_copy(room, room_out, sems.at[1])
    room_copy.start()
    plen_copy.wait()
    room_copy.wait()


def call(kernel, outs, in_specs, out_specs=None, scratch=(), aliases={}, flops=100_000, moved=1_000_000):
    return pl.pallas_call(
        kernel,
        name=kernel.func.__name__,
        out_shape=outs,
        in_specs=in_specs,
        out_specs=[VMEM] * len(outs) if out_specs is None else out_specs,
        scratch_shapes=list(scratch),
        input_output_aliases=aliases,
        cost_estimate=pl.CostEstimate(flops=flops, bytes_accessed=moved, transcendentals=0),
        compiler_params=pltpu.CompilerParams(vmem_limit_bytes=40 * 2**20),
    )


def swap_aisle(value, odd):
    count = lax.axis_size("aisle")
    pairs = [(i, (i ^ 1 if not odd else i + 1 if i % 2 else i - 1) % count) for i in range(count)]
    return lax.ppermute(value, "aisle", pairs)


def swap_span(value, odd):
    count = lax.axis_size("span")
    pairs = []
    for a in range(lax.axis_size("aisle")):
        for s in range(count):
            t = s ^ 1 if not odd else s + 1 if s % 2 else s - 1
            b, t = (a, t) if 0 <= t < count else (a ^ 1, s)
            pairs.append((a * count + s, b * count + t))
    return lax.ppermute(value, ("aisle", "span"), pairs)


def shards(room_pops, plenum_pops, tile_cell, tile_owner, tile_class):
    n_span = lax.axis_size("span")
    _, ca, cs, hr = room_pops.shape
    hp = plenum_pops.shape[3]
    blocks = hr // LANES
    rows = blocks * cs
    tiles = tile_cell.shape[0]
    sizes = (ca, cs, blocks, n_span, tiles // n_span)
    direct = n_span == 4
    near = lambda shape: pltpu.VMEM(shape, F32)
    far = lambda value: pltpu.with_memory_space_constraint(value, pltpu.HBM)
    room_shape, plen_shape = (19, ca, rows, LANES), (19, ca * cs, LANES)
    halo = 5 * (rows + cs)
    halo = halo + -halo % 8
    room = far(room_pops.reshape(19, ca, cs, blocks, LANES).transpose(0, 1, 3, 2, 4).reshape(room_shape))
    plen = far(plenum_pops.reshape(plen_shape))
    tile_cell, tile_owner, tile_class = far(tile_cell), far(tile_owner.reshape(tiles)), far(tile_class)
    numbers = pltpu.SMEM((tiles,), jnp.int32)

    dealt_shape = (n_span * CAP, 1, 5 * hp)
    jet_shapes = [near((count, 1, 5 * hp)) for count in ((CAP + 1, CAP) if direct else ())]
    room_post, plen_post, swap_a, swap_b, dealt = call(
        functools.partial(collide_kernel, sizes, direct),
        [near(room_shape), near(plen_shape), near((halo, LANES)), near((halo + 8, LANES)),
         near(dealt_shape)],
        [HBM] * 5,
        scratch=[near(plen_shape), numbers, numbers, numbers,
                 pltpu.SemaphoreType.DMA((4 + ca,))],
    )(room, plen, tile_cell, tile_owner, tile_class)
    got_b = swap_aisle(swap_b, True)
    got_a = swap_aisle(swap_a, False)

    upto8 = lambda count: count + -count % 8
    wide = upto8(5 * (rows + ca) + (5 * CAP if direct else 0))
    cross_shapes = [near((wide, LANES)), near((wide + 8, LANES))]
    room_post, part_a, part_b, *jets = call(
        functools.partial(early_kernel, sizes, direct),
        [near(room_shape)] + cross_shapes + jet_shapes,
        [VMEM] * 3,
        aliases={0: 0},
    )(room_post, plen_post, dealt)
    if direct:
        own_jets = dealt
        got_jets = [lax.ppermute(jets[apart - 2], "span", [(i, i ^ apart) for i in range(4)]) for apart in (2, 3)]
    else:
        own_jets = lax.all_to_all(dealt, "span", 0, 0, tiled=True)
        got_jets = []
    room_post, part_a, part_b = call(
        functools.partial(late_kernel, sizes, direct),
        [near(room_shape)] + cross_shapes,
        [VMEM] * 5,
        aliases={0: 0, 3: 1, 4: 2},
    )(room_post, plen_post, dealt, part_a, part_b)
    cross_a, cross_b = call(
        functools.partial(pack_kernel, sizes),
        cross_shapes,
        [VMEM] * 4,
    )(got_a, got_b, part_a, part_b)
    in_a = swap_span(cross_a, False)
    in_b = swap_span(cross_b, True)

    room_part, plen_part, places = call(
        functools.partial(local_kernel, sizes),
        [near(room_shape), near(plen_shape), near((n_span * CAP + 1, ca * cs, LANES))],
        [VMEM, VMEM, VMEM, HBM, HBM],
        scratch=[numbers, numbers, pltpu.SemaphoreType.DMA((2,))],
        flops=10**9,
    )(room_post, plen_post, cross_a, tile_cell, tile_owner)
    room_part, plen_part, inflow = call(
        functools.partial(aisle_kernel, sizes, direct),
        [near(room_shape), near(plen_shape), near((5, ca * cs, LANES))],
        [VMEM] * 6,
        aliases={0: 0, 1: 1},
    )(room_part, plen_part, got_a, got_b, own_jets, places)

    _, _, room_next, plenum_next = call(
        functools.partial(finish_kernel, sizes, direct),
        [near(room_shape), near(plen_shape), jax.ShapeDtypeStruct(room_shape, F32),
         jax.ShapeDtypeStruct(plen_shape, F32)],
        [VMEM] * (6 + len(got_jets)),
        out_specs=[VMEM, VMEM, HBM, HBM],
        scratch=[pltpu.SemaphoreType.DMA((2,))],
        aliases={0: 0, 1: 1},
    )(room_part, plen_part, in_a, in_b, places, inflow, *got_jets)
    room_next = room_next.reshape(19, ca, blocks, cs, LANES).transpose(0, 1, 3, 2, 4).reshape(room_pops.shape)
    return room_next, plenum_next.reshape(plenum_pops.shape)


def solution(mesh):
    return jax.shard_map(
        shards,
        mesh=mesh,
        in_specs=(
            P(None, "aisle", "span", None),
            P(None, "aisle", "span", None),
            P("aisle"),
            P("aisle", None),
            P("aisle"),
        ),
        out_specs=(P(None, "aisle", "span", None), P(None, "aisle", "span", None)),
        check_vma=False,
    )
```

```python
import functools

import jax
import jax.numpy as jnp
from jax import lax
from jax.experimental import pallas as pl
from jax.experimental.pallas import tpu as pltpu
from jax.sharding import PartitionSpec as P

VELOCITIES = [
    (0, 0, 0),
    (1, 0, 0),
    (-1, 0, 0),
    (0, 1, 0),
    (0, -1, 0),
    (0, 0, 1),
    (0, 0, -1),
    (1, 1, 0),
    (-1, -1, 0),
    (1, -1, 0),
    (-1, 1, 0),
    (1, 0, 1),
    (-1, 0, -1),
    (1, 0, -1),
    (-1, 0, 1),
    (0, 1, 1),
    (0, -1, -1),
    (0, 1, -1),
    (0, -1, 1),
]
UPWARD = [5, 11, 14, 15, 18]
OMEGA = 1.25
CAP = 4
X_UP = [q for q in range(19) if VELOCITIES[q][0] == 1]
X_DOWN = [q for q in range(19) if VELOCITIES[q][0] == -1]
Y_UP = [q for q in range(19) if VELOCITIES[q][1] == 1]
Y_DOWN = [q for q in range(19) if VELOCITIES[q][1] == -1]
F32 = jnp.float32
LANES = 128
VMEM = pl.BlockSpec(memory_space=pltpu.VMEM)
HBM = pl.BlockSpec(memory_space=pltpu.HBM)


def collide(g):
    total = lambda i: g[i] + g[i + 1]
    apart = lambda i: g[i] - g[i + 1]
    dx, dy, dz = apart(1), apart(3), apart(5)
    d7, d9, d11, d13, d15, d17 = (apart(i) for i in (7, 9, 11, 13, 15, 17))
    edges = (total(7) + total(9)) + (total(11) + total(13)) + (total(15) + total(17))
    faces = total(1) + total(3) + total(5)
    rho = g[0] * (1.0 / 3.0) + faces * (1.0 / 18.0) + edges * (1.0 / 36.0)
    mx = dx * (1.0 / 18.0) + ((d7 + d9) + (d11 + d13)) * (1.0 / 36.0)
    my = dy * (1.0 / 18.0) + ((d7 - d9) + (d15 + d17)) * (1.0 / 36.0)
    mz = dz * (1.0 / 18.0) + ((d11 - d13) + (d15 - d17)) * (1.0 / 36.0)
    inv = 1.0 / rho
    base = OMEGA * rho - (1.5 * OMEGA) * inv * (mx * mx + my * my + mz * mz)
    square = (4.5 * OMEGA) * inv
    out = [None] * 19
    out[0] = base + (1.0 - OMEGA) * g[0]
    along = {1: mx, 3: my, 5: mz, 7: mx + my, 9: mx - my, 11: mx + mz, 13: mx - mz, 15: my + mz, 17: my - mz}
    for i, c in along.items():
        even = base + square * c * c
        odd = (3.0 * OMEGA) * c
        out[i] = (even + odd) + (1.0 - OMEGA) * g[i]
        out[i + 1] = (even - odd) + (1.0 - OMEGA) * g[i + 1]
    return out


def raised(value, cz, rows):
    if cz == 0:
        return value
    lane = lax.broadcasted_iota(jnp.int32, value.shape, 1)
    row = lax.broadcasted_iota(jnp.int32, value.shape, 0)
    total = value.shape[0]
    shift, edge = (1, 0) if cz == 1 else (LANES - 1, LANES - 1)
    turned = pltpu.roll(value, shift, 1)
    if rows == total:
        return jnp.where(lane == edge, value, turned)
    carried = pltpu.roll(turned, rows if cz == 1 else total - rows, 0)
    clamped = row < rows if cz == 1 else row >= total - rows
    return jnp.where(lane == edge, jnp.where(clamped, value, carried), turned)


def crossed(value, cy, cs):
    if cy == 0:
        return value
    row = lax.broadcasted_iota(jnp.int32, value.shape, 0) % cs
    turned = pltpu.roll(value, 1 if cy == 1 else value.shape[0] - 1, 0)
    return jnp.where(row == (0 if cy == 1 else cs - 1), value, turned)


def shifted(value, by):
    return pltpu.roll(value, by % value.shape[0], 0) if by else value


def turned_to(value, source, dest):
    return shifted(value, dest - source)


def repeat(count, body, start):
    if count > 8:
        return lax.fori_loop(0, count, body, start)
    for i in range(count):
        start = body(i, start)
    return start


def collide_plane(room, x):
    for r in range(0, room.shape[2], 8):
        post = collide([room[q, x, r : r + 8] for q in range(19)])
        for q in range(19):
            room[q, x, r : r + 8] = post[q]


def collide_kernel(sizes, direct, room_in, plen_in, cell_in, owner_in, class_in, room_post, plen_post, swap_a, swap_b,
                   dealt, plen_buf, cells, owners, classes, sems):
    ca, cs, blocks, n_span, per_brick = sizes
    rows = blocks * cs
    copies = [pltpu.make_async_copy(src, dst, sems.at[i]) for i, (src, dst) in enumerate(
        ((plen_in, plen_buf), (cell_in, cells), (owner_in, owners), (class_in, classes)))]
    order = [0, ca - 1] + list(range(1, ca - 1))
    planes = [pltpu.make_async_copy(room_in.at[:, x], room_post.at[:, x], sems.at[4 + x]) for x in order]
    for copy in copies[1:] + copies[:1] + planes:
        copy.start()
    dealt[...] = jnp.zeros_like(dealt)
    for copy in copies[1:4]:
        copy.wait()
    here = lax.axis_index("span")
    first = here * per_brick

    def deal(i, slot):
        owner = owners[first + i]
        to = (owner ^ here if direct else owner) * CAP + slot
        return to, 0.15 * (classes[first + i].astype(F32) + 1.0), cells[first + i]

    tiles = []
    if direct:
        named = [owners[first + i] for i in range(per_brick)]
        for i in range(per_brick):
            tiles.append(deal(i, sum([(named[j] == named[i]).astype(jnp.int32) for j in range(i)], jnp.int32(0))))
    copies[0].wait()
    for r in range(0, ca * cs, 8):
        post = collide([plen_buf[q, r : r + 8] for q in range(19)])
        for q in range(19):
            plen_post[q, r : r + 8] = post[q]

    def put(to, share, cell):
        for k, q in enumerate(UPWARD):
            dealt[to, :, k * LANES : (k + 1) * LANES] = share * plen_post[q, pl.ds(cell, 1), :]

    for tile in tiles:
        put(*tile)

    def send_jet(i, carry):
        same = lambda j, n: n + (owners[first + j] == owners[first + i]).astype(jnp.int32)
        put(*deal(i, lax.fori_loop(0, i, same, 0)))
        return carry

    if not direct:
        lax.fori_loop(0, per_brick, send_jet, 0)

    for i in range(2):
        planes[i].wait()
        collide_plane(room_post, order[i])
    even = lax.axis_index("aisle") % 2 == 0
    for k in range(5):
        up, down = X_UP[k], X_DOWN[k]
        rising = raised(room_post[up, ca - 1], VELOCITIES[up][2], cs)
        falling = raised(room_post[down, 0], VELOCITIES[down][2], cs)
        swap_a[k * rows : (k + 1) * rows] = jnp.where(even, rising, falling)
        swap_b[k * rows : (k + 1) * rows] = jnp.where(even, falling, rising)
        rising = raised(plen_post[up, (ca - 1) * cs : ca * cs], VELOCITIES[up][2], cs)
        falling = raised(plen_post[down, 0:cs], VELOCITIES[down][2], cs)
        low = 5 * rows + k * cs
        swap_a[low : low + cs] = jnp.where(even, rising, falling)
        swap_b[low : low + cs] = jnp.where(even, falling, rising)
    for i in range(2, ca):
        planes[i].wait()


def jet_sums(start, places, bricks):
    sums = [start(k) for k in range(5)]
    for b, jet in bricks:
        for s in range(CAP):
            marks = places[b * CAP + s]
            sums = [total + marks * jet(s, k) for k, total in enumerate(sums)]
    return sums


def local_kernel(sizes, room_post, plen_post, crossing, cell_in, owner_in, room_part, plen_part, places, cells, owners,
                 sems):
    del crossing
    ca, cs, blocks, n_span, per_brick = sizes
    rows = blocks * cs
    copies = [pltpu.make_async_copy(src, dst, sems.at[i]) for i, (src, dst) in enumerate(
        ((cell_in, cells), (owner_in, owners)))]
    for copy in copies:
        copy.start()
    for q in range(19):
        cx, cy, cz = VELOCITIES[q]
        for x in range(ca):
            if 0 <= x - cx < ca:
                room_part[q, x] = crossed(raised(room_post[q, x - cx], cz, cs), cy, cs)
        plen_part[q] = crossed(shifted(raised(plen_post[q], cz, ca * cs), cx * cs), cy, cs)
    places[0 : n_span * CAP] = jnp.zeros((n_span * CAP, ca * cs, LANES), F32)
    here = lax.axis_index("span")
    row = lax.broadcasted_iota(jnp.int32, (ca * cs, LANES), 0)
    for copy in copies:
        copy.wait()

    def brick(b, carry):
        def place(i, slot):
            t = b * per_brick + i
            mine = owners[t] == here
            places[jnp.where(mine, b * CAP + slot, n_span * CAP)] = (row == cells[t]).astype(F32)
            return slot + mine.astype(jnp.int32)

        repeat(per_brick, place, 0)
        return carry

    repeat(n_span, brick, 0)


def inner(sizes, direct, room_post, plen_post, jets, cross_a, cross_b):
    ca, cs, blocks, n_span, per_brick = sizes
    rows = blocks * cs
    low = lax.axis_index("span") % 2 == 0
    group = lax.broadcasted_iota(jnp.int32, (rows, LANES), 0) % cs
    for x in range(1, ca - 1):
        collide_plane(room_post, x)
    for k in range(5):
        sides, near = [], []
        for q, edge in ((Y_UP[k], cs - 1), (Y_DOWN[k], 0)):
            cx, cy, cz = VELOCITIES[q]
            packed = None
            for x in range(max(cx, 0), ca + min(cx, 0)):
                ready = turned_to(raised(room_post[q, x - cx], cz, cs), edge, x)
                packed = ready if packed is None else jnp.where(group == x, ready, packed)
            sides.append(packed)
            near.append(shifted(raised(plen_post[q], cz, ca * cs), cx * cs - edge))
        cross_a[k * rows : (k + 1) * rows] = jnp.where(low, sides[0], sides[1])
        cross_b[k * rows : (k + 1) * rows] = jnp.where(low, sides[1], sides[0])
        first, second = jnp.where(low, near[0], near[1]), jnp.where(low, near[1], near[0])
        for x in range(ca):
            to = 5 * rows + k * ca + x
            cross_a[to : to + 1] = first[x * cs : x * cs + 1]
            cross_b[to : to + 1] = second[x * cs : x * cs + 1]
    if direct:
        for s in range(CAP):
            for k in range(5):
                to = 5 * (rows + ca) + s * 5 + k
                cross_a[to : to + 1] = jets[CAP + s, :, k * LANES : (k + 1) * LANES]


def early_kernel(sizes, direct, room_in, plen_post, dealt, room_post, cross_a, cross_b, *jets):
    start = 2 * CAP
    for jet in jets:
        jet[0:CAP] = dealt[start : start + CAP]
        start = start + CAP

    @pl.when(lax.axis_index("span") == 0)
    def _():
        inner(sizes, direct, room_post, plen_post, dealt, cross_a, cross_b)


def corners(cs, up):
    return [q for q in (Y_UP if up else Y_DOWN) if VELOCITIES[q][0]], cs - 1 if up else 0


def late_kernel(sizes, direct, room_in, plen_post, dealt, a_in, b_in, got_a, got_b, room_post, cross_a, cross_b):
    @pl.when(lax.axis_index("span") > 0)
    def _():
        inner(sizes, direct, room_post, plen_post, dealt, cross_a, cross_b)

    ca, cs, blocks, n_span, per_brick = sizes
    rows = blocks * cs
    even = lax.axis_index("aisle") % 2 == 0
    low = lax.axis_index("span") % 2 == 0
    group = lax.broadcasted_iota(jnp.int32, (rows, LANES), 0) % cs

    def came(q, low, high):
        if VELOCITIES[q][0] == 1:
            return jnp.where(even, got_b[low:high], got_a[low:high])
        return jnp.where(even, got_a[low:high], got_b[low:high])

    def complete(cross, up):
        two, edge = corners(cs, up)
        for q in two:
            slot = (X_UP if VELOCITIES[q][0] == 1 else X_DOWN).index(q)
            x = 0 if VELOCITIES[q][0] == 1 else ca - 1
            k = (Y_UP if up else Y_DOWN).index(q)
            column = turned_to(came(q, slot * rows, (slot + 1) * rows), edge, x)
            cross[k * rows : (k + 1) * rows] = jnp.where(group == x, column, cross[k * rows : (k + 1) * rows])
            at, to = 5 * rows + slot * cs + edge, 5 * rows + k * ca + x
            cross[to : to + 1] = came(q, at, at + 1)

    @pl.when(low)
    def _():
        complete(cross_a, True)
        complete(cross_b, False)

    @pl.when(jnp.logical_not(low))
    def _():
        complete(cross_a, False)
        complete(cross_b, True)


def aisle_kernel(sizes, direct, room_in, plen_in, got_a, got_b, jets, places, room, plen, inflow):
    ca, cs, blocks, n_span, per_brick = sizes
    rows = blocks * cs
    even = lax.axis_index("aisle") % 2 == 0
    for k in range(5):
        for q, x, first, second in ((X_UP[k], 0, got_b, got_a), (X_DOWN[k], ca - 1, got_a, got_b)):
            cy = VELOCITIES[q][1]
            low, high = k * rows, (k + 1) * rows
            room[q, x] = crossed(jnp.where(even, first[low:high], second[low:high]), cy, cs)
            low = 5 * rows + k * cs
            value = jnp.where(even, first[low : low + cs], second[low : low + cs])
            at = x * cs
            if cy == 1:
                plen[q, at : at + 1] = value[0:1]
                plen[q, at + 1 : at + cs] = value[: cs - 1]
            elif cy == -1:
                plen[q, at + cs - 1 : at + cs] = value[cs - 1 : cs]
                plen[q, at : at + cs - 1] = value[1:cs]
            else:
                plen[q, at : at + cs] = value
    here = lax.axis_index("span")

    def put(sums):
        for k in range(5):
            inflow[k] = sums[k]

    def reader(source, b):
        return lambda s, k: source[b * CAP + s, :, k * LANES : (k + 1) * LANES]

    if direct:
        put(jet_sums(lambda k: jnp.zeros((ca * cs, LANES), F32), places,
                     [(here, reader(jets, 0))]))
    else:
        inflow[...] = jnp.zeros_like(inflow)

        def add_brick(b, carry):
            put(jet_sums(lambda k: inflow[k], places, [(b, reader(jets, b))]))
            return carry

        lax.fori_loop(0, n_span, add_brick, 0)


def finish_kernel(sizes, direct, room_in, plen_in, got_a, got_b, places, inflow, *rest):
    *got_jets, room, plen, room_out, plen_out, sems = rest
    ca, cs, blocks, n_span, per_brick = sizes
    rows = blocks * cs
    here = lax.axis_index("span")
    low = here % 2 == 0
    group = lax.broadcasted_iota(jnp.int32, (rows, LANES), 0) % cs

    def enter(got, up):
        planes, y = (Y_UP, 0) if up else (Y_DOWN, cs - 1)
        for k, q in enumerate(planes):
            came = got[k * rows : (k + 1) * rows]
            for x in range(ca):
                room[q, x] = jnp.where(group == y, turned_to(came, x, y), room[q, x])
                at = 5 * rows + k * ca + x
                plen[q, x * cs + y : x * cs + y + 1] = got[at : at + 1]

    @pl.when(low)
    def _():
        enter(got_a, False)

    @pl.when(jnp.logical_not(low))
    def _():
        enter(got_a, True)

    @pl.when(jnp.logical_and(low, here > 0))
    def _():
        enter(got_b, True)

    @pl.when(jnp.logical_and(jnp.logical_not(low), here < n_span - 1))
    def _():
        enter(got_b, False)

    plen_copy = pltpu.make_async_copy(plen, plen_out, sems.at[0])
    plen_copy.start()
    bricks = []
    if direct:
        start = 5 * (rows + cs)
        bricks = [(here ^ 1, lambda s, k: got_a[start + s * 5 + k : start + s * 5 + k + 1])]
        for apart, got in zip((2, 3), got_jets):
            bricks.append((here ^ apart, lambda s, k, got=got: got[s, :, k * LANES : (k + 1) * LANES]))
    sums = jet_sums(lambda k: inflow[k], places, bricks)
    for k, q in enumerate(UPWARD):
        for x in range(ca):
            room[q, x, 0:cs] = room[q, x, 0:cs] + sums[k][x * cs : (x + 1) * cs]
    room_copy = pltpu.make_async_copy(room, room_out, sems.at[1])
    room_copy.start()
    plen_copy.wait()
    room_copy.wait()


def call(kernel, outs, in_specs, out_specs=None, scratch=(), aliases={}, flops=100_000, moved=1_000_000):
    return pl.pallas_call(
        kernel,
        name=kernel.func.__name__,
        out_shape=outs,
        in_specs=in_specs,
        out_specs=[VMEM] * len(outs) if out_specs is None else out_specs,
        scratch_shapes=list(scratch),
        input_output_aliases=aliases,
        cost_estimate=pl.CostEstimate(flops=flops, bytes_accessed=moved, transcendentals=0),
        compiler_params=pltpu.CompilerParams(vmem_limit_bytes=40 * 2**20),
    )


def swap_aisle(value, odd):
    count = lax.axis_size("aisle")
    pairs = [(i, (i ^ 1 if not odd else i + 1 if i % 2 else i - 1) % count) for i in range(count)]
    return lax.ppermute(value, "aisle", pairs)


def swap_span(value, odd):
    count = lax.axis_size("span")
    pairs = []
    for a in range(lax.axis_size("aisle")):
        for s in range(count):
            t = s ^ 1 if not odd else s + 1 if s % 2 else s - 1
            b, t = (a, t) if 0 <= t < count else (a ^ 1, s)
            pairs.append((a * count + s, b * count + t))
    return lax.ppermute(value, ("aisle", "span"), pairs)


def shards(room_pops, plenum_pops, tile_cell, tile_owner, tile_class):
    n_span = lax.axis_size("span")
    _, ca, cs, hr = room_pops.shape
    hp = plenum_pops.shape[3]
    blocks = hr // LANES
    rows = blocks * cs
    tiles = tile_cell.shape[0]
    sizes = (ca, cs, blocks, n_span, tiles // n_span)
    direct = n_span == 4
    near = lambda shape: pltpu.VMEM(shape, F32)
    far = lambda value: pltpu.with_memory_space_constraint(value, pltpu.HBM)
    room_shape, plen_shape = (19, ca, rows, LANES), (19, ca * cs, LANES)
    halo = 5 * (rows + cs)
    halo = halo + -halo % 8
    room = far(room_pops.reshape(19, ca, cs, blocks, LANES).transpose(0, 1, 3, 2, 4).reshape(room_shape))
    plen = far(plenum_pops.reshape(plen_shape))
    tile_cell, tile_owner, tile_class = far(tile_cell), far(tile_owner.reshape(tiles)), far(tile_class)
    numbers = pltpu.SMEM((tiles,), jnp.int32)

    dealt_shape = (n_span * CAP, 1, 5 * hp)
    jet_shapes = [near((count, 1, 5 * hp)) for count in ((CAP + 1, CAP) if direct else ())]
    room_post, plen_post, swap_a, swap_b, dealt = call(
        functools.partial(collide_kernel, sizes, direct),
        [near(room_shape), near(plen_shape), near((halo, LANES)), near((halo + 8, LANES)),
         near(dealt_shape)],
        [HBM] * 5,
        scratch=[near(plen_shape), numbers, numbers, numbers,
                 pltpu.SemaphoreType.DMA((4 + ca,))],
    )(room, plen, tile_cell, tile_owner, tile_class)
    got_b = swap_aisle(swap_b, True)
    got_a = swap_aisle(swap_a, False)

    upto8 = lambda count: count + -count % 8
    wide = upto8(5 * (rows + ca) + (5 * CAP if direct else 0))
    cross_shapes = [near((wide, LANES)), near((wide + 8, LANES))]
    room_post, part_a, part_b, *jets = call(
        functools.partial(early_kernel, sizes, direct),
        [near(room_shape)] + cross_shapes + jet_shapes,
        [VMEM] * 3,
        aliases={0: 0},
    )(room_post, plen_post, dealt)
    if direct:
        own_jets = dealt
        got_jets = [lax.ppermute(jets[apart - 2], "span", [(i, i ^ apart) for i in range(4)]) for apart in (2, 3)]
    else:
        own_jets = lax.all_to_all(dealt, "span", 0, 0, tiled=True)
        got_jets = []
    room_post, cross_a, cross_b = call(
        functools.partial(late_kernel, sizes, direct),
        [near(room_shape)] + cross_shapes,
        [VMEM] * 7,
        aliases={0: 0, 3: 1, 4: 2},
    )(room_post, plen_post, dealt, part_a, part_b, got_a, got_b)
    in_a = swap_span(cross_a, False)
    in_b = swap_span(cross_b, True)

    room_part, plen_part, places = call(
        functools.partial(local_kernel, sizes),
        [near(room_shape), near(plen_shape), near((n_span * CAP + 1, ca * cs, LANES))],
        [VMEM, VMEM, VMEM, HBM, HBM],
        scratch=[numbers, numbers, pltpu.SemaphoreType.DMA((2,))],
        flops=10**9,
    )(room_post, plen_post, cross_a, tile_cell, tile_owner)
    room_part, plen_part, inflow = call(
        functools.partial(aisle_kernel, sizes, direct),
        [near(room_shape), near(plen_shape), near((5, ca * cs, LANES))],
        [VMEM] * 6,
        aliases={0: 0, 1: 1},
    )(room_part, plen_part, got_a, got_b, own_jets, places)

    _, _, room_next, plenum_next = call(
        functools.partial(finish_kernel, sizes, direct),
        [near(room_shape), near(plen_shape), jax.ShapeDtypeStruct(room_shape, F32),
         jax.ShapeDtypeStruct(plen_shape, F32)],
        [VMEM] * (6 + len(got_jets)),
        out_specs=[VMEM, VMEM, HBM, HBM],
        scratch=[pltpu.SemaphoreType.DMA((2,))],
        aliases={0: 0, 1: 1},
    )(room_part, plen_part, in_a, in_b, places, inflow, *got_jets)
    room_next = room_next.reshape(19, ca, blocks, cs, LANES).transpose(0, 1, 3, 2, 4).reshape(room_pops.shape)
    return room_next, plenum_next.reshape(plenum_pops.shape)


def solution(mesh):
    return jax.shard_map(
        shards,
        mesh=mesh,
        in_specs=(
            P(None, "aisle", "span", None),
            P(None, "aisle", "span", None),
            P("aisle"),
            P("aisle", None),
            P("aisle"),
        ),
        out_specs=(P(None, "aisle", "span", None), P(None, "aisle", "span", None)),
        check_vma=False,
    )
```

```python
import functools

import jax
import jax.numpy as jnp
from jax import lax
from jax.experimental import pallas as pl
from jax.experimental.pallas import tpu as pltpu
from jax.sharding import PartitionSpec as P

VELOCITIES = [
    (0, 0, 0),
    (1, 0, 0),
    (-1, 0, 0),
    (0, 1, 0),
    (0, -1, 0),
    (0, 0, 1),
    (0, 0, -1),
    (1, 1, 0),
    (-1, -1, 0),
    (1, -1, 0),
    (-1, 1, 0),
    (1, 0, 1),
    (-1, 0, -1),
    (1, 0, -1),
    (-1, 0, 1),
    (0, 1, 1),
    (0, -1, -1),
    (0, 1, -1),
    (0, -1, 1),
]
UPWARD = [5, 11, 14, 15, 18]
OMEGA = 1.25
CAP = 4
X_UP = [q for q in range(19) if VELOCITIES[q][0] == 1]
X_DOWN = [q for q in range(19) if VELOCITIES[q][0] == -1]
Y_UP = [q for q in range(19) if VELOCITIES[q][1] == 1]
Y_DOWN = [q for q in range(19) if VELOCITIES[q][1] == -1]
F32 = jnp.float32
LANES = 128
VMEM = pl.BlockSpec(memory_space=pltpu.VMEM)
HBM = pl.BlockSpec(memory_space=pltpu.HBM)


def collide(g):
    total = lambda i: g[i] + g[i + 1]
    apart = lambda i: g[i] - g[i + 1]
    dx, dy, dz = apart(1), apart(3), apart(5)
    d7, d9, d11, d13, d15, d17 = (apart(i) for i in (7, 9, 11, 13, 15, 17))
    edges = (total(7) + total(9)) + (total(11) + total(13)) + (total(15) + total(17))
    faces = total(1) + total(3) + total(5)
    rho = g[0] * (1.0 / 3.0) + faces * (1.0 / 18.0) + edges * (1.0 / 36.0)
    mx = dx * (1.0 / 18.0) + ((d7 + d9) + (d11 + d13)) * (1.0 / 36.0)
    my = dy * (1.0 / 18.0) + ((d7 - d9) + (d15 + d17)) * (1.0 / 36.0)
    mz = dz * (1.0 / 18.0) + ((d11 - d13) + (d15 - d17)) * (1.0 / 36.0)
    inv = 1.0 / rho
    base = OMEGA * rho - (1.5 * OMEGA) * inv * (mx * mx + my * my + mz * mz)
    square = (4.5 * OMEGA) * inv
    out = [None] * 19
    out[0] = base + (1.0 - OMEGA) * g[0]
    along = {1: mx, 3: my, 5: mz, 7: mx + my, 9: mx - my, 11: mx + mz, 13: mx - mz, 15: my + mz, 17: my - mz}
    for i, c in along.items():
        even = base + square * c * c
        odd = (3.0 * OMEGA) * c
        out[i] = (even + odd) + (1.0 - OMEGA) * g[i]
        out[i + 1] = (even - odd) + (1.0 - OMEGA) * g[i + 1]
    return out


def raised(value, cz, rows):
    if cz == 0:
        return value
    lane = lax.broadcasted_iota(jnp.int32, value.shape, 1)
    row = lax.broadcasted_iota(jnp.int32, value.shape, 0)
    total = value.shape[0]
    shift, edge = (1, 0) if cz == 1 else (LANES - 1, LANES - 1)
    turned = pltpu.roll(value, shift, 1)
    if rows == total:
        return jnp.where(lane == edge, value, turned)
    carried = pltpu.roll(turned, rows if cz == 1 else total - rows, 0)
    clamped = row < rows if cz == 1 else row >= total - rows
    return jnp.where(lane == edge, jnp.where(clamped, value, carried), turned)


def crossed(value, cy, cs):
    if cy == 0:
        return value
    row = lax.broadcasted_iota(jnp.int32, value.shape, 0) % cs
    turned = pltpu.roll(value, 1 if cy == 1 else value.shape[0] - 1, 0)
    return jnp.where(row == (0 if cy == 1 else cs - 1), value, turned)


def shifted(value, by):
    return pltpu.roll(value, by % value.shape[0], 0) if by else value


def turned_to(value, source, dest):
    return shifted(value, dest - source)


def repeat(count, body, start):
    if count > 8:
        return lax.fori_loop(0, count, body, start)
    for i in range(count):
        start = body(i, start)
    return start


def collide_plane(room, x):
    for r in range(0, room.shape[2], 8):
        post = collide([room[q, x, r : r + 8] for q in range(19)])
        for q in range(19):
            room[q, x, r : r + 8] = post[q]


def collide_kernel(sizes, direct, room_in, plen_in, cell_in, owner_in, class_in, room_post, plen_post, swap_a, swap_b,
                   dealt, plen_buf, cells, owners, classes, sems):
    ca, cs, blocks, n_span, per_brick = sizes
    rows = blocks * cs
    copies = [pltpu.make_async_copy(src, dst, sems.at[i]) for i, (src, dst) in enumerate(
        ((plen_in, plen_buf), (cell_in, cells), (owner_in, owners), (class_in, classes)))]
    order = [0, ca - 1] + list(range(1, ca - 1))
    planes = [pltpu.make_async_copy(room_in.at[:, x], room_post.at[:, x], sems.at[4 + x]) for x in order]
    for copy in copies[1:] + copies[:1] + planes:
        copy.start()
    dealt[...] = jnp.zeros_like(dealt)
    for copy in copies[1:4]:
        copy.wait()
    here = lax.axis_index("span")
    first = here * per_brick

    def deal(i, slot):
        owner = owners[first + i]
        to = (owner ^ here if direct else owner) * CAP + slot
        return to, 0.15 * (classes[first + i].astype(F32) + 1.0), cells[first + i]

    tiles = []
    if direct:
        named = [owners[first + i] for i in range(per_brick)]
        for i in range(per_brick):
            tiles.append(deal(i, sum([(named[j] == named[i]).astype(jnp.int32) for j in range(i)], jnp.int32(0))))
    copies[0].wait()
    for r in range(0, ca * cs, 8):
        post = collide([plen_buf[q, r : r + 8] for q in range(19)])
        for q in range(19):
            plen_post[q, r : r + 8] = post[q]

    def put(to, share, cell):
        for k, q in enumerate(UPWARD):
            dealt[to, :, k * LANES : (k + 1) * LANES] = share * plen_post[q, pl.ds(cell, 1), :]

    for tile in tiles:
        put(*tile)

    def send_jet(i, carry):
        same = lambda j, n: n + (owners[first + j] == owners[first + i]).astype(jnp.int32)
        put(*deal(i, lax.fori_loop(0, i, same, 0)))
        return carry

    if not direct:
        lax.fori_loop(0, per_brick, send_jet, 0)

    for i in range(2):
        planes[i].wait()
        collide_plane(room_post, order[i])
    even = lax.axis_index("aisle") % 2 == 0
    for k in range(5):
        up, down = X_UP[k], X_DOWN[k]
        rising = raised(room_post[up, ca - 1], VELOCITIES[up][2], cs)
        falling = raised(room_post[down, 0], VELOCITIES[down][2], cs)
        swap_a[k * rows : (k + 1) * rows] = jnp.where(even, rising, falling)
        swap_b[k * rows : (k + 1) * rows] = jnp.where(even, falling, rising)
        rising = raised(plen_post[up, (ca - 1) * cs : ca * cs], VELOCITIES[up][2], cs)
        falling = raised(plen_post[down, 0:cs], VELOCITIES[down][2], cs)
        low = 5 * rows + k * cs
        swap_a[low : low + cs] = jnp.where(even, rising, falling)
        swap_b[low : low + cs] = jnp.where(even, falling, rising)
    for i in range(2, ca):
        planes[i].wait()


def jet_sums(start, places, bricks):
    sums = [start(k) for k in range(5)]
    for b, jet in bricks:
        for s in range(CAP):
            marks = places[b * CAP + s]
            sums = [total + marks * jet(s, k) for k, total in enumerate(sums)]
    return sums


def local_kernel(sizes, room_post, plen_post, crossing, cell_in, owner_in, room_part, plen_part, places, cells, owners,
                 sems):
    del crossing
    ca, cs, blocks, n_span, per_brick = sizes
    rows = blocks * cs
    copies = [pltpu.make_async_copy(src, dst, sems.at[i]) for i, (src, dst) in enumerate(
        ((cell_in, cells), (owner_in, owners)))]
    for copy in copies:
        copy.start()
    for q in range(19):
        cx, cy, cz = VELOCITIES[q]
        for x in range(ca):
            if 0 <= x - cx < ca:
                room_part[q, x] = crossed(raised(room_post[q, x - cx], cz, cs), cy, cs)
        plen_part[q] = crossed(shifted(raised(plen_post[q], cz, ca * cs), cx * cs), cy, cs)
    places[0 : n_span * CAP] = jnp.zeros((n_span * CAP, ca * cs, LANES), F32)
    here = lax.axis_index("span")
    row = lax.broadcasted_iota(jnp.int32, (ca * cs, LANES), 0)
    for copy in copies:
        copy.wait()

    def brick(b, carry):
        def place(i, slot):
            t = b * per_brick + i
            mine = owners[t] == here
            places[jnp.where(mine, b * CAP + slot, n_span * CAP)] = (row == cells[t]).astype(F32)
            return slot + mine.astype(jnp.int32)

        repeat(per_brick, place, 0)
        return carry

    repeat(n_span, brick, 0)


def inner(sizes, direct, room_post, plen_post, jets, cross_a, cross_b):
    ca, cs, blocks, n_span, per_brick = sizes
    rows = blocks * cs
    low = lax.axis_index("span") % 2 == 0
    group = lax.broadcasted_iota(jnp.int32, (rows, LANES), 0) % cs
    for x in range(1, ca - 1):
        collide_plane(room_post, x)
    for k in range(5):
        sides, near = [], []
        for q, edge in ((Y_UP[k], cs - 1), (Y_DOWN[k], 0)):
            cx, cy, cz = VELOCITIES[q]
            packed = None
            for x in range(max(cx, 0), ca + min(cx, 0)):
                ready = turned_to(raised(room_post[q, x - cx], cz, cs), edge, x)
                packed = ready if packed is None else jnp.where(group == x, ready, packed)
            sides.append(packed)
            near.append(shifted(raised(plen_post[q], cz, ca * cs), cx * cs - edge))
        cross_a[k * rows : (k + 1) * rows] = jnp.where(low, sides[0], sides[1])
        cross_b[k * rows : (k + 1) * rows] = jnp.where(low, sides[1], sides[0])
        first, second = jnp.where(low, near[0], near[1]), jnp.where(low, near[1], near[0])
        for x in range(ca):
            to = 5 * rows + k * ca + x
            cross_a[to : to + 1] = first[x * cs : x * cs + 1]
            cross_b[to : to + 1] = second[x * cs : x * cs + 1]
    if direct:
        for s in range(CAP):
            for k in range(5):
                to = 5 * (rows + ca) + s * 5 + k
                cross_a[to : to + 1] = jets[CAP + s, :, k * LANES : (k + 1) * LANES]


def early_kernel(sizes, direct, room_in, plen_post, dealt, room_post, cross_a, cross_b, *jets):
    start = 2 * CAP
    for jet in jets:
        jet[0:CAP] = dealt[start : start + CAP]
        start = start + CAP

    @pl.when(lax.axis_index("span") == 0)
    def _():
        inner(sizes, direct, room_post, plen_post, dealt, cross_a, cross_b)


def late_kernel(sizes, direct, room_in, plen_post, dealt, a_in, b_in, room_post, cross_a, cross_b):
    @pl.when(lax.axis_index("span") > 0)
    def _():
        inner(sizes, direct, room_post, plen_post, dealt, cross_a, cross_b)


def corners(cs, up):
    return [q for q in (Y_UP if up else Y_DOWN) if VELOCITIES[q][0]], cs - 1 if up else 0


def pack_kernel(sizes, got_a, got_b, part_a, part_b, cross_a, cross_b):
    ca, cs, blocks, n_span, per_brick = sizes
    rows = blocks * cs
    even = lax.axis_index("aisle") % 2 == 0
    low = lax.axis_index("span") % 2 == 0
    group = lax.broadcasted_iota(jnp.int32, (rows, LANES), 0) % cs
    cross_a[...] = part_a[...]
    cross_b[...] = part_b[...]

    def came(q, low, high):
        if VELOCITIES[q][0] == 1:
            return jnp.where(even, got_b[low:high], got_a[low:high])
        return jnp.where(even, got_a[low:high], got_b[low:high])

    def complete(cross, up):
        two, edge = corners(cs, up)
        for q in two:
            slot = (X_UP if VELOCITIES[q][0] == 1 else X_DOWN).index(q)
            x = 0 if VELOCITIES[q][0] == 1 else ca - 1
            k = (Y_UP if up else Y_DOWN).index(q)
            column = turned_to(came(q, slot * rows, (slot + 1) * rows), edge, x)
            cross[k * rows : (k + 1) * rows] = jnp.where(group == x, column, cross[k * rows : (k + 1) * rows])
            at, to = 5 * rows + slot * cs + edge, 5 * rows + k * ca + x
            cross[to : to + 1] = came(q, at, at + 1)

    @pl.when(low)
    def _():
        complete(cross_a, True)
        complete(cross_b, False)

    @pl.when(jnp.logical_not(low))
    def _():
        complete(cross_a, False)
        complete(cross_b, True)


def aisle_kernel(sizes, direct, room_in, plen_in, got_a, got_b, jets, places, room, plen, inflow):
    ca, cs, blocks, n_span, per_brick = sizes
    rows = blocks * cs
    even = lax.axis_index("aisle") % 2 == 0
    for k in range(5):
        for q, x, first, second in ((X_UP[k], 0, got_b, got_a), (X_DOWN[k], ca - 1, got_a, got_b)):
            cy = VELOCITIES[q][1]
            low, high = k * rows, (k + 1) * rows
            room[q, x] = crossed(jnp.where(even, first[low:high], second[low:high]), cy, cs)
            low = 5 * rows + k * cs
            value = jnp.where(even, first[low : low + cs], second[low : low + cs])
            at = x * cs
            if cy == 1:
                plen[q, at : at + 1] = value[0:1]
                plen[q, at + 1 : at + cs] = value[: cs - 1]
            elif cy == -1:
                plen[q, at + cs - 1 : at + cs] = value[cs - 1 : cs]
                plen[q, at : at + cs - 1] = value[1:cs]
            else:
                plen[q, at : at + cs] = value
    here = lax.axis_index("span")

    def put(sums):
        for k in range(5):
            inflow[k] = sums[k]

    def reader(source, b):
        return lambda s, k: source[b * CAP + s, :, k * LANES : (k + 1) * LANES]

    if direct:
        put(jet_sums(lambda k: jnp.zeros((ca * cs, LANES), F32), places,
                     [(here, reader(jets, 0))]))
    else:
        inflow[...] = jnp.zeros_like(inflow)

        def add_brick(b, carry):
            put(jet_sums(lambda k: inflow[k], places, [(b, reader(jets, b))]))
            return carry

        lax.fori_loop(0, n_span, add_brick, 0)


def finish_kernel(sizes, direct, room_in, plen_in, got_a, got_b, places, inflow, *rest):
    *got_jets, room, plen, room_out, plen_out, sems = rest
    ca, cs, blocks, n_span, per_brick = sizes
    rows = blocks * cs
    here = lax.axis_index("span")
    low = here % 2 == 0
    group = lax.broadcasted_iota(jnp.int32, (rows, LANES), 0) % cs

    def enter(got, up):
        planes, y = (Y_UP, 0) if up else (Y_DOWN, cs - 1)
        for k, q in enumerate(planes):
            came = got[k * rows : (k + 1) * rows]
            for x in range(ca):
                room[q, x] = jnp.where(group == y, turned_to(came, x, y), room[q, x])

    def enter_plenum(got, up):
        planes, y = (Y_UP, 0) if up else (Y_DOWN, cs - 1)
        for k, q in enumerate(planes):
            for x in range(ca):
                at = 5 * rows + k * ca + x
                plen[q, x * cs + y : x * cs + y + 1] = got[at : at + 1]

    def entering(enter):
        @pl.when(low)
        def _():
            enter(got_a, False)

        @pl.when(jnp.logical_not(low))
        def _():
            enter(got_a, True)

        @pl.when(jnp.logical_and(low, here > 0))
        def _():
            enter(got_b, True)

        @pl.when(jnp.logical_and(jnp.logical_not(low), here < n_span - 1))
        def _():
            enter(got_b, False)

    entering(enter)
    bricks = []
    if direct:
        start = 5 * (rows + cs)
        bricks = [(here ^ 1, lambda s, k: got_a[start + s * 5 + k : start + s * 5 + k + 1])]
        for apart, got in zip((2, 3), got_jets):
            bricks.append((here ^ apart, lambda s, k, got=got: got[s, :, k * LANES : (k + 1) * LANES]))
    sums = jet_sums(lambda k: inflow[k], places, bricks)
    for k, q in enumerate(UPWARD):
        for x in range(ca):
            room[q, x, 0:cs] = room[q, x, 0:cs] + sums[k][x * cs : (x + 1) * cs]
    room_copy = pltpu.make_async_copy(room, room_out, sems.at[1])
    room_copy.start()
    entering(enter_plenum)
    plen_copy = pltpu.make_async_copy(plen, plen_out, sems.at[0])
    plen_copy.start()
    plen_copy.wait()
    room_copy.wait()


def call(kernel, outs, in_specs, out_specs=None, scratch=(), aliases={}, flops=100_000, moved=1_000_000):
    return pl.pallas_call(
        kernel,
        name=kernel.func.__name__,
        out_shape=outs,
        in_specs=in_specs,
        out_specs=[VMEM] * len(outs) if out_specs is None else out_specs,
        scratch_shapes=list(scratch),
        input_output_aliases=aliases,
        cost_estimate=pl.CostEstimate(flops=flops, bytes_accessed=moved, transcendentals=0),
        compiler_params=pltpu.CompilerParams(vmem_limit_bytes=40 * 2**20),
    )


def swap_aisle(value, odd):
    count = lax.axis_size("aisle")
    pairs = [(i, (i ^ 1 if not odd else i + 1 if i % 2 else i - 1) % count) for i in range(count)]
    return lax.ppermute(value, "aisle", pairs)


def swap_span(value, odd):
    count = lax.axis_size("span")
    pairs = []
    for a in range(lax.axis_size("aisle")):
        for s in range(count):
            t = s ^ 1 if not odd else s + 1 if s % 2 else s - 1
            b, t = (a, t) if 0 <= t < count else (a ^ 1, s)
            pairs.append((a * count + s, b * count + t))
    return lax.ppermute(value, ("aisle", "span"), pairs)


def shards(room_pops, plenum_pops, tile_cell, tile_owner, tile_class):
    n_span = lax.axis_size("span")
    _, ca, cs, hr = room_pops.shape
    hp = plenum_pops.shape[3]
    blocks = hr // LANES
    rows = blocks * cs
    tiles = tile_cell.shape[0]
    sizes = (ca, cs, blocks, n_span, tiles // n_span)
    direct = n_span == 4
    near = lambda shape: pltpu.VMEM(shape, F32)
    far = lambda value: pltpu.with_memory_space_constraint(value, pltpu.HBM)
    room_shape, plen_shape = (19, ca, rows, LANES), (19, ca * cs, LANES)
    halo = 5 * (rows + cs)
    halo = halo + -halo % 8
    room = far(room_pops.reshape(19, ca, cs, blocks, LANES).transpose(0, 1, 3, 2, 4).reshape(room_shape))
    plen = far(plenum_pops.reshape(plen_shape))
    tile_cell, tile_owner, tile_class = far(tile_cell), far(tile_owner.reshape(tiles)), far(tile_class)
    numbers = pltpu.SMEM((tiles,), jnp.int32)

    dealt_shape = (n_span * CAP, 1, 5 * hp)
    jet_shapes = [near((count, 1, 5 * hp)) for count in ((CAP + 1, CAP) if direct else ())]
    room_post, plen_post, swap_a, swap_b, dealt = call(
        functools.partial(collide_kernel, sizes, direct),
        [near(room_shape), near(plen_shape), near((halo, LANES)), near((halo + 8, LANES)),
         near(dealt_shape)],
        [HBM] * 5,
        scratch=[near(plen_shape), numbers, numbers, numbers,
                 pltpu.SemaphoreType.DMA((4 + ca,))],
    )(room, plen, tile_cell, tile_owner, tile_class)
    got_b = swap_aisle(swap_b, True)
    got_a = swap_aisle(swap_a, False)

    upto8 = lambda count: count + -count % 8
    wide = upto8(5 * (rows + ca) + (5 * CAP if direct else 0))
    cross_shapes = [near((wide, LANES)), near((wide + 8, LANES))]
    room_post, part_a, part_b, *jets = call(
        functools.partial(early_kernel, sizes, direct),
        [near(room_shape)] + cross_shapes + jet_shapes,
        [VMEM] * 3,
        aliases={0: 0},
    )(room_post, plen_post, dealt)
    if direct:
        own_jets = dealt
        got_jets = [lax.ppermute(jets[apart - 2], "span", [(i, i ^ apart) for i in range(4)]) for apart in (2, 3)]
    else:
        own_jets = lax.all_to_all(dealt, "span", 0, 0, tiled=True)
        got_jets = []
    room_post, part_a, part_b = call(
        functools.partial(late_kernel, sizes, direct),
        [near(room_shape)] + cross_shapes,
        [VMEM] * 5,
        aliases={0: 0, 3: 1, 4: 2},
    )(room_post, plen_post, dealt, part_a, part_b)
    cross_a, cross_b = call(
        functools.partial(pack_kernel, sizes),
        cross_shapes,
        [VMEM] * 4,
    )(got_a, got_b, part_a, part_b)
    in_a = swap_span(cross_a, False)
    in_b = swap_span(cross_b, True)

    room_part, plen_part, places = call(
        functools.partial(local_kernel, sizes),
        [near(room_shape), near(plen_shape), near((n_span * CAP + 1, ca * cs, LANES))],
        [VMEM, VMEM, VMEM, HBM, HBM],
        scratch=[numbers, numbers, pltpu.SemaphoreType.DMA((2,))],
        flops=10**9,
    )(room_post, plen_post, cross_a, tile_cell, tile_owner)
    room_part, plen_part, inflow = call(
        functools.partial(aisle_kernel, sizes, direct),
        [near(room_shape), near(plen_shape), near((5, ca * cs, LANES))],
        [VMEM] * 6,
        aliases={0: 0, 1: 1},
    )(room_part, plen_part, got_a, got_b, own_jets, places)

    _, _, room_next, plenum_next = call(
        functools.partial(finish_kernel, sizes, direct),
        [near(room_shape), near(plen_shape), jax.ShapeDtypeStruct(room_shape, F32),
         jax.ShapeDtypeStruct(plen_shape, F32)],
        [VMEM] * (6 + len(got_jets)),
        out_specs=[VMEM, VMEM, HBM, HBM],
        scratch=[pltpu.SemaphoreType.DMA((2,))],
        aliases={0: 0, 1: 1},
    )(room_part, plen_part, in_a, in_b, places, inflow, *got_jets)
    room_next = room_next.reshape(19, ca, blocks, cs, LANES).transpose(0, 1, 3, 2, 4).reshape(room_pops.shape)
    return room_next, plenum_next.reshape(plenum_pops.shape)


def solution(mesh):
    return jax.shard_map(
        shards,
        mesh=mesh,
        in_specs=(
            P(None, "aisle", "span", None),
            P(None, "aisle", "span", None),
            P("aisle"),
            P("aisle", None),
            P("aisle"),
        ),
        out_specs=(P(None, "aisle", "span", None), P(None, "aisle", "span", None)),
        check_vma=False,
    )
```
